32 devices in a mesh: head: 4 (over z), blk: 8 (over y, x, core).
Axes of the slice: x: 2, y: 2, z: 4, core: 2. Of those that a mesh axis runs over, the one named last changes fastest.
Arguments:
- tokens: bfloat16 [2, 2048, 1536], P(None, ('head', 'blk')), may hold values from -6 to 6
- lengths: int32 [2], replicated, may hold values from 256 to 2048, as said below
- routes: int32 [2, 2, 2048, 8], P(None, None, ('head', 'blk')), may hold values from 0 to 39, as said below
- queue_ranks: int32 [2, 2, 2048, 8], P(None, None, ('head', 'blk')), may hold values from 0 to 26, as said below
- query_key_value_weight: bfloat16 [2, 1536, 2560], P(None, ('head', 'blk')), may hold values from -0.15625 to 0.15625
- w_out: bfloat16 [2, 1536, 1536], P(None, ('head', 'blk')), may hold values from -2.5 to 2.5
- router: bfloat16 [2, 1536, 40], P(None, ('head', 'blk')), may hold values from -0.078125 to 0.078125
- norm_gains: bfloat16 [2, 2, 1536], P(None, None, ('head', 'blk')), may hold values from 0.5 to 1.5
- w_in: bfloat16 [2, 40, 1536, 1024], P(None, 'head', 'blk'), may hold values from -0.15625 to 0.15625
- w_down: bfloat16 [2, 40, 512, 1536], P(None, 'head', 'blk'), may hold values from -0.75 to 0.75
- cotangent: bfloat16 [2, 2048, 1536], P(None, ('head', 'blk')), may hold values from -6 to 6
Outputs:
- out: bfloat16 [2, 2048, 1536], P(None, ('head', 'blk'))
- grad_tokens: float32 [2, 2048, 1536], P(None, ('head', 'blk'))
- grad_w_qkv: float32 [2, 1536, 2560], P(None, ('head', 'blk'))
- grad_w_out: float32 [2, 1536, 1536], P(None, ('head', 'blk'))
- grad_router: float32 [2, 1536, 40], P(None, ('head', 'blk'))
- grad_attn_gains: float32 [2, 1536], P(None, ('head', 'blk'))
- grad_expert_gains: float32 [2, 1536], P(None, ('head', 'blk'))
- grad_w_in: float32 [2, 40, 1536, 1024], P(None, 'head', 'blk')
- grad_w_down: float32 [2, 40, 512, 1536], P(None, 'head', 'blk')
The draws below stay inside these ranges and needn't reach their ends.
Inputs may be any that keep to these rules, and one draw needn't show every extreme that they name: One slot, chosen by the seed, is full; in each slot positions from lengths[s] on are padding. `routes`: each token names 8 different experts in each layer. `queue_ranks`: positions are cut into aligned blocks of 64; a block's pairs are those of its positions in both slots. In each layer and block, the pairs of valid tokens naming one expert hold distinct ranks 0, 1, 2 and so on, with every rank from 26 on written as 26; every pair of a padding token has rank 26.
All inputs are finite; a program needn't handle non-finite values.
Results may differ from the reference program's by a relative error of at most 0.028.
Values may be sent and summed in bfloat16 or wider, within the bound.
A program may use at most 384 MiB of HBM per device.

```python
import jax
import jax.numpy as jnp
from jax import lax

MODEL_WIDTH = 1536
QUERY_HEAD_COUNT = 24
KEY_VALUE_HEADS = 8
HEAD_SIZE = 64
FF = 512
EXPERTS = 40
TOP = 8
DECODER_LAYERS = 2
SEQUENCE_SLOTS = 2
SEQ_DEV = 64
SLOT_LENGTH = 2048
CAP = 26


def shared_plan(key):
    devices = SLOT_LENGTH // SEQ_DEV
    full_slot = jax.random.randint(jax.random.fold_in(key, 101), (), 0, SEQUENCE_SLOTS)
    shorter = jax.random.randint(jax.random.fold_in(key, 102), (SEQUENCE_SLOTS,), SLOT_LENGTH // 8, SLOT_LENGTH // 2 + 1)
    lengths = jnp.where(jnp.arange(SEQUENCE_SLOTS) == full_slot, SLOT_LENGTH, shorter).astype(jnp.int32)
    live_rows = jnp.arange(SLOT_LENGTH)[None, :] < lengths[:, None]
    pair_count = SEQUENCE_SLOTS * SEQ_DEV * TOP
    expert_ids = jnp.arange(EXPERTS, dtype=jnp.int32)
    route_list = []
    rank_list = []

    def by_device(array):
        return array.reshape(SEQUENCE_SLOTS, devices, SEQ_DEV, TOP).transpose(1, 0, 2, 3).reshape(devices, pair_count)
    for layer_index in range(DECODER_LAYERS):
        layer_key = jax.random.fold_in(key, 200 + layer_index)
        expert_order = jax.random.permutation(jax.random.fold_in(layer_key, 1), EXPERTS).astype(jnp.int32)
        busiest = jnp.argmax(expert_order)
        forced = (jnp.arange(SEQUENCE_SLOTS)[:, None] == full_slot) & (jnp.arange(SLOT_LENGTH)[None, :] % SEQ_DEV < CAP)
        noise_draw = jax.random.randint(jax.random.fold_in(layer_key, 2), (SEQUENCE_SLOTS, SLOT_LENGTH, EXPERTS), 0, 4096)
        forced_lift = jnp.where(forced[:, :, None] & (expert_ids == busiest)[None, None, :], 100000, 0)
        scores = (noise_draw + expert_order[None, None, :] * 60 + forced_lift) * 64 + expert_ids
        routes = lax.top_k(scores, TOP)[1].astype(jnp.int32)
        live_pairs = jnp.broadcast_to(live_rows[:, :, None], routes.shape)
        pair_group = jnp.where(by_device(live_pairs), by_device(routes), EXPERTS)
        priority = jax.random.randint(jax.random.fold_in(layer_key, 3), (devices, pair_count), 0, 4096)
        sort_key = (pair_group * 4096 + priority) * pair_count + jnp.arange(pair_count, dtype=jnp.int32)
        order_pairs = jnp.argsort(sort_key, axis=1)
        sorted_group = jnp.take_along_axis(pair_group, order_pairs, axis=1)
        counts = jnp.sum((pair_group[:, :, None] == jnp.arange(EXPERTS + 1)).astype(jnp.int32), axis=1)
        starts = jnp.cumsum(counts, axis=1) - counts
        places = jnp.arange(pair_count, dtype=jnp.int32)[None, :] - jnp.take_along_axis(starts, sorted_group, axis=1)
        rank_values = jnp.take_along_axis(places, jnp.argsort(order_pairs, axis=1), axis=1)
        rank_values = jnp.where(pair_group < EXPERTS, jnp.minimum(rank_values, CAP), CAP)
        rank_list.append(rank_values.reshape(devices, SEQUENCE_SLOTS, SEQ_DEV, TOP).transpose(1, 0, 2, 3).reshape(SEQUENCE_SLOTS, SLOT_LENGTH, TOP).astype(jnp.int32))
        route_list.append(routes)
    return (lengths, jnp.stack(route_list), jnp.stack(rank_list))


def draw_lengths(key, part):
    return shared_plan(key)[0]


def draw_routes(key, part):
    return shared_plan(key)[1]


def draw_queue_ranks(key, part):
    return shared_plan(key)[2]


def shard_levels(rng, extent, pieces, low, high):
    level = 1.0
    for axis_at, blocks in pieces:
        draws = jax.random.uniform(jax.random.fold_in(jax.random.fold_in(rng, 6), axis_at), (blocks,), jnp.float32, low / len(pieces), high / len(pieces))
        level = level * jnp.repeat(jnp.exp(draws), extent[axis_at] // blocks).reshape((-1,) + (1,) * (len(extent) - 1 - axis_at))
    return level


def scatter_about(stream_key, extent, deviation, reach, pieces=(), kind=jnp.bfloat16):
    level = shard_levels(stream_key, extent, pieces, -0.22, 0.18) if pieces else 1.0
    values = jax.random.normal(stream_key, extent, jnp.float32) * deviation * level
    return jnp.minimum(jnp.maximum(values, -reach), reach).astype(kind)


def setup_inputs(seed: int = 0) -> dict:
    splits = jax.random.split(jax.random.key(seed), 12)
    tokens = scatter_about(splits[0], (SEQUENCE_SLOTS, SLOT_LENGTH, MODEL_WIDTH), 1.0, 6.0, ((1, 32),))
    lengths = draw_lengths(jax.random.fold_in(splits[11], 71), 0)
    routes = draw_routes(jax.random.fold_in(splits[11], 71), 0)
    queue_ranks = draw_queue_ranks(jax.random.fold_in(splits[11], 71), 0)
    query_key_value_weight = scatter_about(splits[4], (DECODER_LAYERS, MODEL_WIDTH, QUERY_HEAD_COUNT * HEAD_SIZE + 2 * KEY_VALUE_HEADS * HEAD_SIZE), MODEL_WIDTH ** -0.5, 0.15625, ((1, 32),))
    w_out = scatter_about(splits[5], (DECODER_LAYERS, QUERY_HEAD_COUNT * HEAD_SIZE, MODEL_WIDTH), (QUERY_HEAD_COUNT * HEAD_SIZE // 256) ** -0.5, 2.5, ((1, 32),))
    router = scatter_about(splits[6], (DECODER_LAYERS, MODEL_WIDTH, EXPERTS), (4 * MODEL_WIDTH) ** -0.5, 0.078125, ((1, 32),))
    norm_gains = jnp.clip(1.0 + 0.1 * jax.random.normal(splits[7], (DECODER_LAYERS, 2, MODEL_WIDTH), jnp.float32), 0.5, 1.5).astype(jnp.bfloat16)
    w_in = scatter_about(splits[8], (DECODER_LAYERS, EXPERTS, MODEL_WIDTH, 2 * FF), MODEL_WIDTH ** -0.5, 0.15625, ((1, 4), (2, 8)))
    w_down = scatter_about(splits[9], (DECODER_LAYERS, EXPERTS, FF, MODEL_WIDTH), (FF // 8) ** -0.5, 0.75, ((1, 4), (2, 8)))
    cotangent = scatter_about(splits[10], (SEQUENCE_SLOTS, SLOT_LENGTH, MODEL_WIDTH), 1.0, 6.0, ((1, 32),))
    return {"tokens": tokens, "lengths": lengths, "routes": routes, "queue_ranks": queue_ranks, "query_key_value_weight": query_key_value_weight, "w_out": w_out, "router": router, "norm_gains": norm_gains, "w_in": w_in, "w_down": w_down, "cotangent": cotangent}


highest = lax.Precision.HIGHEST
epsilon = 1e-06
negative = -1e+30
theta_log = 9.210340371976184

@jax.custom_vjp
def low(v):
    return lax.optimization_barrier(v.astype(jnp.bfloat16)).astype(jnp.float32)

@jax.custom_vjp
def low_back(v):
    return v

def low_keep(v):
    return (low(v), None)

def low_pass(kept, grad):
    return (grad,)

def back_keep(v):
    return (v, None)

def back_low(kept, grad):
    return (low(grad),)
low.defvjp(low_keep, low_pass)
low_back.defvjp(back_keep, back_low)

def round_both(value):
    return low_back(low(value))

def rotate(values, positions, direction):
    half_width = values.shape[-1] // 2
    frequency = jnp.exp(jnp.arange(half_width, dtype=jnp.float32) * (-2.0 * theta_log / values.shape[-1]))
    angles = positions[:, None, None] * frequency
    cosine = jnp.cos(angles)
    sine_part = jnp.sin(angles) * direction
    first_half = values[..., :half_width]
    second_half = values[..., half_width:]
    return jnp.concatenate([first_half * cosine - second_half * sine_part, second_half * cosine + first_half * sine_part], axis=-1)

def norm_rows(hidden, gain_row):
    inverse = lax.rsqrt(lax.optimization_barrier(jnp.mean(hidden * hidden, axis=-1, keepdims=True)) + epsilon)
    return hidden * inverse * gain_row

def attend(query_matrix, key_rows, value_rows, length):
    block_size = min(512, SLOT_LENGTH)
    key_places = jnp.arange(SLOT_LENGTH, dtype=jnp.int32)

    def one_block(offset):
        query_rows = lax.dynamic_slice_in_dim(query_matrix, offset, block_size, 0)
        query_places = offset + jnp.arange(block_size, dtype=jnp.int32)
        scores = low_back(jnp.einsum('qgrd,kgd->grqk', query_rows, key_rows, precision=highest) * 0.125)
        allowed = (key_places[None, :] <= query_places[:, None]) & (key_places[None, :] < length)
        scores = jnp.where(allowed, scores, negative)
        probabilities = low(jax.nn.softmax(scores, axis=-1))
        return jnp.einsum('grqk,kgd->qgrd', probabilities, value_rows, precision=highest)
    starts = jnp.arange(0, SLOT_LENGTH, block_size, dtype=jnp.int32)
    outputs = lax.map(jax.checkpoint(one_block), starts)
    return outputs.reshape(SLOT_LENGTH, QUERY_HEAD_COUNT * HEAD_SIZE)

def one_layer(hidden, weights, routes, queue_ranks, valid_rows, lengths):
    query_key_value_weight, w_out, router, norm_gains, w_in, w_down = weights
    places = jnp.arange(SLOT_LENGTH, dtype=jnp.int32).astype(jnp.float32)
    normed_a = low(norm_rows(hidden, norm_gains[0]))
    projected_rows = low_back(jnp.einsum('std,de->ste', normed_a, query_key_value_weight, precision=highest))
    query_matrix = round_both(rotate(projected_rows[..., :QUERY_HEAD_COUNT * HEAD_SIZE].reshape(SEQUENCE_SLOTS, SLOT_LENGTH, QUERY_HEAD_COUNT, HEAD_SIZE), places, 1.0))
    pair_columns = projected_rows[..., QUERY_HEAD_COUNT * HEAD_SIZE:].reshape(SEQUENCE_SLOTS, SLOT_LENGTH, KEY_VALUE_HEADS, 2, HEAD_SIZE)
    key_rows = round_both(rotate(pair_columns[:, :, :, 0, :], places, 1.0))
    value_rows = round_both(pair_columns[:, :, :, 1, :])
    grouped_queries = query_matrix.reshape(SEQUENCE_SLOTS, SLOT_LENGTH, KEY_VALUE_HEADS, QUERY_HEAD_COUNT // KEY_VALUE_HEADS, HEAD_SIZE)
    attended = round_both(jnp.stack([attend(grouped_queries[slot_index], key_rows[slot_index], value_rows[slot_index], lengths[slot_index]) for slot_index in range(SEQUENCE_SLOTS)]))
    branch = low_back(jnp.einsum('stf,fd->std', attended, w_out, precision=highest))
    middle = hidden + valid_rows[..., None] * branch
    normed_b = low(norm_rows(middle, norm_gains[1]))
    logits = jnp.einsum('std,de->ste', normed_b, router, precision=highest)
    gate_weights = jax.nn.softmax(jnp.take_along_axis(logits, routes, axis=-1), axis=-1)
    per_expert = CAP * (SLOT_LENGTH // SEQ_DEV)
    device_of = (jnp.arange(SLOT_LENGTH, dtype=jnp.int32) // SEQ_DEV)[None, :, None]
    targets = jnp.where(queue_ranks < CAP, routes * per_expert + device_of * CAP + queue_ranks, EXPERTS * per_expert).astype(jnp.int32)
    token_ids = jnp.broadcast_to(jnp.arange(SEQUENCE_SLOTS * SLOT_LENGTH, dtype=jnp.int32).reshape(SEQUENCE_SLOTS, SLOT_LENGTH, 1), targets.shape)
    source = jnp.full((EXPERTS * per_expert + 1,), SEQUENCE_SLOTS * SLOT_LENGTH, jnp.int32).at[targets.reshape(-1)].set(token_ids.reshape(-1))[:EXPERTS * per_expert]
    flat_rows = jnp.concatenate([normed_b.reshape(SEQUENCE_SLOTS * SLOT_LENGTH, MODEL_WIDTH), jnp.zeros((1, MODEL_WIDTH), jnp.float32)], axis=0)
    expert_rows = low_back(flat_rows[source].reshape(EXPERTS, per_expert, MODEL_WIDTH))
    gate_up = low_back(jnp.einsum('erd,edf->erf', expert_rows, w_in, precision=highest))
    hidden_units = low(jax.nn.silu(gate_up[..., :FF]) * gate_up[..., FF:])
    expert_out = round_both(jnp.einsum('erf,efd->erd', hidden_units, w_down, precision=highest))
    flat_out = jnp.concatenate([expert_out.reshape(EXPERTS * per_expert, MODEL_WIDTH), jnp.zeros((1, MODEL_WIDTH), jnp.float32)], axis=0)
    mixture = jnp.einsum('stk,stkd->std', gate_weights, flat_out[targets], precision=highest)
    return middle + valid_rows[..., None] * mixture

def reference(tokens, lengths, routes, queue_ranks, query_key_value_weight, w_out, router, norm_gains, w_in, w_down, cotangent):
    valid_rows = (jnp.arange(SLOT_LENGTH, dtype=jnp.int32)[None, :] < lengths[:, None]).astype(jnp.float32)

    def forward(tokens_in, qkv_all, out_all, router_all, gains_all, in_all, down_all):
        hidden = tokens_in
        for layer_index in range(DECODER_LAYERS):
            weights = (qkv_all[layer_index], out_all[layer_index], router_all[layer_index], gains_all[layer_index], in_all[layer_index], down_all[layer_index])
            hidden = one_layer(hidden, weights, routes[layer_index], queue_ranks[layer_index], valid_rows, lengths)
        return hidden * valid_rows[..., None]
    floats = tuple((array.astype(jnp.float32) for array in (tokens, query_key_value_weight, w_out, router, norm_gains, w_in, w_down)))
    result, pullback = jax.vjp(forward, *floats)
    gradients = pullback(cotangent.astype(jnp.float32))
    return (result.astype(jnp.bfloat16), gradients[0], gradients[1], gradients[2], gradients[3], gradients[4][:, 0, :], gradients[4][:, 1, :], gradients[5], gradients[6])
```

```python
import jax
import jax.numpy as jnp
from jax import lax
from jax.sharding import PartitionSpec as P

MODEL_WIDTH = 1536
QUERY_HEAD_COUNT = 24
KEY_VALUE_HEADS = 8
HEAD_SIZE = 64
FF = 512
EXPERTS = 40
TOP = 8
DECODER_LAYERS = 2
SEQUENCE_SLOTS = 2
CAP = 26


epsilon = 1e-06
negative = -1e30
theta_log = 9.210340371976184


def rotate(values, positions, direction):
    half_width = values.shape[-1] // 2
    frequency = jnp.exp(
        jnp.arange(half_width, dtype=jnp.float32) * (-2.0 * theta_log / values.shape[-1])
    )
    angles = positions[:, None, None] * frequency
    cosine = jnp.cos(angles)
    sine_part = jnp.sin(angles) * direction
    first_half = values[..., :half_width]
    second_half = values[..., half_width:]
    return jnp.concatenate(
        [
            first_half * cosine - second_half * sine_part,
            second_half * cosine + first_half * sine_part,
        ],
        axis=-1,
    )


def norm_rows(hidden):
    inverse = lax.rsqrt(jnp.mean(hidden * hidden, axis=-1, keepdims=True) + epsilon)
    return (hidden * inverse, inverse)


def norm_back(grad_normed, scaled, inverse, gain_row):
    grad_gain = jnp.sum(grad_normed * scaled, axis=0)
    grad_scaled = grad_normed * gain_row
    grad_hidden = inverse * (
        grad_scaled - scaled * jnp.mean(grad_scaled * scaled, axis=-1, keepdims=True)
    )
    return (grad_hidden, grad_gain)


def gather_keys(kv_heads):
    return lax.all_gather(kv_heads, "blk", axis=1, tiled=True)


def ring(count, offset):
    return [(i, (i + offset) % count) for i in range(count)]


def rows_to_owner(matrices, blocks_count, owned, blk_index):
    rows, columns = matrices.shape[1:]
    whole = jnp.zeros((owned, blocks_count * rows, columns), matrices.dtype)
    for offset in range(blocks_count):
        target = (blk_index + offset) % blocks_count
        origin = (blk_index - offset) % blocks_count
        piece = lax.dynamic_slice_in_dim(matrices, target * owned, owned, 0)
        if offset:
            piece = lax.ppermute(piece, "blk", ring(blocks_count, offset))
        whole = lax.dynamic_update_slice_in_dim(whole, piece, origin * rows, 1)
    return whole


def rows_from_owner(whole, blocks_count, owned, blk_index):
    rows = whole.shape[1] // blocks_count
    matrices = jnp.zeros((owned * blocks_count, rows, whole.shape[2]), whole.dtype)
    for offset in range(blocks_count):
        target = (blk_index + offset) % blocks_count
        origin = (blk_index - offset) % blocks_count
        piece = lax.dynamic_slice_in_dim(whole, target * rows, rows, 1)
        if offset:
            piece = lax.ppermute(piece, "blk", ring(blocks_count, offset))
        matrices = lax.dynamic_update_slice_in_dim(matrices, piece, origin * owned, 0)
    return matrices


def head_gather(rows):
    heads = lax.axis_size("head")
    copies = jnp.broadcast_to(rows[None], (heads,) + rows.shape)
    return lax.all_to_all(copies, "head", 0, 0, tiled=True).reshape(-1, rows.shape[-1])


def head_scatter(partial):
    heads = lax.axis_size("head")
    parts = partial.astype(jnp.bfloat16).reshape(heads, -1, partial.shape[-1])
    parts = lax.all_to_all(parts, "head", 0, 0, tiled=True)
    return jnp.sum(parts.astype(jnp.float32), axis=0)


def mm(spec, left, right):
    return jnp.einsum(spec, left, right, preferred_element_type=jnp.float32)


def shards(
    tokens,
    lengths,
    routes,
    queue_ranks,
    query_key_value_weight,
    w_out,
    router,
    norm_gains,
    w_in,
    w_down,
    cotangent,
):
    heads_count = lax.axis_size("head")
    blocks_count = lax.axis_size("blk")
    head_index = lax.axis_index("head")
    blk_index = lax.axis_index("blk")
    resident = tokens.shape[1]
    width = tokens.shape[2]
    rows_local = heads_count * resident
    keys_total = blocks_count * rows_local
    kv_local = KEY_VALUE_HEADS // heads_count
    group = QUERY_HEAD_COUNT // KEY_VALUE_HEADS
    block_size = min(512, keys_total)
    block_count = keys_total // block_size
    slot_rows = SEQUENCE_SLOTS * resident
    experts_local = EXPERTS // heads_count
    owned = experts_local // blocks_count
    owned_total = owned * blocks_count
    slot = heads_count * CAP
    own_places = (head_index * blocks_count + blk_index) * resident + jnp.arange(
        resident, dtype=jnp.int32
    )
    own_float = own_places.astype(jnp.float32)
    valid_rows = (own_places[None, :] < lengths[:, None]).astype(jnp.float32)
    valid_column = valid_rows.reshape(slot_rows, 1)
    local_ids = jnp.arange(rows_local, dtype=jnp.int32)
    query_places = (local_ids // resident * blocks_count + blk_index) * resident + local_ids % resident

    def key_places(row_ids):
        within = row_ids % rows_local
        return (
            within // resident * blocks_count + row_ids // rows_local
        ) * resident + within % resident

    def block_scores(query_matrix, keys_all, offset):
        key_piece = lax.dynamic_slice_in_dim(keys_all, offset, block_size, 1)
        scores = mm("sqgrd,skgd->sqgrk", query_matrix, key_piece[:, :, :, 0, :]) * 0.125
        places = key_places(offset + jnp.arange(block_size, dtype=jnp.int32))
        allowed = (places[None, None, :] <= query_places[None, :, None]) & (
            places[None, None, :] < lengths[:, None, None]
        )
        return (jnp.where(allowed[:, :, None, None, :], scores, negative), key_piece)

    def attend(query_matrix, keys_all):
        def visit(running, block_index):
            row_peak, row_total, weighted = running
            scores, key_piece = block_scores(query_matrix, keys_all, block_index * block_size)
            new_peak = jnp.maximum(row_peak, jnp.max(scores, axis=-1))
            exponents = jnp.exp(scores - new_peak[..., None])
            factor = jnp.exp(row_peak - new_peak)
            row_total = row_total * factor + jnp.sum(exponents, axis=-1)
            weighted = weighted * factor[..., None] + mm(
                "sqgrk,skgd->sqgrd", exponents.astype(jnp.bfloat16), key_piece[:, :, :, 1, :]
            )
            return ((new_peak, row_total, weighted), None)

        stat_shape = query_matrix.shape[:-1]
        start_state = (
            jnp.full(stat_shape, negative, jnp.float32),
            jnp.zeros(stat_shape, jnp.float32),
            jnp.zeros(query_matrix.shape, jnp.float32),
        )
        (row_peak, row_total, weighted), unused = lax.scan(
            visit, start_state, jnp.arange(block_count, dtype=jnp.int32)
        )
        return (weighted / row_total[..., None], row_peak + jnp.log(row_total))

    def attend_back(query_matrix, keys_all, grad_attended, attended, log_total):
        row_delta = jnp.sum(grad_attended.astype(jnp.float32) * attended, axis=-1)

        def revisit(running, block_index):
            grad_queries, grad_keys_all = running
            offset = block_index * block_size
            scores, key_piece = block_scores(query_matrix, keys_all, offset)
            probabilities = jnp.exp(scores - log_total[..., None])
            grad_values = mm("sqgrk,sqgrd->skgd", probabilities.astype(jnp.bfloat16), grad_attended)
            grad_probs = mm("sqgrd,skgd->sqgrk", grad_attended, key_piece[:, :, :, 1, :])
            grad_scores = (probabilities * (grad_probs - row_delta[..., None])).astype(jnp.bfloat16)
            grad_queries = grad_queries + 0.125 * mm(
                "sqgrk,skgd->sqgrd", grad_scores, key_piece[:, :, :, 0, :]
            )
            grad_keys = 0.125 * mm("sqgrk,sqgrd->skgd", grad_scores, query_matrix)
            grad_keys_all = lax.dynamic_update_slice_in_dim(
                grad_keys_all, jnp.stack([grad_keys, grad_values], axis=3), offset, 1
            )
            return ((grad_queries, grad_keys_all), None)

        start_state = (
            jnp.zeros(query_matrix.shape, jnp.float32),
            jnp.zeros(keys_all.shape, jnp.float32),
        )
        (grad_queries, grad_keys_all), unused = lax.scan(
            revisit, start_state, jnp.arange(block_count, dtype=jnp.int32)
        )
        return (grad_queries, grad_keys_all)

    plan = lax.all_gather(
        jnp.stack([routes, queue_ranks]).reshape(2, DECODER_LAYERS, slot_rows, TOP), "head", axis=0
    )
    expert_ids = jnp.arange(EXPERTS, dtype=jnp.int32)
    row_ids = jnp.arange(experts_local * slot, dtype=jnp.int32)
    spread = (
        row_ids[None, :] // slot == jnp.arange(experts_local, dtype=jnp.int32)[:, None]
    ).astype(jnp.bfloat16)
    all_tokens = heads_count * slot_rows
    token_head = jnp.arange(all_tokens, dtype=jnp.int32)[:, None] // slot_rows
    row_head = row_ids[None, :] % slot // CAP
    row_rank = (row_ids % CAP).astype(jnp.float32)[None, :]

    def layer_plan(layer_index):
        plan_routes = plan[:, 0, layer_index].reshape(all_tokens, TOP)
        plan_ranks = plan[:, 1, layer_index].reshape(all_tokens, TOP)
        named = plan_routes[:, :, None] == expert_ids
        chosen = jnp.any(named, axis=1)
        marks = jnp.sum(
            jnp.where(named & (plan_ranks < CAP)[:, :, None], plan_ranks[:, :, None] + 1, 0), axis=1
        )
        marks = lax.dynamic_slice_in_dim(marks, head_index * experts_local, experts_local, 1)
        wide = mm("te,er->tr", marks.astype(jnp.bfloat16), spread) - 1.0
        places = ((wide == row_rank) & (token_head == row_head)).astype(jnp.bfloat16)
        return (chosen, places)

    def to_experts(rows):
        rows = rows.reshape(experts_local, slot, width)
        own = lax.all_to_all(rows[:owned_total], "blk", 0, 1, tiled=True) if owned else None
        return (own, rows[owned_total:])

    def from_experts(own, shared):
        parts = [shared]
        if owned:
            parts = [lax.all_to_all(own, "blk", 1, 0, tiled=True), shared]
        return jnp.concatenate(parts, axis=0).reshape(experts_local * slot, width)

    def expert_weights(layer_index):
        sets = []
        if owned:
            sets.append(
                tuple(
                    rows_to_owner(matrix[layer_index, :owned_total], blocks_count, owned, blk_index)
                    for matrix in (w_in, w_down)
                )
            )
        if owned_total < experts_local:
            sets.append(
                tuple(
                    lax.all_gather(matrix[layer_index, owned_total:], "blk", axis=1, tiled=True)
                    for matrix in (w_in, w_down)
                )
            )
        return sets

    def experts_forward(incoming, weights):
        gate_up = mm("erd,edf->erf", incoming, weights[0])
        units = (jax.nn.silu(gate_up[..., :FF]) * gate_up[..., FF:]).astype(jnp.bfloat16)
        produced = mm("erf,efd->erd", units, weights[1]).astype(jnp.bfloat16)
        return (produced, (incoming, gate_up, units))

    def experts_backward(grad_produced, weights, kept):
        incoming, gate_up, units = kept
        grad_units = mm("erd,efd->erf", grad_produced, weights[1])
        grad_down = mm("erf,erd->efd", units, grad_produced).astype(jnp.bfloat16)
        gate_part = gate_up[..., :FF]
        up_part = gate_up[..., FF:]
        sigmoid_part = jax.nn.sigmoid(gate_part)
        grad_gate_up = jnp.concatenate(
            [
                grad_units * up_part * sigmoid_part * (1.0 + gate_part * (1.0 - sigmoid_part)),
                grad_units * gate_part * sigmoid_part,
            ],
            axis=-1,
        ).astype(jnp.bfloat16)
        grad_in = mm("erd,erf->edf", incoming, grad_gate_up).astype(jnp.bfloat16)
        grad_incoming = mm("erf,edf->erd", grad_gate_up, weights[0]).astype(jnp.bfloat16)
        return (grad_incoming, (grad_in, grad_down))

    hidden = tokens.reshape(slot_rows, width).astype(jnp.float32)
    stored_all = []
    for layer_index in range(DECODER_LAYERS):
        qkv_full = lax.all_gather(
            query_key_value_weight[layer_index], ("head", "blk"), axis=0, tiled=True
        )
        out_full = lax.all_gather(w_out[layer_index], ("head", "blk"), axis=0, tiled=True)
        router_full = lax.all_gather(router[layer_index], ("head", "blk"), axis=0, tiled=True)
        gains_full = lax.all_gather(norm_gains[layer_index], ("head", "blk"), axis=1, tiled=True)
        weight_sets = expert_weights(layer_index)
        chosen, places = layer_plan(layer_index)
        scaled_a, inverse_a = norm_rows(hidden)
        normed_a = (scaled_a * gains_full[0]).astype(jnp.bfloat16)
        projected = mm("td,de->te", normed_a, qkv_full).reshape(SEQUENCE_SLOTS, resident, -1)
        queries = rotate(
            projected[..., : QUERY_HEAD_COUNT * HEAD_SIZE].reshape(
                SEQUENCE_SLOTS, resident, QUERY_HEAD_COUNT, HEAD_SIZE
            ),
            own_float,
            1.0,
        )
        pair_columns = projected[..., QUERY_HEAD_COUNT * HEAD_SIZE :].reshape(
            SEQUENCE_SLOTS, resident, KEY_VALUE_HEADS, 2, HEAD_SIZE
        )
        keys_rot = rotate(pair_columns[:, :, :, 0, :], own_float, 1.0)
        pair_send = (
            jnp.stack([keys_rot, pair_columns[:, :, :, 1, :]], axis=3)
            .astype(jnp.bfloat16)
            .reshape(SEQUENCE_SLOTS, resident, KEY_VALUE_HEADS * 2 * HEAD_SIZE)
        )
        query_send = queries.astype(jnp.bfloat16).reshape(
            SEQUENCE_SLOTS, resident, QUERY_HEAD_COUNT * HEAD_SIZE
        )
        query_heads = lax.all_to_all(query_send, "head", split_axis=2, concat_axis=1, tiled=True)
        kv_heads = lax.all_to_all(pair_send, "head", split_axis=2, concat_axis=1, tiled=True)
        query_heads = query_heads.reshape(SEQUENCE_SLOTS, rows_local, kv_local, group, HEAD_SIZE)
        keys_all = gather_keys(kv_heads).reshape(SEQUENCE_SLOTS, keys_total, kv_local, 2, HEAD_SIZE)
        attended, log_total = attend(query_heads, keys_all)
        heads_out = attended.astype(jnp.bfloat16).reshape(
            SEQUENCE_SLOTS, rows_local, kv_local * group * HEAD_SIZE
        )
        attended_tokens = lax.all_to_all(
            heads_out, "head", split_axis=1, concat_axis=2, tiled=True
        ).reshape(slot_rows, -1)
        middle = hidden + valid_column * mm("tf,fd->td", attended_tokens, out_full)
        scaled_b, inverse_b = norm_rows(middle)
        normed_b = (scaled_b * gains_full[1]).astype(jnp.bfloat16)
        plane_rows = head_gather(normed_b)
        logits = mm("td,de->te", plane_rows, router_full)
        peaks = jnp.max(jnp.where(chosen, logits, negative), axis=-1, keepdims=True)
        lifted = jnp.where(chosen, jnp.exp(logits - peaks), 0.0)
        gates_all = lifted / jnp.sum(lifted, axis=-1, keepdims=True)
        gates = lax.dynamic_slice_in_dim(gates_all, head_index * slot_rows, slot_rows, 0)
        plane_gates = lax.dynamic_slice_in_dim(
            gates_all, head_index * experts_local, experts_local, 1
        )
        weighted_places = (
            mm("te,er->tr", plane_gates.astype(jnp.bfloat16), spread).astype(jnp.bfloat16) * places
        )
        queues = mm("tr,td->rd", places, plane_rows).astype(jnp.bfloat16)
        own_in, shared_in = to_experts(queues)
        kept_sets = []
        produced = []
        for incoming, weights in zip([own_in, shared_in] if owned else [shared_in], weight_sets):
            made, kept = experts_forward(incoming, weights)
            produced.append(made)
            kept_sets.append(kept)
        returned = from_experts(*(produced if owned else [None] + produced))
        mixture = head_scatter(mm("tr,rd->td", weighted_places, returned))
        stored_all.append(
            (
                qkv_full,
                out_full,
                router_full,
                gains_full,
                weight_sets,
                places,
                scaled_a,
                inverse_a,
                normed_a,
                query_heads,
                keys_all,
                attended,
                log_total,
                attended_tokens,
                scaled_b,
                inverse_b,
                normed_b,
                gates,
                weighted_places,
                kept_sets,
                returned,
            )
        )
        hidden = middle + valid_column * mixture
    result = (valid_column * hidden).astype(jnp.bfloat16).reshape(tokens.shape)
    grad_hidden = valid_column * cotangent.reshape(slot_rows, width).astype(jnp.float32)
    small_list = [None] * DECODER_LAYERS
    expert_list = [None] * DECODER_LAYERS
    for layer_index in reversed(range(DECODER_LAYERS)):
        (
            qkv_full,
            out_full,
            router_full,
            gains_full,
            weight_sets,
            places,
            scaled_a,
            inverse_a,
            normed_a,
            query_heads,
            keys_all,
            attended,
            log_total,
            attended_tokens,
            scaled_b,
            inverse_b,
            normed_b,
            gates,
            weighted_places,
            kept_sets,
            returned,
        ) = stored_all[layer_index]
        plane_grads = head_gather((valid_column * grad_hidden).astype(jnp.bfloat16))
        queue_grads = mm("tr,td->rd", weighted_places, plane_grads).astype(jnp.bfloat16)
        own_grad, shared_grad = to_experts(queue_grads)
        grad_in_sets = []
        grad_weight_sets = []
        for grad_produced, weights, kept in zip(
            [own_grad, shared_grad] if owned else [shared_grad], weight_sets, kept_sets
        ):
            grad_incoming, grad_weights = experts_backward(grad_produced, weights, kept)
            grad_in_sets.append(grad_incoming)
            grad_weight_sets.append(grad_weights)
        grad_rows = from_experts(*(grad_in_sets if owned else [None] + grad_in_sets))
        grad_normed_b = head_scatter(mm("tr,rd->td", places, grad_rows))
        pair_dots = mm("td,rd->tr", plane_grads, returned) * places
        plane_grad_gates = mm("tr,er->te", pair_dots, spread.astype(jnp.float32)).reshape(
            heads_count, slot_rows, experts_local
        )
        grad_gates = (
            lax.all_to_all(plane_grad_gates, "head", 0, 0, tiled=True)
            .transpose(1, 0, 2)
            .reshape(slot_rows, EXPERTS)
        )
        grad_logits = gates * (grad_gates - jnp.sum(gates * grad_gates, axis=-1, keepdims=True))
        grad_router = mm("td,te->de", normed_b.astype(jnp.float32), grad_logits)
        grad_normed_b = grad_normed_b + mm(
            "te,de->td", grad_logits, router_full.astype(jnp.float32)
        )
        grad_norm_b, grad_gain_b = norm_back(grad_normed_b, scaled_b, inverse_b, gains_full[1])
        grad_middle = grad_hidden + grad_norm_b
        grad_branch = (valid_column * grad_middle).astype(jnp.bfloat16)
        grad_out_w = mm("tf,td->fd", attended_tokens, grad_branch).astype(jnp.bfloat16)
        grad_tokens_att = (
            mm("td,fd->tf", grad_branch, out_full)
            .astype(jnp.bfloat16)
            .reshape(SEQUENCE_SLOTS, resident, -1)
        )
        grad_heads = lax.all_to_all(
            grad_tokens_att, "head", split_axis=2, concat_axis=1, tiled=True
        ).reshape(SEQUENCE_SLOTS, rows_local, kv_local, group, HEAD_SIZE)
        grad_queries, grad_keys_all = attend_back(
            query_heads, keys_all, grad_heads, attended, log_total
        )
        grad_pairs_own = lax.psum_scatter(
            grad_keys_all.astype(jnp.bfloat16), "blk", scatter_dimension=1, tiled=True
        )
        grad_query_send = grad_queries.astype(jnp.bfloat16).reshape(
            SEQUENCE_SLOTS, rows_local, kv_local * group * HEAD_SIZE
        )
        grad_pair_send = grad_pairs_own.reshape(
            SEQUENCE_SLOTS, rows_local, kv_local * 2 * HEAD_SIZE
        )
        grad_query_tok = lax.all_to_all(
            grad_query_send, "head", split_axis=1, concat_axis=2, tiled=True
        )
        grad_pair_tok = lax.all_to_all(
            grad_pair_send, "head", split_axis=1, concat_axis=2, tiled=True
        )
        grad_query_rot = rotate(
            grad_query_tok.astype(jnp.float32).reshape(
                SEQUENCE_SLOTS, resident, QUERY_HEAD_COUNT, HEAD_SIZE
            ),
            own_float,
            -1.0,
        )
        grad_pair = grad_pair_tok.astype(jnp.float32).reshape(
            SEQUENCE_SLOTS, resident, KEY_VALUE_HEADS, 2, HEAD_SIZE
        )
        grad_key_rot = rotate(grad_pair[:, :, :, 0, :], own_float, -1.0)
        grad_projected = jnp.concatenate(
            [
                grad_query_rot.reshape(slot_rows, QUERY_HEAD_COUNT * HEAD_SIZE),
                jnp.stack([grad_key_rot, grad_pair[:, :, :, 1, :]], axis=3).reshape(
                    slot_rows, KEY_VALUE_HEADS * 2 * HEAD_SIZE
                ),
            ],
            axis=-1,
        ).astype(jnp.bfloat16)
        grad_qkv = mm("td,te->de", normed_a, grad_projected).astype(jnp.bfloat16)
        grad_normed_a = mm("te,de->td", grad_projected, qkv_full)
        grad_norm_a, grad_gain_a = norm_back(grad_normed_a, scaled_a, inverse_a, gains_full[0])
        grad_hidden = grad_middle + grad_norm_a
        small_list[layer_index] = tuple(
            lax.psum_scatter(term, ("head", "blk"), scatter_dimension=0, tiled=True)
            for term in (
                grad_qkv,
                grad_out_w,
                grad_router,
                jnp.stack([grad_gain_a, grad_gain_b], axis=1),
            )
        )
        own_and_shared = []
        if owned:
            own_and_shared.append(
                tuple(
                    rows_from_owner(term, blocks_count, owned, blk_index)
                    for term in grad_weight_sets[0]
                )
            )
        if owned_total < experts_local:
            own_and_shared.append(
                tuple(
                    lax.psum_scatter(term, "blk", scatter_dimension=1, tiled=True)
                    for term in grad_weight_sets[-1]
                )
            )
        expert_list[layer_index] = tuple(
            jnp.concatenate(terms, axis=0).astype(jnp.float32) for terms in zip(*own_and_shared)
        )
    grad_w_qkv = jnp.stack([terms[0].astype(jnp.float32) for terms in small_list])
    grad_w_out = jnp.stack([terms[1].astype(jnp.float32) for terms in small_list])
    grad_router = jnp.stack([terms[2] for terms in small_list])
    grad_gains = jnp.stack([terms[3] for terms in small_list])
    grad_w_in = jnp.stack([terms[0] for terms in expert_list])
    grad_w_down = jnp.stack([terms[1] for terms in expert_list])
    return (
        result,
        grad_hidden.reshape(tokens.shape),
        grad_w_qkv,
        grad_w_out,
        grad_router,
        grad_gains[:, :, 0],
        grad_gains[:, :, 1],
        grad_w_in,
        grad_w_down,
    )


def solution(mesh):
    in_specs = (
        P(None, ("head", "blk"), None),
        P(),
        P(None, None, ("head", "blk"), None),
        P(None, None, ("head", "blk"), None),
        P(None, ("head", "blk"), None),
        P(None, ("head", "blk"), None),
        P(None, ("head", "blk"), None),
        P(None, None, ("head", "blk")),
        P(None, "head", "blk", None),
        P(None, "head", "blk", None),
        P(None, ("head", "blk"), None),
    )
    out_specs = (
        P(None, ("head", "blk"), None),
        P(None, ("head", "blk"), None),
        P(None, ("head", "blk"), None),
        P(None, ("head", "blk"), None),
        P(None, ("head", "blk"), None),
        P(None, ("head", "blk")),
        P(None, ("head", "blk")),
        P(None, "head", "blk", None),
        P(None, "head", "blk", None),
    )
    return jax.shard_map(shards, mesh=mesh, in_specs=in_specs, out_specs=out_specs, check_vma=False)
```

```python
import functools

import jax
import jax.numpy as jnp
from jax import lax
from jax.experimental import pallas as pl
from jax.experimental.pallas import tpu as pltpu
from jax.sharding import PartitionSpec as P

MODEL_WIDTH = 1536
QUERY_HEAD_COUNT = 24
KEY_VALUE_HEADS = 8
HEAD_SIZE = 64
FF = 512
EXPERTS = 40
TOP = 8
DECODER_LAYERS = 2
SEQUENCE_SLOTS = 2
CAP = 26


epsilon = 1e-06
negative = -1e30
theta_log = 9.210340371976184


MESH = pl.DeviceIdType.MESH


def mm(spec, left, right):
    return jnp.einsum(spec, left, right, preferred_element_type=jnp.float32)


def rotate(values, cosine, sine):
    rows = values.shape[0]
    half = HEAD_SIZE // 2
    heads = values.reshape(rows, -1, HEAD_SIZE)
    first_half = heads[..., :half]
    second_half = heads[..., half:]
    cosine = cosine[:, None, :]
    sine = sine[:, None, :]
    return jnp.concatenate(
        [first_half * cosine - second_half * sine, second_half * cosine + first_half * sine],
        axis=-1,
    ).reshape(values.shape)


def norm_rows(hidden):
    inverse = lax.rsqrt(jnp.mean(hidden * hidden, axis=-1, keepdims=True) + epsilon)
    return (hidden * inverse, inverse)


def norm_back(grad_normed, scaled, inverse, gain_row):
    grad_gain = jnp.sum(grad_normed * scaled, axis=0)
    grad_scaled = grad_normed * gain_row
    grad_hidden = inverse * (
        grad_scaled - scaled * jnp.mean(grad_scaled * scaled, axis=-1, keepdims=True)
    )
    return (grad_hidden, grad_gain)


def ring(count, offset):
    return [(i, (i + offset) % count) for i in range(count)]


def rows_to_owner(matrices, blocks_count, owned, blk_index):
    rows, columns = matrices.shape[1:]
    whole = jnp.zeros((owned, blocks_count * rows, columns), matrices.dtype)
    for offset in range(blocks_count):
        target = (blk_index + offset) % blocks_count
        origin = (blk_index - offset) % blocks_count
        piece = lax.dynamic_slice_in_dim(matrices, target * owned, owned, 0)
        if offset:
            piece = lax.ppermute(piece, "blk", ring(blocks_count, offset))
        whole = lax.dynamic_update_slice_in_dim(whole, piece, origin * rows, 1)
    return whole


def rows_from_owner(whole, blocks_count, owned, blk_index):
    rows = whole.shape[1] // blocks_count
    matrices = jnp.zeros((owned * blocks_count, rows, whole.shape[2]), whole.dtype)
    for offset in range(blocks_count):
        target = (blk_index + offset) % blocks_count
        origin = (blk_index - offset) % blocks_count
        piece = lax.dynamic_slice_in_dim(whole, target * rows, rows, 1)
        if offset:
            piece = lax.ppermute(piece, "blk", ring(blocks_count, offset))
        matrices = lax.dynamic_update_slice_in_dim(matrices, piece, origin * owned, 0)
    return matrices


def head_gather_kernel(heads, own_ref, all_ref, send_sems, recv_sems, local_sem):
    head = lax.axis_index("head")
    blk = lax.axis_index("blk")
    peers = [lax.rem(head + step, heads) for step in range(1, heads)]
    barrier = pltpu.get_barrier_semaphore()
    for peer in peers:
        pl.semaphore_signal(barrier, inc=1, device_id=(peer, blk), device_id_type=MESH)
    pl.semaphore_wait(barrier, heads - 1)
    copies = []
    for step, peer in enumerate(peers):
        copy = pltpu.make_async_remote_copy(
            src_ref=own_ref,
            dst_ref=all_ref.at[head],
            send_sem=send_sems.at[step],
            recv_sem=recv_sems.at[step],
            device_id=(peer, blk),
            device_id_type=MESH,
        )
        copy.start()
        copies.append(copy)
    local = pltpu.make_async_copy(own_ref, all_ref.at[head], local_sem)
    local.start()
    local.wait()
    for copy in copies:
        copy.wait()


def head_gather(rows):
    heads = lax.axis_size("head")
    gathered = pl.pallas_call(
        functools.partial(head_gather_kernel, heads),
        out_shape=jax.ShapeDtypeStruct((heads,) + rows.shape, rows.dtype),
        in_specs=[pl.BlockSpec(memory_space=pl.ANY)],
        out_specs=pl.BlockSpec(memory_space=pl.ANY),
        scratch_shapes=[
            pltpu.SemaphoreType.DMA((heads - 1,)),
            pltpu.SemaphoreType.DMA((heads - 1,)),
            pltpu.SemaphoreType.DMA,
        ],
        compiler_params=pltpu.CompilerParams(collective_id=1, has_side_effects=True),
        name="head_gather",
    )(rows)
    return gathered.reshape(-1, rows.shape[-1])


def head_scatter(partial):
    heads = lax.axis_size("head")
    parts = partial.astype(jnp.bfloat16).reshape(heads, -1, partial.shape[-1])
    parts = lax.all_to_all(parts, "head", 0, 0, tiled=True)
    return jnp.sum(parts.astype(jnp.float32), axis=0)


def dot_last(left, right):
    return lax.dot_general(
        left, right, (((1,), (1,)), ((), ())), preferred_element_type=jnp.float32
    )


def dot_first(left, right):
    return lax.dot_general(
        left, right, (((0,), (0,)), ((), ())), preferred_element_type=jnp.float32
    )


def head_columns(ref, rows, first, group, shift):
    pieces = []
    for member in range(group):
        start = (first + member) * HEAD_SIZE
        piece = ref[0, rows, start : start + HEAD_SIZE]
        empty = jnp.zeros_like(piece)
        pieces.append(jnp.concatenate([empty, piece] if shift else [piece, empty], axis=1))
    return jnp.concatenate(pieces, axis=0)


def unit_scores(queries, pairs, blk, resident, chunk):
    scores = dot_last(queries, pairs) * 0.125
    count, keys = scores.shape
    places = lax.broadcasted_iota(jnp.int32, (count, chunk), 1)
    own = blk * resident + lax.broadcasted_iota(jnp.int32, (count, chunk), 0) % resident
    last = jnp.where(places <= own, scores[:, keys - chunk :], negative)
    if keys > chunk:
        scores = jnp.concatenate([scores[:, : keys - chunk], last], axis=1)
    else:
        scores = last
    exponents = jnp.exp(scores - jnp.max(scores, axis=1, keepdims=True))
    return (exponents, jnp.sum(exponents, axis=1, keepdims=True))


def attend_kernel(heads, blocks, resident, group, kv_local, info_ref, query_ref, pair_ref, out_ref):
    slot_index = pl.program_id(0)
    blk = info_ref[0]
    length = info_ref[1 + slot_index]
    chunk = blocks * resident
    for head in range(heads):
        rows = pl.ds(head * resident, resident)
        live = head * chunk + blk * resident < length

        @pl.when(live)
        def _(head=head, rows=rows):
            keys = (head + 1) * chunk
            for kv_head in range(kv_local):
                lanes = pl.ds(kv_head * 2 * HEAD_SIZE, 2 * HEAD_SIZE)
                pairs = pair_ref[0, pl.ds(0, keys), lanes]
                queries = head_columns(query_ref, rows, kv_head * group, group, False)
                exponents, totals = unit_scores(queries, pairs, blk, resident, chunk)
                weighted = jnp.dot(
                    exponents.astype(jnp.bfloat16), pairs, preferred_element_type=jnp.float32
                )
                weighted = weighted / totals
                for member in range(group):
                    start = (kv_head * group + member) * HEAD_SIZE
                    out_ref[0, rows, start : start + HEAD_SIZE] = weighted[
                        member * resident : (member + 1) * resident, HEAD_SIZE:
                    ].astype(out_ref.dtype)

        @pl.when(jnp.logical_not(live))
        def _(rows=rows):
            out_ref[0, rows, :] = jnp.zeros((resident, out_ref.shape[2]), out_ref.dtype)


def attend_back_kernel(
    heads,
    blocks,
    resident,
    group,
    kv_local,
    info_ref,
    query_ref,
    pair_ref,
    grad_ref,
    grad_query_ref,
    grad_pair_ref,
    total_ref,
):
    slot_index = pl.program_id(0)
    blk = info_ref[0]
    length = info_ref[1 + slot_index]
    chunk = blocks * resident
    total_ref[...] = jnp.zeros_like(total_ref)
    for head in range(heads):
        rows = pl.ds(head * resident, resident)
        live = head * chunk + blk * resident < length

        @pl.when(live)
        def _(head=head, rows=rows):
            keys = (head + 1) * chunk
            for kv_head in range(kv_local):
                lanes = pl.ds(kv_head * 2 * HEAD_SIZE, 2 * HEAD_SIZE)
                pairs = pair_ref[0, pl.ds(0, keys), lanes]
                queries = head_columns(query_ref, rows, kv_head * group, group, False)
                grads = head_columns(grad_ref, rows, kv_head * group, group, True)
                exponents, totals = unit_scores(queries, pairs, blk, resident, chunk)
                probabilities = exponents * (1.0 / totals)
                grad_probs = dot_last(grads, pairs)
                delta = jnp.sum(probabilities * grad_probs, axis=1, keepdims=True)
                grad_scores = (probabilities * (grad_probs - delta)).astype(jnp.bfloat16)
                grad_queries = 0.125 * jnp.dot(
                    grad_scores, pairs, preferred_element_type=jnp.float32
                )
                for member in range(group):
                    start = (kv_head * group + member) * HEAD_SIZE
                    grad_query_ref[0, rows, start : start + HEAD_SIZE] = grad_queries[
                        member * resident : (member + 1) * resident, :HEAD_SIZE
                    ].astype(grad_query_ref.dtype)
                total_ref[pl.ds(0, keys), lanes] += dot_first(
                    grad_scores, queries * jnp.bfloat16(0.125)
                ) + dot_first(probabilities.astype(jnp.bfloat16), grads)

        @pl.when(jnp.logical_not(live))
        def _(rows=rows):
            grad_query_ref[0, rows, :] = jnp.zeros(
                (resident, grad_query_ref.shape[2]), grad_query_ref.dtype
            )

    grad_pair_ref[0] = total_ref[...].astype(grad_pair_ref.dtype)


def attention_call(kernel, info, arrays, outs, scratch, flops, name):
    def spec(array):
        shape = array.shape
        return pl.BlockSpec((1,) + shape[1:], lambda slot, info: (slot, 0, 0))

    return pl.pallas_call(
        kernel,
        grid_spec=pltpu.PrefetchScalarGridSpec(
            num_scalar_prefetch=1,
            grid=(SEQUENCE_SLOTS,),
            in_specs=[spec(array) for array in arrays],
            out_specs=[spec(array) for array in outs],
            scratch_shapes=scratch,
        ),
        out_shape=outs,
        compiler_params=pltpu.CompilerParams(vmem_limit_bytes=56 * 1024 * 1024),
        cost_estimate=pl.CostEstimate(
            flops=flops, bytes_accessed=8 << 20, transcendentals=flops // 256
        ),
        name=name,
    )(info, *arrays)


def shards(
    tokens,
    lengths,
    routes,
    queue_ranks,
    query_key_value_weight,
    w_out,
    router,
    norm_gains,
    w_in,
    w_down,
    cotangent,
):
    heads_count = lax.axis_size("head")
    blocks_count = lax.axis_size("blk")
    head_index = lax.axis_index("head")
    blk_index = lax.axis_index("blk")
    resident = tokens.shape[1]
    width = tokens.shape[2]
    weight_rows = w_out.shape[1]
    rows_local = heads_count * resident
    keys_total = blocks_count * rows_local
    kv_local = KEY_VALUE_HEADS // heads_count
    group = QUERY_HEAD_COUNT // KEY_VALUE_HEADS
    query_columns = kv_local * group * HEAD_SIZE
    pair_columns = kv_local * 2 * HEAD_SIZE
    slot_rows = SEQUENCE_SLOTS * resident
    all_tokens = heads_count * slot_rows
    experts_local = EXPERTS // heads_count
    owned = experts_local // blocks_count
    owned_total = owned * blocks_count
    slot = -(-heads_count * CAP // 16) * 16
    half = HEAD_SIZE // 2

    own_places = (head_index * blocks_count + blk_index) * resident + jnp.arange(
        resident, dtype=jnp.int32
    )
    valid_column = (
        (own_places[None, :] < lengths[:, None]).astype(jnp.float32).reshape(slot_rows, 1)
    )
    plane_ids = jnp.arange(all_tokens, dtype=jnp.int32)
    plane_places = (
        (plane_ids // slot_rows * blocks_count + blk_index) * resident + plane_ids % resident
    ).astype(jnp.float32)
    frequency = jnp.exp(jnp.arange(half, dtype=jnp.float32) * (-2.0 * theta_log / HEAD_SIZE))
    angles = plane_places[:, None] * frequency[None, :]
    cosine = jnp.cos(angles)
    sine = jnp.sin(angles)
    info = jnp.concatenate([blk_index[None].astype(jnp.int32), lengths])

    plan = lax.all_gather(
        jnp.stack([routes, queue_ranks]).reshape(2, DECODER_LAYERS, slot_rows, TOP), "head", axis=0
    )
    expert_ids = jnp.arange(EXPERTS, dtype=jnp.int32)
    row_ids = jnp.arange(experts_local * slot, dtype=jnp.int32)
    spread = (
        row_ids[None, :] // slot == jnp.arange(experts_local, dtype=jnp.int32)[:, None]
    ).astype(jnp.bfloat16)
    token_head = plane_ids[:, None] // slot_rows
    row_head = row_ids[None, :] % slot // CAP
    row_rank = (row_ids % slot % CAP).astype(jnp.float32)[None, :]

    def layer_plan(layer_index):
        plan_routes = plan[:, 0, layer_index].reshape(all_tokens, TOP)
        plan_ranks = plan[:, 1, layer_index].reshape(all_tokens, TOP)
        named = plan_routes[:, :, None] == expert_ids
        chosen = jnp.any(named, axis=1)
        marks = jnp.sum(
            jnp.where(named & (plan_ranks < CAP)[:, :, None], plan_ranks[:, :, None] + 1, 0), axis=1
        )
        marks = lax.dynamic_slice_in_dim(marks, head_index * experts_local, experts_local, 1)
        wide = mm("te,er->tr", marks.astype(jnp.bfloat16), spread) - 1.0
        places = ((wide == row_rank) & (token_head == row_head)).astype(jnp.bfloat16)
        return (chosen, places)

    def to_experts(rows):
        rows = rows.reshape(experts_local, slot, width)
        own = None
        if owned:
            own = rows[:owned_total].reshape(blocks_count, owned * slot, width)
            own = lax.all_to_all(own, "blk", 0, 0, tiled=True)
            own = own.reshape(blocks_count, owned, slot, width).transpose(1, 0, 2, 3)
            own = own.reshape(owned, blocks_count * slot, width)
        return (own, rows[owned_total:])

    def from_experts(own, shared):
        parts = [shared]
        if owned:
            own = own.reshape(owned, blocks_count, slot, width).transpose(1, 0, 2, 3)
            own = own.reshape(blocks_count, owned * slot, width)
            own = lax.all_to_all(own, "blk", 0, 0, tiled=True)
            parts = [own.reshape(owned_total, slot, width), shared]
        return jnp.concatenate(parts, axis=0).reshape(experts_local * slot, width)

    def expert_weights(layer_index):
        sets = []
        if owned:
            sets.append(
                tuple(
                    rows_to_owner(matrix[layer_index, :owned_total], blocks_count, owned, blk_index)
                    for matrix in (w_in, w_down)
                )
            )
        if owned_total < experts_local:
            sets.append(
                tuple(
                    lax.all_gather(matrix[layer_index, owned_total:], "blk", axis=1, tiled=True)
                    for matrix in (w_in, w_down)
                )
            )
        return sets

    def experts_forward(incoming, weights):
        gate_up = mm("erd,edf->erf", incoming, weights[0])
        units = (jax.nn.silu(gate_up[..., :FF]) * gate_up[..., FF:]).astype(jnp.bfloat16)
        produced = mm("erf,efd->erd", units, weights[1]).astype(jnp.bfloat16)
        return (produced, (incoming, gate_up, units))

    def experts_backward(grad_produced, weights, kept):
        incoming, gate_up, units = kept
        grad_units = mm("erd,efd->erf", grad_produced, weights[1])
        grad_down = mm("erf,erd->efd", units, grad_produced).astype(jnp.bfloat16)
        gate_part = gate_up[..., :FF]
        up_part = gate_up[..., FF:]
        sigmoid_part = jax.nn.sigmoid(gate_part)
        grad_gate_up = jnp.concatenate(
            [
                grad_units * up_part * sigmoid_part * (1.0 + gate_part * (1.0 - sigmoid_part)),
                grad_units * gate_part * sigmoid_part,
            ],
            axis=-1,
        ).astype(jnp.bfloat16)
        grad_in = mm("erd,erf->edf", incoming, grad_gate_up).astype(jnp.bfloat16)
        grad_incoming = mm("erf,edf->erd", grad_gate_up, weights[0]).astype(jnp.bfloat16)
        return (grad_incoming, (grad_in, grad_down))

    def by_slot(rows):
        return (
            rows.reshape(heads_count, SEQUENCE_SLOTS, resident, -1)
            .transpose(1, 0, 2, 3)
            .reshape(SEQUENCE_SLOTS, rows_local, -1)
        )

    def by_head(rows):
        return (
            rows.reshape(SEQUENCE_SLOTS, heads_count, resident, -1)
            .transpose(1, 0, 2, 3)
            .reshape(all_tokens, -1)
        )

    small_columns = 128
    send = []
    for layer_index in range(DECODER_LAYERS):
        weight = query_key_value_weight[layer_index]
        split = QUERY_HEAD_COUNT * HEAD_SIZE
        small = jnp.concatenate([router[layer_index], norm_gains[layer_index].T], axis=1)
        small = jnp.pad(small, ((0, 0), (0, small_columns - small.shape[1])))
        send.append(
            jnp.concatenate(
                [
                    weight[:, :split]
                    .reshape(weight_rows, heads_count, query_columns)
                    .transpose(1, 0, 2),
                    weight[:, split:]
                    .reshape(weight_rows, heads_count, pair_columns)
                    .transpose(1, 0, 2),
                    jnp.broadcast_to(small[None], (heads_count,) + small.shape),
                ],
                axis=-1,
            )
        )
    send = lax.all_to_all(jnp.stack(send, axis=1), "head", 0, 0, tiled=True)
    attention_weights = []
    for layer_index in range(DECODER_LAYERS):
        wide = lax.all_gather(send[:, layer_index], "blk", axis=1, tiled=True).reshape(width, -1)
        out_full = lax.all_gather(w_out[layer_index], "blk", axis=0, tiled=True)
        columns = query_columns + pair_columns
        small = wide[:, columns:]
        gains = small.T[EXPERTS : EXPERTS + 2].astype(jnp.float32)
        attention_weights.append((wide[:, :columns], out_full, small[:, :EXPERTS], gains))

    hidden = tokens.reshape(slot_rows, width).astype(jnp.float32)
    plane_tokens = head_gather(tokens.reshape(slot_rows, width))
    stored_all = []
    for layer_index in range(DECODER_LAYERS):
        qkv_full, out_full, router_full, gains = attention_weights[layer_index]
        weight_sets = expert_weights(layer_index)
        chosen, places = layer_plan(layer_index)
        scaled_a, inverse_a = norm_rows(hidden)
        if layer_index:
            plane_normed_a = head_gather((scaled_a * gains[:1]).astype(jnp.bfloat16))
        else:
            plane_normed_a = (
                norm_rows(plane_tokens.astype(jnp.float32))[0] * gains[:1]
            ).astype(jnp.bfloat16)
        projected = mm("td,de->te", plane_normed_a, qkv_full)
        queries = by_slot(rotate(projected[:, :query_columns], cosine, sine).astype(jnp.bfloat16))
        pairs = projected[:, query_columns:].reshape(all_tokens, kv_local, 2, HEAD_SIZE)
        keys = rotate(pairs[:, :, 0].reshape(all_tokens, -1), cosine, sine)
        pairs = jnp.stack([keys.reshape(all_tokens, kv_local, HEAD_SIZE), pairs[:, :, 1]], axis=2)
        pairs = pairs.reshape(all_tokens, pair_columns).astype(jnp.bfloat16)
        pairs = lax.all_to_all(
            jnp.broadcast_to(pairs[None], (blocks_count,) + pairs.shape), "blk", 0, 0, tiled=True
        )
        pairs_all = (
            pairs.reshape(blocks_count, heads_count, SEQUENCE_SLOTS, resident, pair_columns)
            .transpose(2, 1, 0, 3, 4)
            .reshape(SEQUENCE_SLOTS, keys_total, pair_columns)
        )
        (attended,) = attention_call(
            functools.partial(
                attend_kernel, heads_count, blocks_count, resident, group, kv_local
            ),
            info,
            [queries, pairs_all],
            [jax.ShapeDtypeStruct(queries.shape, jnp.bfloat16)],
            [],
            4 * rows_local * keys_total * query_columns,
            "attend",
        )
        attended = by_head(attended)
        middle = hidden + valid_column * head_scatter(mm("tf,fd->td", attended, out_full))
        scaled_b, inverse_b = norm_rows(middle)
        normed_b = (scaled_b * gains[1:]).astype(jnp.bfloat16)
        plane_rows = head_gather(normed_b)
        logits = mm("td,de->te", plane_rows, router_full)
        peaks = jnp.max(jnp.where(chosen, logits, negative), axis=-1, keepdims=True)
        lifted = jnp.where(chosen, jnp.exp(logits - peaks), 0.0)
        gates_all = lifted / jnp.sum(lifted, axis=-1, keepdims=True)
        plane_gates = lax.dynamic_slice_in_dim(
            gates_all, head_index * experts_local, experts_local, 1
        )
        weighted_places = (
            mm("te,er->tr", plane_gates.astype(jnp.bfloat16), spread).astype(jnp.bfloat16) * places
        )
        queues = mm("tr,td->rd", places, plane_rows).astype(jnp.bfloat16)
        own_in, shared_in = to_experts(queues)
        kept_sets = []
        produced = []
        for incoming, weights in zip([own_in, shared_in] if owned else [shared_in], weight_sets):
            made, kept = experts_forward(incoming, weights)
            produced.append(made)
            kept_sets.append(kept)
        returned = from_experts(*(produced if owned else [None] + produced))
        mixture = head_scatter(mm("tr,rd->td", weighted_places, returned))
        stored_all.append(
            (
                weight_sets,
                places,
                scaled_a,
                inverse_a,
                plane_normed_a,
                queries,
                pairs_all,
                attended,
                scaled_b,
                inverse_b,
                plane_rows,
                gates_all,
                weighted_places,
                kept_sets,
                returned,
            )
        )
        hidden = middle + valid_column * mixture
    result = (valid_column * hidden).astype(jnp.bfloat16).reshape(tokens.shape)
    grad_hidden = valid_column * cotangent.reshape(slot_rows, width).astype(jnp.float32)
    qkv_list = [None] * DECODER_LAYERS
    out_list = [None] * DECODER_LAYERS
    router_list = [None] * DECODER_LAYERS
    gains_list = [None] * DECODER_LAYERS
    expert_list = [None] * DECODER_LAYERS
    for layer_index in reversed(range(DECODER_LAYERS)):
        qkv_full, out_full, router_full, gains = attention_weights[layer_index]
        (
            weight_sets,
            places,
            scaled_a,
            inverse_a,
            plane_normed_a,
            queries,
            pairs_all,
            attended,
            scaled_b,
            inverse_b,
            plane_rows,
            gates_all,
            weighted_places,
            kept_sets,
            returned,
        ) = stored_all[layer_index]
        plane_grads = head_gather((valid_column * grad_hidden).astype(jnp.bfloat16))
        queue_grads = mm("tr,td->rd", weighted_places, plane_grads).astype(jnp.bfloat16)
        own_grad, shared_grad = to_experts(queue_grads)
        grad_in_sets = []
        grad_weight_sets = []
        for grad_produced, weights, kept in zip(
            [own_grad, shared_grad] if owned else [shared_grad], weight_sets, kept_sets
        ):
            grad_incoming, grad_weights = experts_backward(grad_produced, weights, kept)
            grad_in_sets.append(grad_incoming)
            grad_weight_sets.append(grad_weights)
        grad_rows = from_experts(*(grad_in_sets if owned else [None] + grad_in_sets))
        grad_normed_b = head_scatter(mm("tr,rd->td", places, grad_rows))
        pair_dots = mm("td,rd->tr", plane_grads, returned) * places
        plane_grad_gates = mm("er,tr->et", spread.astype(jnp.float32), pair_dots)
        grad_gates = (
            lax.all_to_all(
                jnp.broadcast_to(plane_grad_gates[None], (heads_count, experts_local, all_tokens)),
                "head",
                0,
                0,
                tiled=True,
            )
            .reshape(EXPERTS, all_tokens)
            .T
        )
        grad_logits = gates_all * (
            grad_gates - jnp.sum(gates_all * grad_gates, axis=-1, keepdims=True)
        )
        plane_width = width // heads_count
        grad_router = mm(
            "td,te->de",
            lax.dynamic_slice_in_dim(plane_rows, head_index * plane_width, plane_width, 1),
            grad_logits.astype(jnp.bfloat16),
        )
        own_logits = lax.dynamic_slice_in_dim(grad_logits, head_index * slot_rows, slot_rows, 0)
        grad_normed_b = grad_normed_b + mm(
            "te,de->td", own_logits.astype(jnp.bfloat16), router_full
        )
        grad_norm_b, grad_gain_b = norm_back(grad_normed_b, scaled_b, inverse_b, gains[1:])
        grad_middle = grad_hidden + grad_norm_b
        plane_branch = head_gather((valid_column * grad_middle).astype(jnp.bfloat16))
        grad_out_w = mm("tf,td->fd", attended, plane_branch)
        grad_attended = by_slot(mm("td,fd->tf", plane_branch, out_full).astype(jnp.bfloat16))
        grad_queries, grad_pairs = attention_call(
            functools.partial(
                attend_back_kernel, heads_count, blocks_count, resident, group, kv_local
            ),
            info,
            [queries, pairs_all, grad_attended],
            [
                jax.ShapeDtypeStruct(queries.shape, jnp.bfloat16),
                jax.ShapeDtypeStruct(pairs_all.shape, jnp.bfloat16),
            ],
            [pltpu.VMEM((keys_total, pair_columns), jnp.float32)],
            10 * rows_local * keys_total * query_columns,
            "attend_back",
        )
        grad_pairs = (
            grad_pairs.reshape(SEQUENCE_SLOTS, heads_count, blocks_count, resident, pair_columns)
            .transpose(2, 1, 0, 3, 4)
            .reshape(blocks_count, all_tokens, pair_columns)
        )
        grad_pairs = lax.all_to_all(grad_pairs, "blk", 0, 0, tiled=True)
        grad_pairs = jnp.sum(grad_pairs.astype(jnp.float32), axis=0)
        grad_pairs = grad_pairs.astype(jnp.bfloat16).astype(jnp.float32)
        grad_pairs = grad_pairs.reshape(all_tokens, kv_local, 2, HEAD_SIZE)
        grad_keys = rotate(grad_pairs[:, :, 0].reshape(all_tokens, -1), cosine, -sine)
        grad_projected = jnp.concatenate(
            [
                rotate(by_head(grad_queries).astype(jnp.float32), cosine, -sine),
                jnp.stack(
                    [grad_keys.reshape(all_tokens, kv_local, HEAD_SIZE), grad_pairs[:, :, 1]],
                    axis=2,
                ).reshape(all_tokens, pair_columns),
            ],
            axis=-1,
        ).astype(jnp.bfloat16)
        grad_qkv = mm("td,te->de", plane_normed_a, grad_projected)
        grad_normed_a = head_scatter(mm("te,de->td", grad_projected, qkv_full))
        grad_norm_a, grad_gain_a = norm_back(grad_normed_a, scaled_a, inverse_a, gains[:1])
        grad_hidden = grad_middle + grad_norm_a

        grad_out_w = jnp.concatenate(
            [grad_out_w, jnp.pad(grad_router, ((0, 0), (0, small_columns - EXPERTS)))], axis=1
        ).astype(jnp.bfloat16)
        grad_out_w = lax.psum_scatter(grad_out_w, "blk", scatter_dimension=0, tiled=True)
        out_list[layer_index] = grad_out_w[:, :width].astype(jnp.float32)
        router_list[layer_index] = grad_out_w[:, width : width + EXPERTS].astype(jnp.float32)
        grad_qkv = (
            grad_qkv.astype(jnp.bfloat16)
            .reshape(heads_count, blocks_count, weight_rows, -1)
            .transpose(1, 0, 2, 3)
            .reshape(width, -1)
        )
        grad_qkv = lax.psum_scatter(grad_qkv, "blk", scatter_dimension=0, tiled=True)
        grad_qkv = lax.all_to_all(
            grad_qkv.reshape(heads_count, weight_rows, -1), "head", 0, 0, tiled=True
        ).transpose(1, 0, 2)
        qkv_list[layer_index] = jnp.concatenate(
            [
                grad_qkv[..., :query_columns].reshape(weight_rows, -1),
                grad_qkv[..., query_columns:].reshape(weight_rows, -1),
            ],
            axis=1,
        ).astype(jnp.float32)
        gains_list[layer_index] = jnp.stack([grad_gain_a, grad_gain_b])
        own_and_shared = []
        if owned:
            own_and_shared.append(
                tuple(
                    rows_from_owner(term, blocks_count, owned, blk_index)
                    for term in grad_weight_sets[0]
                )
            )
        if owned_total < experts_local:
            own_and_shared.append(
                tuple(
                    lax.psum_scatter(term, "blk", scatter_dimension=1, tiled=True)
                    for term in grad_weight_sets[-1]
                )
            )
        expert_list[layer_index] = tuple(
            jnp.concatenate(terms, axis=0).astype(jnp.float32) for terms in zip(*own_and_shared)
        )
    devices = heads_count * blocks_count
    grad_gains = jnp.stack(gains_list).reshape(2 * DECODER_LAYERS, devices, weight_rows)
    grad_gains = lax.all_to_all(
        grad_gains.transpose(1, 0, 2).reshape(devices, -1), ("head", "blk"), 0, 0, tiled=True
    )
    grad_gains = jnp.sum(grad_gains, axis=0).reshape(DECODER_LAYERS, 2, weight_rows)
    return (
        result,
        grad_hidden.reshape(tokens.shape),
        jnp.stack(qkv_list),
        jnp.stack(out_list),
        jnp.stack(router_list),
        grad_gains[:, 0],
        grad_gains[:, 1],
        jnp.stack([terms[0] for terms in expert_list]),
        jnp.stack([terms[1] for terms in expert_list]),
    )


def solution(mesh):
    in_specs = (
        P(None, ("head", "blk"), None),
        P(),
        P(None, None, ("head", "blk"), None),
        P(None, None, ("head", "blk"), None),
        P(None, ("head", "blk"), None),
        P(None, ("head", "blk"), None),
        P(None, ("head", "blk"), None),
        P(None, None, ("head", "blk")),
        P(None, "head", "blk", None),
        P(None, "head", "blk", None),
        P(None, ("head", "blk"), None),
    )
    out_specs = (
        P(None, ("head", "blk"), None),
        P(None, ("head", "blk"), None),
        P(None, ("head", "blk"), None),
        P(None, ("head", "blk"), None),
        P(None, ("head", "blk"), None),
        P(None, ("head", "blk")),
        P(None, ("head", "blk")),
        P(None, "head", "blk", None),
        P(None, "head", "blk", None),
    )
    return jax.shard_map(shards, mesh=mesh, in_specs=in_specs, out_specs=out_specs, check_vma=False)
```

```python
import functools

import jax
import jax.numpy as jnp
from jax import lax
from jax.experimental import pallas as pl
from jax.experimental.pallas import tpu as pltpu
from jax.sharding import PartitionSpec as P

MODEL_WIDTH = 1536
QUERY_HEAD_COUNT = 24
KEY_VALUE_HEADS = 8
HEAD_SIZE = 64
FF = 512
EXPERTS = 40
TOP = 8
DECODER_LAYERS = 2
SEQUENCE_SLOTS = 2
CAP = 26


epsilon = 1e-06
negative = -1e30
theta_log = 9.210340371976184


MESH = pl.DeviceIdType.MESH


def mm(spec, left, right):
    return jnp.einsum(spec, left, right, preferred_element_type=jnp.float32)


def rotate(values, cosine, sine):
    rows = values.shape[0]
    half = HEAD_SIZE // 2
    heads = values.reshape(rows, -1, HEAD_SIZE)
    first_half = heads[..., :half]
    second_half = heads[..., half:]
    cosine = cosine[:, None, :]
    sine = sine[:, None, :]
    return jnp.concatenate(
        [first_half * cosine - second_half * sine, second_half * cosine + first_half * sine],
        axis=-1,
    ).reshape(values.shape)


def norm_rows(hidden):
    inverse = lax.rsqrt(jnp.mean(hidden * hidden, axis=-1, keepdims=True) + epsilon)
    return (hidden * inverse, inverse)


def norm_back(grad_normed, scaled, inverse, gain_row):
    grad_gain = jnp.sum(grad_normed * scaled, axis=0)
    grad_scaled = grad_normed * gain_row
    grad_hidden = inverse * (
        grad_scaled - scaled * jnp.mean(grad_scaled * scaled, axis=-1, keepdims=True)
    )
    return (grad_hidden, grad_gain)


def exchange_kernel(heads, blocks, items, waited, *refs):
    count = len(items)
    sources = refs[:count]
    targets = refs[count + waited : 2 * count + waited]
    send_sems, recv_sems, local_sems = refs[2 * count + waited :]
    head = lax.axis_index("head")
    blk = lax.axis_index("blk")
    chips = blocks // 2
    chip, core = blk // 2, lax.rem(blk, 2)
    sibling = chip * 2 + 1 - core
    kinds = {kind for kind, _ in items}
    head_peers = [(lax.rem(head + step, heads), blk) for step in range(1, heads)]
    blk_peers = [(head, lax.rem(blk + step, blocks)) for step in range(1, blocks)]
    pair_peers = [
        (head, lax.rem(chip + step, chips) * 2 + core) for step in range(1, chips)
    ] + [(head, sibling)]
    greeted = []
    if kinds & {"head_gather", "head_swap"}:
        greeted += head_peers
    if "blk_swap" in kinds:
        greeted += blk_peers
    elif "blk_pairs" in kinds:
        greeted += pair_peers
    barrier = pltpu.get_barrier_semaphore()
    for peer in greeted:
        pl.semaphore_signal(barrier, inc=1, device_id=peer, device_id_type=MESH)
    pl.semaphore_wait(barrier, len(greeted))
    used = 0
    copies = []
    forwards = []

    def send(source, target, peer):
        nonlocal used
        copy = pltpu.make_async_remote_copy(
            src_ref=source,
            dst_ref=target,
            send_sem=send_sems.at[used],
            recv_sem=recv_sems.at[used],
            device_id=peer,
            device_id_type=MESH,
        )
        copy.start()
        used += 1
        return copy

    locals_started = []
    for number, (kind, layer) in enumerate(items):
        source, target = sources[number], targets[number]

        def piece(index, source=source, layer=layer):
            return source.at[index] if layer is None else source.at[layer, index]

        if kind == "head_gather":
            mine, place = source, head
            copies += [send(source, target.at[head], peer) for peer in head_peers]
        elif kind == "head_swap":
            mine, place = piece(head), head
            copies += [send(piece(peer[0]), target.at[head], peer) for peer in head_peers]
        elif kind == "blk_swap":
            mine, place = piece(blk), blk
            copies += [send(piece(peer[1]), target.at[blk], peer) for peer in blk_peers]
        else:
            mine, place = source, blk
            sent = [send(source, target.at[blk], peer) for peer in pair_peers]
            copies += sent[-1:]
            forwards.append((sent[:-1], target))
        local = pltpu.make_async_copy(mine, target.at[place], local_sems.at[number])
        local.start()
        locals_started.append(local)
    for sent, target in forwards:
        for step, copy in enumerate(sent, start=1):
            copy.wait_recv()
            origin = lax.rem(chip + chips - step, chips) * 2 + core
            copies.append(send(target.at[origin], target.at[origin], (head, sibling)))
    for sent, _ in forwards:
        for copy in sent:
            copy.wait_send()
    for local in locals_started:
        local.wait()
    for copy in copies:
        copy.wait()


kernel_numbers = {}


def kernel_number(*key):
    return kernel_numbers.setdefault(key, 1 + len(kernel_numbers))


def exchange(*items, after=()):
    heads, blocks = lax.axis_size("head"), lax.axis_size("blk")
    arrays = [item[1] for item in items]
    plan = [(item[0], item[2] if len(item) > 2 else None) for item in items]
    outs = []
    total = 0
    for (kind, layer), array in zip(plan, arrays):
        group = heads if kind.startswith("head") else blocks
        tail = array.shape
        if kind.endswith("swap"):
            tail = tail[1:] if layer is None else tail[2:]
        outs.append(jax.ShapeDtypeStruct((group,) + tail, array.dtype))
        total += group - 1
    collective_id = kernel_number(
        "exchange", tuple(plan), *((array.shape, str(array.dtype)) for array in (*arrays, *after))
    )
    results = pl.pallas_call(
        functools.partial(exchange_kernel, heads, blocks, plan, len(after)),
        out_shape=outs,
        in_specs=[pl.BlockSpec(memory_space=pl.ANY)] * (len(arrays) + len(after)),
        out_specs=[pl.BlockSpec(memory_space=pl.ANY)] * len(arrays),
        scratch_shapes=[
            pltpu.SemaphoreType.DMA((total,)),
            pltpu.SemaphoreType.DMA((total,)),
            pltpu.SemaphoreType.DMA((len(arrays),)),
        ],
        compiler_params=pltpu.CompilerParams(collective_id=collective_id, has_side_effects=True),
        cost_estimate=pl.CostEstimate(flops=0, bytes_accessed=110 << 20, transcendentals=0),
        name="exchange",
    )(*arrays, *after)
    return results


def greet(peers):
    barrier = pltpu.get_barrier_semaphore()
    for peer in peers:
        pl.semaphore_signal(barrier, inc=1, device_id=peer, device_id_type=MESH)
    pl.semaphore_wait(barrier, len(peers))


def plane_peers(heads, blocks):
    head = lax.axis_index("head")
    blk = lax.axis_index("blk")
    head_peers = [(lax.rem(head + step, heads), blk) for step in range(1, heads)]
    blk_peers = [(head, lax.rem(blk + step, blocks)) for step in range(1, blocks)]
    return head, blk, head_peers, blk_peers


def remote(source, target, sems, index, peer, landing=None):
    return pltpu.make_async_remote_copy(
        src_ref=source,
        dst_ref=target,
        send_sem=sems[0].at[index],
        recv_sem=sems[1].at[index if landing is None else landing],
        device_id=peer,
        device_id_type=MESH,
    )


def started(copy):
    copy.start()
    return copy


def weight_part(ref, columns, by_columns):
    return ref[:, columns] if by_columns else ref[columns, :]


def meet(left, part, by_columns):
    return (
        dot_last(left, part)
        if by_columns
        else jnp.dot(left, part, preferred_element_type=jnp.float32)
    )


def dispatch_kernel(
    heads,
    blocks,
    pieces,
    window,
    by_columns,
    own_ref,
    place_ref,
    weight_ref,
    shared_weight_ref,
    plane_ref,
    queue_ref,
    shared_ref,
    out_ref,
    shared_out_ref,
    send_ref,
    held_ref,
    shared_held_ref,
    head_send,
    head_recv,
    blk_send,
    blk_recv,
    local_sems,
):
    head, blk, head_peers, blk_peers = plane_peers(heads, blocks)
    rows, width = own_ref.shape
    slot = queue_ref.shape[1]
    shared = shared_ref.shape[0]
    step_width = width // pieces
    outputs = out_ref.shape[1]
    tile = 256
    greet(head_peers + blk_peers)
    loads = [
        pltpu.make_async_copy(weight_ref, held_ref, local_sems.at[0]),
        pltpu.make_async_copy(shared_weight_ref, shared_held_ref, local_sems.at[1]),
    ]
    for load in loads:
        load.start()
    head_copies = []
    blk_copies = []

    def far(peer):
        return jnp.abs(peer[0] - head) == heads - 1

    relay = heads == 4
    inner = jnp.logical_and(head > 0, head < heads - 1)
    relayed = []

    def spread(piece):
        columns = pl.ds(piece * step_width, step_width)
        copies = []
        for number, peer in enumerate(head_peers):
            copy = remote(
                own_ref.at[:, columns],
                plane_ref.at[head, :, columns],
                (head_send, head_recv),
                piece * heads + number,
                peer,
            )
            copies.append(copy)
            if relay and number != 1:
                pl.when(jnp.logical_not(far(peer)))(copy.start)
            else:
                copy.start()
        head_copies.append(copies)

    def pass_on(piece):
        columns = pl.ds(piece * step_width, step_width)
        origin = lax.rem(head + 2, heads)
        rows_there = plane_ref.at[origin, :, columns]
        copy = remote(
            rows_there,
            rows_there,
            (head_send, head_recv),
            piece * heads + heads - 1,
            ((head - 1) * (heads - 1), blk),
            piece * heads + jnp.where(head == 1, 0, heads - 2),
        )
        relayed.append(copy)
        pl.when(inner)(copy.start)

    for piece in range(min(window, pieces)):
        spread(piece)
    plane_ref[head] = own_ref[...]

    def consume(piece):
        columns = pl.ds(piece * step_width, step_width)
        for copy in blk_copies[piece]:
            copy.wait_recv()
        queue = queue_ref[:, :, columns].reshape(blocks * slot, step_width)

        def one_tile(index, carry):
            lanes = pl.ds(pl.multiple_of(index * tile, tile), tile)
            if by_columns:
                product = dot_last(queue, held_ref[lanes, columns])
            else:
                product = jnp.dot(
                    queue, held_ref[columns, lanes], preferred_element_type=jnp.float32
                )
            if piece:
                product = product + out_ref[:, lanes]
            out_ref[:, lanes] = product
            return carry

        lax.fori_loop(0, outputs // tile, one_tile, 0)

    for piece in range(pieces):
        columns = pl.ds(piece * step_width, step_width)
        if relay:
            head_copies[piece][1].wait_recv()
            pass_on(piece)
        for number, copy in enumerate(head_copies[piece]):
            if not relay or number != 1:
                copy.wait_recv()
        if piece + window < pieces:
            spread(piece + window)
        plane = plane_ref[:, :, columns].reshape(heads * rows, step_width)

        def fill(expert, carry):
            start = pl.multiple_of(expert * slot, 16)
            send_ref[expert, :, columns] = jnp.dot(
                place_ref[pl.ds(start, slot), :], plane, preferred_element_type=jnp.float32
            ).astype(send_ref.dtype)
            return carry

        lax.fori_loop(0, blocks, fill, 0)
        blk_copies.append(
            [
                started(
                    remote(
                        send_ref.at[peer[1], :, columns],
                        queue_ref.at[blk, :, columns],
                        (blk_send, blk_recv),
                        piece * (blocks - 1) + number,
                        peer,
                    )
                )
                for number, peer in enumerate(blk_peers)
            ]
        )
        queue_ref[blk, :, columns] = send_ref[blk, :, columns]
        if not piece:
            for load in loads:
                load.wait()
        for expert in range(shared):
            taken = jnp.dot(
                place_ref[pl.ds((blocks + expert) * slot, slot), :],
                plane,
                preferred_element_type=jnp.float32,
            ).astype(shared_ref.dtype)
            shared_ref[expert, :, columns] = taken
            product = meet(
                taken, weight_part(shared_held_ref.at[expert], columns, by_columns), by_columns
            )
            if piece:
                product = product + shared_out_ref[expert]
            shared_out_ref[expert] = product
        if piece:
            consume(piece - 1)
    consume(pieces - 1)
    for copies in head_copies:
        for number, copy in enumerate(copies):
            if relay and number != 1:
                pl.when(jnp.logical_not(far(head_peers[number])))(copy.wait_send)
            else:
                copy.wait_send()
    for copy in relayed:
        pl.when(inner)(copy.wait_send)
    for copies in blk_copies:
        for copy in copies:
            copy.wait_send()


def dispatch(rows, places, weights, by_columns, pieces=6, window=2):
    heads, blocks = lax.axis_size("head"), lax.axis_size("blk")
    count, width = rows.shape
    (own_weight, shared_weight) = weights
    shared = shared_weight.shape[0]
    slot = places.shape[0] // (blocks + shared)
    outputs = own_weight.shape[0 if by_columns else 1]
    outs = [
        jax.ShapeDtypeStruct((heads, count, width), jnp.bfloat16),
        jax.ShapeDtypeStruct((blocks, slot, width), jnp.bfloat16),
        jax.ShapeDtypeStruct((shared, slot, width), jnp.bfloat16),
        jax.ShapeDtypeStruct((blocks * slot, outputs), jnp.float32),
        jax.ShapeDtypeStruct((shared, slot, outputs), jnp.float32),
    ]
    vmem = pl.BlockSpec(memory_space=pltpu.VMEM)
    anywhere = pl.BlockSpec(memory_space=pl.ANY)
    return pl.pallas_call(
        functools.partial(dispatch_kernel, heads, blocks, pieces, window, by_columns),
        out_shape=outs,
        in_specs=[vmem, vmem, anywhere, anywhere],
        out_specs=[vmem] * 5,
        scratch_shapes=[
            pltpu.VMEM((blocks, slot, width), jnp.bfloat16),
            pltpu.VMEM(own_weight.shape, jnp.bfloat16),
            pltpu.VMEM(shared_weight.shape, jnp.bfloat16),
            pltpu.SemaphoreType.DMA((pieces * heads,)),
            pltpu.SemaphoreType.DMA((pieces * heads,)),
            pltpu.SemaphoreType.DMA((pieces * (blocks - 1),)),
            pltpu.SemaphoreType.DMA((pieces * (blocks - 1),)),
            pltpu.SemaphoreType.DMA((2,)),
        ],
        compiler_params=pltpu.CompilerParams(
            collective_id=kernel_number("dispatch", by_columns),
            has_side_effects=True,
            vmem_limit_bytes=56 * 1024 * 1024,
        ),
        cost_estimate=pl.CostEstimate(flops=0, bytes_accessed=170 << 20, transcendentals=0),
        name="dispatch",
    )(rows, places, own_weight, shared_weight)


def combine_kernel(
    heads,
    blocks,
    pieces,
    by_columns,
    extra,
    units_ref,
    shared_units_ref,
    place_ref,
    weight_ref,
    shared_weight_ref,
    *refs,
):
    extra_ref, *refs = refs if extra else (None, *refs)
    out_ref, returned_ref, *refs = refs
    extra_out_ref, *refs = refs if extra else (None, *refs)
    (
    made_ref,
    part_ref,
    landed_ref,
    relay_ref,
    held_ref,
    shared_held_ref,
    head_send,
    head_recv,
    blk_send,
    blk_recv,
    local_sems,
    ) = refs
    head, blk, head_peers, blk_peers = plane_peers(heads, blocks)
    rows, width = out_ref.shape
    slot = returned_ref.shape[1]
    shared = shared_units_ref.shape[0]
    step_width = width // pieces
    relay = heads == 4
    inner = jnp.logical_and(head > 0, head < heads - 1)
    greet(head_peers + blk_peers)
    loads = [
        pltpu.make_async_copy(weight_ref, held_ref, local_sems.at[0]),
        pltpu.make_async_copy(shared_weight_ref, shared_held_ref, local_sems.at[1]),
    ]
    for load in loads:
        load.start()
    extra_copies = []
    if extra:
        loads.append(
            pltpu.make_async_copy(extra_ref, extra_out_ref.at[head], local_sems.at[2])
        )
        loads[-1].start()
        extra_copies = [
            started(
                remote(
                    extra_ref,
                    extra_out_ref.at[head],
                    (head_send, head_recv),
                    pieces * heads + number,
                    peer,
                )
            )
            for number, peer in enumerate(head_peers)
        ]
    for load in loads:
        load.wait()
    head_copies = []
    blk_copies = []

    def produce(piece):
        columns = pl.ds(piece * step_width, step_width)

        def make(block, carry):
            start = pl.multiple_of(block * slot, 16)
            made_ref[block, :, columns] = meet(
                units_ref[pl.ds(start, slot), :],
                weight_part(held_ref, columns, not by_columns),
                by_columns,
            ).astype(made_ref.dtype)
            return carry

        lax.fori_loop(0, blocks, make, 0)
        blk_copies.append(
            [
                started(
                    remote(
                        made_ref.at[peer[1], :, columns],
                        returned_ref.at[blk, :, columns],
                        (blk_send, blk_recv),
                        piece * (blocks - 1) + number,
                        peer,
                    )
                )
                for number, peer in enumerate(blk_peers)
            ]
        )
        returned_ref[blk, :, columns] = made_ref[blk, :, columns]
        for expert in range(shared):
            returned_ref[blocks + expert, :, columns] = meet(
                shared_units_ref[expert],
                weight_part(shared_held_ref.at[expert], columns, not by_columns),
                by_columns,
            ).astype(returned_ref.dtype)

    def gather(piece):
        columns = pl.ds(piece * step_width, step_width)
        for copy in blk_copies[piece]:
            copy.wait_recv()
        returned = returned_ref[:, :, columns].reshape((blocks + shared) * slot, step_width)

        def part(owner):
            start = pl.multiple_of(owner * rows, 16)
            return jnp.dot(
                place_ref[pl.ds(start, rows), :], returned, preferred_element_type=jnp.float32
            )

        sent = []
        for number, peer in enumerate(head_peers):
            part_ref[peer[0], :, columns] = part(peer[0]).astype(part_ref.dtype)
            copy = remote(
                part_ref.at[peer[0], :, columns],
                landed_ref.at[head, :, columns],
                (head_send, head_recv),
                piece * heads + number,
                peer,
            )
            sent.append(copy)
            if not relay:
                copy.start()
            elif number == 1:
                pl.when(jnp.logical_not(inner))(copy.start)
            else:
                distant = far(peer)
                pl.when(jnp.logical_not(distant))(copy.start)
                through = through_copy(piece, peer)
                pl.when(distant)(through.start)
        head_copies.append(sent)
        out_ref[:, columns] = part(head)

    def far(peer):
        return jnp.abs(peer[0] - head) == heads - 1

    def through_copy(piece, peer):
        columns = pl.ds(piece * step_width, step_width)
        return remote(
            part_ref.at[peer[0], :, columns],
            relay_ref.at[:, columns],
            (head_send, head_recv),
            piece * heads + heads - 1,
            (jnp.where(head == 0, 1, heads - 2), blk),
        )

    def pass_on(piece):
        columns = pl.ds(piece * step_width, step_width)
        target = lax.rem(head + 2, heads)

        @pl.when(inner)
        def _():
            through_copy(piece, (target, blk)).wait_recv()
            part_ref[target, :, columns] = (
                part_ref[target, :, columns].astype(jnp.float32)
                + relay_ref[:, columns].astype(jnp.float32)
            ).astype(part_ref.dtype)
            head_copies[piece][1].start()

    def finish(piece):
        columns = pl.ds(piece * step_width, step_width)
        for number, peer in enumerate(head_peers):
            copy = head_copies[piece][number]

            def add(copy=copy, peer=peer):
                copy.wait_recv()
                out_ref[:, columns] += landed_ref[peer_origin(peer), :, columns].astype(
                    jnp.float32
                )

            if relay and number != 1:
                pl.when(jnp.logical_not(far((peer_origin(peer), blk))))(add)
            else:
                add()

    def peer_origin(peer):
        return lax.rem(2 * head + heads - peer[0], heads)

    lag = 3 if relay else 2
    for step in range(pieces + lag):
        if step < pieces:
            produce(step)
        if 0 < step <= pieces:
            gather(step - 1)
        if relay and 1 < step <= pieces + 1:
            pass_on(step - 2)
        if step >= lag:
            finish(step - lag)
    for piece, copies in enumerate(head_copies):
        for number, copy in enumerate(copies):
            if relay and number != 1:
                distant = far(head_peers[number])
                pl.when(jnp.logical_not(distant))(copy.wait_send)
                pl.when(distant)(through_copy(piece, head_peers[number]).wait_send)
            else:
                copy.wait_send()
    for copy in extra_copies:
        copy.wait()
    for copies in blk_copies:
        for copy in copies:
            copy.wait_send()


def combine(
    units, shared_units, places, weights, by_columns, extra=None, pieces=6
):
    heads, blocks = lax.axis_size("head"), lax.axis_size("blk")
    (own_weight, shared_weight) = weights
    shared, slot = shared_units.shape[:2]
    count = places.shape[0] // heads
    width = own_weight.shape[0 if by_columns else 1]
    outs = [
        jax.ShapeDtypeStruct((count, width), jnp.float32),
        jax.ShapeDtypeStruct((blocks + shared, slot, width), jnp.bfloat16),
    ]
    vmem = pl.BlockSpec(memory_space=pltpu.VMEM)
    anywhere = pl.BlockSpec(memory_space=pl.ANY)
    extras = [] if extra is None else [extra]
    outs += [jax.ShapeDtypeStruct((heads,) + array.shape, array.dtype) for array in extras]
    return pl.pallas_call(
        functools.partial(combine_kernel, heads, blocks, pieces, by_columns, bool(extras)),
        out_shape=outs,
        in_specs=[vmem, vmem, vmem, anywhere, anywhere] + [anywhere] * len(extras),
        out_specs=[vmem] * 2 + [anywhere] * len(extras),
        scratch_shapes=[
            pltpu.VMEM((blocks, slot, width), jnp.bfloat16),
            pltpu.VMEM((heads, count, width), jnp.bfloat16),
            pltpu.VMEM((heads, count, width), jnp.bfloat16),
            pltpu.VMEM((count, width), jnp.bfloat16),
            pltpu.VMEM(own_weight.shape, jnp.bfloat16),
            pltpu.VMEM(shared_weight.shape, jnp.bfloat16),
            pltpu.SemaphoreType.DMA(((pieces + 1) * heads,)),
            pltpu.SemaphoreType.DMA(((pieces + 1) * heads,)),
            pltpu.SemaphoreType.DMA((pieces * (blocks - 1),)),
            pltpu.SemaphoreType.DMA((pieces * (blocks - 1),)),
            pltpu.SemaphoreType.DMA((3,)),
        ],
        compiler_params=pltpu.CompilerParams(
            collective_id=kernel_number("combine", by_columns),
            has_side_effects=True,
            vmem_limit_bytes=56 * 1024 * 1024,
        ),
        cost_estimate=pl.CostEstimate(flops=0, bytes_accessed=170 << 20, transcendentals=0),
        name="combine",
    )(units, shared_units, places, own_weight, shared_weight, *extras)


def head_parts(partial):
    heads = lax.axis_size("head")
    return partial.astype(jnp.bfloat16).reshape(heads, -1, partial.shape[-1])


def head_sum(parts):
    return jnp.sum(parts.astype(jnp.float32), axis=0)


def dot_last(left, right):
    return lax.dot_general(
        left, right, (((1,), (1,)), ((), ())), preferred_element_type=jnp.float32
    )


def dot_first(left, right):
    return lax.dot_general(
        left, right, (((0,), (0,)), ((), ())), preferred_element_type=jnp.float32
    )


def head_columns(ref, rows, first, group, shift):
    pieces = []
    for member in range(group):
        start = (first + member) * HEAD_SIZE
        piece = ref[0, rows, start : start + HEAD_SIZE]
        empty = jnp.zeros_like(piece)
        pieces.append(jnp.concatenate([empty, piece] if shift else [piece, empty], axis=1))
    return jnp.concatenate(pieces, axis=0)


def unit_scores(queries, pairs, blk, resident, chunk):
    scores = dot_last(queries, pairs) * 0.125
    count, keys = scores.shape
    places = lax.broadcasted_iota(jnp.int32, (count, chunk), 1)
    own = blk * resident + lax.broadcasted_iota(jnp.int32, (count, chunk), 0) % resident
    last = jnp.where(places <= own, scores[:, keys - chunk :], negative)
    if keys > chunk:
        scores = jnp.concatenate([scores[:, : keys - chunk], last], axis=1)
    else:
        scores = last
    exponents = jnp.exp(scores - jnp.max(scores, axis=1, keepdims=True))
    return (exponents, jnp.sum(exponents, axis=1, keepdims=True))


def attend_kernel(heads, blocks, resident, group, kv_local, info_ref, query_ref, pair_ref, out_ref):
    slot_index = pl.program_id(0)
    blk = info_ref[0]
    length = info_ref[1 + slot_index]
    chunk = blocks * resident
    for head in range(heads):
        rows = pl.ds(head * resident, resident)
        live = head * chunk + blk * resident < length

        @pl.when(live)
        def _(head=head, rows=rows):
            keys = (head + 1) * chunk
            for kv_head in range(kv_local):
                lanes = pl.ds(kv_head * 2 * HEAD_SIZE, 2 * HEAD_SIZE)
                pairs = pair_ref[0, pl.ds(0, keys), lanes]
                queries = head_columns(query_ref, rows, kv_head * group, group, False)
                exponents, totals = unit_scores(queries, pairs, blk, resident, chunk)
                weighted = jnp.dot(
                    exponents.astype(jnp.bfloat16), pairs, preferred_element_type=jnp.float32
                )
                weighted = weighted / totals
                for member in range(group):
                    start = (kv_head * group + member) * HEAD_SIZE
                    out_ref[0, rows, start : start + HEAD_SIZE] = weighted[
                        member * resident : (member + 1) * resident, HEAD_SIZE:
                    ].astype(out_ref.dtype)

        @pl.when(jnp.logical_not(live))
        def _(rows=rows):
            out_ref[0, rows, :] = jnp.zeros((resident, out_ref.shape[2]), out_ref.dtype)


def attend_back_kernel(
    heads,
    blocks,
    resident,
    group,
    kv_local,
    info_ref,
    query_ref,
    pair_ref,
    grad_ref,
    grad_query_ref,
    grad_pair_ref,
    total_ref,
):
    slot_index = pl.program_id(0)
    blk = info_ref[0]
    length = info_ref[1 + slot_index]
    chunk = blocks * resident
    total_ref[...] = jnp.zeros_like(total_ref)
    for head in range(heads):
        rows = pl.ds(head * resident, resident)
        live = head * chunk + blk * resident < length

        @pl.when(live)
        def _(head=head, rows=rows):
            keys = (head + 1) * chunk
            for kv_head in range(kv_local):
                lanes = pl.ds(kv_head * 2 * HEAD_SIZE, 2 * HEAD_SIZE)
                pairs = pair_ref[0, pl.ds(0, keys), lanes]
                queries = head_columns(query_ref, rows, kv_head * group, group, False)
                grads = head_columns(grad_ref, rows, kv_head * group, group, True)
                exponents, totals = unit_scores(queries, pairs, blk, resident, chunk)
                probabilities = exponents * (1.0 / totals)
                grad_probs = dot_last(grads, pairs)
                delta = jnp.sum(probabilities * grad_probs, axis=1, keepdims=True)
                grad_scores = (probabilities * (grad_probs - delta)).astype(jnp.bfloat16)
                grad_queries = 0.125 * jnp.dot(
                    grad_scores, pairs, preferred_element_type=jnp.float32
                )
                for member in range(group):
                    start = (kv_head * group + member) * HEAD_SIZE
                    grad_query_ref[0, rows, start : start + HEAD_SIZE] = grad_queries[
                        member * resident : (member + 1) * resident, :HEAD_SIZE
                    ].astype(grad_query_ref.dtype)
                total_ref[pl.ds(0, keys), lanes] += dot_first(
                    grad_scores, queries * jnp.bfloat16(0.125)
                ) + dot_first(probabilities.astype(jnp.bfloat16), grads)

        @pl.when(jnp.logical_not(live))
        def _(rows=rows):
            grad_query_ref[0, rows, :] = jnp.zeros(
                (resident, grad_query_ref.shape[2]), grad_query_ref.dtype
            )

    grad_pair_ref[0] = total_ref[...].astype(grad_pair_ref.dtype)


def attention_call(kernel, info, arrays, outs, scratch, flops, name):
    def spec(array):
        shape = array.shape
        return pl.BlockSpec((1,) + shape[1:], lambda slot, info: (slot, 0, 0))

    return pl.pallas_call(
        kernel,
        grid_spec=pltpu.PrefetchScalarGridSpec(
            num_scalar_prefetch=1,
            grid=(SEQUENCE_SLOTS,),
            in_specs=[spec(array) for array in arrays],
            out_specs=[spec(array) for array in outs],
            scratch_shapes=scratch,
        ),
        out_shape=outs,
        compiler_params=pltpu.CompilerParams(vmem_limit_bytes=56 * 1024 * 1024),
        cost_estimate=pl.CostEstimate(
            flops=flops, bytes_accessed=8 << 20, transcendentals=flops // 256
        ),
        name=name,
    )(info, *arrays)


def shards(
    tokens,
    lengths,
    routes,
    queue_ranks,
    query_key_value_weight,
    w_out,
    router,
    norm_gains,
    w_in,
    w_down,
    cotangent,
):
    kernel_numbers.clear()
    heads_count = lax.axis_size("head")
    blocks_count = lax.axis_size("blk")
    head_index = lax.axis_index("head")
    blk_index = lax.axis_index("blk")
    resident = tokens.shape[1]
    width = tokens.shape[2]
    weight_rows = w_out.shape[1]
    rows_local = heads_count * resident
    keys_total = blocks_count * rows_local
    kv_local = KEY_VALUE_HEADS // heads_count
    group = QUERY_HEAD_COUNT // KEY_VALUE_HEADS
    query_columns = kv_local * group * HEAD_SIZE
    pair_columns = kv_local * 2 * HEAD_SIZE
    slot_rows = SEQUENCE_SLOTS * resident
    all_tokens = heads_count * slot_rows
    experts_local = EXPERTS // heads_count
    owned = experts_local // blocks_count
    owned_total = owned * blocks_count
    slot = -(-heads_count * CAP // 16) * 16
    half = HEAD_SIZE // 2

    own_places = (head_index * blocks_count + blk_index) * resident + jnp.arange(
        resident, dtype=jnp.int32
    )
    valid_column = (
        (own_places[None, :] < lengths[:, None]).astype(jnp.float32).reshape(slot_rows, 1)
    )
    plane_ids = jnp.arange(all_tokens, dtype=jnp.int32)
    plane_places = (
        (plane_ids // slot_rows * blocks_count + blk_index) * resident + plane_ids % resident
    ).astype(jnp.float32)
    frequency = jnp.exp(jnp.arange(half, dtype=jnp.float32) * (-2.0 * theta_log / HEAD_SIZE))
    angles = plane_places[:, None] * frequency[None, :]
    cosine = jnp.cos(angles)
    sine = jnp.sin(angles)
    info = jnp.concatenate([blk_index[None].astype(jnp.int32), lengths])

    expert_ids = jnp.arange(EXPERTS, dtype=jnp.int32)
    row_ids = jnp.arange(experts_local * slot, dtype=jnp.int32)
    spread = (
        row_ids[None, :] // slot == jnp.arange(experts_local, dtype=jnp.int32)[:, None]
    ).astype(jnp.bfloat16)
    token_head = plane_ids[:, None] // slot_rows
    row_head = row_ids[None, :] % slot // CAP
    row_rank = (row_ids % slot % CAP).astype(jnp.float32)[None, :]

    def layer_plan(layer_index):
        plan_routes = plan[:, 0, layer_index].reshape(all_tokens, TOP)
        plan_ranks = plan[:, 1, layer_index].reshape(all_tokens, TOP)
        named = plan_routes[:, :, None] == expert_ids
        chosen = jnp.any(named, axis=1)
        marks = jnp.sum(
            jnp.where(named & (plan_ranks < CAP)[:, :, None], plan_ranks[:, :, None] + 1, 0), axis=1
        )
        marks = lax.dynamic_slice_in_dim(marks, head_index * experts_local, experts_local, 1)
        wide = mm("te,er->tr", marks.astype(jnp.bfloat16), spread) - 1.0
        places = ((wide == row_rank) & (token_head == row_head)).astype(jnp.bfloat16)
        return (chosen, places)

    def to_experts(rows):
        rows = rows.reshape(experts_local, slot, width)
        own = None
        if owned:
            own = rows[:owned_total].reshape(blocks_count, owned * slot, width)
            own = lax.all_to_all(own, "blk", 0, 0, tiled=True)
            own = own.reshape(blocks_count, owned, slot, width).transpose(1, 0, 2, 3)
            own = own.reshape(owned, blocks_count * slot, width)
        return (own, rows[owned_total:])

    def from_experts(own, shared):
        parts = [shared]
        if owned:
            own = own.reshape(owned, blocks_count, slot, width).transpose(1, 0, 2, 3)
            own = own.reshape(blocks_count, owned * slot, width)
            own = lax.all_to_all(own, "blk", 0, 0, tiled=True)
            parts = [own.reshape(owned_total, slot, width), shared]
        return jnp.concatenate(parts, axis=0).reshape(experts_local * slot, width)

    def shared_weights(layer_index):
        if owned_total == experts_local:
            return []
        return [
            tuple(
                lax.all_gather(matrix[layer_index, owned_total:], "blk", axis=1, tiled=True)
                for matrix in (w_in, w_down)
            )
        ]

    def to_owner(matrix, layer_index):
        if not owned:
            return []
        if owned == 1:
            return [("blk_swap", matrix, layer_index)]
        pieces = matrix[layer_index, :owned_total]
        return [("blk_swap", pieces.reshape((blocks_count, owned) + pieces.shape[1:]))]

    def owned_matrix(received):
        if not owned:
            return None
        columns = received.shape[-1]
        pieces = received.reshape(blocks_count, owned, -1, columns)
        return pieces.transpose(1, 0, 2, 3).reshape(owned, -1, columns)

    def from_owner(term):
        if not owned:
            return []
        columns = term.shape[-1]
        pieces = term.reshape(owned, blocks_count, -1, columns).transpose(1, 0, 2, 3)
        return [("blk_swap", pieces)]

    def owned_rows(received):
        if not owned:
            return []
        return [received.reshape(owned_total, -1, received.shape[-1])]

    def moe_in(rows, turned_places, sets, which):
        if owned == 1 and owned_total < experts_local:
            own_weight, shared_weight = (matrices[which] for matrices in sets)
            plane, own, shared, own_out, shared_out = dispatch(
                rows, turned_places, (own_weight[0], shared_weight), which == 1
            )
            return (
                plane.reshape(all_tokens, width),
                [own.reshape(1, -1, width), shared],
                [own_out[None], shared_out],
            )
        (plane,) = exchange(("head_gather", rows))
        plane = plane.reshape(all_tokens, width)
        queues = [
            part
            for part in to_experts(mm("rt,td->rd", turned_places, plane).astype(jnp.bfloat16))
            if part is not None
        ]
        spec = ("erd,edf->erf", "erd,efd->erf")[which]
        return (plane, queues, [mm(spec, rows, mats[which]) for rows, mats in zip(queues, sets)])

    def moe_out(units, places, sets, which, extra=None):
        if owned == 1 and owned_total < experts_local:
            own_weight, shared_weight = (matrices[which] for matrices in sets)
            total, returned, *extras = combine(
                units[0][0],
                units[1],
                places,
                (own_weight[0], shared_weight),
                which == 0,
                extra,
            )
            return (total, returned.reshape(-1, width), *extras)
        spec = ("erf,edf->erd", "erf,efd->erd")[which]
        made = [mm(spec, part, mats[which]).astype(jnp.bfloat16) for part, mats in zip(units, sets)]
        returned = from_experts(*(made if owned else [None] + made))
        parts, *extras = exchange(
            ("head_swap", head_parts(mm("tr,rd->td", places, returned))),
            *([] if extra is None else [("head_gather", extra)]),
        )
        return (head_sum(parts), returned, *extras)

    def gated(gate_up):
        return (jax.nn.silu(gate_up[..., :FF]) * gate_up[..., FF:]).astype(jnp.bfloat16)

    def gated_back(gate_up, grad_units):
        gate_part = gate_up[..., :FF]
        up_part = gate_up[..., FF:]
        sigmoid_part = jax.nn.sigmoid(gate_part)
        return jnp.concatenate(
            [
                grad_units * up_part * sigmoid_part * (1.0 + gate_part * (1.0 - sigmoid_part)),
                grad_units * gate_part * sigmoid_part,
            ],
            axis=-1,
        ).astype(jnp.bfloat16)

    def by_slot(rows):
        return (
            rows.reshape(heads_count, SEQUENCE_SLOTS, resident, -1)
            .transpose(1, 0, 2, 3)
            .reshape(SEQUENCE_SLOTS, rows_local, -1)
        )

    def by_head(rows):
        return (
            rows.reshape(SEQUENCE_SLOTS, heads_count, resident, -1)
            .transpose(1, 0, 2, 3)
            .reshape(all_tokens, -1)
        )

    small_columns = 128
    send = []
    for layer_index in range(DECODER_LAYERS):
        weight = query_key_value_weight[layer_index]
        split = QUERY_HEAD_COUNT * HEAD_SIZE
        small = jnp.concatenate([router[layer_index], norm_gains[layer_index].T], axis=1)
        small = jnp.pad(small, ((0, 0), (0, small_columns - small.shape[1])))
        send.append(
            jnp.concatenate(
                [
                    weight[:, :split]
                    .reshape(weight_rows, heads_count, query_columns)
                    .transpose(1, 0, 2),
                    weight[:, split:]
                    .reshape(weight_rows, heads_count, pair_columns)
                    .transpose(1, 0, 2),
                    jnp.broadcast_to(small[None], (heads_count,) + small.shape),
                ],
                axis=-1,
            )
        )
    plan = jnp.stack([routes, queue_ranks]).reshape(2 * DECODER_LAYERS, slot_rows * TOP)
    plan, plane_tokens, first_send, first_out, *own_in_next = exchange(
        ("head_gather", plan),
        ("head_gather", tokens.reshape(slot_rows, width)),
        ("head_swap", send[0]),
        ("blk_pairs", w_out[0]),
        *to_owner(w_in, 0),
    )
    plan = plan.reshape(heads_count, 2, DECODER_LAYERS, slot_rows, TOP)
    plane_tokens = plane_tokens.reshape(all_tokens, width)

    def attention_set(wide, out_full):
        wide = wide.transpose(1, 0, 2, 3).reshape(width, -1)
        columns = query_columns + pair_columns
        small = wide[:, columns:]
        gains = small.T[EXPERTS : EXPERTS + 2].astype(jnp.float32)
        return (wide[:, :columns], out_full.reshape(-1, width), small[:, :EXPERTS], gains)

    (wide,) = exchange(("blk_pairs", first_send))
    attention_weights = [
        attention_set(wide, first_out),
    ]

    hidden = tokens.reshape(slot_rows, width).astype(jnp.float32)
    stored_all = []
    for layer_index in range(DECODER_LAYERS):
        qkv_full, out_full, router_full, gains = attention_weights[layer_index]
        chosen, places = layer_plan(layer_index)
        scaled_a, inverse_a = norm_rows(hidden)
        if layer_index:
            plane_normed_a, *own_in_next = exchange(
                ("head_gather", (scaled_a * gains[:1]).astype(jnp.bfloat16)),
                *to_owner(w_in, layer_index),
            )
            plane_normed_a = plane_normed_a.reshape(all_tokens, width)
        else:
            plane_normed_a = (
                norm_rows(plane_tokens.astype(jnp.float32))[0] * gains[:1]
            ).astype(jnp.bfloat16)
        projected = mm("td,de->te", plane_normed_a, qkv_full)
        queries = by_slot(rotate(projected[:, :query_columns], cosine, sine).astype(jnp.bfloat16))
        pairs = projected[:, query_columns:].reshape(all_tokens, kv_local, 2, HEAD_SIZE)
        keys = rotate(pairs[:, :, 0].reshape(all_tokens, -1), cosine, sine)
        pairs = jnp.stack([keys.reshape(all_tokens, kv_local, HEAD_SIZE), pairs[:, :, 1]], axis=2)
        pairs = pairs.reshape(all_tokens, pair_columns).astype(jnp.bfloat16)
        if layer_index + 1 < DECODER_LAYERS:
            pairs, next_send = exchange(
                ("blk_pairs", pairs), ("head_swap", send[layer_index + 1])
            )
            attention_weights.append(
                attention_set(
                    lax.all_gather(next_send, "blk", axis=0),
                    lax.all_gather(w_out[layer_index + 1], "blk", axis=0),
                )
            )
        else:
            (pairs,) = exchange(("blk_pairs", pairs))
        pairs_all = (
            pairs.reshape(blocks_count, heads_count, SEQUENCE_SLOTS, resident, pair_columns)
            .transpose(2, 1, 0, 3, 4)
            .reshape(SEQUENCE_SLOTS, keys_total, pair_columns)
        )
        (attended,) = attention_call(
            functools.partial(
                attend_kernel, heads_count, blocks_count, resident, group, kv_local
            ),
            info,
            [queries, pairs_all],
            [jax.ShapeDtypeStruct(queries.shape, jnp.bfloat16)],
            [],
            4 * rows_local * keys_total * query_columns,
            "attend",
        )
        attended = by_head(attended)
        branch, *own_down_next = exchange(
            ("head_swap", head_parts(mm("tf,fd->td", attended, out_full))),
            *to_owner(w_down, layer_index),
        )
        weight_sets = shared_weights(layer_index)
        if owned:
            weight_sets = [
                (owned_matrix(own_in_next[0]), owned_matrix(own_down_next[0]))
            ] + weight_sets
        middle = hidden + valid_column * head_sum(branch)
        scaled_b, inverse_b = norm_rows(middle)
        normed_b = (scaled_b * gains[1:]).astype(jnp.bfloat16)
        plane_rows, incoming, gate_up = moe_in(normed_b, places.T, weight_sets, 0)
        units = [gated(part) for part in gate_up]
        logits = mm("td,de->te", plane_rows, router_full)
        peaks = jnp.max(jnp.where(chosen, logits, negative), axis=-1, keepdims=True)
        lifted = jnp.where(chosen, jnp.exp(logits - peaks), 0.0)
        gates_all = lifted / jnp.sum(lifted, axis=-1, keepdims=True)
        plane_gates = lax.dynamic_slice_in_dim(
            gates_all, head_index * experts_local, experts_local, 1
        )
        weighted_places = (
            mm("te,er->tr", plane_gates.astype(jnp.bfloat16), spread).astype(jnp.bfloat16) * places
        )
        mixture, returned = moe_out(units, weighted_places, weight_sets, 1)
        stored_all.append(
            (
                weight_sets,
                places,
                scaled_a,
                inverse_a,
                plane_normed_a,
                queries,
                pairs_all,
                attended,
                scaled_b,
                inverse_b,
                plane_rows,
                gates_all,
                weighted_places,
                incoming,
                gate_up,
                units,
                returned,
            )
        )
        hidden = middle + valid_column * mixture
    result = (valid_column * hidden).astype(jnp.bfloat16).reshape(tokens.shape)
    grad_hidden = valid_column * cotangent.reshape(slot_rows, width).astype(jnp.float32)
    qkv_list = [None] * DECODER_LAYERS
    out_list = [None] * DECODER_LAYERS
    router_list = [None] * DECODER_LAYERS
    gains_list = [None] * DECODER_LAYERS
    expert_list = [None] * DECODER_LAYERS
    pending = []
    for layer_index in reversed(range(DECODER_LAYERS)):
        qkv_full, out_full, router_full, gains = attention_weights[layer_index]
        (
            weight_sets,
            places,
            scaled_a,
            inverse_a,
            plane_normed_a,
            queries,
            pairs_all,
            attended,
            scaled_b,
            inverse_b,
            plane_rows,
            gates_all,
            weighted_places,
            incoming,
            gate_up,
            units,
            returned,
        ) = stored_all[layer_index]
        plane_grads, grad_produced, grad_units = moe_in(
            (valid_column * grad_hidden).astype(jnp.bfloat16),
            weighted_places.T,
            weight_sets,
            1,
        )
        grad_gate_up = [gated_back(*parts) for parts in zip(gate_up, grad_units)]
        pair_dots = (mm("td,rd->tr", plane_grads, returned) * places).astype(jnp.bfloat16)
        plane_grad_gates = mm("tr,er->te", pair_dots, spread).T
        grad_normed_b, _, grad_gates = moe_out(
            grad_gate_up, places, weight_sets, 0, plane_grad_gates
        )
        grad_gates = grad_gates.reshape(EXPERTS, all_tokens).T
        grad_weight_sets = [
            (
                mm("erd,erf->edf", rows, grads).astype(jnp.bfloat16),
                mm("erf,erd->efd", inner, out_grads).astype(jnp.bfloat16),
            )
            for rows, grads, inner, out_grads in zip(incoming, grad_gate_up, units, grad_produced)
        ]
        grad_logits = gates_all * (
            grad_gates - jnp.sum(gates_all * grad_gates, axis=-1, keepdims=True)
        )
        plane_width = width // heads_count
        grad_router = mm(
            "td,te->de",
            lax.dynamic_slice_in_dim(plane_rows, head_index * plane_width, plane_width, 1),
            grad_logits.astype(jnp.bfloat16),
        )
        own_logits = lax.dynamic_slice_in_dim(grad_logits, head_index * slot_rows, slot_rows, 0)
        grad_normed_b = grad_normed_b + mm(
            "te,de->td", own_logits.astype(jnp.bfloat16), router_full
        )
        grad_norm_b, grad_gain_b = norm_back(grad_normed_b, scaled_b, inverse_b, gains[1:])
        grad_middle = grad_hidden + grad_norm_b
        plane_branch, *own_grad_in = exchange(
            ("head_gather", (valid_column * grad_middle).astype(jnp.bfloat16)),
            *(from_owner(grad_weight_sets[0][0]) if owned else []),
            after=[*pending, *(grad_weight_sets[-1] if owned_total < experts_local else ())],
        )
        pending = []
        shared_terms = []
        if owned_total < experts_local:
            shared_terms = [
                lax.psum_scatter(term, "blk", scatter_dimension=1, tiled=True)
                for term in grad_weight_sets[-1]
            ]
        plane_branch = plane_branch.reshape(all_tokens, width)
        grad_out_w = mm("tf,td->fd", attended, plane_branch)
        grad_attended = by_slot(mm("td,fd->tf", plane_branch, out_full).astype(jnp.bfloat16))
        grad_queries, grad_pairs = attention_call(
            functools.partial(
                attend_back_kernel, heads_count, blocks_count, resident, group, kv_local
            ),
            info,
            [queries, pairs_all, grad_attended],
            [
                jax.ShapeDtypeStruct(queries.shape, jnp.bfloat16),
                jax.ShapeDtypeStruct(pairs_all.shape, jnp.bfloat16),
            ],
            [pltpu.VMEM((keys_total, pair_columns), jnp.float32)],
            10 * rows_local * keys_total * query_columns,
            "attend_back",
        )
        grad_pairs = (
            grad_pairs.reshape(SEQUENCE_SLOTS, heads_count, blocks_count, resident, pair_columns)
            .transpose(2, 1, 0, 3, 4)
            .reshape(blocks_count, all_tokens, pair_columns)
        )
        (grad_pairs,) = exchange(("blk_swap", grad_pairs))
        grad_pairs = jnp.sum(grad_pairs.astype(jnp.float32), axis=0)
        grad_pairs = grad_pairs.astype(jnp.bfloat16).astype(jnp.float32)
        grad_pairs = grad_pairs.reshape(all_tokens, kv_local, 2, HEAD_SIZE)
        grad_keys = rotate(grad_pairs[:, :, 0].reshape(all_tokens, -1), cosine, -sine)
        grad_projected = jnp.concatenate(
            [
                rotate(by_head(grad_queries).astype(jnp.float32), cosine, -sine),
                jnp.stack(
                    [grad_keys.reshape(all_tokens, kv_local, HEAD_SIZE), grad_pairs[:, :, 1]],
                    axis=2,
                ).reshape(all_tokens, pair_columns),
            ],
            axis=-1,
        ).astype(jnp.bfloat16)
        grad_qkv = mm("td,te->de", plane_normed_a, grad_projected)
        grad_out_w = jnp.concatenate(
            [grad_out_w, jnp.pad(grad_router, ((0, 0), (0, small_columns - EXPERTS)))], axis=1
        ).astype(jnp.bfloat16)
        grad_qkv = (
            grad_qkv.astype(jnp.bfloat16)
            .reshape(heads_count, blocks_count, weight_rows, -1)
            .transpose(1, 0, 2, 3)
        )
        grad_normed_a, grad_out_w, *others = exchange(
            ("head_swap", head_parts(mm("te,de->td", grad_projected, qkv_full))),
            ("blk_swap", grad_out_w.reshape(blocks_count, weight_rows, -1)),
            *([] if layer_index else [("blk_swap", grad_qkv)]),
            *(from_owner(grad_weight_sets[0][1]) if owned else []),
            after=shared_terms,
        )
        if layer_index:
            own_grad_down = others
            grad_qkv = lax.psum_scatter(
                grad_qkv.reshape(width, -1), "blk", scatter_dimension=0, tiled=True
            )
            pending.append(grad_qkv)
        else:
            grad_qkv, *own_grad_down = others
            grad_qkv = jnp.sum(grad_qkv.astype(jnp.float32), axis=0).astype(jnp.bfloat16)
        grad_out_w = jnp.sum(grad_out_w.astype(jnp.float32), axis=0)
        grad_normed_a = head_sum(grad_normed_a)
        grad_norm_a, grad_gain_a = norm_back(grad_normed_a, scaled_a, inverse_a, gains[:1])
        grad_hidden = grad_middle + grad_norm_a

        out_list[layer_index] = grad_out_w[:, :width]
        router_list[layer_index] = grad_out_w[:, width : width + EXPERTS]
        grad_qkv = lax.all_to_all(
            grad_qkv.reshape(heads_count, weight_rows, -1), "head", 0, 0, tiled=True
        ).transpose(1, 0, 2)
        qkv_list[layer_index] = jnp.concatenate(
            [
                grad_qkv[..., :query_columns].reshape(weight_rows, -1),
                grad_qkv[..., query_columns:].reshape(weight_rows, -1),
            ],
            axis=1,
        ).astype(jnp.float32)
        gains_list[layer_index] = jnp.stack([grad_gain_a, grad_gain_b])
        terms = []
        for number, received in enumerate((own_grad_in, own_grad_down)):
            parts = owned_rows(received[0]) if owned else []
            if owned_total < experts_local:
                parts.append(shared_terms[number])
            terms.append(jnp.concatenate(parts, axis=0).astype(jnp.float32))
        expert_list[layer_index] = tuple(terms)
    devices = heads_count * blocks_count
    grad_gains = jnp.stack(gains_list).reshape(2 * DECODER_LAYERS, devices, weight_rows)
    grad_gains = lax.all_to_all(
        grad_gains.transpose(1, 0, 2).reshape(devices, -1), ("head", "blk"), 0, 0, tiled=True
    )
    grad_gains = jnp.sum(grad_gains, axis=0).reshape(DECODER_LAYERS, 2, weight_rows)
    return (
        result,
        grad_hidden.reshape(tokens.shape),
        jnp.stack(qkv_list),
        jnp.stack(out_list),
        jnp.stack(router_list),
        grad_gains[:, 0],
        grad_gains[:, 1],
        jnp.stack([terms[0] for terms in expert_list]),
        jnp.stack([terms[1] for terms in expert_list]),
    )


def solution(mesh):
    in_specs = (
        P(None, ("head", "blk"), None),
        P(),
        P(None, None, ("head", "blk"), None),
        P(None, None, ("head", "blk"), None),
        P(None, ("head", "blk"), None),
        P(None, ("head", "blk"), None),
        P(None, ("head", "blk"), None),
        P(None, None, ("head", "blk")),
        P(None, "head", "blk", None),
        P(None, "head", "blk", None),
        P(None, ("head", "blk"), None),
    )
    out_specs = (
        P(None, ("head", "blk"), None),
        P(None, ("head", "blk"), None),
        P(None, ("head", "blk"), None),
        P(None, ("head", "blk"), None),
        P(None, ("head", "blk"), None),
        P(None, ("head", "blk")),
        P(None, ("head", "blk")),
        P(None, "head", "blk", None),
        P(None, "head", "blk", None),
    )
    return jax.shard_map(shards, mesh=mesh, in_specs=in_specs, out_specs=out_specs, check_vma=False)
```

```python
import functools

import jax
import jax.numpy as jnp
from jax import lax
from jax.experimental import pallas as pl
from jax.experimental.pallas import tpu as pltpu
from jax.sharding import PartitionSpec as P

MODEL_WIDTH = 1536
QUERY_HEAD_COUNT = 24
KEY_VALUE_HEADS = 8
HEAD_SIZE = 64
FF = 512
EXPERTS = 40
TOP = 8
DECODER_LAYERS = 2
SEQUENCE_SLOTS = 2
CAP = 26


epsilon = 1e-06
negative = -1e30
theta_log = 9.210340371976184


MESH = pl.DeviceIdType.MESH


def mm(spec, left, right):
    return jnp.einsum(spec, left, right, preferred_element_type=jnp.float32)


def rotate(values, cosine, sine):
    rows = values.shape[0]
    half = HEAD_SIZE // 2
    heads = values.reshape(rows, -1, HEAD_SIZE)
    first_half = heads[..., :half]
    second_half = heads[..., half:]
    cosine = cosine[:, None, :]
    sine = sine[:, None, :]
    return jnp.concatenate(
        [first_half * cosine - second_half * sine, second_half * cosine + first_half * sine],
        axis=-1,
    ).reshape(values.shape)


def norm_rows(hidden):
    inverse = lax.rsqrt(jnp.mean(hidden * hidden, axis=-1, keepdims=True) + epsilon)
    return (hidden * inverse, inverse)


def norm_back(grad_normed, scaled, inverse, gain_row):
    grad_gain = jnp.sum(grad_normed * scaled, axis=0)
    grad_scaled = grad_normed * gain_row
    grad_hidden = inverse * (
        grad_scaled - scaled * jnp.mean(grad_scaled * scaled, axis=-1, keepdims=True)
    )
    return (grad_hidden, grad_gain)


def exchange_kernel(heads, blocks, items, waited, *refs):
    count = len(items)
    sources = refs[:count]
    targets = refs[count + waited : 2 * count + waited]
    send_sems, recv_sems, local_sems = refs[2 * count + waited :]
    head = lax.axis_index("head")
    blk = lax.axis_index("blk")
    chips = blocks // 2
    chip, core = blk // 2, lax.rem(blk, 2)
    sibling = chip * 2 + 1 - core
    kinds = {kind for kind, _ in items}
    head_peers = [(lax.rem(head + step, heads), blk) for step in range(1, heads)]
    blk_peers = [(head, lax.rem(blk + step, blocks)) for step in range(1, blocks)]
    pair_peers = [
        (head, lax.rem(chip + step, chips) * 2 + core) for step in range(1, chips)
    ] + [(head, sibling)]
    greeted = []
    if kinds & {"head_gather", "head_swap"}:
        greeted += head_peers
    if "blk_swap" in kinds:
        greeted += blk_peers
    elif "blk_pairs" in kinds:
        greeted += pair_peers
    barrier = pltpu.get_barrier_semaphore()
    for peer in greeted:
        pl.semaphore_signal(barrier, inc=1, device_id=peer, device_id_type=MESH)
    pl.semaphore_wait(barrier, len(greeted))
    used = 0
    copies = []
    forwards = []

    def send(source, target, peer):
        nonlocal used
        copy = pltpu.make_async_remote_copy(
            src_ref=source,
            dst_ref=target,
            send_sem=send_sems.at[used],
            recv_sem=recv_sems.at[used],
            device_id=peer,
            device_id_type=MESH,
        )
        copy.start()
        used += 1
        return copy

    locals_started = []
    for number, (kind, layer) in enumerate(items):
        source, target = sources[number], targets[number]

        def piece(index, source=source, layer=layer):
            return source.at[index] if layer is None else source.at[layer, index]

        if kind == "head_gather":
            mine, place = source, head
            copies += [send(source, target.at[head], peer) for peer in head_peers]
        elif kind == "head_swap":
            mine, place = piece(head), head
            copies += [send(piece(peer[0]), target.at[head], peer) for peer in head_peers]
        elif kind == "blk_swap":
            mine, place = piece(blk), blk
            copies += [send(piece(peer[1]), target.at[blk], peer) for peer in blk_peers]
        else:
            mine, place = source, blk
            sent = [send(source, target.at[blk], peer) for peer in pair_peers]
            copies += sent[-1:]
            forwards.append((sent[:-1], target))
        local = pltpu.make_async_copy(mine, target.at[place], local_sems.at[number])
        local.start()
        locals_started.append(local)
    for sent, target in forwards:
        for step, copy in enumerate(sent, start=1):
            copy.wait_recv()
            origin = lax.rem(chip + chips - step, chips) * 2 + core
            copies.append(send(target.at[origin], target.at[origin], (head, sibling)))
    for sent, _ in forwards:
        for copy in sent:
            copy.wait_send()
    for local in locals_started:
        local.wait()
    for copy in copies:
        copy.wait()


kernel_numbers = {}


def kernel_number(*key):
    return kernel_numbers.setdefault(key, 1 + len(kernel_numbers))


def exchange(*items, after=()):
    heads, blocks = lax.axis_size("head"), lax.axis_size("blk")
    arrays = [item[1] for item in items]
    plan = [(item[0], item[2] if len(item) > 2 else None) for item in items]
    outs = []
    total = 0
    for (kind, layer), array in zip(plan, arrays):
        group = heads if kind.startswith("head") else blocks
        tail = array.shape
        if kind.endswith("swap"):
            tail = tail[1:] if layer is None else tail[2:]
        outs.append(jax.ShapeDtypeStruct((group,) + tail, array.dtype))
        total += group - 1
    collective_id = kernel_number(
        "exchange", tuple(plan), *((array.shape, str(array.dtype)) for array in (*arrays, *after))
    )
    results = pl.pallas_call(
        functools.partial(exchange_kernel, heads, blocks, plan, len(after)),
        out_shape=outs,
        in_specs=[pl.BlockSpec(memory_space=pl.ANY)] * (len(arrays) + len(after)),
        out_specs=[pl.BlockSpec(memory_space=pl.ANY)] * len(arrays),
        scratch_shapes=[
            pltpu.SemaphoreType.DMA((total,)),
            pltpu.SemaphoreType.DMA((total,)),
            pltpu.SemaphoreType.DMA((len(arrays),)),
        ],
        compiler_params=pltpu.CompilerParams(collective_id=collective_id, has_side_effects=True),
        cost_estimate=pl.CostEstimate(flops=0, bytes_accessed=110 << 20, transcendentals=0),
        name="exchange",
    )(*arrays, *after)
    return results


def greet(peers):
    barrier = pltpu.get_barrier_semaphore()
    for peer in peers:
        pl.semaphore_signal(barrier, inc=1, device_id=peer, device_id_type=MESH)
    pl.semaphore_wait(barrier, len(peers))


def plane_peers(heads, blocks):
    head = lax.axis_index("head")
    blk = lax.axis_index("blk")
    head_peers = [(lax.rem(head + step, heads), blk) for step in range(1, heads)]
    blk_peers = [(head, lax.rem(blk + step, blocks)) for step in range(1, blocks)]
    return head, blk, head_peers, blk_peers


def remote(source, target, sems, index, peer, landing=None):
    return pltpu.make_async_remote_copy(
        src_ref=source,
        dst_ref=target,
        send_sem=sems[0].at[index],
        recv_sem=sems[1].at[index if landing is None else landing],
        device_id=peer,
        device_id_type=MESH,
    )


def started(copy):
    copy.start()
    return copy


def weight_part(ref, columns, by_columns):
    return ref[:, columns] if by_columns else ref[columns, :]


def meet(left, part, by_columns):
    return (
        dot_last(left, part)
        if by_columns
        else jnp.dot(left, part, preferred_element_type=jnp.float32)
    )


DISPATCH_PIECES, DISPATCH_WINDOW, DISPATCH_LAG = 6, 3, 2
COMBINE_PIECES = 6


def dispatch_stages(heads, blocks, by_columns, refs):
    (
        own_ref,
        place_ref,
        scale_ref,
        weight_ref,
        shared_weight_ref,
        plane_ref,
        queue_ref,
        shared_ref,
        out_ref,
        shared_out_ref,
        send_ref,
        held_ref,
        shared_held_ref,
        head_send,
        head_recv,
        blk_send,
        blk_recv,
        local_sems,
    ) = refs
    pieces, window, lag = DISPATCH_PIECES, DISPATCH_WINDOW, DISPATCH_LAG
    head, blk, head_peers, blk_peers = plane_peers(heads, blocks)
    rows, width = own_ref.shape
    slot = queue_ref.shape[1]
    shared = shared_ref.shape[0]
    step_width = width // pieces
    outputs = out_ref.shape[1]
    tile = 256
    relay = heads == 4
    inner = jnp.logical_and(head > 0, head < heads - 1)
    loads = [
        pltpu.make_async_copy(weight_ref, held_ref, local_sems.at[0]),
        pltpu.make_async_copy(shared_weight_ref, shared_held_ref, local_sems.at[1]),
    ]
    head_copies = []
    blk_copies = []
    relayed = []

    def far(peer):
        return jnp.abs(peer[0] - head) == heads - 1

    def spread(piece):
        columns = pl.ds(piece * step_width, step_width)
        copies = []
        for number, peer in enumerate(head_peers):
            copy = remote(
                own_ref.at[:, columns],
                plane_ref.at[head, :, columns],
                (head_send, head_recv),
                piece * heads + number,
                peer,
            )
            copies.append(copy)
            if relay and number != 1:
                pl.when(jnp.logical_not(far(peer)))(copy.start)
            else:
                copy.start()
        head_copies.append(copies)

    def pass_on(piece):
        columns = pl.ds(piece * step_width, step_width)
        origin = lax.rem(head + 2, heads)
        rows_there = plane_ref.at[origin, :, columns]
        copy = remote(
            rows_there,
            rows_there,
            (head_send, head_recv),
            piece * heads + heads - 1,
            ((head - 1) * (heads - 1), blk),
            piece * heads + jnp.where(head == 1, 0, heads - 2),
        )
        relayed.append(copy)
        pl.when(inner)(copy.start)

    def scaled(values, start):
        if scale_ref is not None:
            values = values * scale_ref[pl.ds(start, slot), :]
        return values.astype(queue_ref.dtype)

    def begin():
        for load in loads:
            load.start()
        for piece in range(min(window, pieces)):
            spread(piece)
        plane_ref[head] = own_ref[...]

    def consume(piece):
        columns = pl.ds(piece * step_width, step_width)
        for copy in blk_copies[piece]:
            copy.wait_recv()
        queue = queue_ref[:, :, columns].reshape(blocks * slot, step_width)

        def one_tile(index, carry):
            lanes = pl.ds(pl.multiple_of(index * tile, tile), tile)
            if by_columns:
                product = dot_last(queue, held_ref[lanes, columns])
            else:
                product = jnp.dot(
                    queue, held_ref[columns, lanes], preferred_element_type=jnp.float32
                )
            if piece:
                product = product + out_ref[:, lanes]
            out_ref[:, lanes] = product
            return carry

        lax.fori_loop(0, outputs // tile, one_tile, 0)

    def take(piece):
        columns = pl.ds(piece * step_width, step_width)
        if relay:
            for later in range(piece + 1 if piece else 0, min(piece + 2, pieces)):
                head_copies[later][1].wait_recv()
                pass_on(later)
        for number, copy in enumerate(head_copies[piece]):
            if not relay or number != 1:
                copy.wait_recv()
        if piece + window < pieces:
            spread(piece + window)
        plane = plane_ref[:, :, columns].reshape(heads * rows, step_width)

        def fill(expert, carry):
            start = pl.multiple_of(expert * slot, 16)
            taken = jnp.dot(
                place_ref[pl.ds(start, slot), :], plane, preferred_element_type=jnp.float32
            )
            send_ref[expert, :, columns] = scaled(taken, start)
            return carry

        lax.fori_loop(0, blocks, fill, 0)
        blk_copies.append(
            [
                started(
                    remote(
                        send_ref.at[peer[1], :, columns],
                        queue_ref.at[blk, :, columns],
                        (blk_send, blk_recv),
                        piece * (blocks - 1) + number,
                        peer,
                    )
                )
                for number, peer in enumerate(blk_peers)
            ]
        )
        queue_ref[blk, :, columns] = send_ref[blk, :, columns]
        if not piece:
            for load in loads:
                load.wait()
        for expert in range(shared):
            start = (blocks + expert) * slot
            taken = jnp.dot(
                place_ref[pl.ds(start, slot), :], plane, preferred_element_type=jnp.float32
            )
            taken = scaled(taken, start)
            shared_ref[expert, :, columns] = taken
            product = meet(
                taken, weight_part(shared_held_ref.at[expert], columns, by_columns), by_columns
            )
            if piece:
                product = product + shared_out_ref[expert]
            shared_out_ref[expert] = product

    def step(number):
        if number < pieces:
            take(number)
        if number >= lag:
            consume(number - lag)

    def end():
        for copies in head_copies:
            for number, copy in enumerate(copies):
                if relay and number != 1:
                    pl.when(jnp.logical_not(far(head_peers[number])))(copy.wait_send)
                else:
                    copy.wait_send()
        for copy in relayed:
            pl.when(inner)(copy.wait_send)
        for copies in blk_copies:
            for copy in copies:
                copy.wait_send()

    steps = [functools.partial(step, number) for number in range(pieces + lag)]
    return [begin, *steps, end]


def dispatch_plan(rows, places, scale, weights, by_columns):
    heads, blocks = lax.axis_size("head"), lax.axis_size("blk")
    count, width = rows.shape
    (own_weight, shared_weight) = weights
    shared = shared_weight.shape[0]
    slot = places.shape[0] // (blocks + shared)
    outputs = own_weight.shape[0 if by_columns else 1]
    pieces = DISPATCH_PIECES
    vmem = pl.BlockSpec(memory_space=pltpu.VMEM)
    anywhere = pl.BlockSpec(memory_space=pl.ANY)
    scales = [] if scale is None else [scale]
    return (
        [rows, places, *scales, own_weight, shared_weight],
        [vmem, vmem, *([vmem] * len(scales)), anywhere, anywhere],
        [
            jax.ShapeDtypeStruct((heads, count, width), jnp.bfloat16),
            jax.ShapeDtypeStruct((blocks, slot, width), jnp.bfloat16),
            jax.ShapeDtypeStruct((shared, slot, width), jnp.bfloat16),
            jax.ShapeDtypeStruct((blocks * slot, outputs), jnp.float32),
            jax.ShapeDtypeStruct((shared, slot, outputs), jnp.float32),
        ],
        [vmem] * 5,
        [
            pltpu.VMEM((blocks, slot, width), jnp.bfloat16),
            pltpu.VMEM(own_weight.shape, jnp.bfloat16),
            pltpu.VMEM(shared_weight.shape, jnp.bfloat16),
            pltpu.SemaphoreType.DMA((pieces * heads,)),
            pltpu.SemaphoreType.DMA((pieces * heads,)),
            pltpu.SemaphoreType.DMA((pieces * (blocks - 1),)),
            pltpu.SemaphoreType.DMA((pieces * (blocks - 1),)),
            pltpu.SemaphoreType.DMA((2,)),
        ],
    )


def staged_call(plans, name, millions):
    heads, blocks = lax.axis_size("head"), lax.axis_size("blk")
    inputs = [len(plan[2]) for plan in plans]
    outputs = [len(plan[4]) for plan in plans]
    scratches = [len(plan[6]) for plan in plans]

    def kernel(*refs):
        _, _, head_peers, blk_peers = plane_peers(heads, blocks)
        greet(head_peers + blk_peers)
        lists = []
        for number, plan in enumerate(plans):
            first = sum(inputs[:number])
            given = list(refs[first : first + inputs[number]])
            if not plan[7]:
                given.insert(2 if plan[0][0] == "dispatch" else 3, None)
            first = sum(inputs) + sum(outputs[:number])
            given += refs[first : first + outputs[number]]
            first = sum(inputs) + sum(outputs) + sum(scratches[:number])
            given += refs[first : first + scratches[number]]
            lists.append(plan[1](given))
        for index in range(max(len(stages) for stages in lists)):
            for stages in lists:
                if index < len(stages):
                    stages[index]()

    arrays = [array for plan in plans for array in plan[2]]
    results = pl.pallas_call(
        kernel,
        out_shape=[out for plan in plans for out in plan[4]],
        in_specs=[spec for plan in plans for spec in plan[3]],
        out_specs=[spec for plan in plans for spec in plan[5]],
        scratch_shapes=[scratch for plan in plans for scratch in plan[6]],
        compiler_params=pltpu.CompilerParams(
            collective_id=kernel_number(*(plan[0] for plan in plans)),
            has_side_effects=True,
            vmem_limit_bytes=60 * 1024 * 1024,
        ),
        cost_estimate=pl.CostEstimate(
            flops=0, bytes_accessed=millions << 20, transcendentals=0
        ),
        name=name,
    )(*arrays)
    return [
        results[sum(outputs[:number]) : sum(outputs[: number + 1])] for number in range(len(plans))
    ]


def dispatch_call(rows, places, scale, weights, by_columns):
    heads, blocks = lax.axis_size("head"), lax.axis_size("blk")
    return (
        ("dispatch", by_columns, scale is not None),
        functools.partial(dispatch_stages, heads, blocks, by_columns),
        *dispatch_plan(rows, places, scale, weights, by_columns),
        scale is not None,
    )


def turn_heads(values, cosine, sine):
    lane = lax.broadcasted_iota(jnp.int32, values.shape, 1) % HEAD_SIZE
    half = HEAD_SIZE // 2
    width = values.shape[1]
    swapped = jnp.where(
        lane < half, pltpu.roll(values, width - half, 1), pltpu.roll(values, half, 1)
    )
    return values * cosine + swapped * sine


def project_kernel(
    heads,
    blocks,
    pieces,
    layer,
    own_ref,
    weight_ref,
    cosine_ref,
    sine_ref,
    moved_ref,
    plane_ref,
    query_ref,
    pair_ref,
    moved_out_ref,
    head_send,
    head_recv,
    pair_send,
    pair_recv,
    moved_send,
    moved_recv,
    local_sem,
):
    head, blk, head_peers, blk_peers = plane_peers(heads, blocks)
    chips = blocks // 2
    chip, core = blk // 2, lax.rem(blk, 2)
    sibling = (head, chip * 2 + 1 - core)
    rows, width = own_ref.shape
    count = rows // pieces
    slots, _, _, resident, pair_columns = pair_ref.shape
    query_columns = query_ref.shape[2]
    inner = jnp.logical_and(head > 0, head < heads - 1)
    greet(head_peers + blk_peers)

    def far(peer):
        return jnp.abs(peer[0] - head) == heads - 1

    def place(piece):
        return piece * count // resident, pl.ds(piece * count % resident, count)

    head_copies = []
    relayed = []
    for piece in range(pieces):
        part = pl.ds(piece * count, count)
        copies = []
        for number, peer in enumerate(head_peers):
            copy = remote(
                own_ref.at[part],
                plane_ref.at[head, part],
                (head_send, head_recv),
                piece * heads + number,
                peer,
            )
            copies.append(copy)
            if number != 1:
                pl.when(jnp.logical_not(far(peer)))(copy.start)
            else:
                copy.start()
        head_copies.append(copies)
    moved = []
    if layer is not None:
        moved = [
            started(
                remote(
                    moved_ref.at[layer, peer[1]],
                    moved_out_ref.at[blk],
                    (moved_send, moved_recv),
                    number,
                    peer,
                )
            )
            for number, peer in enumerate(blk_peers)
        ]
        local = pltpu.make_async_copy(moved_ref.at[layer, blk], moved_out_ref.at[blk], local_sem)
        local.start()
    plane_ref[head] = own_ref[...]

    def pass_on(piece):
        head_copies[piece][1].wait_recv()
        part = pl.ds(piece * count, count)
        rows_there = plane_ref.at[lax.rem(head + 2, heads), part]
        copy = remote(
            rows_there,
            rows_there,
            (head_send, head_recv),
            piece * heads + heads - 1,
            ((head - 1) * (heads - 1), blk),
            piece * heads + jnp.where(head == 1, 0, heads - 2),
        )
        relayed.append(copy)
        pl.when(inner)(copy.start)

    pair_copies = []
    forwards = []

    def forward(piece):
        slot, part = place(piece)
        for step in range(1, chips):
            pair_copies[piece][step - 1].wait_recv()
            origin = lax.rem(chip + chips - step, chips) * 2 + core
            there = pair_ref.at[slot, :, origin, part]
            forwards.append(
                started(
                    remote(
                        there,
                        there,
                        (pair_send, pair_recv),
                        piece * blocks + chips - 1 + step,
                        sibling,
                    )
                )
            )

    tile = 2 * HEAD_SIZE
    for piece in range(pieces):
        for later in range(piece + 1 if piece else 0, min(piece + 2, pieces)):
            pass_on(later)
        for number in range(heads - 1):
            if number != 1:
                head_copies[piece][number].wait_recv()
        part = pl.ds(piece * count, count)
        slot, inside = place(piece)
        projected = jnp.dot(
            plane_ref[:, part, :].reshape(heads * count, width),
            weight_ref[...],
            preferred_element_type=jnp.float32,
        )
        cosine = cosine_ref[:, part, :].reshape(heads * count, tile)
        sine = sine_ref[:, part, :].reshape(heads * count, tile)
        turned = jnp.concatenate(
            [
                turn_heads(projected[:, start : start + tile], cosine, sine)
                for start in range(0, query_columns, tile)
            ],
            axis=1,
        ).astype(query_ref.dtype)
        is_key = lax.broadcasted_iota(jnp.int32, cosine.shape, 1) < HEAD_SIZE
        key_cosine = jnp.where(is_key, cosine, 1.0)
        key_sine = jnp.where(is_key, sine, 0.0)
        pairs = jnp.concatenate(
            [
                turn_heads(projected[:, start : start + tile], key_cosine, key_sine)
                for start in range(query_columns, query_columns + pair_columns, tile)
            ],
            axis=1,
        ).astype(pair_ref.dtype)
        for there in range(heads):
            taken = slice(there * count, (there + 1) * count)
            query_ref[slot, pl.ds(there * resident + piece * count % resident, count), :] = turned[
                taken
            ]
            pair_ref[slot, there, blk, inside, :] = pairs[taken]
        mine = pair_ref.at[slot, :, blk, inside]
        targets = [
            (head, lax.rem(chip + step, chips) * 2 + core) for step in range(1, chips)
        ] + [sibling]
        pair_copies.append(
            [
                started(
                    remote(mine, mine, (pair_send, pair_recv), piece * blocks + number, peer)
                )
                for number, peer in enumerate(targets)
            ]
        )
        if piece:
            forward(piece - 1)
    forward(pieces - 1)
    for copies in pair_copies:
        for copy in copies[:-1]:
            copy.wait_send()
        copies[-1].wait()
    for copy in forwards:
        copy.wait()
    for copies in head_copies:
        for number, copy in enumerate(copies):
            if number != 1:
                pl.when(jnp.logical_not(far(head_peers[number])))(copy.wait_send)
            else:
                copy.wait_send()
    for copy in relayed:
        pl.when(inner)(copy.wait_send)
    for copy in moved:
        copy.wait()
    if moved:
        local.wait()


def project(rows, weight, cosine, sine, moved, layer, pair_columns, resident, pieces=4):
    heads, blocks = lax.axis_size("head"), lax.axis_size("blk")
    count, width = rows.shape
    slots = count // resident
    outs = [
        jax.ShapeDtypeStruct((heads, count, width), jnp.bfloat16),
        jax.ShapeDtypeStruct(
            (slots, heads * resident, weight.shape[1] - pair_columns), jnp.bfloat16
        ),
        jax.ShapeDtypeStruct((slots, heads, blocks, resident, pair_columns), jnp.bfloat16),
        jax.ShapeDtypeStruct((blocks,) + moved.shape[2:], moved.dtype),
    ]
    vmem = pl.BlockSpec(memory_space=pltpu.VMEM)
    anywhere = pl.BlockSpec(memory_space=pl.ANY)
    return pl.pallas_call(
        functools.partial(project_kernel, heads, blocks, pieces, layer),
        out_shape=outs,
        in_specs=[vmem] * 4 + [anywhere],
        out_specs=[vmem] * 3 + [anywhere],
        scratch_shapes=[
            pltpu.SemaphoreType.DMA((pieces * heads,)),
            pltpu.SemaphoreType.DMA((pieces * heads,)),
            pltpu.SemaphoreType.DMA((pieces * blocks,)),
            pltpu.SemaphoreType.DMA((pieces * blocks,)),
            pltpu.SemaphoreType.DMA((blocks,)),
            pltpu.SemaphoreType.DMA((blocks,)),
            pltpu.SemaphoreType.DMA,
        ],
        compiler_params=pltpu.CompilerParams(
            collective_id=kernel_number("project", layer),
            has_side_effects=True,
            vmem_limit_bytes=56 * 1024 * 1024,
        ),
        cost_estimate=pl.CostEstimate(flops=0, bytes_accessed=130 << 20, transcendentals=0),
        name="project",
    )(rows, weight, cosine, sine, moved)


def unproject_kernel(
    heads,
    blocks,
    pieces,
    items,
    grad_query_ref,
    grad_pair_ref,
    weight_ref,
    cosine_ref,
    sine_ref,
    *refs,
):
    moved_refs = refs[:items]
    grad_ref, out_ref = refs[items : items + 2]
    moved_out_refs = refs[items + 2 : 2 * items + 2]
    (
        near_ref,
        sum_ref,
        far_ref,
        product_ref,
        part_ref,
        landed_ref,
        relay_ref,
        near_send,
        near_recv,
        chip_send,
        chip_recv,
        head_send,
        head_recv,
        moved_send,
        moved_recv,
        local_sems,
    ) = refs[2 * items + 2 :]
    head, blk, head_peers, blk_peers = plane_peers(heads, blocks)
    chips = blocks // 2
    chip, core = blk // 2, lax.rem(blk, 2)
    sibling = (head, chip * 2 + 1 - core)
    rows, width = out_ref.shape
    count = rows // pieces
    resident, pair_columns = grad_pair_ref.shape[4:]
    query_columns = grad_query_ref.shape[2]
    inner = jnp.logical_and(head > 0, head < heads - 1)
    chip_peers = [(head, lax.rem(chip + step, chips) * 2 + core) for step in range(1, chips)]
    greet(head_peers + blk_peers)

    def far(peer):
        return jnp.abs(peer[0] - head) == heads - 1

    def peer_origin(peer):
        return lax.rem(2 * head + heads - peer[0], heads)

    def place(piece):
        return piece * count // resident, pl.ds(piece * count % resident, count)

    near_copies = []
    for piece in range(pieces):
        slot, inside = place(piece)
        near_copies.append(
            started(
                remote(
                    grad_pair_ref.at[slot, :, :, 1 - core, inside],
                    near_ref.at[piece],
                    (near_send, near_recv),
                    piece,
                    sibling,
                )
            )
        )
    chip_copies = []
    head_copies = []
    moved = []

    def add_cores(piece):
        slot, inside = place(piece)
        near_copies[piece].wait_recv()
        sum_ref[piece] = (
            grad_pair_ref[slot, :, :, core, inside, :].astype(jnp.float32)
            + near_ref[piece].astype(jnp.float32)
        ).astype(sum_ref.dtype)
        chip_copies.append(
            [
                started(
                    remote(
                        sum_ref.at[piece, :, peer[1] // 2],
                        far_ref.at[piece, chip],
                        (chip_send, chip_recv),
                        piece * chips + number,
                        peer,
                    )
                )
                for number, peer in enumerate(chip_peers)
            ]
        )

    def through_copy(piece, peer):
        part = pl.ds(piece * count, count)
        return remote(
            part_ref.at[peer[0], part],
            relay_ref.at[part],
            (head_send, head_recv),
            piece * heads + heads - 1,
            (jnp.where(head == 0, 1, heads - 2), blk),
        )

    tile = 2 * HEAD_SIZE

    def multiply(piece):
        slot, inside = place(piece)
        part = pl.ds(piece * count, count)
        for copy in chip_copies[piece]:
            copy.wait_recv()
        pairs = sum_ref[piece, :, chip].astype(jnp.float32)
        for peer in chip_peers:
            pairs = pairs + far_ref[piece, peer[1] // 2].astype(jnp.float32)
        pairs = pairs.reshape(heads * count, pair_columns)
        pairs = pairs.astype(jnp.bfloat16).astype(jnp.float32)
        queries = jnp.concatenate(
            [
                grad_query_ref[
                    slot, pl.ds(there * resident + piece * count % resident, count), :
                ]
                for there in range(heads)
            ],
            axis=0,
        ).astype(jnp.float32)
        cosine = cosine_ref[:, part, :].reshape(heads * count, tile)
        sine = -sine_ref[:, part, :].reshape(heads * count, tile)
        is_key = lax.broadcasted_iota(jnp.int32, cosine.shape, 1) < HEAD_SIZE
        key_cosine = jnp.where(is_key, cosine, 1.0)
        key_sine = jnp.where(is_key, sine, 0.0)
        turned = jnp.concatenate(
            [
                turn_heads(queries[:, start : start + tile], cosine, sine)
                for start in range(0, query_columns, tile)
            ]
            + [
                turn_heads(pairs[:, start : start + tile], key_cosine, key_sine)
                for start in range(0, pair_columns, tile)
            ],
            axis=1,
        ).astype(grad_ref.dtype)
        grad_ref[:, part, :] = turned.reshape(heads, count, query_columns + pair_columns)
        product_ref[...] = dot_last(turned, weight_ref[...]).reshape(heads, count, width)
        sent = []
        for number, peer in enumerate(head_peers):
            part_ref[peer[0], part, :] = product_ref[peer[0]].astype(part_ref.dtype)
            copy = remote(
                part_ref.at[peer[0], part],
                landed_ref.at[head, part],
                (head_send, head_recv),
                piece * heads + number,
                peer,
            )
            sent.append(copy)
            if number == 1:
                pl.when(jnp.logical_not(inner))(copy.start)
            else:
                distant = far(peer)
                pl.when(jnp.logical_not(distant))(copy.start)
                pl.when(distant)(through_copy(piece, peer).start)
        head_copies.append(sent)
        out_ref[part, :] = product_ref[head]

    def pass_on(piece):
        part = pl.ds(piece * count, count)
        target = lax.rem(head + 2, heads)

        @pl.when(inner)
        def _():
            through_copy(piece, (target, blk)).wait_recv()
            part_ref[target, part, :] = (
                part_ref[target, part, :].astype(jnp.float32)
                + relay_ref[part, :].astype(jnp.float32)
            ).astype(part_ref.dtype)
            head_copies[piece][1].start()

    def finish(piece):
        part = pl.ds(piece * count, count)
        for number, peer in enumerate(head_peers):
            copy = head_copies[piece][number]

            def add(copy=copy, peer=peer):
                copy.wait_recv()
                out_ref[part, :] += landed_ref[peer_origin(peer), part, :].astype(jnp.float32)

            if number != 1:
                pl.when(jnp.logical_not(far((peer_origin(peer), blk))))(add)
            else:
                add()

    for step in range(pieces + 3):
        if step < pieces:
            add_cores(step)
        if step == pieces - 1:
            for item in range(items):
                source, target = moved_refs[item], moved_out_refs[item]
                moved += [
                    started(
                        remote(
                            source.at[peer[1]],
                            target.at[blk],
                            (moved_send, moved_recv),
                            item * blocks + number,
                            peer,
                        )
                    )
                    for number, peer in enumerate(blk_peers)
                ]
                local = pltpu.make_async_copy(
                    source.at[blk], target.at[blk], local_sems.at[item]
                )
                moved.append(started(local))
        if 0 < step <= pieces:
            multiply(step - 1)
        if 1 < step <= pieces + 1:
            pass_on(step - 2)
        if step > 2:
            finish(step - 3)
    for copy in near_copies:
        copy.wait_send()
    for copies in chip_copies:
        for copy in copies:
            copy.wait_send()
    for piece, copies in enumerate(head_copies):
        for number, copy in enumerate(copies):
            if number != 1:
                distant = far(head_peers[number])
                pl.when(jnp.logical_not(distant))(copy.wait_send)
                pl.when(distant)(through_copy(piece, head_peers[number]).wait_send)
            else:
                copy.wait_send()
    for copy in moved:
        copy.wait()


def unproject(grad_queries, grad_pairs, weight, cosine, sine, moved, after, pieces=4):
    heads, blocks = lax.axis_size("head"), lax.axis_size("blk")
    chips = blocks // 2
    slots, _, _, _, resident, pair_columns = grad_pairs.shape
    rows = slots * resident
    count = rows // pieces
    width, columns = weight.shape
    outs = [
        jax.ShapeDtypeStruct((heads, rows, columns), jnp.bfloat16),
        jax.ShapeDtypeStruct((rows, width), jnp.float32),
    ] + [jax.ShapeDtypeStruct(array.shape, array.dtype) for array in moved]
    vmem = pl.BlockSpec(memory_space=pltpu.VMEM)
    anywhere = pl.BlockSpec(memory_space=pl.ANY)
    items = len(moved)

    def kernel(*refs):
        given = refs[: 5 + items]
        unproject_kernel(
            heads, blocks, pieces, items, *given, *refs[5 + items + len(after) :]
        )

    return pl.pallas_call(
        kernel,
        out_shape=outs,
        in_specs=[vmem] * 5 + [anywhere] * (items + len(after)),
        out_specs=[vmem] * 2 + [anywhere] * items,
        scratch_shapes=[
            pltpu.VMEM((pieces, heads, chips, count, pair_columns), jnp.bfloat16),
            pltpu.VMEM((pieces, heads, chips, count, pair_columns), jnp.bfloat16),
            pltpu.VMEM((pieces, chips, heads, count, pair_columns), jnp.bfloat16),
            pltpu.VMEM((heads, count, width), jnp.float32),
            pltpu.VMEM((heads, rows, width), jnp.bfloat16),
            pltpu.VMEM((heads, rows, width), jnp.bfloat16),
            pltpu.VMEM((rows, width), jnp.bfloat16),
            pltpu.SemaphoreType.DMA((pieces,)),
            pltpu.SemaphoreType.DMA((pieces,)),
            pltpu.SemaphoreType.DMA((pieces * chips,)),
            pltpu.SemaphoreType.DMA((pieces * chips,)),
            pltpu.SemaphoreType.DMA((pieces * heads,)),
            pltpu.SemaphoreType.DMA((pieces * heads,)),
            pltpu.SemaphoreType.DMA((items * blocks,)),
            pltpu.SemaphoreType.DMA((items * blocks,)),
            pltpu.SemaphoreType.DMA((items,)),
        ],
        compiler_params=pltpu.CompilerParams(
            collective_id=kernel_number(
                "unproject", *(array.shape for array in (*moved, *after))
            ),
            has_side_effects=True,
            vmem_limit_bytes=56 * 1024 * 1024,
        ),
        cost_estimate=pl.CostEstimate(flops=0, bytes_accessed=150 << 20, transcendentals=0),
        name="unproject",
    )(grad_queries, grad_pairs, weight, cosine, sine, *moved, *after)


def combine_stages(heads, blocks, by_columns, extra, refs):
    units_ref, shared_units_ref, place_ref, scale_ref, weight_ref, shared_weight_ref, *refs = refs
    extra_ref, *refs = refs if extra else (None, *refs)
    out_ref, returned_ref, *refs = refs
    extra_out_ref, *refs = refs if extra else (None, *refs)
    (
        made_ref,
        part_ref,
        landed_ref,
        relay_ref,
        held_ref,
        shared_held_ref,
        head_send,
        head_recv,
        blk_send,
        blk_recv,
        local_sems,
    ) = refs
    pieces = COMBINE_PIECES
    head, blk, head_peers, blk_peers = plane_peers(heads, blocks)
    rows, width = out_ref.shape
    slot = returned_ref.shape[1]
    shared = shared_units_ref.shape[0]
    step_width = width // pieces
    relay = heads == 4
    inner = jnp.logical_and(head > 0, head < heads - 1)
    loads = [
        pltpu.make_async_copy(weight_ref, held_ref, local_sems.at[0]),
        pltpu.make_async_copy(shared_weight_ref, shared_held_ref, local_sems.at[1]),
    ]
    extra_copies = []
    head_copies = []
    blk_copies = []

    def begin():
        if extra:
            loads.append(
                pltpu.make_async_copy(extra_ref, extra_out_ref.at[head], local_sems.at[2])
            )
        for load in loads:
            load.start()
        if extra:
            extra_copies.extend(
                started(
                    remote(
                        extra_ref,
                        extra_out_ref.at[head],
                        (head_send, head_recv),
                        pieces * heads + number,
                        peer,
                    )
                )
                for number, peer in enumerate(head_peers)
            )
        for load in loads:
            load.wait()

    def produce(piece):
        columns = pl.ds(piece * step_width, step_width)

        def make(block, carry):
            start = pl.multiple_of(block * slot, 16)
            made_ref[block, :, columns] = meet(
                units_ref[pl.ds(start, slot), :],
                weight_part(held_ref, columns, not by_columns),
                by_columns,
            ).astype(made_ref.dtype)
            return carry

        lax.fori_loop(0, blocks, make, 0)
        blk_copies.append(
            [
                started(
                    remote(
                        made_ref.at[peer[1], :, columns],
                        returned_ref.at[blk, :, columns],
                        (blk_send, blk_recv),
                        piece * (blocks - 1) + number,
                        peer,
                    )
                )
                for number, peer in enumerate(blk_peers)
            ]
        )
        returned_ref[blk, :, columns] = made_ref[blk, :, columns]
        for expert in range(shared):
            returned_ref[blocks + expert, :, columns] = meet(
                shared_units_ref[expert],
                weight_part(shared_held_ref.at[expert], columns, not by_columns),
                by_columns,
            ).astype(returned_ref.dtype)

    def far(peer):
        return jnp.abs(peer[0] - head) == heads - 1

    def peer_origin(peer):
        return lax.rem(2 * head + heads - peer[0], heads)

    def through_copy(piece, peer):
        columns = pl.ds(piece * step_width, step_width)
        return remote(
            part_ref.at[peer[0], :, columns],
            relay_ref.at[:, columns],
            (head_send, head_recv),
            piece * heads + heads - 1,
            (jnp.where(head == 0, 1, heads - 2), blk),
        )

    def gather(piece):
        columns = pl.ds(piece * step_width, step_width)
        for copy in blk_copies[piece]:
            copy.wait_recv()
        returned = returned_ref[:, :, columns].reshape((blocks + shared) * slot, step_width)
        if scale_ref is not None:
            returned = (returned.astype(jnp.float32) * scale_ref[...]).astype(returned_ref.dtype)

        def part(owner):
            start = pl.multiple_of(owner * rows, 16)
            return jnp.dot(
                place_ref[pl.ds(start, rows), :], returned, preferred_element_type=jnp.float32
            )

        sent = []
        for number, peer in enumerate(head_peers):
            part_ref[peer[0], :, columns] = part(peer[0]).astype(part_ref.dtype)
            copy = remote(
                part_ref.at[peer[0], :, columns],
                landed_ref.at[head, :, columns],
                (head_send, head_recv),
                piece * heads + number,
                peer,
            )
            sent.append(copy)
            if not relay:
                copy.start()
            elif number == 1:
                pl.when(jnp.logical_not(inner))(copy.start)
            else:
                distant = far(peer)
                pl.when(jnp.logical_not(distant))(copy.start)
                pl.when(distant)(through_copy(piece, peer).start)
        head_copies.append(sent)
        out_ref[:, columns] = part(head)

    def pass_on(piece):
        columns = pl.ds(piece * step_width, step_width)
        target = lax.rem(head + 2, heads)

        @pl.when(inner)
        def _():
            through_copy(piece, (target, blk)).wait_recv()
            part_ref[target, :, columns] = (
                part_ref[target, :, columns].astype(jnp.float32)
                + relay_ref[:, columns].astype(jnp.float32)
            ).astype(part_ref.dtype)
            head_copies[piece][1].start()

    def finish(piece):
        columns = pl.ds(piece * step_width, step_width)
        for number, peer in enumerate(head_peers):
            copy = head_copies[piece][number]

            def add(copy=copy, peer=peer):
                copy.wait_recv()
                out_ref[:, columns] += landed_ref[peer_origin(peer), :, columns].astype(
                    jnp.float32
                )

            if relay and number != 1:
                pl.when(jnp.logical_not(far((peer_origin(peer), blk))))(add)
            else:
                add()

    lag = 3 if relay else 2

    def step(number):
        if number < pieces:
            produce(number)
        if 0 < number <= pieces:
            gather(number - 1)
        if relay and 1 < number <= pieces + 1:
            pass_on(number - 2)
        if number >= lag:
            finish(number - lag)

    def end():
        for piece, copies in enumerate(head_copies):
            for number, copy in enumerate(copies):
                if relay and number != 1:
                    distant = far(head_peers[number])
                    pl.when(jnp.logical_not(distant))(copy.wait_send)
                    pl.when(distant)(through_copy(piece, head_peers[number]).wait_send)
                else:
                    copy.wait_send()
        for copy in extra_copies:
            copy.wait()
        for copies in blk_copies:
            for copy in copies:
                copy.wait_send()

    steps = [functools.partial(step, number) for number in range(pieces + lag)]
    return [begin, *steps, end]


def combine_call(units, shared_units, places, scale, weights, by_columns, extra=None):
    heads, blocks = lax.axis_size("head"), lax.axis_size("blk")
    (own_weight, shared_weight) = weights
    shared, slot = shared_units.shape[:2]
    count = places.shape[0] // heads
    width = own_weight.shape[0 if by_columns else 1]
    pieces = COMBINE_PIECES
    vmem = pl.BlockSpec(memory_space=pltpu.VMEM)
    anywhere = pl.BlockSpec(memory_space=pl.ANY)
    scales = [] if scale is None else [scale]
    extras = [] if extra is None else [extra]
    return (
        ("combine", by_columns, scale is not None, extra is not None),
        functools.partial(combine_stages, heads, blocks, by_columns, bool(extras)),
        [units, shared_units, places, *scales, own_weight, shared_weight, *extras],
        [vmem] * (3 + len(scales)) + [anywhere] * (2 + len(extras)),
        [
            jax.ShapeDtypeStruct((count, width), jnp.float32),
            jax.ShapeDtypeStruct((blocks + shared, slot, width), jnp.bfloat16),
            *(jax.ShapeDtypeStruct((heads,) + array.shape, array.dtype) for array in extras),
        ],
        [vmem] * 2 + [anywhere] * len(extras),
        [
            pltpu.VMEM((blocks, slot, width), jnp.bfloat16),
            pltpu.VMEM((heads, count, width), jnp.bfloat16),
            pltpu.VMEM((heads, count, width), jnp.bfloat16),
            pltpu.VMEM((count, width), jnp.bfloat16),
            pltpu.VMEM(own_weight.shape, jnp.bfloat16),
            pltpu.VMEM(shared_weight.shape, jnp.bfloat16),
            pltpu.SemaphoreType.DMA(((pieces + 1) * heads,)),
            pltpu.SemaphoreType.DMA(((pieces + 1) * heads,)),
            pltpu.SemaphoreType.DMA((pieces * (blocks - 1),)),
            pltpu.SemaphoreType.DMA((pieces * (blocks - 1),)),
            pltpu.SemaphoreType.DMA((3,)),
        ],
        scale is not None,
    )


def head_parts(partial):
    heads = lax.axis_size("head")
    return partial.astype(jnp.bfloat16).reshape(heads, -1, partial.shape[-1])


def head_sum(parts):
    return jnp.sum(parts.astype(jnp.float32), axis=0)


def dot_last(left, right):
    return lax.dot_general(
        left, right, (((1,), (1,)), ((), ())), preferred_element_type=jnp.float32
    )


def dot_first(left, right):
    return lax.dot_general(
        left, right, (((0,), (0,)), ((), ())), preferred_element_type=jnp.float32
    )


def head_columns(ref, rows, first, group, shift):
    pieces = []
    for member in range(group):
        start = (first + member) * HEAD_SIZE
        piece = ref[0, rows, start : start + HEAD_SIZE]
        empty = jnp.zeros_like(piece)
        pieces.append(jnp.concatenate([empty, piece] if shift else [piece, empty], axis=1))
    return jnp.concatenate(pieces, axis=0)


def unit_scores(queries, pairs, blk, resident, chunk):
    scores = dot_last(queries, pairs) * 0.125
    count, keys = scores.shape
    places = lax.broadcasted_iota(jnp.int32, (count, chunk), 1)
    own = blk * resident + lax.broadcasted_iota(jnp.int32, (count, chunk), 0) % resident
    last = jnp.where(places <= own, scores[:, keys - chunk :], negative)
    if keys > chunk:
        scores = jnp.concatenate([scores[:, : keys - chunk], last], axis=1)
    else:
        scores = last
    exponents = jnp.exp(scores - jnp.max(scores, axis=1, keepdims=True))
    return (exponents, jnp.sum(exponents, axis=1, keepdims=True))


def attend_kernel(heads, blocks, resident, group, kv_local, info_ref, query_ref, pair_ref, out_ref):
    slot_index = pl.program_id(0)
    blk = info_ref[0]
    length = info_ref[1 + slot_index]
    chunk = blocks * resident
    for head in range(heads):
        rows = pl.ds(head * resident, resident)
        live = head * chunk + blk * resident < length

        @pl.when(live)
        def _(head=head, rows=rows):
            keys = (head + 1) * chunk
            for kv_head in range(kv_local):
                lanes = pl.ds(kv_head * 2 * HEAD_SIZE, 2 * HEAD_SIZE)
                pairs = pair_ref[0, pl.ds(0, keys), lanes]
                queries = head_columns(query_ref, rows, kv_head * group, group, False)
                exponents, totals = unit_scores(queries, pairs, blk, resident, chunk)
                weighted = jnp.dot(
                    exponents.astype(jnp.bfloat16), pairs, preferred_element_type=jnp.float32
                )
                weighted = weighted / totals
                for member in range(group):
                    start = (kv_head * group + member) * HEAD_SIZE
                    out_ref[0, rows, start : start + HEAD_SIZE] = weighted[
                        member * resident : (member + 1) * resident, HEAD_SIZE:
                    ].astype(out_ref.dtype)

        @pl.when(jnp.logical_not(live))
        def _(rows=rows):
            out_ref[0, rows, :] = jnp.zeros((resident, out_ref.shape[2]), out_ref.dtype)


def attend_back_kernel(
    heads,
    blocks,
    resident,
    group,
    kv_local,
    info_ref,
    query_ref,
    pair_ref,
    grad_ref,
    grad_query_ref,
    grad_pair_ref,
    total_ref,
):
    slot_index = pl.program_id(0)
    blk = info_ref[0]
    length = info_ref[1 + slot_index]
    chunk = blocks * resident
    total_ref[...] = jnp.zeros_like(total_ref)
    for head in range(heads):
        rows = pl.ds(head * resident, resident)
        live = head * chunk + blk * resident < length

        @pl.when(live)
        def _(head=head, rows=rows):
            keys = (head + 1) * chunk
            for kv_head in range(kv_local):
                lanes = pl.ds(kv_head * 2 * HEAD_SIZE, 2 * HEAD_SIZE)
                pairs = pair_ref[0, pl.ds(0, keys), lanes]
                queries = head_columns(query_ref, rows, kv_head * group, group, False)
                grads = head_columns(grad_ref, rows, kv_head * group, group, True)
                exponents, totals = unit_scores(queries, pairs, blk, resident, chunk)
                probabilities = exponents * (1.0 / totals)
                grad_probs = dot_last(grads, pairs)
                delta = jnp.sum(probabilities * grad_probs, axis=1, keepdims=True)
                grad_scores = (probabilities * (grad_probs - delta)).astype(jnp.bfloat16)
                grad_queries = 0.125 * jnp.dot(
                    grad_scores, pairs, preferred_element_type=jnp.float32
                )
                for member in range(group):
                    start = (kv_head * group + member) * HEAD_SIZE
                    grad_query_ref[0, rows, start : start + HEAD_SIZE] = grad_queries[
                        member * resident : (member + 1) * resident, :HEAD_SIZE
                    ].astype(grad_query_ref.dtype)
                total_ref[pl.ds(0, keys), lanes] += dot_first(
                    grad_scores, queries * jnp.bfloat16(0.125)
                ) + dot_first(probabilities.astype(jnp.bfloat16), grads)

        @pl.when(jnp.logical_not(live))
        def _(rows=rows):
            grad_query_ref[0, rows, :] = jnp.zeros(
                (resident, grad_query_ref.shape[2]), grad_query_ref.dtype
            )

    grad_pair_ref[0] = total_ref[...].astype(grad_pair_ref.dtype)


def attention_call(kernel, info, arrays, outs, scratch, flops, name):
    def spec(array):
        shape = array.shape
        return pl.BlockSpec((1,) + shape[1:], lambda slot, info: (slot, 0, 0))

    return pl.pallas_call(
        kernel,
        grid_spec=pltpu.PrefetchScalarGridSpec(
            num_scalar_prefetch=1,
            grid=(SEQUENCE_SLOTS,),
            in_specs=[spec(array) for array in arrays],
            out_specs=[spec(array) for array in outs],
            scratch_shapes=scratch,
        ),
        out_shape=outs,
        compiler_params=pltpu.CompilerParams(vmem_limit_bytes=56 * 1024 * 1024),
        cost_estimate=pl.CostEstimate(
            flops=flops, bytes_accessed=8 << 20, transcendentals=flops // 256
        ),
        name=name,
    )(info, *arrays)


def shards(
    tokens,
    lengths,
    routes,
    queue_ranks,
    query_key_value_weight,
    w_out,
    router,
    norm_gains,
    w_in,
    w_down,
    cotangent,
):
    kernel_numbers.clear()
    heads_count = lax.axis_size("head")
    blocks_count = lax.axis_size("blk")
    head_index = lax.axis_index("head")
    blk_index = lax.axis_index("blk")
    resident = tokens.shape[1]
    width = tokens.shape[2]
    weight_rows = w_out.shape[1]
    rows_local = heads_count * resident
    keys_total = blocks_count * rows_local
    kv_local = KEY_VALUE_HEADS // heads_count
    group = QUERY_HEAD_COUNT // KEY_VALUE_HEADS
    query_columns = kv_local * group * HEAD_SIZE
    pair_columns = kv_local * 2 * HEAD_SIZE
    slot_rows = SEQUENCE_SLOTS * resident
    all_tokens = heads_count * slot_rows
    experts_local = EXPERTS // heads_count
    owned = experts_local // blocks_count
    owned_total = owned * blocks_count
    slot = -(-heads_count * CAP // 16) * 16
    half = HEAD_SIZE // 2

    own_places = (head_index * blocks_count + blk_index) * resident + jnp.arange(
        resident, dtype=jnp.int32
    )
    valid_column = (
        (own_places[None, :] < lengths[:, None]).astype(jnp.float32).reshape(slot_rows, 1)
    )
    plane_ids = jnp.arange(all_tokens, dtype=jnp.int32)
    plane_places = (
        (plane_ids // slot_rows * blocks_count + blk_index) * resident + plane_ids % resident
    ).astype(jnp.float32)
    frequency = jnp.exp(jnp.arange(half, dtype=jnp.float32) * (-2.0 * theta_log / HEAD_SIZE))
    angles = plane_places[:, None] * frequency[None, :]
    cosine = jnp.cos(angles)
    sine = jnp.sin(angles)
    repeats = 2 * HEAD_SIZE // half
    tile_cosine = jnp.concatenate([cosine] * repeats, axis=1).reshape(heads_count, slot_rows, -1)
    tile_sine = jnp.concatenate([-sine, sine] * (repeats // 2), axis=1)
    tile_sine = tile_sine.reshape(heads_count, slot_rows, -1)
    info = jnp.concatenate([blk_index[None].astype(jnp.int32), lengths])

    expert_ids = jnp.arange(EXPERTS, dtype=jnp.int32)
    row_ids = jnp.arange(experts_local * slot, dtype=jnp.int32)
    spread = (
        row_ids[None, :] // slot == jnp.arange(experts_local, dtype=jnp.int32)[:, None]
    ).astype(jnp.bfloat16)
    token_head = plane_ids[:, None] // slot_rows
    row_head = row_ids[None, :] % slot // CAP
    row_rank = (row_ids % slot % CAP).astype(jnp.float32)[None, :]

    def layer_plan(layer_index):
        plan_routes = plan[:, 0, layer_index].reshape(all_tokens, TOP)
        plan_ranks = plan[:, 1, layer_index].reshape(all_tokens, TOP)
        named = plan_routes[:, :, None] == expert_ids
        chosen = jnp.any(named, axis=1)
        marks = jnp.sum(
            jnp.where(named & (plan_ranks < CAP)[:, :, None], plan_ranks[:, :, None] + 1, 0), axis=1
        )
        marks = lax.dynamic_slice_in_dim(marks, head_index * experts_local, experts_local, 1)
        wide = mm("te,er->tr", marks.astype(jnp.bfloat16), spread) - 1.0
        places = ((wide == row_rank) & (token_head == row_head)).astype(jnp.bfloat16)
        return (chosen, places)

    def to_experts(rows):
        rows = rows.reshape(experts_local, slot, width)
        own = None
        if owned:
            own = rows[:owned_total].reshape(blocks_count, owned * slot, width)
            own = lax.all_to_all(own, "blk", 0, 0, tiled=True)
            own = own.reshape(blocks_count, owned, slot, width).transpose(1, 0, 2, 3)
            own = own.reshape(owned, blocks_count * slot, width)
        return (own, rows[owned_total:])

    def from_experts(own, shared):
        parts = [shared]
        if owned:
            own = own.reshape(owned, blocks_count, slot, width).transpose(1, 0, 2, 3)
            own = own.reshape(blocks_count, owned * slot, width)
            own = lax.all_to_all(own, "blk", 0, 0, tiled=True)
            parts = [own.reshape(owned_total, slot, width), shared]
        return jnp.concatenate(parts, axis=0).reshape(experts_local * slot, width)

    def shared_weights(layer_index):
        if owned_total == experts_local:
            return []
        return [
            tuple(
                lax.all_gather(matrix[layer_index, owned_total:], "blk", axis=1, tiled=True)
                for matrix in (w_in, w_down)
            )
        ]

    def to_owner(matrix, layer_index):
        if not owned:
            return []
        if owned == 1:
            return [("blk_swap", matrix, layer_index)]
        pieces = matrix[layer_index, :owned_total]
        return [("blk_swap", pieces.reshape((blocks_count, owned) + pieces.shape[1:]))]

    def owned_matrix(received):
        if not owned:
            return None
        columns = received.shape[-1]
        pieces = received.reshape(blocks_count, owned, -1, columns)
        return pieces.transpose(1, 0, 2, 3).reshape(owned, -1, columns)

    def from_owner(term):
        if not owned:
            return []
        columns = term.shape[-1]
        pieces = term.reshape(owned, blocks_count, -1, columns).transpose(1, 0, 2, 3)
        return [("blk_swap", pieces)]

    def owned_rows(received):
        if not owned:
            return []
        return [received.reshape(owned_total, -1, received.shape[-1])]

    staged = owned == 1 and owned_total < experts_local

    def matrices(sets, which):
        own_weight, shared_weight = (mats[which] for mats in sets)
        return (own_weight[0], shared_weight)

    def unpack_in(results):
        plane, own, shared, own_out, shared_out = results
        return (
            plane.reshape(all_tokens, width),
            [own.reshape(1, -1, width), shared],
            [own_out[None], shared_out],
        )

    def unpack_out(results):
        total, returned, *extras = results
        return (total, returned.reshape(-1, width), *extras)

    def moe_in(rows, turned_places, scale, sets, which):
        if staged:
            plan = dispatch_call(rows, turned_places, scale, matrices(sets, which), which == 1)
            return unpack_in(staged_call([plan], "dispatch", 170)[0])
        (plane,) = exchange(("head_gather", rows))
        plane = plane.reshape(all_tokens, width)
        queues = mm("rt,td->rd", turned_places, plane)
        if scale is not None:
            queues = queues * scale
        queues = [part for part in to_experts(queues.astype(jnp.bfloat16)) if part is not None]
        spec = ("erd,edf->erf", "erd,efd->erf")[which]
        return (plane, queues, [mm(spec, rows, mats[which]) for rows, mats in zip(queues, sets)])

    def moe_out(units, places, scale, sets, which, extra=None):
        if staged:
            plan = combine_call(
                units[0][0], units[1], places, scale, matrices(sets, which), which == 0, extra
            )
            return unpack_out(staged_call([plan], "combine", 170)[0])
        spec = ("erf,edf->erd", "erf,efd->erd")[which]
        made = [mm(spec, part, mats[which]).astype(jnp.bfloat16) for part, mats in zip(units, sets)]
        returned = from_experts(*(made if owned else [None] + made))
        rows = returned
        if scale is not None:
            rows = (returned.astype(jnp.float32) * scale).astype(jnp.bfloat16)
        parts, *extras = exchange(
            ("head_swap", head_parts(mm("tr,rd->td", places, rows))),
            *([] if extra is None else [("head_gather", extra)]),
        )
        return (head_sum(parts), returned, *extras)

    def moe_turn(units, places, turned_places, scale, grad_rows, sets):
        if not staged:
            return (
                moe_out(units, places, scale, sets, 1),
                moe_in(grad_rows, turned_places, scale, sets, 1),
            )
        weights = matrices(sets, 1)
        out_plan = combine_call(units[0][0], units[1], places, scale, weights, False)
        in_plan = dispatch_call(grad_rows, turned_places, scale, weights, True)
        out_results, in_results = staged_call([out_plan, in_plan], "turn", 260)
        return (unpack_out(out_results), unpack_in(in_results))

    def gated(gate_up):
        return (jax.nn.silu(gate_up[..., :FF]) * gate_up[..., FF:]).astype(jnp.bfloat16)

    def gated_back(gate_up, grad_units):
        gate_part = gate_up[..., :FF]
        up_part = gate_up[..., FF:]
        sigmoid_part = jax.nn.sigmoid(gate_part)
        return jnp.concatenate(
            [
                grad_units * up_part * sigmoid_part * (1.0 + gate_part * (1.0 - sigmoid_part)),
                grad_units * gate_part * sigmoid_part,
            ],
            axis=-1,
        ).astype(jnp.bfloat16)

    def by_slot(rows):
        return (
            rows.reshape(heads_count, SEQUENCE_SLOTS, resident, -1)
            .transpose(1, 0, 2, 3)
            .reshape(SEQUENCE_SLOTS, rows_local, -1)
        )

    def by_head(rows):
        return (
            rows.reshape(SEQUENCE_SLOTS, heads_count, resident, -1)
            .transpose(1, 0, 2, 3)
            .reshape(all_tokens, -1)
        )

    small_columns = 128
    send = []
    for layer_index in range(DECODER_LAYERS):
        weight = query_key_value_weight[layer_index]
        split = QUERY_HEAD_COUNT * HEAD_SIZE
        small = jnp.concatenate([router[layer_index], norm_gains[layer_index].T], axis=1)
        small = jnp.pad(small, ((0, 0), (0, small_columns - small.shape[1])))
        send.append(
            jnp.concatenate(
                [
                    weight[:, :split]
                    .reshape(weight_rows, heads_count, query_columns)
                    .transpose(1, 0, 2),
                    weight[:, split:]
                    .reshape(weight_rows, heads_count, pair_columns)
                    .transpose(1, 0, 2),
                    jnp.broadcast_to(small[None], (heads_count,) + small.shape),
                ],
                axis=-1,
            )
        )
    plan = jnp.stack([routes, queue_ranks]).reshape(2 * DECODER_LAYERS, slot_rows * TOP)
    plan, first_send = exchange(("head_gather", plan), ("head_swap", send[0]))
    plan = plan.reshape(heads_count, 2, DECODER_LAYERS, slot_rows, TOP)

    def attention_set(wide, out_full):
        wide = wide.transpose(1, 0, 2, 3).reshape(width, -1)
        columns = query_columns + pair_columns
        small = wide[:, columns:]
        gains = small.T[EXPERTS : EXPERTS + 2].astype(jnp.float32)
        return (wide[:, :columns], out_full.reshape(-1, width), small[:, :EXPERTS], gains)

    wide, first_out = exchange(("blk_pairs", first_send), ("blk_pairs", w_out[0]))
    attention_weights = [
        attention_set(wide, first_out),
    ]

    hidden = tokens.reshape(slot_rows, width).astype(jnp.float32)
    stored_all = []
    for layer_index in range(DECODER_LAYERS):
        qkv_full, out_full, router_full, gains = attention_weights[layer_index]
        chosen, places = layer_plan(layer_index)
        scaled_a, inverse_a = norm_rows(hidden)
        normed_a = (scaled_a * gains[:1]).astype(jnp.bfloat16)
        next_layer = layer_index + 1 < DECODER_LAYERS
        fused = owned == 1 and heads_count == 4
        if fused:
            plane_normed_a, queries, pairs_all, own_down = project(
                normed_a,
                qkv_full,
                tile_cosine,
                tile_sine,
                w_down,
                layer_index,
                pair_columns,
                resident,
            )
            plane_normed_a = plane_normed_a.reshape(all_tokens, width)
            own_down_next = [own_down]
        else:
            plane_normed_a, *own_down_next = exchange(
                ("head_gather", normed_a), *to_owner(w_down, layer_index)
            )
            plane_normed_a = plane_normed_a.reshape(all_tokens, width)
            projected = mm("td,de->te", plane_normed_a, qkv_full)
            queries = by_slot(
                rotate(projected[:, :query_columns], cosine, sine).astype(jnp.bfloat16)
            )
            pairs = projected[:, query_columns:].reshape(all_tokens, kv_local, 2, HEAD_SIZE)
            keys = rotate(pairs[:, :, 0].reshape(all_tokens, -1), cosine, sine)
            pairs = jnp.stack(
                [keys.reshape(all_tokens, kv_local, HEAD_SIZE), pairs[:, :, 1]], axis=2
            )
            pairs = pairs.reshape(all_tokens, pair_columns).astype(jnp.bfloat16)
            (pairs,) = exchange(("blk_pairs", pairs))
            pairs_all = pairs.reshape(
                blocks_count, heads_count, SEQUENCE_SLOTS, resident, pair_columns
            ).transpose(2, 1, 0, 3, 4)
        pairs_all = pairs_all.reshape(SEQUENCE_SLOTS, keys_total, pair_columns)
        (attended,) = attention_call(
            functools.partial(
                attend_kernel, heads_count, blocks_count, resident, group, kv_local
            ),
            info,
            [queries, pairs_all],
            [jax.ShapeDtypeStruct(queries.shape, jnp.bfloat16)],
            [],
            4 * rows_local * keys_total * query_columns,
            "attend",
        )
        attended = by_head(attended)
        weight_sets = shared_weights(layer_index)
        branch, *others = exchange(
            ("head_swap", head_parts(mm("tf,fd->td", attended, out_full))),
            *([("head_swap", send[layer_index + 1])] if next_layer else []),
            *to_owner(w_in, layer_index),
            after=weight_sets[0] if weight_sets else (),
        )
        if next_layer:
            next_send, *others = others
            attention_weights.append(
                attention_set(
                    lax.all_gather(next_send, "blk", axis=0),
                    lax.all_gather(w_out[layer_index + 1], "blk", axis=0),
                )
            )
        own_in_next = others
        if owned:
            weight_sets = [
                (owned_matrix(own_in_next[0]), owned_matrix(own_down_next[0]))
            ] + weight_sets
        middle = hidden + valid_column * head_sum(branch)
        scaled_b, inverse_b = norm_rows(middle)
        normed_b = (scaled_b * gains[1:]).astype(jnp.bfloat16)
        turned_places = places.T
        plane_rows, incoming, gate_up = moe_in(normed_b, turned_places, None, weight_sets, 0)
        units = [gated(part) for part in gate_up]
        logits = mm("td,de->te", plane_rows, router_full)
        peaks = jnp.max(jnp.where(chosen, logits, negative), axis=-1, keepdims=True)
        lifted = jnp.where(chosen, jnp.exp(logits - peaks), 0.0)
        gates_all = lifted / jnp.sum(lifted, axis=-1, keepdims=True)
        plane_gates = lax.dynamic_slice_in_dim(
            gates_all, head_index * experts_local, experts_local, 1
        )
        row_gates = mm("rt,te->re", turned_places, plane_gates.astype(jnp.bfloat16))
        row_gates = jnp.sum(row_gates * spread.T.astype(jnp.float32), axis=1, keepdims=True)
        if next_layer:
            mixture, returned = moe_out(units, places, row_gates, weight_sets, 1)
        else:
            (mixture, returned), turned = moe_turn(
                units,
                places,
                turned_places,
                row_gates,
                (valid_column * cotangent.reshape(slot_rows, width)).astype(jnp.bfloat16),
                weight_sets,
            )
        stored_all.append(
            (
                weight_sets,
                places,
                scaled_a,
                inverse_a,
                plane_normed_a,
                queries,
                pairs_all,
                attended,
                scaled_b,
                inverse_b,
                plane_rows,
                gates_all,
                turned_places,
                row_gates,
                incoming,
                gate_up,
                units,
                returned,
            )
        )
        hidden = middle + valid_column * mixture
    result = (valid_column * hidden).astype(jnp.bfloat16).reshape(tokens.shape)
    grad_hidden = valid_column * cotangent.reshape(slot_rows, width).astype(jnp.float32)
    qkv_list = [None] * DECODER_LAYERS
    out_list = [None] * DECODER_LAYERS
    router_list = [None] * DECODER_LAYERS
    gains_list = [None] * DECODER_LAYERS
    expert_list = [None] * DECODER_LAYERS
    pending = []
    for layer_index in reversed(range(DECODER_LAYERS)):
        qkv_full, out_full, router_full, gains = attention_weights[layer_index]
        (
            weight_sets,
            places,
            scaled_a,
            inverse_a,
            plane_normed_a,
            queries,
            pairs_all,
            attended,
            scaled_b,
            inverse_b,
            plane_rows,
            gates_all,
            turned_places,
            row_gates,
            incoming,
            gate_up,
            units,
            returned,
        ) = stored_all[layer_index]
        if layer_index + 1 < DECODER_LAYERS:
            turned = moe_in(
                (valid_column * grad_hidden).astype(jnp.bfloat16),
                turned_places,
                row_gates,
                weight_sets,
                1,
            )
        plane_grads, grad_produced, grad_units = turned
        grad_gate_up = [gated_back(*parts) for parts in zip(gate_up, grad_units)]
        pair_dots = (mm("td,rd->tr", plane_grads, returned) * places).astype(jnp.bfloat16)
        plane_grad_gates = mm("tr,er->te", pair_dots, spread).T
        grad_normed_b, _, grad_gates = moe_out(
            grad_gate_up, places, None, weight_sets, 0, plane_grad_gates
        )
        grad_gates = grad_gates.reshape(EXPERTS, all_tokens).T
        grad_weight_sets = [
            (
                mm("erd,erf->edf", rows, grads).astype(jnp.bfloat16),
                mm("erf,erd->efd", inner, out_grads).astype(jnp.bfloat16),
            )
            for rows, grads, inner, out_grads in zip(incoming, grad_gate_up, units, grad_produced)
        ]
        grad_logits = gates_all * (
            grad_gates - jnp.sum(gates_all * grad_gates, axis=-1, keepdims=True)
        )
        plane_width = width // heads_count
        grad_router = mm(
            "td,te->de",
            lax.dynamic_slice_in_dim(plane_rows, head_index * plane_width, plane_width, 1),
            grad_logits.astype(jnp.bfloat16),
        )
        own_logits = lax.dynamic_slice_in_dim(grad_logits, head_index * slot_rows, slot_rows, 0)
        grad_normed_b = grad_normed_b + mm(
            "te,de->td", own_logits.astype(jnp.bfloat16), router_full
        )
        grad_norm_b, grad_gain_b = norm_back(grad_normed_b, scaled_b, inverse_b, gains[1:])
        grad_middle = grad_hidden + grad_norm_b
        plane_branch, *own_grad_in = exchange(
            ("head_gather", (valid_column * grad_middle).astype(jnp.bfloat16)),
            *(from_owner(grad_weight_sets[0][0]) if owned else []),
            after=[*pending, *(grad_weight_sets[-1] if owned_total < experts_local else ())],
        )
        pending = []
        shared_terms = []
        if owned_total < experts_local:
            shared_terms = [
                lax.psum_scatter(term, "blk", scatter_dimension=1, tiled=True)
                for term in grad_weight_sets[-1]
            ]
        plane_branch = plane_branch.reshape(all_tokens, width)
        grad_out_w = mm("tf,td->fd", attended, plane_branch)
        grad_attended = by_slot(mm("td,fd->tf", plane_branch, out_full).astype(jnp.bfloat16))
        grad_queries, grad_pairs = attention_call(
            functools.partial(
                attend_back_kernel, heads_count, blocks_count, resident, group, kv_local
            ),
            info,
            [queries, pairs_all, grad_attended],
            [
                jax.ShapeDtypeStruct(queries.shape, jnp.bfloat16),
                jax.ShapeDtypeStruct(pairs_all.shape, jnp.bfloat16),
            ],
            [pltpu.VMEM((keys_total, pair_columns), jnp.float32)],
            10 * rows_local * keys_total * query_columns,
            "attend_back",
        )
        grad_out_w = jnp.concatenate(
            [grad_out_w, jnp.pad(grad_router, ((0, 0), (0, small_columns - EXPERTS)))], axis=1
        ).astype(jnp.bfloat16)
        swapped = [("blk_swap", grad_out_w.reshape(blocks_count, weight_rows, -1))]
        if owned:
            swapped += from_owner(grad_weight_sets[0][1])
        if fused:
            grad_projected, grad_normed_a, grad_out_w, *own_grad_down = unproject(
                grad_queries,
                grad_pairs.reshape(
                    SEQUENCE_SLOTS, heads_count, blocks_count // 2, 2, resident, pair_columns
                ),
                qkv_full,
                tile_cosine,
                tile_sine,
                [array for _, array in swapped],
                shared_terms,
            )
            grad_projected = grad_projected.reshape(all_tokens, -1)
        else:
            grad_pairs = (
                grad_pairs.reshape(
                    SEQUENCE_SLOTS, heads_count, blocks_count, resident, pair_columns
                )
                .transpose(2, 1, 0, 3, 4)
                .reshape(blocks_count, all_tokens, pair_columns)
            )
            (grad_pairs,) = exchange(("blk_swap", grad_pairs))
            grad_pairs = jnp.sum(grad_pairs.astype(jnp.float32), axis=0)
            grad_pairs = grad_pairs.astype(jnp.bfloat16).astype(jnp.float32)
            grad_pairs = grad_pairs.reshape(all_tokens, kv_local, 2, HEAD_SIZE)
            grad_keys = rotate(grad_pairs[:, :, 0].reshape(all_tokens, -1), cosine, -sine)
            grad_projected = jnp.concatenate(
                [
                    rotate(by_head(grad_queries).astype(jnp.float32), cosine, -sine),
                    jnp.stack(
                        [grad_keys.reshape(all_tokens, kv_local, HEAD_SIZE), grad_pairs[:, :, 1]],
                        axis=2,
                    ).reshape(all_tokens, pair_columns),
                ],
                axis=-1,
            ).astype(jnp.bfloat16)
            grad_normed_a, grad_out_w, *own_grad_down = exchange(
                ("head_swap", head_parts(mm("te,de->td", grad_projected, qkv_full))),
                *swapped,
                after=shared_terms,
            )
            grad_normed_a = head_sum(grad_normed_a)
        grad_out_w = jnp.sum(grad_out_w.astype(jnp.float32), axis=0)
        grad_qkv = (
            mm("td,te->de", plane_normed_a, grad_projected)
            .astype(jnp.bfloat16)
            .reshape(heads_count, blocks_count, weight_rows, -1)
            .transpose(1, 0, 2, 3)
        )
        if layer_index:
            grad_qkv = lax.psum_scatter(
                grad_qkv.reshape(width, -1), "blk", scatter_dimension=0, tiled=True
            )
            pending.append(grad_qkv)
        else:
            (grad_qkv,) = exchange(("blk_swap", grad_qkv))
            grad_qkv = jnp.sum(grad_qkv.astype(jnp.float32), axis=0).astype(jnp.bfloat16)
        grad_norm_a, grad_gain_a = norm_back(grad_normed_a, scaled_a, inverse_a, gains[:1])
        grad_hidden = grad_middle + grad_norm_a

        out_list[layer_index] = grad_out_w[:, :width]
        router_list[layer_index] = grad_out_w[:, width : width + EXPERTS]
        grad_qkv = lax.all_to_all(
            grad_qkv.reshape(heads_count, weight_rows, -1), "head", 0, 0, tiled=True
        ).transpose(1, 0, 2)
        qkv_list[layer_index] = jnp.concatenate(
            [
                grad_qkv[..., :query_columns].reshape(weight_rows, -1),
                grad_qkv[..., query_columns:].reshape(weight_rows, -1),
            ],
            axis=1,
        ).astype(jnp.float32)
        gains_list[layer_index] = jnp.stack([grad_gain_a, grad_gain_b])
        terms = []
        for number, received in enumerate((own_grad_in, own_grad_down)):
            parts = owned_rows(received[0]) if owned else []
            if owned_total < experts_local:
                parts.append(shared_terms[number])
            terms.append(jnp.concatenate(parts, axis=0).astype(jnp.float32))
        expert_list[layer_index] = tuple(terms)
    devices = heads_count * blocks_count
    grad_gains = jnp.stack(gains_list).reshape(2 * DECODER_LAYERS, devices, weight_rows)
    grad_gains = lax.all_to_all(
        grad_gains.transpose(1, 0, 2).reshape(devices, -1), ("head", "blk"), 0, 0, tiled=True
    )
    grad_gains = jnp.sum(grad_gains, axis=0).reshape(DECODER_LAYERS, 2, weight_rows)
    return (
        result,
        grad_hidden.reshape(tokens.shape),
        jnp.stack(qkv_list),
        jnp.stack(out_list),
        jnp.stack(router_list),
        grad_gains[:, 0],
        grad_gains[:, 1],
        jnp.stack([terms[0] for terms in expert_list]),
        jnp.stack([terms[1] for terms in expert_list]),
    )


def solution(mesh):
    in_specs = (
        P(None, ("head", "blk"), None),
        P(),
        P(None, None, ("head", "blk"), None),
        P(None, None, ("head", "blk"), None),
        P(None, ("head", "blk"), None),
        P(None, ("head", "blk"), None),
        P(None, ("head", "blk"), None),
        P(None, None, ("head", "blk")),
        P(None, "head", "blk", None),
        P(None, "head", "blk", None),
        P(None, ("head", "blk"), None),
    )
    out_specs = (
        P(None, ("head", "blk"), None),
        P(None, ("head", "blk"), None),
        P(None, ("head", "blk"), None),
        P(None, ("head", "blk"), None),
        P(None, ("head", "blk"), None),
        P(None, ("head", "blk")),
        P(None, ("head", "blk")),
        P(None, "head", "blk", None),
        P(None, "head", "blk", None),
    )
    return jax.shard_map(shards, mesh=mesh, in_specs=in_specs, out_specs=out_specs, check_vma=False)
```

```python
import functools

import jax
import jax.numpy as jnp
from jax import lax
from jax.experimental import pallas as pl
from jax.experimental.pallas import tpu as pltpu
from jax.sharding import PartitionSpec as P

MODEL_WIDTH = 1536
QUERY_HEAD_COUNT = 24
KEY_VALUE_HEADS = 8
HEAD_SIZE = 64
FF = 512
EXPERTS = 40
TOP = 8
DECODER_LAYERS = 2
SEQUENCE_SLOTS = 2
CAP = 26


epsilon = 1e-06
negative = -1e30
theta_log = 9.210340371976184


MESH = pl.DeviceIdType.MESH


def mm(spec, left, right):
    return jnp.einsum(spec, left, right, preferred_element_type=jnp.float32)


def rotate(values, cosine, sine):
    rows = values.shape[0]
    half = HEAD_SIZE // 2
    heads = values.reshape(rows, -1, HEAD_SIZE)
    first_half = heads[..., :half]
    second_half = heads[..., half:]
    cosine = cosine[:, None, :]
    sine = sine[:, None, :]
    return jnp.concatenate(
        [first_half * cosine - second_half * sine, second_half * cosine + first_half * sine],
        axis=-1,
    ).reshape(values.shape)


def norm_rows(hidden):
    inverse = lax.rsqrt(jnp.mean(hidden * hidden, axis=-1, keepdims=True) + epsilon)
    return (hidden * inverse, inverse)


def norm_back(grad_normed, scaled, inverse, gain_row):
    grad_gain = jnp.sum(grad_normed * scaled, axis=0)
    grad_scaled = grad_normed * gain_row
    grad_hidden = inverse * (
        grad_scaled - scaled * jnp.mean(grad_scaled * scaled, axis=-1, keepdims=True)
    )
    return (grad_hidden, grad_gain)


RELAY_PIECES = 4


def relayed_gather(heads, head, blk, head_peers, source, target, sems, first):
    count = source.shape[0] // RELAY_PIECES
    inner = jnp.logical_and(head > 0, head < heads - 1)
    rounds = []
    for piece in range(RELAY_PIECES):
        part = pl.ds(piece * count, count)
        index = first + piece * heads
        copies = []
        for number, peer in enumerate(head_peers):
            copy = remote(source.at[part], target.at[head, part], sems, index + number, peer)
            near = jnp.abs(peer[0] - head) < heads - 1
            copies.append((copy, near))
            pl.when(near)(copy.start)
        rounds.append(copies)
    passed = []
    for piece, copies in enumerate(rounds):
        copies[1][0].wait_recv()
        there = target.at[lax.rem(head + 2, heads), pl.ds(piece * count, count)]
        index = first + piece * heads
        copy = remote(
            there,
            there,
            sems,
            index + heads - 1,
            ((head - 1) * (heads - 1), blk),
            index + jnp.where(head == 1, 0, heads - 2),
        )
        pl.when(inner)(copy.start)
        passed.append(copy)
    for copies, copy in zip(rounds, passed):
        copies[0][0].wait_recv()
        copies[2][0].wait_recv()
        for sent, near in copies:
            pl.when(near)(sent.wait_send)
        pl.when(inner)(copy.wait_send)


def exchange_kernel(heads, blocks, items, waited, *refs):
    count = len(items)
    sources = refs[:count]
    targets = refs[count + waited : 2 * count + waited]
    send_sems, recv_sems, local_sems = refs[2 * count + waited :]
    head = lax.axis_index("head")
    blk = lax.axis_index("blk")
    chips = blocks // 2
    chip, core = blk // 2, lax.rem(blk, 2)
    sibling = chip * 2 + 1 - core
    kinds = {kind for kind, _ in items}
    head_peers = [(lax.rem(head + step, heads), blk) for step in range(1, heads)]
    blk_peers = [(head, lax.rem(blk + step, blocks)) for step in range(1, blocks)]
    pair_peers = [
        (head, lax.rem(chip + step, chips) * 2 + core) for step in range(1, chips)
    ] + [(head, sibling)]
    greeted = []
    if kinds & {"head_gather", "head_swap"}:
        greeted += head_peers
    if "blk_swap" in kinds:
        greeted += blk_peers
    elif "blk_pairs" in kinds:
        greeted += pair_peers
    barrier = pltpu.get_barrier_semaphore()
    for peer in greeted:
        pl.semaphore_signal(barrier, inc=1, device_id=peer, device_id_type=MESH)
    pl.semaphore_wait(barrier, len(greeted))
    used = 0
    copies = []
    forwards = []

    def send(source, target, peer):
        nonlocal used
        copy = pltpu.make_async_remote_copy(
            src_ref=source,
            dst_ref=target,
            send_sem=send_sems.at[used],
            recv_sem=recv_sems.at[used],
            device_id=peer,
            device_id_type=MESH,
        )
        copy.start()
        used += 1
        return copy

    locals_started = []
    gathers = []
    for number, (kind, layer) in enumerate(items):
        source, target = sources[number], targets[number]

        def piece(index, source=source, layer=layer):
            return source.at[index] if layer is None else source.at[layer, index]

        if kind == "head_gather" and heads == 4 and source.shape[0] % 64 == 0:
            mine, place = source, head
            gathers.append((source, target))
        elif kind == "head_gather":
            mine, place = source, head
            copies += [send(source, target.at[head], peer) for peer in head_peers]
        elif kind == "head_swap":
            mine, place = piece(head), head
            copies += [send(piece(peer[0]), target.at[head], peer) for peer in head_peers]
        elif kind == "blk_swap":
            mine, place = piece(blk), blk
            copies += [send(piece(peer[1]), target.at[blk], peer) for peer in blk_peers]
        else:
            mine, place = source, blk
            sent = [send(source, target.at[blk], peer) for peer in pair_peers]
            copies += sent[-1:]
            forwards.append((sent[:-1], target))
        local = pltpu.make_async_copy(mine, target.at[place], local_sems.at[number])
        local.start()
        locals_started.append(local)
    for source, target in gathers:
        relayed_gather(heads, head, blk, head_peers, source, target, (send_sems, recv_sems), used)
        used += RELAY_PIECES * heads
    for sent, target in forwards:
        for step, copy in enumerate(sent, start=1):
            copy.wait_recv()
            origin = lax.rem(chip + chips - step, chips) * 2 + core
            copies.append(send(target.at[origin], target.at[origin], (head, sibling)))
    for sent, _ in forwards:
        for copy in sent:
            copy.wait_send()
    for local in locals_started:
        local.wait()
    for copy in copies:
        copy.wait()


kernel_numbers = {}


def kernel_number(*key):
    return kernel_numbers.setdefault(key, 1 + len(kernel_numbers))


def exchange(*items, after=()):
    heads, blocks = lax.axis_size("head"), lax.axis_size("blk")
    arrays = [item[1] for item in items]
    plan = [(item[0], item[2] if len(item) > 2 else None) for item in items]
    outs = []
    total = 0
    for (kind, layer), array in zip(plan, arrays):
        group = heads if kind.startswith("head") else blocks
        tail = array.shape
        if kind.endswith("swap"):
            tail = tail[1:] if layer is None else tail[2:]
        outs.append(jax.ShapeDtypeStruct((group,) + tail, array.dtype))
        total += RELAY_PIECES * group
    collective_id = kernel_number(
        "exchange", tuple(plan), *((array.shape, str(array.dtype)) for array in (*arrays, *after))
    )
    results = pl.pallas_call(
        functools.partial(exchange_kernel, heads, blocks, plan, len(after)),
        out_shape=outs,
        in_specs=[pl.BlockSpec(memory_space=pl.ANY)] * (len(arrays) + len(after)),
        out_specs=[pl.BlockSpec(memory_space=pl.ANY)] * len(arrays),
        scratch_shapes=[
            pltpu.SemaphoreType.DMA((total,)),
            pltpu.SemaphoreType.DMA((total,)),
            pltpu.SemaphoreType.DMA((len(arrays),)),
        ],
        compiler_params=pltpu.CompilerParams(collective_id=collective_id, has_side_effects=True),
        cost_estimate=pl.CostEstimate(flops=0, bytes_accessed=110 << 20, transcendentals=0),
        name="exchange",
    )(*arrays, *after)
    return results


def greet(peers):
    barrier = pltpu.get_barrier_semaphore()
    for peer in peers:
        pl.semaphore_signal(barrier, inc=1, device_id=peer, device_id_type=MESH)
    pl.semaphore_wait(barrier, len(peers))


def plane_peers(heads, blocks):
    head = lax.axis_index("head")
    blk = lax.axis_index("blk")
    head_peers = [(lax.rem(head + step, heads), blk) for step in range(1, heads)]
    blk_peers = [(head, lax.rem(blk + step, blocks)) for step in range(1, blocks)]
    return head, blk, head_peers, blk_peers


def remote(source, target, sems, index, peer, landing=None):
    return pltpu.make_async_remote_copy(
        src_ref=source,
        dst_ref=target,
        send_sem=sems[0].at[index],
        recv_sem=sems[1].at[index if landing is None else landing],
        device_id=peer,
        device_id_type=MESH,
    )


def started(copy):
    copy.start()
    return copy


def weight_part(ref, columns, by_columns):
    return ref[:, columns] if by_columns else ref[columns, :]


def meet(left, part, by_columns):
    return (
        dot_last(left, part)
        if by_columns
        else jnp.dot(left, part, preferred_element_type=jnp.float32)
    )


STORED_TURNED, STORED_GATES = 12, 13
DISPATCH_PIECES, DISPATCH_WINDOW, DISPATCH_LAG = 6, 3, 2
COMBINE_PIECES = 6


def dispatch_stages(heads, blocks, by_columns, refs):
    (
        own_ref,
        place_ref,
        scale_ref,
        weight_ref,
        shared_weight_ref,
        plane_ref,
        queue_ref,
        shared_ref,
        out_ref,
        shared_out_ref,
        send_ref,
        held_ref,
        shared_held_ref,
        head_send,
        head_recv,
        blk_send,
        blk_recv,
        local_sems,
    ) = refs
    pieces, window, lag = DISPATCH_PIECES, DISPATCH_WINDOW, DISPATCH_LAG
    head, blk, head_peers, blk_peers = plane_peers(heads, blocks)
    rows, width = own_ref.shape
    slot = queue_ref.shape[1]
    shared = shared_ref.shape[0]
    step_width = width // pieces
    outputs = out_ref.shape[1]
    tile = 256
    relay = heads == 4
    inner = jnp.logical_and(head > 0, head < heads - 1)
    loads = [pltpu.make_async_copy(shared_weight_ref, shared_held_ref, local_sems.at[1])]
    if weight_ref is not None:
        loads.append(pltpu.make_async_copy(weight_ref, held_ref, local_sems.at[0]))
    head_copies = []
    blk_copies = []
    relayed = []

    def far(peer):
        return jnp.abs(peer[0] - head) == heads - 1

    def spread(piece):
        columns = pl.ds(piece * step_width, step_width)
        copies = []
        for number, peer in enumerate(head_peers):
            copy = remote(
                own_ref.at[:, columns],
                plane_ref.at[head, :, columns],
                (head_send, head_recv),
                piece * heads + number,
                peer,
            )
            copies.append(copy)
            if relay and number != 1:
                pl.when(jnp.logical_not(far(peer)))(copy.start)
            else:
                copy.start()
        head_copies.append(copies)

    def pass_on(piece):
        columns = pl.ds(piece * step_width, step_width)
        origin = lax.rem(head + 2, heads)
        rows_there = plane_ref.at[origin, :, columns]
        copy = remote(
            rows_there,
            rows_there,
            (head_send, head_recv),
            piece * heads + heads - 1,
            ((head - 1) * (heads - 1), blk),
            piece * heads + jnp.where(head == 1, 0, heads - 2),
        )
        relayed.append(copy)
        pl.when(inner)(copy.start)

    def scaled(values, start):
        if scale_ref is not None:
            values = values * scale_ref[pl.ds(start, slot), :]
        return values.astype(queue_ref.dtype)

    def begin():
        for load in loads:
            load.start()
        for piece in range(min(window, pieces)):
            spread(piece)
        plane_ref[head] = own_ref[...]

    def consume(piece):
        columns = pl.ds(piece * step_width, step_width)
        for copy in blk_copies[piece]:
            copy.wait_recv()
        queue = queue_ref[:, :, columns].reshape(blocks * slot, step_width)

        def one_tile(index, carry):
            lanes = pl.ds(pl.multiple_of(index * tile, tile), tile)
            if by_columns:
                product = dot_last(queue, held_ref[lanes, columns])
            else:
                product = jnp.dot(
                    queue, held_ref[columns, lanes], preferred_element_type=jnp.float32
                )
            if piece:
                product = product + out_ref[:, lanes]
            out_ref[:, lanes] = product
            return carry

        lax.fori_loop(0, outputs // tile, one_tile, 0)

    def take(piece):
        columns = pl.ds(piece * step_width, step_width)
        if relay:
            for later in range(piece + 1 if piece else 0, min(piece + 2, pieces)):
                head_copies[later][1].wait_recv()
                pass_on(later)
        for number, copy in enumerate(head_copies[piece]):
            if not relay or number != 1:
                copy.wait_recv()
        if piece + window < pieces:
            spread(piece + window)
        plane = plane_ref[:, :, columns].reshape(heads * rows, step_width)

        def fill(expert, carry):
            start = pl.multiple_of(expert * slot, 16)
            taken = jnp.dot(
                place_ref[pl.ds(start, slot), :], plane, preferred_element_type=jnp.float32
            )
            send_ref[expert, :, columns] = scaled(taken, start)
            return carry

        lax.fori_loop(0, blocks, fill, 0)
        blk_copies.append(
            [
                started(
                    remote(
                        send_ref.at[peer[1], :, columns],
                        queue_ref.at[blk, :, columns],
                        (blk_send, blk_recv),
                        piece * (blocks - 1) + number,
                        peer,
                    )
                )
                for number, peer in enumerate(blk_peers)
            ]
        )
        queue_ref[blk, :, columns] = send_ref[blk, :, columns]
        if not piece:
            for load in loads:
                load.wait()
        for expert in range(shared):
            start = (blocks + expert) * slot
            taken = jnp.dot(
                place_ref[pl.ds(start, slot), :], plane, preferred_element_type=jnp.float32
            )
            taken = scaled(taken, start)
            shared_ref[expert, :, columns] = taken
            product = meet(
                taken, weight_part(shared_held_ref.at[expert], columns, by_columns), by_columns
            )
            if piece:
                product = product + shared_out_ref[expert]
            shared_out_ref[expert] = product

    def step(number):
        if number < pieces:
            take(number)
        if number >= lag:
            consume(number - lag)

    def end():
        for copies in head_copies:
            for number, copy in enumerate(copies):
                if relay and number != 1:
                    pl.when(jnp.logical_not(far(head_peers[number])))(copy.wait_send)
                else:
                    copy.wait_send()
        for copy in relayed:
            pl.when(inner)(copy.wait_send)
        for copies in blk_copies:
            for copy in copies:
                copy.wait_send()

    steps = [functools.partial(step, number) for number in range(pieces + lag)]
    return [begin, *steps, end]


def dispatch_plan(rows, places, scale, weights, by_columns):
    heads, blocks = lax.axis_size("head"), lax.axis_size("blk")
    count, width = rows.shape
    (own_weight, shared_weight) = weights
    shared = shared_weight.shape[0]
    slot = places.shape[0] // (blocks + shared)
    outputs = own_weight.shape[0 if by_columns else 1]
    pieces = DISPATCH_PIECES
    vmem = pl.BlockSpec(memory_space=pltpu.VMEM)
    anywhere = pl.BlockSpec(memory_space=pl.ANY)
    scales = [] if scale is None else [scale]
    return (
        [rows, places, *scales, own_weight, shared_weight],
        [vmem, vmem, *([vmem] * len(scales)), anywhere, anywhere],
        [
            jax.ShapeDtypeStruct((heads, count, width), jnp.bfloat16),
            jax.ShapeDtypeStruct((blocks, slot, width), jnp.bfloat16),
            jax.ShapeDtypeStruct((shared, slot, width), jnp.bfloat16),
            jax.ShapeDtypeStruct((blocks * slot, outputs), jnp.float32),
            jax.ShapeDtypeStruct((shared, slot, outputs), jnp.float32),
        ],
        [vmem] * 5,
        [
            pltpu.VMEM((blocks, slot, width), jnp.bfloat16),
            pltpu.VMEM(own_weight.shape, jnp.bfloat16),
            pltpu.VMEM(shared_weight.shape, jnp.bfloat16),
            pltpu.SemaphoreType.DMA((pieces * heads,)),
            pltpu.SemaphoreType.DMA((pieces * heads,)),
            pltpu.SemaphoreType.DMA((pieces * (blocks - 1),)),
            pltpu.SemaphoreType.DMA((pieces * (blocks - 1),)),
            pltpu.SemaphoreType.DMA((2,)),
        ],
    )


def staged_call(plans, name, millions, after=()):
    heads, blocks = lax.axis_size("head"), lax.axis_size("blk")
    inputs = [len(plan[2]) for plan in plans]
    outputs = [len(plan[4]) for plan in plans]
    scratches = [len(plan[6]) for plan in plans]

    def kernel(*refs):
        _, _, head_peers, blk_peers = plane_peers(heads, blocks)
        greet(head_peers + blk_peers)
        lists = []
        refs = refs[: sum(inputs)] + refs[sum(inputs) + len(after) :]
        for number, plan in enumerate(plans):
            first = sum(inputs[:number])
            given = list(refs[first : first + inputs[number]])
            if not plan[7]:
                given.insert(2 if plan[0][0] == "dispatch" else 3, None)
            first = sum(inputs) + sum(outputs[:number])
            given += refs[first : first + outputs[number]]
            first = sum(inputs) + sum(outputs) + sum(scratches[:number])
            given += refs[first : first + scratches[number]]
            lists.append(plan[1](given))
        for index in range(max(len(stages) for stages in lists)):
            for stages in lists:
                if index < len(stages):
                    stages[index]()

    arrays = [array for plan in plans for array in plan[2]]
    results = pl.pallas_call(
        kernel,
        out_shape=[out for plan in plans for out in plan[4]],
        in_specs=[spec for plan in plans for spec in plan[3]]
        + [pl.BlockSpec(memory_space=pl.ANY)] * len(after),
        out_specs=[spec for plan in plans for spec in plan[5]],
        scratch_shapes=[scratch for plan in plans for scratch in plan[6]],
        compiler_params=pltpu.CompilerParams(
            collective_id=kernel_number(
                *(plan[0] for plan in plans), *(array.shape for array in after)
            ),
            has_side_effects=True,
            vmem_limit_bytes=60 * 1024 * 1024,
        ),
        cost_estimate=pl.CostEstimate(
            flops=0, bytes_accessed=millions << 20, transcendentals=0
        ),
        name=name,
    )(*arrays, *after)
    return [
        results[sum(outputs[:number]) : sum(outputs[: number + 1])] for number in range(len(plans))
    ]


def dispatch_call(rows, places, scale, weights, by_columns):
    heads, blocks = lax.axis_size("head"), lax.axis_size("blk")
    return (
        ("dispatch", by_columns, scale is not None),
        functools.partial(dispatch_stages, heads, blocks, by_columns),
        *dispatch_plan(rows, places, scale, weights, by_columns),
        scale is not None,
    )


def enter_kernel(heads, blocks, layer, swaps, *refs):
    attended_ref, out_weight_ref, hidden_ref, valid_ref, gain_ref, place_ref, *refs = refs
    moved_ref, shared_weight_ref, *refs = refs
    swap_refs, refs = refs[:swaps], refs[swaps:]
    middle_ref, scaled_ref, inverse_ref, plane_ref, queue_ref, shared_ref, *refs = refs
    out_ref, shared_out_ref, matrix_ref, *refs = refs
    swap_out_refs, refs = refs[:swaps], refs[swaps:]
    own_ref, part_ref, landed_ref, relay_ref, sum_send, sum_recv, *refs = refs
    moved_send, moved_recv, swap_send, swap_recv, side_sems, *refs = refs
    send_ref, held_ref, shared_held_ref, head_send, head_recv, blk_send, blk_recv, local_sems = refs
    head, blk, head_peers, blk_peers = plane_peers(heads, blocks)
    rows, width = middle_ref.shape
    pieces = COMBINE_PIECES
    step_width = width // pieces
    matrix_rows = moved_ref.shape[2]
    inner = jnp.logical_and(head > 0, head < heads - 1)
    greet(head_peers + blk_peers)

    def far(peer):
        return jnp.abs(peer[0] - head) == heads - 1

    def peer_origin(peer):
        return lax.rem(2 * head + heads - peer[0], heads)

    sent = []

    def through_copy(piece, peer):
        columns = pl.ds(piece * step_width, step_width)
        return remote(
            part_ref.at[peer[0], :, columns],
            relay_ref.at[:, columns],
            (sum_send, sum_recv),
            piece * heads + heads - 1,
            (jnp.where(head == 0, 1, heads - 2), blk),
        )

    def spread(piece):
        columns = pl.ds(piece * step_width, step_width)
        weight = out_weight_ref[:, columns]

        def part(owner):
            start = pl.multiple_of(owner * rows, 16)
            return jnp.dot(
                attended_ref[pl.ds(start, rows), :], weight, preferred_element_type=jnp.float32
            )

        copies = []
        for number, peer in enumerate(head_peers):
            part_ref[peer[0], :, columns] = part(peer[0]).astype(part_ref.dtype)
            copy = remote(
                part_ref.at[peer[0], :, columns],
                landed_ref.at[head, :, columns],
                (sum_send, sum_recv),
                piece * heads + number,
                peer,
            )
            copies.append(copy)
            if number == 1:
                pl.when(jnp.logical_not(inner))(copy.start)
            else:
                distant = far(peer)
                pl.when(jnp.logical_not(distant))(copy.start)
                pl.when(distant)(through_copy(piece, peer).start)
        sent.append(copies)
        middle_ref[:, columns] = part(head)

    def pass_on(piece):
        columns = pl.ds(piece * step_width, step_width)
        target = lax.rem(head + 2, heads)

        @pl.when(inner)
        def _():
            through_copy(piece, (target, blk)).wait_recv()
            part_ref[target, :, columns] = (
                part_ref[target, :, columns].astype(jnp.float32)
                + relay_ref[:, columns].astype(jnp.float32)
            ).astype(part_ref.dtype)
            sent[piece][1].start()

    def finish(piece):
        columns = pl.ds(piece * step_width, step_width)
        for number, peer in enumerate(head_peers):
            copy = sent[piece][number]

            def add(copy=copy, peer=peer):
                copy.wait_recv()
                middle_ref[:, columns] += landed_ref[peer_origin(peer), :, columns].astype(
                    jnp.float32
                )

            if number != 1:
                pl.when(jnp.logical_not(far((peer_origin(peer), blk))))(add)
            else:
                add()

    moved = []

    def move():
        for number, peer in enumerate(blk_peers):
            place = pl.ds(pl.multiple_of(blk * matrix_rows, 16), matrix_rows)
            moved.append(
                started(
                    remote(
                        moved_ref.at[layer, peer[1]],
                        held_ref.at[place],
                        (moved_send, moved_recv),
                        number,
                        peer,
                    )
                )
            )
        place = pl.ds(pl.multiple_of(blk * matrix_rows, 16), matrix_rows)
        moved.append(
            started(
                pltpu.make_async_copy(
                    moved_ref.at[layer, blk], held_ref.at[place], side_sems.at[0]
                )
            )
        )
        for item in range(swaps):
            for number, peer in enumerate(head_peers):
                swapped.append(
                    started(
                        remote(
                            swap_refs[item].at[peer[0]],
                            swap_out_refs[item].at[head],
                            (swap_send, swap_recv),
                            item * heads + number,
                            peer,
                        )
                    )
                )
            swapped.append(
                started(
                    pltpu.make_async_copy(
                        swap_refs[item].at[head], swap_out_refs[item].at[head], side_sems.at[2]
                    )
                )
            )

    swapped = []
    lag = 2
    for step in range(pieces + lag):
        if step < pieces:
            spread(step)
        if not step:
            move()
        if 0 < step <= pieces:
            pass_on(step - 1)
        if step >= lag:
            finish(step - lag)
    middle = hidden_ref[...] + valid_ref[...] * middle_ref[...]
    inverse = lax.rsqrt(jnp.mean(middle * middle, axis=1, keepdims=True) + epsilon)
    scaled = middle * inverse
    middle_ref[...] = middle
    scaled_ref[...] = scaled
    inverse_ref[...] = jnp.broadcast_to(inverse, inverse_ref.shape)
    own_ref[...] = (scaled * gain_ref[...]).astype(own_ref.dtype)
    stages = dispatch_stages(
        heads,
        blocks,
        False,
        (
            own_ref,
            place_ref,
            None,
            None,
            shared_weight_ref,
            plane_ref,
            queue_ref,
            shared_ref,
            out_ref,
            shared_out_ref,
            send_ref,
            held_ref,
            shared_held_ref,
            head_send,
            head_recv,
            blk_send,
            blk_recv,
            local_sems,
        ),
    )
    stages[0]()
    for copy in moved:
        if hasattr(copy, "wait_recv") and copy is not moved[-1]:
            copy.wait_recv()
        else:
            copy.wait()
    saved = pltpu.make_async_copy(held_ref, matrix_ref, side_sems.at[1])
    saved.start()
    for stage in stages[1:]:
        stage()
    saved.wait()
    for copy in moved[:-1]:
        copy.wait_send()
    for copy in swapped:
        copy.wait()
    for piece, copies in enumerate(sent):
        for number, copy in enumerate(copies):
            if number != 1:
                distant = far(head_peers[number])
                pl.when(jnp.logical_not(distant))(copy.wait_send)
                pl.when(distant)(through_copy(piece, head_peers[number]).wait_send)
            else:
                copy.wait_send()


def enter(attended, out_weight, hidden, valid, gain, places, moved, layer, shared_weight, swaps):
    heads, blocks = lax.axis_size("head"), lax.axis_size("blk")
    count, width = hidden.shape
    matrix = jax.ShapeDtypeStruct((blocks * moved.shape[2], moved.shape[3]), moved.dtype)
    rows = jax.ShapeDtypeStruct((count, width), jnp.bfloat16)
    _, _, outs, _, scratch = dispatch_plan(rows, places, None, (matrix, shared_weight), False)
    vmem = pl.BlockSpec(memory_space=pltpu.VMEM)
    anywhere = pl.BlockSpec(memory_space=pl.ANY)
    pieces = COMBINE_PIECES
    return pl.pallas_call(
        functools.partial(enter_kernel, heads, blocks, layer, len(swaps)),
        out_shape=[
            jax.ShapeDtypeStruct((count, width), jnp.float32),
            jax.ShapeDtypeStruct((count, width), jnp.float32),
            jax.ShapeDtypeStruct((count, 128), jnp.float32),
            *outs,
            matrix,
            *(jax.ShapeDtypeStruct(array.shape, array.dtype) for array in swaps),
        ],
        in_specs=[vmem] * 6 + [anywhere] * (2 + len(swaps)),
        out_specs=[vmem] * (3 + len(outs)) + [anywhere] * (1 + len(swaps)),
        scratch_shapes=[
            pltpu.VMEM((count, width), jnp.bfloat16),
            pltpu.VMEM((heads, count, width), jnp.bfloat16),
            pltpu.VMEM((heads, count, width), jnp.bfloat16),
            pltpu.VMEM((count, width), jnp.bfloat16),
            pltpu.SemaphoreType.DMA((pieces * heads,)),
            pltpu.SemaphoreType.DMA((pieces * heads,)),
            pltpu.SemaphoreType.DMA((blocks,)),
            pltpu.SemaphoreType.DMA((blocks,)),
            pltpu.SemaphoreType.DMA((max(1, len(swaps)) * heads,)),
            pltpu.SemaphoreType.DMA((max(1, len(swaps)) * heads,)),
            pltpu.SemaphoreType.DMA((3,)),
            *scratch,
        ],
        compiler_params=pltpu.CompilerParams(
            collective_id=kernel_number("enter", layer, len(swaps)),
            has_side_effects=True,
            vmem_limit_bytes=60 * 1024 * 1024,
        ),
        cost_estimate=pl.CostEstimate(flops=0, bytes_accessed=270 << 20, transcendentals=0),
        name="enter",
    )(attended, out_weight, hidden, valid, gain, places, moved, shared_weight, *swaps)


def turn_heads(values, cosine, sine):
    lane = lax.broadcasted_iota(jnp.int32, values.shape, 1) % HEAD_SIZE
    half = HEAD_SIZE // 2
    width = values.shape[1]
    swapped = jnp.where(
        lane < half, pltpu.roll(values, width - half, 1), pltpu.roll(values, half, 1)
    )
    return values * cosine + swapped * sine


def project_kernel(
    heads,
    blocks,
    pieces,
    layer,
    greeted,
    own_ref,
    weight_ref,
    cosine_ref,
    sine_ref,
    moved_ref,
    plane_ref,
    query_ref,
    pair_ref,
    moved_out_ref,
    head_send,
    head_recv,
    pair_send,
    pair_recv,
    moved_send,
    moved_recv,
    local_sem,
):
    head, blk, head_peers, blk_peers = plane_peers(heads, blocks)
    chips = blocks // 2
    chip, core = blk // 2, lax.rem(blk, 2)
    sibling = (head, chip * 2 + 1 - core)
    rows, width = own_ref.shape
    count = rows // pieces
    slots, _, _, resident, pair_columns = pair_ref.shape
    query_columns = query_ref.shape[2]
    inner = jnp.logical_and(head > 0, head < heads - 1)
    if not greeted:
        greet(head_peers + blk_peers)

    def far(peer):
        return jnp.abs(peer[0] - head) == heads - 1

    def place(piece):
        return piece * count // resident, pl.ds(piece * count % resident, count)

    head_copies = []
    relayed = []
    for piece in range(pieces):
        part = pl.ds(piece * count, count)
        copies = []
        for number, peer in enumerate(head_peers):
            copy = remote(
                own_ref.at[part],
                plane_ref.at[head, part],
                (head_send, head_recv),
                piece * heads + number,
                peer,
            )
            copies.append(copy)
            if number != 1:
                pl.when(jnp.logical_not(far(peer)))(copy.start)
            else:
                copy.start()
        head_copies.append(copies)
    moved = []
    if layer is not None:
        moved = [
            started(
                remote(
                    moved_ref.at[layer, peer[1]],
                    moved_out_ref.at[blk],
                    (moved_send, moved_recv),
                    number,
                    peer,
                )
            )
            for number, peer in enumerate(blk_peers)
        ]
        local = pltpu.make_async_copy(moved_ref.at[layer, blk], moved_out_ref.at[blk], local_sem)
        local.start()
    plane_ref[head] = own_ref[...]

    def pass_on(piece):
        head_copies[piece][1].wait_recv()
        part = pl.ds(piece * count, count)
        rows_there = plane_ref.at[lax.rem(head + 2, heads), part]
        copy = remote(
            rows_there,
            rows_there,
            (head_send, head_recv),
            piece * heads + heads - 1,
            ((head - 1) * (heads - 1), blk),
            piece * heads + jnp.where(head == 1, 0, heads - 2),
        )
        relayed.append(copy)
        pl.when(inner)(copy.start)

    pair_copies = []
    forwards = []

    def forward(piece):
        slot, part = place(piece)
        for step in range(1, chips):
            pair_copies[piece][step - 1].wait_recv()
            origin = lax.rem(chip + chips - step, chips) * 2 + core
            there = pair_ref.at[slot, :, origin, part]
            forwards.append(
                started(
                    remote(
                        there,
                        there,
                        (pair_send, pair_recv),
                        piece * blocks + chips - 1 + step,
                        sibling,
                    )
                )
            )

    tile = 2 * HEAD_SIZE
    for piece in range(pieces):
        for later in range(piece + 1 if piece else 0, min(piece + 2, pieces)):
            pass_on(later)
        for number in range(heads - 1):
            if number != 1:
                head_copies[piece][number].wait_recv()
        part = pl.ds(piece * count, count)
        slot, inside = place(piece)
        projected = jnp.dot(
            plane_ref[:, part, :].reshape(heads * count, width),
            weight_ref[...],
            preferred_element_type=jnp.float32,
        )
        cosine = cosine_ref[:, part, :].reshape(heads * count, tile)
        sine = sine_ref[:, part, :].reshape(heads * count, tile)
        turned = jnp.concatenate(
            [
                turn_heads(projected[:, start : start + tile], cosine, sine)
                for start in range(0, query_columns, tile)
            ],
            axis=1,
        ).astype(query_ref.dtype)
        is_key = lax.broadcasted_iota(jnp.int32, cosine.shape, 1) < HEAD_SIZE
        key_cosine = jnp.where(is_key, cosine, 1.0)
        key_sine = jnp.where(is_key, sine, 0.0)
        pairs = jnp.concatenate(
            [
                turn_heads(projected[:, start : start + tile], key_cosine, key_sine)
                for start in range(query_columns, query_columns + pair_columns, tile)
            ],
            axis=1,
        ).astype(pair_ref.dtype)
        for there in range(heads):
            taken = slice(there * count, (there + 1) * count)
            query_ref[slot, pl.ds(there * resident + piece * count % resident, count), :] = turned[
                taken
            ]
            pair_ref[slot, there, blk, inside, :] = pairs[taken]
        mine = pair_ref.at[slot, :, blk, inside]
        targets = [
            (head, lax.rem(chip + step, chips) * 2 + core) for step in range(1, chips)
        ] + [sibling]
        pair_copies.append(
            [
                started(
                    remote(mine, mine, (pair_send, pair_recv), piece * blocks + number, peer)
                )
                for number, peer in enumerate(targets)
            ]
        )
        if piece:
            forward(piece - 1)
    forward(pieces - 1)
    for copies in pair_copies:
        for copy in copies[:-1]:
            copy.wait_send()
        copies[-1].wait()
    for copy in forwards:
        copy.wait()
    for copies in head_copies:
        for number, copy in enumerate(copies):
            if number != 1:
                pl.when(jnp.logical_not(far(head_peers[number])))(copy.wait_send)
            else:
                copy.wait_send()
    for copy in relayed:
        pl.when(inner)(copy.wait_send)
    for copy in moved:
        copy.wait()
    if moved:
        local.wait()


PROJECT_PIECES = 4


def project_plan(count, width, weight, moved, layer, pair_columns, resident):
    heads, blocks = lax.axis_size("head"), lax.axis_size("blk")
    pieces = PROJECT_PIECES
    slots = count // resident
    moves = [] if layer is None else [moved]
    vmem = pl.BlockSpec(memory_space=pltpu.VMEM)
    anywhere = pl.BlockSpec(memory_space=pl.ANY)
    return (
        [
            jax.ShapeDtypeStruct((heads, count, width), jnp.bfloat16),
            jax.ShapeDtypeStruct(
                (slots, heads * resident, weight.shape[1] - pair_columns), jnp.bfloat16
            ),
            jax.ShapeDtypeStruct((slots, heads, blocks, resident, pair_columns), jnp.bfloat16),
            *(jax.ShapeDtypeStruct((blocks,) + array.shape[2:], array.dtype) for array in moves),
        ],
        [vmem] * 3 + [anywhere] * len(moves),
        [
            pltpu.SemaphoreType.DMA((pieces * heads,)),
            pltpu.SemaphoreType.DMA((pieces * heads,)),
            pltpu.SemaphoreType.DMA((pieces * blocks,)),
            pltpu.SemaphoreType.DMA((pieces * blocks,)),
            pltpu.SemaphoreType.DMA((blocks,)),
            pltpu.SemaphoreType.DMA((blocks,)),
            pltpu.SemaphoreType.DMA,
        ],
    )


def project(rows, weight, cosine, sine, moved, layer, pair_columns, resident):
    heads, blocks = lax.axis_size("head"), lax.axis_size("blk")
    outs, out_specs, scratch = project_plan(
        *rows.shape, weight, moved, layer, pair_columns, resident
    )
    moves = [] if layer is None else [moved]
    vmem = pl.BlockSpec(memory_space=pltpu.VMEM)
    anywhere = pl.BlockSpec(memory_space=pl.ANY)
    return pl.pallas_call(
        functools.partial(project_kernel, heads, blocks, PROJECT_PIECES, layer, False),
        out_shape=outs,
        in_specs=[vmem] * 4 + [anywhere] * len(moves),
        out_specs=out_specs,
        scratch_shapes=scratch,
        compiler_params=pltpu.CompilerParams(
            collective_id=kernel_number("project", layer),
            has_side_effects=True,
            vmem_limit_bytes=56 * 1024 * 1024,
        ),
        cost_estimate=pl.CostEstimate(flops=0, bytes_accessed=130 << 20, transcendentals=0),
        name="project",
    )(rows, weight, cosine, sine, *moves)


def cross(plan, middle, valid, gain, weight, cosine, sine, moved, layer, pair_columns, resident):
    heads, blocks = lax.axis_size("head"), lax.axis_size("blk")
    key, maker, arrays, specs, outs, out_specs, scratch, scaled_rows = plan
    count, width = middle.shape
    more_outs, more_specs, more_scratch = project_plan(
        count, width, weight, moved, layer, pair_columns, resident
    )
    inputs, results, temps = len(arrays), len(outs), len(scratch)
    vmem = pl.BlockSpec(memory_space=pltpu.VMEM)
    anywhere = pl.BlockSpec(memory_space=pl.ANY)
    norm_outs = [
        jax.ShapeDtypeStruct((count, width), jnp.float32),
        jax.ShapeDtypeStruct((count, width), jnp.float32),
        jax.ShapeDtypeStruct((count, 128), jnp.float32),
    ]

    def kernel(*refs):
        _, _, head_peers, blk_peers = plane_peers(heads, blocks)
        greet(head_peers + blk_peers)
        given, refs = list(refs[:inputs]), refs[inputs:]
        middle_ref, valid_ref, gain_ref, weight_ref, cosine_ref, sine_ref, *refs = refs
        moved_ref, *refs = refs
        given += refs[:results]
        sum_ref, refs = refs[0], refs[results:]
        hidden_ref, scaled_ref, inverse_ref, *refs = refs
        made, refs = refs[: len(more_outs)], refs[len(more_outs) :]
        given += refs[:temps]
        own_ref, *rest = refs[temps:]
        if not scaled_rows:
            given.insert(3, None)
        for stage in maker(given):
            stage()
        hidden = middle_ref[...] + valid_ref[...] * sum_ref[...]
        inverse = lax.rsqrt(jnp.mean(hidden * hidden, axis=1, keepdims=True) + epsilon)
        scaled = hidden * inverse
        hidden_ref[...] = hidden
        scaled_ref[...] = scaled
        inverse_ref[...] = jnp.broadcast_to(inverse, inverse_ref.shape)
        own_ref[...] = (scaled * gain_ref[...]).astype(own_ref.dtype)
        project_kernel(
            heads,
            blocks,
            PROJECT_PIECES,
            layer,
            True,
            own_ref,
            weight_ref,
            cosine_ref,
            sine_ref,
            moved_ref,
            *made,
            *rest,
        )

    values = pl.pallas_call(
        kernel,
        out_shape=[*outs, *norm_outs, *more_outs],
        in_specs=[*specs, *([vmem] * 6), anywhere],
        out_specs=[*out_specs, *([vmem] * 3), *more_specs],
        scratch_shapes=[*scratch, pltpu.VMEM((count, width), jnp.bfloat16), *more_scratch],
        compiler_params=pltpu.CompilerParams(
            collective_id=kernel_number("cross", key, layer),
            has_side_effects=True,
            vmem_limit_bytes=60 * 1024 * 1024,
        ),
        cost_estimate=pl.CostEstimate(flops=0, bytes_accessed=290 << 20, transcendentals=0),
        name="cross",
    )(*arrays, middle, valid, gain, weight, cosine, sine, moved)
    return values[:results], values[results : results + 3], values[results + 3 :]


def unproject_kernel(
    heads,
    blocks,
    pieces,
    items,
    grad_query_ref,
    grad_pair_ref,
    weight_ref,
    cosine_ref,
    sine_ref,
    *refs,
):
    moved_refs = refs[:items]
    grad_ref, out_ref = refs[items : items + 2]
    moved_out_refs = refs[items + 2 : 2 * items + 2]
    (
        near_ref,
        sum_ref,
        far_ref,
        product_ref,
        part_ref,
        landed_ref,
        relay_ref,
        near_send,
        near_recv,
        chip_send,
        chip_recv,
        head_send,
        head_recv,
        moved_send,
        moved_recv,
        local_sems,
    ) = refs[2 * items + 2 :]
    head, blk, head_peers, blk_peers = plane_peers(heads, blocks)
    chips = blocks // 2
    chip, core = blk // 2, lax.rem(blk, 2)
    sibling = (head, chip * 2 + 1 - core)
    rows, width = out_ref.shape
    count = rows // pieces
    resident, pair_columns = grad_pair_ref.shape[4:]
    query_columns = grad_query_ref.shape[2]
    inner = jnp.logical_and(head > 0, head < heads - 1)
    chip_peers = [(head, lax.rem(chip + step, chips) * 2 + core) for step in range(1, chips)]
    greet(head_peers + blk_peers)

    def far(peer):
        return jnp.abs(peer[0] - head) == heads - 1

    def peer_origin(peer):
        return lax.rem(2 * head + heads - peer[0], heads)

    def place(piece):
        return piece * count // resident, pl.ds(piece * count % resident, count)

    near_copies = []
    for piece in range(pieces):
        slot, inside = place(piece)
        near_copies.append(
            started(
                remote(
                    grad_pair_ref.at[slot, :, :, 1 - core, inside],
                    near_ref.at[piece],
                    (near_send, near_recv),
                    piece,
                    sibling,
                )
            )
        )
    chip_copies = []
    head_copies = []
    moved = []

    def add_cores(piece):
        slot, inside = place(piece)
        near_copies[piece].wait_recv()
        sum_ref[piece] = (
            grad_pair_ref[slot, :, :, core, inside, :].astype(jnp.float32)
            + near_ref[piece].astype(jnp.float32)
        ).astype(sum_ref.dtype)
        chip_copies.append(
            [
                started(
                    remote(
                        sum_ref.at[piece, :, peer[1] // 2],
                        far_ref.at[piece, chip],
                        (chip_send, chip_recv),
                        piece * chips + number,
                        peer,
                    )
                )
                for number, peer in enumerate(chip_peers)
            ]
        )

    def through_copy(piece, peer):
        part = pl.ds(piece * count, count)
        return remote(
            part_ref.at[peer[0], part],
            relay_ref.at[part],
            (head_send, head_recv),
            piece * heads + heads - 1,
            (jnp.where(head == 0, 1, heads - 2), blk),
        )

    tile = 2 * HEAD_SIZE

    def multiply(piece):
        slot, inside = place(piece)
        part = pl.ds(piece * count, count)
        for copy in chip_copies[piece]:
            copy.wait_recv()
        pairs = sum_ref[piece, :, chip].astype(jnp.float32)
        for peer in chip_peers:
            pairs = pairs + far_ref[piece, peer[1] // 2].astype(jnp.float32)
        pairs = pairs.reshape(heads * count, pair_columns)
        pairs = pairs.astype(jnp.bfloat16).astype(jnp.float32)
        queries = jnp.concatenate(
            [
                grad_query_ref[
                    slot, pl.ds(there * resident + piece * count % resident, count), :
                ]
                for there in range(heads)
            ],
            axis=0,
        ).astype(jnp.float32)
        cosine = cosine_ref[:, part, :].reshape(heads * count, tile)
        sine = -sine_ref[:, part, :].reshape(heads * count, tile)
        is_key = lax.broadcasted_iota(jnp.int32, cosine.shape, 1) < HEAD_SIZE
        key_cosine = jnp.where(is_key, cosine, 1.0)
        key_sine = jnp.where(is_key, sine, 0.0)
        turned = jnp.concatenate(
            [
                turn_heads(queries[:, start : start + tile], cosine, sine)
                for start in range(0, query_columns, tile)
            ]
            + [
                turn_heads(pairs[:, start : start + tile], key_cosine, key_sine)
                for start in range(0, pair_columns, tile)
            ],
            axis=1,
        ).astype(grad_ref.dtype)
        grad_ref[:, part, :] = turned.reshape(heads, count, query_columns + pair_columns)
        product_ref[...] = dot_last(turned, weight_ref[...]).reshape(heads, count, width)
        sent = []
        for number, peer in enumerate(head_peers):
            part_ref[peer[0], part, :] = product_ref[peer[0]].astype(part_ref.dtype)
            copy = remote(
                part_ref.at[peer[0], part],
                landed_ref.at[head, part],
                (head_send, head_recv),
                piece * heads + number,
                peer,
            )
            sent.append(copy)
            if number == 1:
                pl.when(jnp.logical_not(inner))(copy.start)
            else:
                distant = far(peer)
                pl.when(jnp.logical_not(distant))(copy.start)
                pl.when(distant)(through_copy(piece, peer).start)
        head_copies.append(sent)
        out_ref[part, :] = product_ref[head]

    def pass_on(piece):
        part = pl.ds(piece * count, count)
        target = lax.rem(head + 2, heads)

        @pl.when(inner)
        def _():
            through_copy(piece, (target, blk)).wait_recv()
            part_ref[target, part, :] = (
                part_ref[target, part, :].astype(jnp.float32)
                + relay_ref[part, :].astype(jnp.float32)
            ).astype(part_ref.dtype)
            head_copies[piece][1].start()

    def finish(piece):
        part = pl.ds(piece * count, count)
        for number, peer in enumerate(head_peers):
            copy = head_copies[piece][number]

            def add(copy=copy, peer=peer):
                copy.wait_recv()
                out_ref[part, :] += landed_ref[peer_origin(peer), part, :].astype(jnp.float32)

            if number != 1:
                pl.when(jnp.logical_not(far((peer_origin(peer), blk))))(add)
            else:
                add()

    for step in range(pieces + 3):
        if step < pieces:
            add_cores(step)
        if step == pieces - 1:
            for item in range(items):
                source, target = moved_refs[item], moved_out_refs[item]
                moved += [
                    started(
                        remote(
                            source.at[peer[1]],
                            target.at[blk],
                            (moved_send, moved_recv),
                            item * blocks + number,
                            peer,
                        )
                    )
                    for number, peer in enumerate(blk_peers)
                ]
                local = pltpu.make_async_copy(
                    source.at[blk], target.at[blk], local_sems.at[item]
                )
                moved.append(started(local))
        if 0 < step <= pieces:
            multiply(step - 1)
        if 1 < step <= pieces + 1:
            pass_on(step - 2)
        if step > 2:
            finish(step - 3)
    for copy in near_copies:
        copy.wait_send()
    for copies in chip_copies:
        for copy in copies:
            copy.wait_send()
    for piece, copies in enumerate(head_copies):
        for number, copy in enumerate(copies):
            if number != 1:
                distant = far(head_peers[number])
                pl.when(jnp.logical_not(distant))(copy.wait_send)
                pl.when(distant)(through_copy(piece, head_peers[number]).wait_send)
            else:
                copy.wait_send()
    for copy in moved:
        copy.wait()


UNPROJECT_PIECES = 4


def unproject_plan(grad_pairs, weight, moved):
    heads, blocks = lax.axis_size("head"), lax.axis_size("blk")
    chips = blocks // 2
    pieces = UNPROJECT_PIECES
    slots, _, _, _, resident, pair_columns = grad_pairs.shape
    rows = slots * resident
    count = rows // pieces
    width, columns = weight.shape
    items = len(moved)
    vmem = pl.BlockSpec(memory_space=pltpu.VMEM)
    anywhere = pl.BlockSpec(memory_space=pl.ANY)
    return (
        [
            jax.ShapeDtypeStruct((heads, rows, columns), jnp.bfloat16),
            jax.ShapeDtypeStruct((rows, width), jnp.float32),
            *(jax.ShapeDtypeStruct(array.shape, array.dtype) for array in moved),
        ],
        [vmem] * 2 + [anywhere] * items,
        [
            pltpu.VMEM((pieces, heads, chips, count, pair_columns), jnp.bfloat16),
            pltpu.VMEM((pieces, heads, chips, count, pair_columns), jnp.bfloat16),
            pltpu.VMEM((pieces, chips, heads, count, pair_columns), jnp.bfloat16),
            pltpu.VMEM((heads, count, width), jnp.float32),
            pltpu.VMEM((heads, rows, width), jnp.bfloat16),
            pltpu.VMEM((heads, rows, width), jnp.bfloat16),
            pltpu.VMEM((rows, width), jnp.bfloat16),
            pltpu.SemaphoreType.DMA((pieces,)),
            pltpu.SemaphoreType.DMA((pieces,)),
            pltpu.SemaphoreType.DMA((pieces * chips,)),
            pltpu.SemaphoreType.DMA((pieces * chips,)),
            pltpu.SemaphoreType.DMA((pieces * heads,)),
            pltpu.SemaphoreType.DMA((pieces * heads,)),
            pltpu.SemaphoreType.DMA((items * blocks,)),
            pltpu.SemaphoreType.DMA((items * blocks,)),
            pltpu.SemaphoreType.DMA((items,)),
        ],
    )


def unproject(grad_queries, grad_pairs, weight, cosine, sine, moved, after, onward=None):
    heads, blocks = lax.axis_size("head"), lax.axis_size("blk")
    outs, out_specs, scratch = unproject_plan(grad_pairs, weight, moved)
    results, temps = len(outs), len(scratch)
    items = len(moved)
    vmem = pl.BlockSpec(memory_space=pltpu.VMEM)
    anywhere = pl.BlockSpec(memory_space=pl.ANY)
    norm_arrays, arrays, specs, more_outs, more_specs, more_scratch = [], [], [], [], [], []
    if onward is not None:
        *norm_arrays, (places, scale, matrices) = onward
        rows, width = norm_arrays[0].shape
        arrays, specs, more_outs, more_specs, more_scratch = dispatch_plan(
            jax.ShapeDtypeStruct((rows, width), jnp.bfloat16), places, scale, matrices, True
        )
        arrays, specs = arrays[1:], specs[1:]
        more_outs = [
            jax.ShapeDtypeStruct((rows, width), jnp.float32),
            jax.ShapeDtypeStruct((1, width), jnp.float32),
            *more_outs,
        ]
        more_specs = [vmem, vmem, *more_specs]
        more_scratch = [pltpu.VMEM((rows, width), jnp.bfloat16), *more_scratch]

    def kernel(*refs):
        given, refs = refs[: 5 + items], refs[5 + items + len(after) :]
        norm_refs, refs = refs[: len(norm_arrays)], refs[len(norm_arrays) :]
        dispatch_refs, refs = list(refs[: len(arrays)]), refs[len(arrays) :]
        made, refs = refs[:results], refs[results:]
        more, refs = refs[: len(more_outs)], refs[len(more_outs) :]
        unproject_kernel(heads, blocks, UNPROJECT_PIECES, items, *given, *made, *refs[:temps])
        if onward is None:
            return
        refs = refs[temps:]
        other_ref, valid_ref, gain_ref, scaled_ref, inverse_ref = norm_refs
        hidden_ref, grad_gain_ref, *more = more
        own_ref, *rest = refs
        grad = made[1][...]
        scaled = scaled_ref[...]
        grad_gain_ref[...] = jnp.sum(grad * scaled, axis=0, keepdims=True)
        grad = grad * gain_ref[...]
        grad = inverse_ref[:, :1] * (
            grad - scaled * jnp.mean(grad * scaled, axis=1, keepdims=True)
        )
        hidden = other_ref[...] + grad
        hidden_ref[...] = hidden
        own_ref[...] = (valid_ref[...] * hidden).astype(own_ref.dtype)
        for stage in dispatch_stages(
            heads, blocks, True, (own_ref, *dispatch_refs, *more, *rest)
        ):
            stage()

    values = pl.pallas_call(
        kernel,
        out_shape=[*outs, *more_outs],
        in_specs=[vmem] * 5
        + [anywhere] * (items + len(after))
        + [vmem] * len(norm_arrays)
        + specs,
        out_specs=[*out_specs, *more_specs],
        scratch_shapes=[*scratch, *more_scratch],
        compiler_params=pltpu.CompilerParams(
            collective_id=kernel_number(
                "unproject", onward is None, *(array.shape for array in (*moved, *after))
            ),
            has_side_effects=True,
            vmem_limit_bytes=60 * 1024 * 1024,
        ),
        cost_estimate=pl.CostEstimate(
            flops=0, bytes_accessed=(150 if onward is None else 320) << 20, transcendentals=0
        ),
        name="unproject",
    )(grad_queries, grad_pairs, weight, cosine, sine, *moved, *after, *norm_arrays, *arrays)
    return values[:results], values[results:]


def combine_stages(heads, blocks, by_columns, backward, refs):
    units_ref, shared_units_ref, place_ref, scale_ref, weight_ref, shared_weight_ref, *refs = refs
    if backward:
        gate_up_ref, grad_units_ref = units_ref, refs[0]
        sources, refs = refs[1:6], refs[6:]
    out_ref, returned_ref, *refs = refs
    if backward:
        grad_in_ref, grad_down_ref, gates_ref, *refs = refs
        units_ref, dots_ref, gate_part_ref, *held = refs[-10:]
        queue_ref, inner_ref, made_grad_ref, plane_ref, came_ref, late_sems, _ = held
        refs = refs[:-10]
    (
        made_ref,
        part_ref,
        landed_ref,
        relay_ref,
        held_ref,
        shared_held_ref,
        head_send,
        head_recv,
        blk_send,
        blk_recv,
        local_sems,
    ) = refs
    pieces = COMBINE_PIECES
    head, blk, head_peers, blk_peers = plane_peers(heads, blocks)
    rows, width = out_ref.shape
    slot = returned_ref.shape[1]
    shared = shared_units_ref.shape[0]
    step_width = width // pieces
    relay = heads == 4
    inner = jnp.logical_and(head > 0, head < heads - 1)
    loads = [
        pltpu.make_async_copy(weight_ref, held_ref, local_sems.at[0]),
        pltpu.make_async_copy(shared_weight_ref, shared_held_ref, local_sems.at[1]),
    ]
    gate_copies = []
    head_copies = []
    blk_copies = []
    late = []
    if backward:
        late = [
            pltpu.make_async_copy(source, target, late_sems.at[number])
            for number, (source, target) in enumerate(
                zip(sources, (queue_ref, inner_ref, made_grad_ref, plane_ref, came_ref))
            )
        ]

    def begin():
        for load in loads + late:
            load.start()
        if backward:
            half = grad_units_ref.shape[1]

            def turn(block, carry):
                rows_here = pl.ds(pl.multiple_of(block * slot, 16), slot)
                gate = gate_up_ref[rows_here, pl.ds(0, half)]
                up = gate_up_ref[rows_here, pl.ds(half, half)]
                grad = grad_units_ref[rows_here, :]
                share = 1.0 / (1.0 + jnp.exp(-gate))
                units_ref[rows_here, pl.ds(0, half)] = (
                    grad * up * share * (1.0 + gate * (1.0 - share))
                ).astype(units_ref.dtype)
                units_ref[rows_here, pl.ds(half, half)] = (grad * gate * share).astype(
                    units_ref.dtype
                )
                return carry

            lax.fori_loop(0, blocks, turn, 0)
        for load in loads:
            load.wait()

    def fill(number):
        if number == 1:
            for load in late:
                load.wait()
        piece = number - 1
        columns = pl.ds(piece * step_width, step_width)
        if 0 <= piece < pieces:
            grad_in_ref[columns, :] = dot_first(queue_ref[:, columns], units_ref[...]).astype(
                grad_in_ref.dtype
            )
            dots = dot_last(plane_ref[:, columns], came_ref[:, columns])
            if piece:
                dots = dots + dots_ref[...]
            dots_ref[...] = dots
        tile = 128
        if 0 <= piece < inner_ref.shape[1] // tile:
            lanes = pl.ds(piece * tile, tile)
            grad_down_ref[lanes, :] = dot_first(inner_ref[:, lanes], made_grad_ref[...]).astype(
                grad_down_ref.dtype
            )
        if piece == pieces:
            count = dots_ref.shape[1]
            shape = (gate_part_ref.shape[0], count)
            spread = jnp.where(
                lax.broadcasted_iota(jnp.int32, shape, 1) // slot
                == lax.broadcasted_iota(jnp.int32, shape, 0),
                1.0,
                0.0,
            ).astype(jnp.bfloat16)
            dots = dots_ref[...].astype(jnp.bfloat16) * place_ref[...]
            gate_part_ref[...] = dot_last(spread, dots)
            gates_ref[head] = gate_part_ref[...]
            gate_copies.extend(
                started(
                    remote(
                        gate_part_ref,
                        gates_ref.at[head],
                        (head_send, head_recv),
                        pieces * heads + index,
                        peer,
                    )
                )
                for index, peer in enumerate(head_peers)
            )

    def produce(piece):
        columns = pl.ds(piece * step_width, step_width)

        def make(block, carry):
            start = pl.multiple_of(block * slot, 16)
            made_ref[block, :, columns] = meet(
                units_ref[pl.ds(start, slot), :],
                weight_part(held_ref, columns, not by_columns),
                by_columns,
            ).astype(made_ref.dtype)
            return carry

        lax.fori_loop(0, blocks, make, 0)
        blk_copies.append(
            [
                started(
                    remote(
                        made_ref.at[peer[1], :, columns],
                        returned_ref.at[blk, :, columns],
                        (blk_send, blk_recv),
                        piece * (blocks - 1) + number,
                        peer,
                    )
                )
                for number, peer in enumerate(blk_peers)
            ]
        )
        returned_ref[blk, :, columns] = made_ref[blk, :, columns]
        for expert in range(shared):
            returned_ref[blocks + expert, :, columns] = meet(
                shared_units_ref[expert],
                weight_part(shared_held_ref.at[expert], columns, not by_columns),
                by_columns,
            ).astype(returned_ref.dtype)

    def far(peer):
        return jnp.abs(peer[0] - head) == heads - 1

    def peer_origin(peer):
        return lax.rem(2 * head + heads - peer[0], heads)

    def through_copy(piece, peer):
        columns = pl.ds(piece * step_width, step_width)
        return remote(
            part_ref.at[peer[0], :, columns],
            relay_ref.at[:, columns],
            (head_send, head_recv),
            piece * heads + heads - 1,
            (jnp.where(head == 0, 1, heads - 2), blk),
        )

    def gather(piece):
        columns = pl.ds(piece * step_width, step_width)
        for copy in blk_copies[piece]:
            copy.wait_recv()
        returned = returned_ref[:, :, columns].reshape((blocks + shared) * slot, step_width)
        if scale_ref is not None:
            returned = (returned.astype(jnp.float32) * scale_ref[...]).astype(returned_ref.dtype)

        def part(owner):
            start = pl.multiple_of(owner * rows, 16)
            return jnp.dot(
                place_ref[pl.ds(start, rows), :], returned, preferred_element_type=jnp.float32
            )

        sent = []
        for number, peer in enumerate(head_peers):
            part_ref[peer[0], :, columns] = part(peer[0]).astype(part_ref.dtype)
            copy = remote(
                part_ref.at[peer[0], :, columns],
                landed_ref.at[head, :, columns],
                (head_send, head_recv),
                piece * heads + number,
                peer,
            )
            sent.append(copy)
            if not relay:
                copy.start()
            elif number == 1:
                pl.when(jnp.logical_not(inner))(copy.start)
            else:
                distant = far(peer)
                pl.when(jnp.logical_not(distant))(copy.start)
                pl.when(distant)(through_copy(piece, peer).start)
        head_copies.append(sent)
        out_ref[:, columns] = part(head)

    def pass_on(piece):
        columns = pl.ds(piece * step_width, step_width)
        target = lax.rem(head + 2, heads)

        @pl.when(inner)
        def _():
            through_copy(piece, (target, blk)).wait_recv()
            part_ref[target, :, columns] = (
                part_ref[target, :, columns].astype(jnp.float32)
                + relay_ref[:, columns].astype(jnp.float32)
            ).astype(part_ref.dtype)
            head_copies[piece][1].start()

    def finish(piece):
        columns = pl.ds(piece * step_width, step_width)
        for number, peer in enumerate(head_peers):
            copy = head_copies[piece][number]

            def add(copy=copy, peer=peer):
                copy.wait_recv()
                out_ref[:, columns] += landed_ref[peer_origin(peer), :, columns].astype(
                    jnp.float32
                )

            if relay and number != 1:
                pl.when(jnp.logical_not(far((peer_origin(peer), blk))))(add)
            else:
                add()

    lag = 3 if relay else 2

    def step(number):
        if number < pieces:
            produce(number)
        if backward:
            fill(number)
        if 0 < number <= pieces:
            gather(number - 1)
        if relay and 1 < number <= pieces + 1:
            pass_on(number - 2)
        if number >= lag:
            finish(number - lag)

    def end():
        for piece, copies in enumerate(head_copies):
            for number, copy in enumerate(copies):
                if relay and number != 1:
                    distant = far(head_peers[number])
                    pl.when(jnp.logical_not(distant))(copy.wait_send)
                    pl.when(distant)(through_copy(piece, head_peers[number]).wait_send)
                else:
                    copy.wait_send()
        for copy in gate_copies:
            copy.wait()
        for copies in blk_copies:
            for copy in copies:
                copy.wait_send()

    steps = [functools.partial(step, number) for number in range(pieces + lag)]
    return [begin, *steps, end]


def combine_call(units, shared_units, places, scale, weights, by_columns, backward=None):
    heads, blocks = lax.axis_size("head"), lax.axis_size("blk")
    (own_weight, shared_weight) = weights
    shared, slot = shared_units.shape[:2]
    count = places.shape[0] // heads
    width = own_weight.shape[0 if by_columns else 1]
    pieces = COMBINE_PIECES
    vmem = pl.BlockSpec(memory_space=pltpu.VMEM)
    anywhere = pl.BlockSpec(memory_space=pl.ANY)
    scales = [] if scale is None else [scale]
    outs = [
        jax.ShapeDtypeStruct((count, width), jnp.float32),
        jax.ShapeDtypeStruct((blocks + shared, slot, width), jnp.bfloat16),
    ]
    scratch = [
        pltpu.VMEM((blocks, slot, width), jnp.bfloat16),
        pltpu.VMEM((heads, count, width), jnp.bfloat16),
        pltpu.VMEM((heads, count, width), jnp.bfloat16),
        pltpu.VMEM((count, width), jnp.bfloat16),
        pltpu.VMEM(own_weight.shape, jnp.bfloat16),
        pltpu.VMEM(shared_weight.shape, jnp.bfloat16),
        pltpu.SemaphoreType.DMA(((pieces + 1) * heads,)),
        pltpu.SemaphoreType.DMA(((pieces + 1) * heads,)),
        pltpu.SemaphoreType.DMA((pieces * (blocks - 1),)),
        pltpu.SemaphoreType.DMA((pieces * (blocks - 1),)),
        pltpu.SemaphoreType.DMA((2,)),
    ]
    arrays = [units, shared_units, places, *scales, own_weight, shared_weight]
    specs = [vmem] * (3 + len(scales)) + [anywhere] * 2
    if backward is not None:
        grad_units, *late = backward
        arrays += [grad_units, *late]
        specs += [vmem] + [anywhere] * len(late)
        inner = late[1].shape[1]
        gate_rows = -(-(blocks + shared) // 8) * 8
        outs += [
            jax.ShapeDtypeStruct((width, units.shape[1]), jnp.bfloat16),
            jax.ShapeDtypeStruct((inner, width), jnp.bfloat16),
            jax.ShapeDtypeStruct((heads, gate_rows, places.shape[0]), jnp.float32),
        ]
        scratch += [
            pltpu.VMEM(units.shape, jnp.bfloat16),
            pltpu.VMEM(places.shape, jnp.float32),
            pltpu.VMEM((gate_rows, places.shape[0]), jnp.float32),
            *(pltpu.VMEM(array.shape, array.dtype) for array in late),
            pltpu.SemaphoreType.DMA((len(late),)),
            pltpu.SemaphoreType.DMA,
        ]
    return (
        ("combine", by_columns, scale is not None, backward is not None),
        functools.partial(combine_stages, heads, blocks, by_columns, backward is not None),
        arrays,
        specs,
        outs,
        [vmem] * len(outs),
        scratch,
        scale is not None,
    )


def head_parts(partial):
    heads = lax.axis_size("head")
    return partial.astype(jnp.bfloat16).reshape(heads, -1, partial.shape[-1])


def head_sum(parts):
    return jnp.sum(parts.astype(jnp.float32), axis=0)


def dot_last(left, right):
    return lax.dot_general(
        left, right, (((1,), (1,)), ((), ())), preferred_element_type=jnp.float32
    )


def dot_first(left, right):
    return lax.dot_general(
        left, right, (((0,), (0,)), ((), ())), preferred_element_type=jnp.float32
    )


def head_columns(ref, rows, first, group, shift):
    pieces = []
    for member in range(group):
        start = (first + member) * HEAD_SIZE
        piece = ref[0, rows, start : start + HEAD_SIZE]
        empty = jnp.zeros_like(piece)
        pieces.append(jnp.concatenate([empty, piece] if shift else [piece, empty], axis=1))
    return jnp.concatenate(pieces, axis=0)


def unit_scores(queries, pairs, blk, resident, chunk):
    scores = dot_last(queries, pairs) * 0.125
    count, keys = scores.shape
    places = lax.broadcasted_iota(jnp.int32, (count, chunk), 1)
    own = blk * resident + lax.broadcasted_iota(jnp.int32, (count, chunk), 0) % resident
    last = jnp.where(places <= own, scores[:, keys - chunk :], negative)
    if keys > chunk:
        scores = jnp.concatenate([scores[:, : keys - chunk], last], axis=1)
    else:
        scores = last
    exponents = jnp.exp(scores - jnp.max(scores, axis=1, keepdims=True))
    return (exponents, jnp.sum(exponents, axis=1, keepdims=True))


def attend_kernel(heads, blocks, resident, group, kv_local, info_ref, query_ref, pair_ref, out_ref):
    slot_index = pl.program_id(0)
    blk = info_ref[0]
    length = info_ref[1 + slot_index]
    chunk = blocks * resident
    for head in range(heads):
        rows = pl.ds(head * resident, resident)
        live = head * chunk + blk * resident < length

        @pl.when(live)
        def _(head=head, rows=rows):
            keys = (head + 1) * chunk
            for kv_head in range(kv_local):
                lanes = pl.ds(kv_head * 2 * HEAD_SIZE, 2 * HEAD_SIZE)
                pairs = pair_ref[0, pl.ds(0, keys), lanes]
                queries = head_columns(query_ref, rows, kv_head * group, group, False)
                exponents, totals = unit_scores(queries, pairs, blk, resident, chunk)
                weighted = jnp.dot(
                    exponents.astype(jnp.bfloat16), pairs, preferred_element_type=jnp.float32
                )
                weighted = weighted / totals
                for member in range(group):
                    start = (kv_head * group + member) * HEAD_SIZE
                    out_ref[head, 0, :, start : start + HEAD_SIZE] = weighted[
                        member * resident : (member + 1) * resident, HEAD_SIZE:
                    ].astype(out_ref.dtype)

        @pl.when(jnp.logical_not(live))
        def _(head=head):
            out_ref[head, 0] = jnp.zeros(out_ref.shape[2:], out_ref.dtype)


def attend_back_kernel(
    heads,
    blocks,
    resident,
    group,
    kv_local,
    info_ref,
    query_ref,
    pair_ref,
    grad_ref,
    grad_query_ref,
    grad_pair_ref,
    total_ref,
):
    slot_index = pl.program_id(0)
    blk = info_ref[0]
    length = info_ref[1 + slot_index]
    chunk = blocks * resident
    total_ref[...] = jnp.zeros_like(total_ref)
    for head in range(heads):
        rows = pl.ds(head * resident, resident)
        live = head * chunk + blk * resident < length

        @pl.when(live)
        def _(head=head, rows=rows):
            keys = (head + 1) * chunk
            for kv_head in range(kv_local):
                lanes = pl.ds(kv_head * 2 * HEAD_SIZE, 2 * HEAD_SIZE)
                pairs = pair_ref[0, pl.ds(0, keys), lanes]
                queries = head_columns(query_ref, rows, kv_head * group, group, False)
                grads = head_columns(grad_ref, rows, kv_head * group, group, True)
                exponents, totals = unit_scores(queries, pairs, blk, resident, chunk)
                probabilities = exponents * (1.0 / totals)
                grad_probs = dot_last(grads, pairs)
                delta = jnp.sum(probabilities * grad_probs, axis=1, keepdims=True)
                grad_scores = (probabilities * (grad_probs - delta)).astype(jnp.bfloat16)
                grad_queries = 0.125 * jnp.dot(
                    grad_scores, pairs, preferred_element_type=jnp.float32
                )
                for member in range(group):
                    start = (kv_head * group + member) * HEAD_SIZE
                    grad_query_ref[0, rows, start : start + HEAD_SIZE] = grad_queries[
                        member * resident : (member + 1) * resident, :HEAD_SIZE
                    ].astype(grad_query_ref.dtype)
                total_ref[pl.ds(0, keys), lanes] += dot_first(
                    grad_scores, queries * jnp.bfloat16(0.125)
                ) + dot_first(probabilities.astype(jnp.bfloat16), grads)

        @pl.when(jnp.logical_not(live))
        def _(rows=rows):
            grad_query_ref[0, rows, :] = jnp.zeros(
                (resident, grad_query_ref.shape[2]), grad_query_ref.dtype
            )

    grad_pair_ref[0] = total_ref[...].astype(grad_pair_ref.dtype)


def plan_kernel(heads, experts_local, slot, info_ref, routes_ref, ranks_ref, chosen_ref, place_ref, turned_ref):
    routes = routes_ref[0]
    ranks = ranks_ref[0]
    tokens = routes.shape[1]
    count = place_ref.shape[2]
    first = info_ref[0] * experts_local
    lanes = 128
    named = [
        jnp.max(jnp.where(routes == expert, 1, 0), axis=0, keepdims=True)
        for expert in range(EXPERTS)
    ]
    named.append(jnp.zeros((lanes - EXPERTS, tokens), jnp.int32))
    chosen_ref[0] = jnp.concatenate(named, axis=0).astype(jnp.float32).T
    marks = [
        jnp.sum(
            jnp.where((routes == first + expert) & (ranks < CAP), ranks + 1, 0),
            axis=0,
            keepdims=True,
        )
        for expert in range(experts_local)
    ]
    marks.append(jnp.zeros((lanes - experts_local, tokens), jnp.int32))
    marks = jnp.concatenate(marks, axis=0).astype(jnp.float32)
    slot_rows = tokens // heads

    def fits(shape, row_axis, wide):
        row = lax.broadcasted_iota(jnp.int32, shape, row_axis)
        token = lax.broadcasted_iota(jnp.int32, shape, 1 - row_axis)
        inside = row % slot
        same = (inside // CAP == token // slot_rows) & (wide.astype(jnp.int32) == inside % CAP + 1)
        return jnp.where(same, 1.0, 0.0).astype(jnp.bfloat16)

    def spread(shape, row_axis):
        row = lax.broadcasted_iota(jnp.int32, shape, row_axis)
        expert = lax.broadcasted_iota(jnp.int32, shape, 1 - row_axis)
        return jnp.where(row // slot == expert, 1.0, 0.0).astype(jnp.bfloat16)

    place_ref[0] = fits(
        (tokens, count),
        1,
        jnp.dot(
            marks.T.astype(jnp.bfloat16),
            spread((lanes, count), 1),
            preferred_element_type=jnp.float32,
        ),
    )
    turned_ref[0] = fits(
        (count, tokens),
        0,
        jnp.dot(
            spread((count, lanes), 0),
            marks.astype(jnp.bfloat16),
            preferred_element_type=jnp.float32,
        ),
    )


def plans(heads, experts_local, slot, head_index, routes, ranks):
    layers, top, tokens = routes.shape
    count = experts_local * slot

    def spec(*shape):
        return pl.BlockSpec((1,) + shape, lambda layer, info: (layer, 0, 0))

    chosen, places, turned = pl.pallas_call(
        functools.partial(plan_kernel, heads, experts_local, slot),
        grid_spec=pltpu.PrefetchScalarGridSpec(
            num_scalar_prefetch=1,
            grid=(layers,),
            in_specs=[spec(top, tokens)] * 2,
            out_specs=[spec(tokens, 128), spec(tokens, count), spec(count, tokens)],
        ),
        out_shape=[
            jax.ShapeDtypeStruct((layers, tokens, 128), jnp.float32),
            jax.ShapeDtypeStruct((layers, tokens, count), jnp.bfloat16),
            jax.ShapeDtypeStruct((layers, count, tokens), jnp.bfloat16),
        ],
        compiler_params=pltpu.CompilerParams(vmem_limit_bytes=40 * 1024 * 1024),
        cost_estimate=pl.CostEstimate(flops=0, bytes_accessed=16 << 20, transcendentals=0),
        name="plans",
    )(head_index[None].astype(jnp.int32), routes, ranks)
    return chosen[:, :, :EXPERTS] > 0.0, places, turned


def attention_call(kernel, info, arrays, outs, scratch, flops, name):
    def spec(array):
        shape = array.shape
        if len(shape) == 4:
            return pl.BlockSpec(
                (shape[0], 1) + shape[2:], lambda slot, info: (0, slot, 0, 0)
            )
        return pl.BlockSpec((1,) + shape[1:], lambda slot, info: (slot, 0, 0))

    return pl.pallas_call(
        kernel,
        grid_spec=pltpu.PrefetchScalarGridSpec(
            num_scalar_prefetch=1,
            grid=(SEQUENCE_SLOTS,),
            in_specs=[spec(array) for array in arrays],
            out_specs=[spec(array) for array in outs],
            scratch_shapes=scratch,
        ),
        out_shape=outs,
        compiler_params=pltpu.CompilerParams(vmem_limit_bytes=56 * 1024 * 1024),
        cost_estimate=pl.CostEstimate(
            flops=flops, bytes_accessed=8 << 20, transcendentals=flops // 256
        ),
        name=name,
    )(info, *arrays)


def shards(
    tokens,
    lengths,
    routes,
    queue_ranks,
    query_key_value_weight,
    w_out,
    router,
    norm_gains,
    w_in,
    w_down,
    cotangent,
):
    kernel_numbers.clear()
    heads_count = lax.axis_size("head")
    blocks_count = lax.axis_size("blk")
    head_index = lax.axis_index("head")
    blk_index = lax.axis_index("blk")
    resident = tokens.shape[1]
    width = tokens.shape[2]
    weight_rows = w_out.shape[1]
    rows_local = heads_count * resident
    keys_total = blocks_count * rows_local
    kv_local = KEY_VALUE_HEADS // heads_count
    group = QUERY_HEAD_COUNT // KEY_VALUE_HEADS
    query_columns = kv_local * group * HEAD_SIZE
    pair_columns = kv_local * 2 * HEAD_SIZE
    slot_rows = SEQUENCE_SLOTS * resident
    all_tokens = heads_count * slot_rows
    experts_local = EXPERTS // heads_count
    owned = experts_local // blocks_count
    owned_total = owned * blocks_count
    slot = -(-heads_count * CAP // 16) * 16
    half = HEAD_SIZE // 2

    own_places = (head_index * blocks_count + blk_index) * resident + jnp.arange(
        resident, dtype=jnp.int32
    )
    valid_column = (
        (own_places[None, :] < lengths[:, None]).astype(jnp.float32).reshape(slot_rows, 1)
    )
    plane_ids = jnp.arange(all_tokens, dtype=jnp.int32)
    plane_places = (
        (plane_ids // slot_rows * blocks_count + blk_index) * resident + plane_ids % resident
    ).astype(jnp.float32)
    frequency = jnp.exp(jnp.arange(half, dtype=jnp.float32) * (-2.0 * theta_log / HEAD_SIZE))
    angles = plane_places[:, None] * frequency[None, :]
    cosine = jnp.cos(angles)
    sine = jnp.sin(angles)
    repeats = 2 * HEAD_SIZE // half
    tile_cosine = jnp.concatenate([cosine] * repeats, axis=1).reshape(heads_count, slot_rows, -1)
    tile_sine = jnp.concatenate([-sine, sine] * (repeats // 2), axis=1)
    tile_sine = tile_sine.reshape(heads_count, slot_rows, -1)
    info = jnp.concatenate([blk_index[None].astype(jnp.int32), lengths])

    row_ids = jnp.arange(experts_local * slot, dtype=jnp.int32)
    spread = (
        row_ids[None, :] // slot == jnp.arange(experts_local, dtype=jnp.int32)[:, None]
    ).astype(jnp.bfloat16)
    def to_experts(rows):
        rows = rows.reshape(experts_local, slot, width)
        own = None
        if owned:
            own = rows[:owned_total].reshape(blocks_count, owned * slot, width)
            own = lax.all_to_all(own, "blk", 0, 0, tiled=True)
            own = own.reshape(blocks_count, owned, slot, width).transpose(1, 0, 2, 3)
            own = own.reshape(owned, blocks_count * slot, width)
        return (own, rows[owned_total:])

    def from_experts(own, shared):
        parts = [shared]
        if owned:
            own = own.reshape(owned, blocks_count, slot, width).transpose(1, 0, 2, 3)
            own = own.reshape(blocks_count, owned * slot, width)
            own = lax.all_to_all(own, "blk", 0, 0, tiled=True)
            parts = [own.reshape(owned_total, slot, width), shared]
        return jnp.concatenate(parts, axis=0).reshape(experts_local * slot, width)

    def shared_weights(layer_index, reached):
        if owned_total == experts_local:
            return []
        parts = tuple(matrix[layer_index, owned_total:] for matrix in (w_in, w_down))
        parts, _ = lax.optimization_barrier((parts, reached))
        return [tuple(lax.all_gather(part, "blk", axis=1, tiled=True) for part in parts)]

    def to_owner(matrix, layer_index):
        if not owned:
            return []
        if owned == 1:
            return [("blk_swap", matrix, layer_index)]
        pieces = matrix[layer_index, :owned_total]
        return [("blk_swap", pieces.reshape((blocks_count, owned) + pieces.shape[1:]))]

    def owned_matrix(received):
        if not owned:
            return None
        columns = received.shape[-1]
        pieces = received.reshape(blocks_count, owned, -1, columns)
        return pieces.transpose(1, 0, 2, 3).reshape(owned, -1, columns)

    def from_owner(term):
        if not owned:
            return []
        columns = term.shape[-1]
        pieces = term.reshape(owned, blocks_count, -1, columns).transpose(1, 0, 2, 3)
        return [("blk_swap", pieces)]

    def owned_rows(received):
        if not owned:
            return []
        return [received.reshape(owned_total, -1, received.shape[-1])]

    staged = owned == 1 and owned_total < experts_local

    def matrices(sets, which):
        own_weight, shared_weight = (mats[which] for mats in sets)
        return (own_weight[0], shared_weight)

    def unpack_in(results):
        plane, own, shared, own_out, shared_out = results
        return (
            plane.reshape(all_tokens, width),
            [own.reshape(1, -1, width), shared],
            [own_out[None], shared_out],
        )

    def unpack_out(results):
        total, returned, *extras = results
        return (total, returned.reshape(-1, width), *extras)

    def moe_in(rows, turned_places, scale, sets, which, after=()):
        if staged:
            plan = dispatch_call(rows, turned_places, scale, matrices(sets, which), which == 1)
            return unpack_in(staged_call([plan], "dispatch", 170, after)[0])
        (plane,) = exchange(("head_gather", rows))
        plane = plane.reshape(all_tokens, width)
        queues = mm("rt,td->rd", turned_places, plane)
        if scale is not None:
            queues = queues * scale
        queues = [part for part in to_experts(queues.astype(jnp.bfloat16)) if part is not None]
        spec = ("erd,edf->erf", "erd,efd->erf")[which]
        return (plane, queues, [mm(spec, rows, mats[which]) for rows, mats in zip(queues, sets)])

    def moe_out(units, places, scale, sets):
        if staged:
            plan = combine_call(
                units[0][0], units[1], places, scale, matrices(sets, 1), False
            )
            return unpack_out(staged_call([plan], "combine", 170)[0])
        made = [
            mm("erf,efd->erd", part, mats[1]).astype(jnp.bfloat16)
            for part, mats in zip(units, sets)
        ]
        returned = from_experts(*(made if owned else [None] + made))
        rows = (returned.astype(jnp.float32) * scale).astype(jnp.bfloat16)
        (parts,) = exchange(("head_swap", head_parts(mm("tr,rd->td", places, rows))))
        return (head_sum(parts), returned)

    def moe_back(places, sets, gate_up, grad_units, incoming, units, grad_rows, plane_grads, came):
        grad_gate_up = [
            gated_back(*parts) if number or not staged else None
            for number, parts in enumerate(zip(gate_up, grad_units))
        ]
        grad_weights = [
            (
                mm("erd,erf->edf", rows, grads).astype(jnp.bfloat16),
                mm("erf,erd->efd", inner, out_grads).astype(jnp.bfloat16),
            )
            if grads is not None
            else None
            for rows, grads, inner, out_grads in zip(incoming, grad_gate_up, units, grad_rows)
        ]
        if staged:
            plan = combine_call(
                gate_up[0][0],
                grad_gate_up[1],
                places,
                None,
                matrices(sets, 0),
                True,
                [grad_units[0][0], incoming[0][0], units[0][0], grad_rows[0][0], plane_grads, came],
            )
            total, _, grad_in, grad_down, gates = staged_call([plan], "combine_back", 170)[0]
            grad_weights[0] = (grad_in[None], grad_down[None])
            return (total, gates[:, :experts_local].reshape(EXPERTS, all_tokens), grad_weights)
        pair_dots = (mm("td,rd->tr", plane_grads, came) * places).astype(jnp.bfloat16)
        made = [
            mm("erf,edf->erd", part, mats[0]).astype(jnp.bfloat16)
            for part, mats in zip(grad_gate_up, sets)
        ]
        returned = from_experts(*(made if owned else [None] + made))
        parts, gates = exchange(
            ("head_swap", head_parts(mm("tr,rd->td", places, returned))),
            ("head_gather", mm("tr,er->te", pair_dots, spread).T),
        )
        return (head_sum(parts), gates.reshape(EXPERTS, all_tokens), grad_weights)

    def moe_turn(units, places, turned_places, scale, grad_rows, sets):
        if not staged:
            return (
                moe_out(units, places, scale, sets),
                moe_in(grad_rows, turned_places, scale, sets, 1),
            )
        weights = matrices(sets, 1)
        out_plan = combine_call(units[0][0], units[1], places, scale, weights, False)
        in_plan = dispatch_call(grad_rows, turned_places, scale, weights, True)
        out_results, in_results = staged_call([out_plan, in_plan], "turn", 260)
        return (unpack_out(out_results), unpack_in(in_results))

    def gated(gate_up):
        return (jax.nn.silu(gate_up[..., :FF]) * gate_up[..., FF:]).astype(jnp.bfloat16)

    def gated_back(gate_up, grad_units):
        gate_part = gate_up[..., :FF]
        up_part = gate_up[..., FF:]
        sigmoid_part = jax.nn.sigmoid(gate_part)
        return jnp.concatenate(
            [
                grad_units * up_part * sigmoid_part * (1.0 + gate_part * (1.0 - sigmoid_part)),
                grad_units * gate_part * sigmoid_part,
            ],
            axis=-1,
        ).astype(jnp.bfloat16)

    def by_slot(rows):
        return (
            rows.reshape(heads_count, SEQUENCE_SLOTS, resident, -1)
            .transpose(1, 0, 2, 3)
            .reshape(SEQUENCE_SLOTS, rows_local, -1)
        )

    def by_head(rows):
        return (
            rows.reshape(SEQUENCE_SLOTS, heads_count, resident, -1)
            .transpose(1, 0, 2, 3)
            .reshape(all_tokens, -1)
        )

    small_columns = 128
    send = []
    for layer_index in range(DECODER_LAYERS):
        weight = query_key_value_weight[layer_index]
        split = QUERY_HEAD_COUNT * HEAD_SIZE
        small = jnp.concatenate([router[layer_index], norm_gains[layer_index].T], axis=1)
        small = jnp.pad(small, ((0, 0), (0, small_columns - small.shape[1])))
        send.append(
            jnp.concatenate(
                [
                    weight[:, :split]
                    .reshape(weight_rows, heads_count, query_columns)
                    .transpose(1, 0, 2),
                    weight[:, split:]
                    .reshape(weight_rows, heads_count, pair_columns)
                    .transpose(1, 0, 2),
                    jnp.broadcast_to(small[None], (heads_count,) + small.shape),
                ],
                axis=-1,
            )
        )
    plan = jnp.stack([routes, queue_ranks]).reshape(2 * DECODER_LAYERS, slot_rows, TOP)
    plan = plan.transpose(0, 2, 1).reshape(2 * DECODER_LAYERS * TOP, slot_rows)
    plan, first_send = exchange(("head_gather", plan), ("head_swap", send[0]))
    plan = plan.reshape(heads_count, 2, DECODER_LAYERS, TOP, slot_rows)
    plan = plan.transpose(1, 2, 3, 0, 4).reshape(2, DECODER_LAYERS, TOP, all_tokens)
    chosen_all, places_all, turned_all = plans(
        heads_count, experts_local, slot, head_index, plan[0], plan[1]
    )

    def attention_set(wide, out_full):
        wide = wide.transpose(1, 0, 2, 3).reshape(width, -1)
        columns = query_columns + pair_columns
        small = wide[:, columns:]
        gains = small.T[EXPERTS : EXPERTS + 2].astype(jnp.float32)
        return (wide[:, :columns], out_full.reshape(-1, width), small[:, :EXPERTS], gains)

    wide, first_out, *next_sends = exchange(
        ("blk_pairs", first_send),
        ("blk_pairs", w_out[0]),
        *(("head_swap", array) for array in send[1:]),
    )
    attention_weights = [
        attention_set(wide, first_out),
    ]
    for layer_index, array in enumerate(next_sends, start=1):
        attention_weights.append(
            attention_set(
                lax.all_gather(array, "blk", axis=0),
                lax.all_gather(w_out[layer_index], "blk", axis=0),
            )
        )

    hidden = tokens.reshape(slot_rows, width).astype(jnp.float32)
    stored_all = []
    for layer_index in range(DECODER_LAYERS):
        qkv_full, out_full, router_full, gains = attention_weights[layer_index]
        chosen, places, turned_places = (
            part[layer_index] for part in (chosen_all, places_all, turned_all)
        )
        next_layer = layer_index + 1 < DECODER_LAYERS
        fused = staged and heads_count == 4
        if not fused or not layer_index:
            scaled_a, inverse_a = norm_rows(hidden)
            normed_a = (scaled_a * gains[:1]).astype(jnp.bfloat16)
        if fused and layer_index:
            plane_normed_a, queries, pairs_all, *own_down_next = crossed
            plane_normed_a = plane_normed_a.reshape(all_tokens, width)
        elif fused:
            plane_normed_a, queries, pairs_all, own_down = project(
                normed_a,
                qkv_full,
                tile_cosine,
                tile_sine,
                w_down,
                layer_index,
                pair_columns,
                resident,
            )
            plane_normed_a = plane_normed_a.reshape(all_tokens, width)
            own_down_next = [own_down]
        else:
            plane_normed_a, *own_down_next = exchange(
                ("head_gather", normed_a), *to_owner(w_down, layer_index)
            )
            plane_normed_a = plane_normed_a.reshape(all_tokens, width)
            projected = mm("td,de->te", plane_normed_a, qkv_full)
            queries = by_slot(
                rotate(projected[:, :query_columns], cosine, sine).astype(jnp.bfloat16)
            )
            pairs = projected[:, query_columns:].reshape(all_tokens, kv_local, 2, HEAD_SIZE)
            keys = rotate(pairs[:, :, 0].reshape(all_tokens, -1), cosine, sine)
            pairs = jnp.stack(
                [keys.reshape(all_tokens, kv_local, HEAD_SIZE), pairs[:, :, 1]], axis=2
            )
            pairs = pairs.reshape(all_tokens, pair_columns).astype(jnp.bfloat16)
            (pairs,) = exchange(("blk_pairs", pairs))
            pairs_all = pairs.reshape(
                blocks_count, heads_count, SEQUENCE_SLOTS, resident, pair_columns
            ).transpose(2, 1, 0, 3, 4)
        pairs_all = pairs_all.reshape(SEQUENCE_SLOTS, keys_total, pair_columns)
        (attended,) = attention_call(
            functools.partial(
                attend_kernel, heads_count, blocks_count, resident, group, kv_local
            ),
            info,
            [queries, pairs_all],
            [
                jax.ShapeDtypeStruct(
                    (heads_count, SEQUENCE_SLOTS, resident, query_columns), jnp.bfloat16
                )
            ],
            [],
            4 * rows_local * keys_total * query_columns,
            "attend",
        )
        attended = attended.reshape(all_tokens, query_columns)
        weight_sets = shared_weights(layer_index, middle if layer_index else wide)
        swaps = []
        if fused and staged:
            middle, scaled_b, inverse_b, *results = enter(
                attended,
                out_full,
                hidden,
                valid_column,
                gains[1:],
                turned_places,
                w_in,
                layer_index,
                weight_sets[0][0],
                swaps,
            )
            inverse_b = inverse_b[:, :1]
            results, own_in = results[:5], results[5]
            plane_rows, incoming, gate_up = unpack_in(results)
            weight_sets = [(own_in[None], owned_matrix(own_down_next[0]))] + weight_sets
        else:
            branch, *others = exchange(
                ("head_swap", head_parts(mm("tf,fd->td", attended, out_full))),
                *to_owner(w_in, layer_index),
            )
            own_in_next = others
            if owned:
                weight_sets = [
                    (owned_matrix(own_in_next[0]), owned_matrix(own_down_next[0]))
                ] + weight_sets
            middle = hidden + valid_column * head_sum(branch)
            scaled_b, inverse_b = norm_rows(middle)
            normed_b = (scaled_b * gains[1:]).astype(jnp.bfloat16)
            plane_rows, incoming, gate_up = moe_in(normed_b, turned_places, None, weight_sets, 0)
        units = [gated(part) for part in gate_up]
        logits = mm("td,de->te", plane_rows, router_full)
        peaks = jnp.max(jnp.where(chosen, logits, negative), axis=-1, keepdims=True)
        lifted = jnp.where(chosen, jnp.exp(logits - peaks), 0.0)
        gates_all = lifted / jnp.sum(lifted, axis=-1, keepdims=True)
        plane_gates = lax.dynamic_slice_in_dim(
            gates_all, head_index * experts_local, experts_local, 1
        )
        row_gates = mm("rt,te->re", turned_places, plane_gates.astype(jnp.bfloat16))
        row_gates = jnp.sum(row_gates * spread.T.astype(jnp.float32), axis=1, keepdims=True)
        if next_layer and fused:
            next_weights = attention_weights[layer_index + 1]
            (_, returned), norms, crossed = cross(
                combine_call(
                    units[0][0], units[1], places, row_gates, matrices(weight_sets, 1), False
                ),
                middle,
                valid_column,
                next_weights[3][:1],
                next_weights[0],
                tile_cosine,
                tile_sine,
                w_down,
                layer_index + 1,
                pair_columns,
                resident,
            )
            returned = returned.reshape(-1, width)
        elif next_layer:
            mixture, returned = moe_out(units, places, row_gates, weight_sets)
        else:
            (mixture, returned), turned = moe_turn(
                units,
                places,
                turned_places,
                row_gates,
                (valid_column * cotangent.reshape(slot_rows, width)).astype(jnp.bfloat16),
                weight_sets,
            )
        stored_all.append(
            (
                weight_sets,
                places,
                scaled_a,
                inverse_a,
                plane_normed_a,
                queries,
                pairs_all,
                attended,
                scaled_b,
                inverse_b,
                plane_rows,
                gates_all,
                turned_places,
                row_gates,
                incoming,
                gate_up,
                units,
                returned,
            )
        )
        if next_layer and fused:
            hidden, scaled_a, inverse_a = norms
            inverse_a = inverse_a[:, :1]
        else:
            hidden = middle + valid_column * mixture
    result = (valid_column * hidden).astype(jnp.bfloat16).reshape(tokens.shape)
    grad_hidden = valid_column * cotangent.reshape(slot_rows, width).astype(jnp.float32)
    qkv_list = [None] * DECODER_LAYERS
    out_list = [None] * DECODER_LAYERS
    router_list = [None] * DECODER_LAYERS
    gains_list = [None] * DECODER_LAYERS
    expert_list = [None] * DECODER_LAYERS
    pending = []
    waiting = []
    for layer_index in reversed(range(DECODER_LAYERS)):
        qkv_full, out_full, router_full, gains = attention_weights[layer_index]
        (
            weight_sets,
            places,
            scaled_a,
            inverse_a,
            plane_normed_a,
            queries,
            pairs_all,
            attended,
            scaled_b,
            inverse_b,
            plane_rows,
            gates_all,
            turned_places,
            row_gates,
            incoming,
            gate_up,
            units,
            returned,
        ) = stored_all[layer_index]
        if layer_index + 1 < DECODER_LAYERS and not fused:
            turned = moe_in(
                (valid_column * grad_hidden).astype(jnp.bfloat16),
                turned_places,
                row_gates,
                weight_sets,
                1,
                waiting,
            )
        plane_grads, grad_produced, grad_units = turned
        grad_normed_b, grad_gates, grad_weight_sets = moe_back(
            places,
            weight_sets,
            gate_up,
            grad_units,
            incoming,
            units,
            grad_produced,
            plane_grads,
            returned,
        )
        grad_gates = grad_gates.T
        grad_logits = gates_all * (
            grad_gates - jnp.sum(gates_all * grad_gates, axis=-1, keepdims=True)
        )
        plane_width = width // heads_count
        grad_router = mm(
            "td,te->de",
            lax.dynamic_slice_in_dim(plane_rows, head_index * plane_width, plane_width, 1),
            grad_logits.astype(jnp.bfloat16),
        )
        own_logits = lax.dynamic_slice_in_dim(grad_logits, head_index * slot_rows, slot_rows, 0)
        grad_normed_b = grad_normed_b + mm(
            "te,de->td", own_logits.astype(jnp.bfloat16), router_full
        )
        grad_norm_b, grad_gain_b = norm_back(grad_normed_b, scaled_b, inverse_b, gains[1:])
        grad_middle = grad_hidden + grad_norm_b
        plane_branch, *own_grad_in = exchange(
            ("head_gather", (valid_column * grad_middle).astype(jnp.bfloat16)),
            *(from_owner(grad_weight_sets[0][0]) if owned else []),
            after=[
                *pending,
                *(waiting if fused else ()),
                *(grad_weight_sets[-1] if owned_total < experts_local else ()),
            ],
        )
        pending = []
        shared_terms = []
        if owned_total < experts_local:
            shared_terms = [
                lax.psum_scatter(term, "blk", scatter_dimension=1, tiled=True)
                for term in grad_weight_sets[-1]
            ]
        plane_branch = plane_branch.reshape(all_tokens, width)
        grad_out_w = mm("tf,td->fd", attended, plane_branch)
        grad_attended = by_slot(mm("td,fd->tf", plane_branch, out_full).astype(jnp.bfloat16))
        grad_queries, grad_pairs = attention_call(
            functools.partial(
                attend_back_kernel, heads_count, blocks_count, resident, group, kv_local
            ),
            info,
            [queries, pairs_all, grad_attended],
            [
                jax.ShapeDtypeStruct(queries.shape, jnp.bfloat16),
                jax.ShapeDtypeStruct(pairs_all.shape, jnp.bfloat16),
            ],
            [pltpu.VMEM((keys_total, pair_columns), jnp.float32)],
            10 * rows_local * keys_total * query_columns,
            "attend_back",
        )
        grad_out_w = jnp.concatenate(
            [grad_out_w, jnp.pad(grad_router, ((0, 0), (0, small_columns - EXPERTS)))], axis=1
        ).astype(jnp.bfloat16)
        swapped = [("blk_swap", grad_out_w.reshape(blocks_count, weight_rows, -1))]
        if owned:
            swapped += from_owner(grad_weight_sets[0][1])
        if fused:
            onward = None
            if layer_index:
                before = stored_all[layer_index - 1]
                onward = (
                    grad_middle,
                    valid_column,
                    gains[:1],
                    scaled_a,
                    jnp.broadcast_to(inverse_a, (slot_rows, 128)),
                    (before[STORED_TURNED], before[STORED_GATES], matrices(before[0], 1)),
                )
            (grad_projected, grad_normed_a, grad_out_w, *own_grad_down), further = unproject(
                grad_queries,
                grad_pairs.reshape(
                    SEQUENCE_SLOTS, heads_count, blocks_count // 2, 2, resident, pair_columns
                ),
                qkv_full,
                tile_cosine,
                tile_sine,
                [array for _, array in swapped],
                shared_terms if layer_index else [],
                onward,
            )
            waiting = [] if layer_index else shared_terms
            grad_projected = grad_projected.reshape(all_tokens, -1)
        else:
            grad_pairs = (
                grad_pairs.reshape(
                    SEQUENCE_SLOTS, heads_count, blocks_count, resident, pair_columns
                )
                .transpose(2, 1, 0, 3, 4)
                .reshape(blocks_count, all_tokens, pair_columns)
            )
            (grad_pairs,) = exchange(("blk_swap", grad_pairs))
            grad_pairs = jnp.sum(grad_pairs.astype(jnp.float32), axis=0)
            grad_pairs = grad_pairs.astype(jnp.bfloat16).astype(jnp.float32)
            grad_pairs = grad_pairs.reshape(all_tokens, kv_local, 2, HEAD_SIZE)
            grad_keys = rotate(grad_pairs[:, :, 0].reshape(all_tokens, -1), cosine, -sine)
            grad_projected = jnp.concatenate(
                [
                    rotate(by_head(grad_queries).astype(jnp.float32), cosine, -sine),
                    jnp.stack(
                        [grad_keys.reshape(all_tokens, kv_local, HEAD_SIZE), grad_pairs[:, :, 1]],
                        axis=2,
                    ).reshape(all_tokens, pair_columns),
                ],
                axis=-1,
            ).astype(jnp.bfloat16)
            grad_normed_a, grad_out_w, *own_grad_down = exchange(
                ("head_swap", head_parts(mm("te,de->td", grad_projected, qkv_full))),
                *swapped,
                after=shared_terms,
            )
            grad_normed_a = head_sum(grad_normed_a)
        grad_out_w = jnp.sum(grad_out_w.astype(jnp.float32), axis=0)
        if fused and layer_index:
            grad_hidden, grad_gain_a, *further = further
            grad_gain_a = grad_gain_a[0]
            turned = unpack_in(further)
        else:
            grad_norm_a, grad_gain_a = norm_back(grad_normed_a, scaled_a, inverse_a, gains[:1])
            grad_hidden = grad_middle + grad_norm_a
        grad_qkv = (
            mm("td,te->de", plane_normed_a, grad_projected)
            .astype(jnp.bfloat16)
            .reshape(heads_count, blocks_count, weight_rows, -1)
            .transpose(1, 0, 2, 3)
        )
        if layer_index:
            grad_qkv = lax.psum_scatter(
                grad_qkv.reshape(width, -1), "blk", scatter_dimension=0, tiled=True
            )
            pending.append(grad_qkv)
            qkv_list[layer_index] = grad_qkv
            gains_list[layer_index] = jnp.stack([grad_gain_a, grad_gain_b])
        else:
            gains_list[0] = jnp.stack([grad_gain_a, grad_gain_b])
            grad_gains = (
                jnp.stack(gains_list)
                .reshape(2 * DECODER_LAYERS, heads_count, blocks_count, weight_rows)
                .transpose(1, 2, 0, 3)
                .reshape(heads_count, -1)
            )
            grad_qkv, grad_gains = exchange(
                ("blk_swap", grad_qkv),
                ("head_swap", grad_gains[:, None]),
                after=waiting,
            )
            grad_qkv = jnp.sum(grad_qkv.astype(jnp.float32), axis=0).astype(jnp.bfloat16)
            grad_gains = jnp.sum(grad_gains, axis=0).reshape(blocks_count, 1, -1)
            qkv_list[0] = grad_qkv
            *qkv_list, grad_gains = exchange(
                *(
                    ("head_swap", term.reshape(heads_count, weight_rows, -1))
                    for term in qkv_list
                ),
                ("blk_swap", grad_gains),
            )
            qkv_list = [
                jnp.concatenate(
                    [
                        term[..., :query_columns].transpose(1, 0, 2).reshape(weight_rows, -1),
                        term[..., query_columns:].transpose(1, 0, 2).reshape(weight_rows, -1),
                    ],
                    axis=1,
                ).astype(jnp.float32)
                for term in qkv_list
            ]
            grad_gains = jnp.sum(grad_gains, axis=0).reshape(DECODER_LAYERS, 2, weight_rows)

        out_list[layer_index] = grad_out_w[:, :width]
        router_list[layer_index] = grad_out_w[:, width : width + EXPERTS]
        terms = []
        for number, received in enumerate((own_grad_in, own_grad_down)):
            parts = owned_rows(received[0]) if owned else []
            if owned_total < experts_local:
                parts.append(shared_terms[number])
            terms.append(jnp.concatenate(parts, axis=0).astype(jnp.float32))
        expert_list[layer_index] = tuple(terms)
    return (
        result,
        grad_hidden.reshape(tokens.shape),
        jnp.stack(qkv_list),
        jnp.stack(out_list),
        jnp.stack(router_list),
        grad_gains[:, 0],
        grad_gains[:, 1],
        jnp.stack([terms[0] for terms in expert_list]),
        jnp.stack([terms[1] for terms in expert_list]),
    )


def solution(mesh):
    in_specs = (
        P(None, ("head", "blk"), None),
        P(),
        P(None, None, ("head", "blk"), None),
        P(None, None, ("head", "blk"), None),
        P(None, ("head", "blk"), None),
        P(None, ("head", "blk"), None),
        P(None, ("head", "blk"), None),
        P(None, None, ("head", "blk")),
        P(None, "head", "blk", None),
        P(None, "head", "blk", None),
        P(None, ("head", "blk"), None),
    )
    out_specs = (
        P(None, ("head", "blk"), None),
        P(None, ("head", "blk"), None),
        P(None, ("head", "blk"), None),
        P(None, ("head", "blk"), None),
        P(None, ("head", "blk"), None),
        P(None, ("head", "blk")),
        P(None, ("head", "blk")),
        P(None, "head", "blk", None),
        P(None, "head", "blk", None),
    )
    return jax.shard_map(shards, mesh=mesh, in_specs=in_specs, out_specs=out_specs, check_vma=False)
```

```python
import functools

import jax
import jax.numpy as jnp
from jax import lax
from jax.experimental import pallas as pl
from jax.experimental.pallas import tpu as pltpu
from jax.sharding import PartitionSpec as P

MODEL_WIDTH = 1536
QUERY_HEAD_COUNT = 24
KEY_VALUE_HEADS = 8
HEAD_SIZE = 64
FF = 512
EXPERTS = 40
TOP = 8
DECODER_LAYERS = 2
SEQUENCE_SLOTS = 2
CAP = 26


epsilon = 1e-06
negative = -1e30
theta_log = 9.210340371976184


MESH = pl.DeviceIdType.MESH


def mm(spec, left, right):
    return jnp.einsum(spec, left, right, preferred_element_type=jnp.float32)


def rotate(values, cosine, sine):
    rows = values.shape[0]
    half = HEAD_SIZE // 2
    heads = values.reshape(rows, -1, HEAD_SIZE)
    first_half = heads[..., :half]
    second_half = heads[..., half:]
    cosine = cosine[:, None, :]
    sine = sine[:, None, :]
    return jnp.concatenate(
        [first_half * cosine - second_half * sine, second_half * cosine + first_half * sine],
        axis=-1,
    ).reshape(values.shape)


def norm_rows(hidden):
    inverse = lax.rsqrt(jnp.mean(hidden * hidden, axis=-1, keepdims=True) + epsilon)
    return (hidden * inverse, inverse)


def norm_back(grad_normed, scaled, inverse, gain_row):
    grad_gain = jnp.sum(grad_normed * scaled, axis=0)
    grad_scaled = grad_normed * gain_row
    grad_hidden = inverse * (
        grad_scaled - scaled * jnp.mean(grad_scaled * scaled, axis=-1, keepdims=True)
    )
    return (grad_hidden, grad_gain)


RELAY_PIECES = 4


def relayed_gather(heads, head, blk, head_peers, source, target, sems, first):
    count = source.shape[0] // RELAY_PIECES
    inner = jnp.logical_and(head > 0, head < heads - 1)
    rounds = []
    for piece in range(RELAY_PIECES):
        part = pl.ds(piece * count, count)
        index = first + piece * heads
        copies = []
        for number, peer in enumerate(head_peers):
            copy = remote(source.at[part], target.at[head, part], sems, index + number, peer)
            near = jnp.abs(peer[0] - head) < heads - 1
            copies.append((copy, near))
            pl.when(near)(copy.start)
        rounds.append(copies)
    passed = []
    for piece, copies in enumerate(rounds):
        copies[1][0].wait_recv()
        there = target.at[lax.rem(head + 2, heads), pl.ds(piece * count, count)]
        index = first + piece * heads
        copy = remote(
            there,
            there,
            sems,
            index + heads - 1,
            ((head - 1) * (heads - 1), blk),
            index + jnp.where(head == 1, 0, heads - 2),
        )
        pl.when(inner)(copy.start)
        passed.append(copy)
    for copies, copy in zip(rounds, passed):
        copies[0][0].wait_recv()
        copies[2][0].wait_recv()
        for sent, near in copies:
            pl.when(near)(sent.wait_send)
        pl.when(inner)(copy.wait_send)


def exchange_kernel(heads, blocks, items, waited, *refs):
    count = len(items)
    sources = refs[:count]
    targets = refs[count + waited : 2 * count + waited]
    send_sems, recv_sems, local_sems = refs[2 * count + waited :]
    head = lax.axis_index("head")
    blk = lax.axis_index("blk")
    chips = blocks // 2
    chip, core = blk // 2, lax.rem(blk, 2)
    sibling = chip * 2 + 1 - core
    kinds = {kind for kind, _ in items}
    head_peers = [(lax.rem(head + step, heads), blk) for step in range(1, heads)]
    blk_peers = [(head, lax.rem(blk + step, blocks)) for step in range(1, blocks)]
    pair_peers = [
        (head, lax.rem(chip + step, chips) * 2 + core) for step in range(1, chips)
    ] + [(head, sibling)]
    greeted = []
    if kinds & {"head_gather", "head_swap"}:
        greeted += head_peers
    if "blk_swap" in kinds:
        greeted += blk_peers
    elif "blk_pairs" in kinds:
        greeted += pair_peers
    barrier = pltpu.get_barrier_semaphore()
    for peer in greeted:
        pl.semaphore_signal(barrier, inc=1, device_id=peer, device_id_type=MESH)
    pl.semaphore_wait(barrier, len(greeted))
    used = 0
    copies = []
    forwards = []

    def send(source, target, peer):
        nonlocal used
        copy = pltpu.make_async_remote_copy(
            src_ref=source,
            dst_ref=target,
            send_sem=send_sems.at[used],
            recv_sem=recv_sems.at[used],
            device_id=peer,
            device_id_type=MESH,
        )
        copy.start()
        used += 1
        return copy

    locals_started = []
    gathers = []
    for number, (kind, layer) in enumerate(items):
        source, target = sources[number], targets[number]

        def piece(index, source=source, layer=layer):
            return source.at[index] if layer is None else source.at[layer, index]

        if kind == "head_gather" and heads == 4 and source.shape[0] % 64 == 0:
            mine, place = source, head
            gathers.append((source, target))
        elif kind == "head_gather":
            mine, place = source, head
            copies += [send(source, target.at[head], peer) for peer in head_peers]
        elif kind == "head_swap":
            mine, place = piece(head), head
            copies += [send(piece(peer[0]), target.at[head], peer) for peer in head_peers]
        elif kind == "blk_swap":
            mine, place = piece(blk), blk
            copies += [send(piece(peer[1]), target.at[blk], peer) for peer in blk_peers]
        else:
            mine, place = source, blk
            sent = [send(source, target.at[blk], peer) for peer in pair_peers]
            copies += sent[-1:]
            forwards.append((sent[:-1], target))
        local = pltpu.make_async_copy(mine, target.at[place], local_sems.at[number])
        local.start()
        locals_started.append(local)
    for source, target in gathers:
        relayed_gather(heads, head, blk, head_peers, source, target, (send_sems, recv_sems), used)
        used += RELAY_PIECES * heads
    for sent, target in forwards:
        for step, copy in enumerate(sent, start=1):
            copy.wait_recv()
            origin = lax.rem(chip + chips - step, chips) * 2 + core
            copies.append(send(target.at[origin], target.at[origin], (head, sibling)))
    for sent, _ in forwards:
        for copy in sent:
            copy.wait_send()
    for local in locals_started:
        local.wait()
    for copy in copies:
        copy.wait()


kernel_numbers = {}


def kernel_number(*key):
    return kernel_numbers.setdefault(key, 1 + len(kernel_numbers))


def exchange(*items, after=()):
    heads, blocks = lax.axis_size("head"), lax.axis_size("blk")
    arrays = [item[1] for item in items]
    plan = [(item[0], item[2] if len(item) > 2 else None) for item in items]
    outs = []
    total = 0
    for (kind, layer), array in zip(plan, arrays):
        group = heads if kind.startswith("head") else blocks
        tail = array.shape
        if kind.endswith("swap"):
            tail = tail[1:] if layer is None else tail[2:]
        outs.append(jax.ShapeDtypeStruct((group,) + tail, array.dtype))
        total += RELAY_PIECES * group
    collective_id = kernel_number(
        "exchange", tuple(plan), *((array.shape, str(array.dtype)) for array in (*arrays, *after))
    )
    results = pl.pallas_call(
        functools.partial(exchange_kernel, heads, blocks, plan, len(after)),
        out_shape=outs,
        in_specs=[pl.BlockSpec(memory_space=pl.ANY)] * (len(arrays) + len(after)),
        out_specs=[pl.BlockSpec(memory_space=pl.ANY)] * len(arrays),
        scratch_shapes=[
            pltpu.SemaphoreType.DMA((total,)),
            pltpu.SemaphoreType.DMA((total,)),
            pltpu.SemaphoreType.DMA((len(arrays),)),
        ],
        compiler_params=pltpu.CompilerParams(collective_id=collective_id, has_side_effects=True),
        cost_estimate=pl.CostEstimate(flops=0, bytes_accessed=110 << 20, transcendentals=0),
        name="exchange",
    )(*arrays, *after)
    return results


def greet(peers):
    barrier = pltpu.get_barrier_semaphore()
    for peer in peers:
        pl.semaphore_signal(barrier, inc=1, device_id=peer, device_id_type=MESH)
    pl.semaphore_wait(barrier, len(peers))


def plane_peers(heads, blocks):
    head = lax.axis_index("head")
    blk = lax.axis_index("blk")
    head_peers = [(lax.rem(head + step, heads), blk) for step in range(1, heads)]
    blk_peers = [(head, lax.rem(blk + step, blocks)) for step in range(1, blocks)]
    return head, blk, head_peers, blk_peers


def remote(source, target, sems, index, peer, landing=None):
    return pltpu.make_async_remote_copy(
        src_ref=source,
        dst_ref=target,
        send_sem=sems[0].at[index],
        recv_sem=sems[1].at[index if landing is None else landing],
        device_id=peer,
        device_id_type=MESH,
    )


def started(copy):
    copy.start()
    return copy


def weight_part(ref, columns, by_columns):
    return ref[:, columns] if by_columns else ref[columns, :]


def meet(left, part, by_columns):
    return (
        dot_last(left, part)
        if by_columns
        else jnp.dot(left, part, preferred_element_type=jnp.float32)
    )


STORED_TURNED, STORED_GATES = 12, 13
DISPATCH_PIECES, DISPATCH_WINDOW, DISPATCH_LAG = 6, 3, 2
COMBINE_PIECES = 6


def dispatch_stages(heads, blocks, by_columns, refs):
    (
        own_ref,
        place_ref,
        scale_ref,
        weight_ref,
        shared_weight_ref,
        plane_ref,
        queue_ref,
        shared_ref,
        out_ref,
        shared_out_ref,
        send_ref,
        held_ref,
        shared_held_ref,
        head_send,
        head_recv,
        blk_send,
        blk_recv,
        local_sems,
    ) = refs
    pieces, window, lag = DISPATCH_PIECES, DISPATCH_WINDOW, DISPATCH_LAG
    head, blk, head_peers, blk_peers = plane_peers(heads, blocks)
    rows, width = own_ref.shape
    slot = queue_ref.shape[1]
    shared = shared_ref.shape[0]
    step_width = width // pieces
    outputs = out_ref.shape[1]
    tile = 256
    relay = heads == 4
    inner = jnp.logical_and(head > 0, head < heads - 1)
    loads = [pltpu.make_async_copy(shared_weight_ref, shared_held_ref, local_sems.at[1])]
    if weight_ref is not None:
        loads.append(pltpu.make_async_copy(weight_ref, held_ref, local_sems.at[0]))
    head_copies = []
    blk_copies = []
    relayed = []

    def far(peer):
        return jnp.abs(peer[0] - head) == heads - 1

    def spread(piece):
        columns = pl.ds(piece * step_width, step_width)
        copies = []
        for number, peer in enumerate(head_peers):
            copy = remote(
                own_ref.at[:, columns],
                plane_ref.at[head, :, columns],
                (head_send, head_recv),
                piece * heads + number,
                peer,
            )
            copies.append(copy)
            if relay and number != 1:
                pl.when(jnp.logical_not(far(peer)))(copy.start)
            else:
                copy.start()
        head_copies.append(copies)

    def pass_on(piece):
        columns = pl.ds(piece * step_width, step_width)
        origin = lax.rem(head + 2, heads)
        rows_there = plane_ref.at[origin, :, columns]
        copy = remote(
            rows_there,
            rows_there,
            (head_send, head_recv),
            piece * heads + heads - 1,
            ((head - 1) * (heads - 1), blk),
            piece * heads + jnp.where(head == 1, 0, heads - 2),
        )
        relayed.append(copy)
        pl.when(inner)(copy.start)

    def scaled(values, start):
        if scale_ref is not None:
            values = values * scale_ref[pl.ds(start, slot), :]
        return values.astype(queue_ref.dtype)

    def begin():
        for load in loads:
            load.start()
        for piece in range(min(window, pieces)):
            spread(piece)
        plane_ref[head] = own_ref[...]

    def consume(piece):
        columns = pl.ds(piece * step_width, step_width)
        for copy in blk_copies[piece]:
            copy.wait_recv()
        queue = queue_ref[:, :, columns].reshape(blocks * slot, step_width)

        def one_tile(index, carry):
            lanes = pl.ds(pl.multiple_of(index * tile, tile), tile)
            if by_columns:
                product = dot_last(queue, held_ref[lanes, columns])
            else:
                product = jnp.dot(
                    queue, held_ref[columns, lanes], preferred_element_type=jnp.float32
                )
            if piece:
                product = product + out_ref[:, lanes]
            out_ref[:, lanes] = product
            return carry

        lax.fori_loop(0, outputs // tile, one_tile, 0)

    def take(piece):
        columns = pl.ds(piece * step_width, step_width)
        if relay:
            for later in range(piece + 1 if piece else 0, min(piece + 2, pieces)):
                head_copies[later][1].wait_recv()
                pass_on(later)
        for number, copy in enumerate(head_copies[piece]):
            if not relay or number != 1:
                copy.wait_recv()
        if piece + window < pieces:
            spread(piece + window)
        plane = plane_ref[:, :, columns].reshape(heads * rows, step_width)

        def fill(expert, carry):
            start = pl.multiple_of(expert * slot, 16)
            taken = jnp.dot(
                place_ref[pl.ds(start, slot), :], plane, preferred_element_type=jnp.float32
            )
            send_ref[expert, :, columns] = scaled(taken, start)
            return carry

        lax.fori_loop(0, blocks, fill, 0)
        blk_copies.append(
            [
                started(
                    remote(
                        send_ref.at[peer[1], :, columns],
                        queue_ref.at[blk, :, columns],
                        (blk_send, blk_recv),
                        piece * (blocks - 1) + number,
                        peer,
                    )
                )
                for number, peer in enumerate(blk_peers)
            ]
        )
        queue_ref[blk, :, columns] = send_ref[blk, :, columns]
        if not piece:
            for load in loads:
                load.wait()
        for expert in range(shared):
            start = (blocks + expert) * slot
            taken = jnp.dot(
                place_ref[pl.ds(start, slot), :], plane, preferred_element_type=jnp.float32
            )
            taken = scaled(taken, start)
            shared_ref[expert, :, columns] = taken
            product = meet(
                taken, weight_part(shared_held_ref.at[expert], columns, by_columns), by_columns
            )
            if piece:
                product = product + shared_out_ref[expert]
            shared_out_ref[expert] = product

    def step(number):
        if number < pieces:
            take(number)
        if number >= lag:
            consume(number - lag)

    def end():
        for copies in head_copies:
            for number, copy in enumerate(copies):
                if relay and number != 1:
                    pl.when(jnp.logical_not(far(head_peers[number])))(copy.wait_send)
                else:
                    copy.wait_send()
        for copy in relayed:
            pl.when(inner)(copy.wait_send)
        for copies in blk_copies:
            for copy in copies:
                copy.wait_send()

    steps = [functools.partial(step, number) for number in range(pieces + lag)]
    return [begin, *steps, end]


def dispatch_plan(rows, places, scale, weights, by_columns):
    heads, blocks = lax.axis_size("head"), lax.axis_size("blk")
    count, width = rows.shape
    (own_weight, shared_weight) = weights
    shared = shared_weight.shape[0]
    slot = places.shape[0] // (blocks + shared)
    outputs = own_weight.shape[0 if by_columns else 1]
    pieces = DISPATCH_PIECES
    vmem = pl.BlockSpec(memory_space=pltpu.VMEM)
    anywhere = pl.BlockSpec(memory_space=pl.ANY)
    scales = [] if scale is None else [scale]
    return (
        [rows, places, *scales, own_weight, shared_weight],
        [vmem, vmem, *([vmem] * len(scales)), anywhere, anywhere],
        [
            jax.ShapeDtypeStruct((heads, count, width), jnp.bfloat16),
            jax.ShapeDtypeStruct((blocks, slot, width), jnp.bfloat16),
            jax.ShapeDtypeStruct((shared, slot, width), jnp.bfloat16),
            jax.ShapeDtypeStruct((blocks * slot, outputs), jnp.float32),
            jax.ShapeDtypeStruct((shared, slot, outputs), jnp.float32),
        ],
        [vmem] * 5,
        [
            pltpu.VMEM((blocks, slot, width), jnp.bfloat16),
            pltpu.VMEM(own_weight.shape, jnp.bfloat16),
            pltpu.VMEM(shared_weight.shape, jnp.bfloat16),
            pltpu.SemaphoreType.DMA((pieces * heads,)),
            pltpu.SemaphoreType.DMA((pieces * heads,)),
            pltpu.SemaphoreType.DMA((pieces * (blocks - 1),)),
            pltpu.SemaphoreType.DMA((pieces * (blocks - 1),)),
            pltpu.SemaphoreType.DMA((2,)),
        ],
    )


def staged_call(plans, name, millions, after=()):
    heads, blocks = lax.axis_size("head"), lax.axis_size("blk")
    inputs = [len(plan[2]) for plan in plans]
    outputs = [len(plan[4]) for plan in plans]
    scratches = [len(plan[6]) for plan in plans]

    def kernel(*refs):
        _, _, head_peers, blk_peers = plane_peers(heads, blocks)
        greet(head_peers + blk_peers)
        lists = []
        refs = refs[: sum(inputs)] + refs[sum(inputs) + len(after) :]
        for number, plan in enumerate(plans):
            first = sum(inputs[:number])
            given = list(refs[first : first + inputs[number]])
            if not plan[7]:
                given.insert(2 if plan[0][0] == "dispatch" else 3, None)
            first = sum(inputs) + sum(outputs[:number])
            given += refs[first : first + outputs[number]]
            first = sum(inputs) + sum(outputs) + sum(scratches[:number])
            given += refs[first : first + scratches[number]]
            lists.append(plan[1](given))
        for index in range(max(len(stages) for stages in lists)):
            for stages in lists:
                if index < len(stages):
                    stages[index]()

    arrays = [array for plan in plans for array in plan[2]]
    results = pl.pallas_call(
        kernel,
        out_shape=[out for plan in plans for out in plan[4]],
        in_specs=[spec for plan in plans for spec in plan[3]]
        + [pl.BlockSpec(memory_space=pl.ANY)] * len(after),
        out_specs=[spec for plan in plans for spec in plan[5]],
        scratch_shapes=[scratch for plan in plans for scratch in plan[6]],
        compiler_params=pltpu.CompilerParams(
            collective_id=kernel_number(
                *(plan[0] for plan in plans), *(array.shape for array in after)
            ),
            has_side_effects=True,
            vmem_limit_bytes=60 * 1024 * 1024,
        ),
        cost_estimate=pl.CostEstimate(
            flops=0, bytes_accessed=millions << 20, transcendentals=0
        ),
        name=name,
    )(*arrays, *after)
    return [
        results[sum(outputs[:number]) : sum(outputs[: number + 1])] for number in range(len(plans))
    ]


def dispatch_call(rows, places, scale, weights, by_columns):
    heads, blocks = lax.axis_size("head"), lax.axis_size("blk")
    return (
        ("dispatch", by_columns, scale is not None),
        functools.partial(dispatch_stages, heads, blocks, by_columns),
        *dispatch_plan(rows, places, scale, weights, by_columns),
        scale is not None,
    )


def enter_kernel(heads, blocks, layer, swaps, *refs):
    attended_ref, out_weight_ref, hidden_ref, valid_ref, gain_ref, place_ref, *refs = refs
    moved_ref, shared_weight_ref, *refs = refs
    swap_refs, refs = refs[:swaps], refs[swaps:]
    middle_ref, scaled_ref, inverse_ref, plane_ref, queue_ref, shared_ref, *refs = refs
    out_ref, shared_out_ref, matrix_ref, *refs = refs
    swap_out_refs, refs = refs[:swaps], refs[swaps:]
    own_ref, part_ref, landed_ref, relay_ref, sum_send, sum_recv, *refs = refs
    moved_send, moved_recv, swap_send, swap_recv, side_sems, *refs = refs
    send_ref, held_ref, shared_held_ref, head_send, head_recv, blk_send, blk_recv, local_sems = refs
    head, blk, head_peers, blk_peers = plane_peers(heads, blocks)
    rows, width = middle_ref.shape
    pieces = COMBINE_PIECES
    step_width = width // pieces
    matrix_rows = moved_ref.shape[2]
    inner = jnp.logical_and(head > 0, head < heads - 1)
    greet(head_peers + blk_peers)

    def far(peer):
        return jnp.abs(peer[0] - head) == heads - 1

    def peer_origin(peer):
        return lax.rem(2 * head + heads - peer[0], heads)

    sent = []

    def through_copy(piece, peer):
        columns = pl.ds(piece * step_width, step_width)
        return remote(
            part_ref.at[peer[0], :, columns],
            relay_ref.at[:, columns],
            (sum_send, sum_recv),
            piece * heads + heads - 1,
            (jnp.where(head == 0, 1, heads - 2), blk),
        )

    def spread(piece):
        columns = pl.ds(piece * step_width, step_width)
        weight = out_weight_ref[:, columns]

        def part(owner):
            start = pl.multiple_of(owner * rows, 16)
            return jnp.dot(
                attended_ref[pl.ds(start, rows), :], weight, preferred_element_type=jnp.float32
            )

        copies = []
        for number, peer in enumerate(head_peers):
            part_ref[peer[0], :, columns] = part(peer[0]).astype(part_ref.dtype)
            copy = remote(
                part_ref.at[peer[0], :, columns],
                landed_ref.at[head, :, columns],
                (sum_send, sum_recv),
                piece * heads + number,
                peer,
            )
            copies.append(copy)
            if number == 1:
                pl.when(jnp.logical_not(inner))(copy.start)
            else:
                distant = far(peer)
                pl.when(jnp.logical_not(distant))(copy.start)
                pl.when(distant)(through_copy(piece, peer).start)
        sent.append(copies)
        middle_ref[:, columns] = part(head)

    def pass_on(piece):
        columns = pl.ds(piece * step_width, step_width)
        target = lax.rem(head + 2, heads)

        @pl.when(inner)
        def _():
            through_copy(piece, (target, blk)).wait_recv()
            part_ref[target, :, columns] = (
                part_ref[target, :, columns].astype(jnp.float32)
                + relay_ref[:, columns].astype(jnp.float32)
            ).astype(part_ref.dtype)
            sent[piece][1].start()

    def finish(piece):
        columns = pl.ds(piece * step_width, step_width)
        for number, peer in enumerate(head_peers):
            copy = sent[piece][number]

            def add(copy=copy, peer=peer):
                copy.wait_recv()
                middle_ref[:, columns] += landed_ref[peer_origin(peer), :, columns].astype(
                    jnp.float32
                )

            if number != 1:
                pl.when(jnp.logical_not(far((peer_origin(peer), blk))))(add)
            else:
                add()

    moved = []

    def move():
        for number, peer in enumerate(blk_peers):
            place = pl.ds(pl.multiple_of(blk * matrix_rows, 16), matrix_rows)
            moved.append(
                started(
                    remote(
                        moved_ref.at[layer, peer[1]],
                        held_ref.at[place],
                        (moved_send, moved_recv),
                        number,
                        peer,
                    )
                )
            )
        place = pl.ds(pl.multiple_of(blk * matrix_rows, 16), matrix_rows)
        moved.append(
            started(
                pltpu.make_async_copy(
                    moved_ref.at[layer, blk], held_ref.at[place], side_sems.at[0]
                )
            )
        )
        for item in range(swaps):
            for number, peer in enumerate(head_peers):
                swapped.append(
                    started(
                        remote(
                            swap_refs[item].at[peer[0]],
                            swap_out_refs[item].at[head],
                            (swap_send, swap_recv),
                            item * heads + number,
                            peer,
                        )
                    )
                )
            swapped.append(
                started(
                    pltpu.make_async_copy(
                        swap_refs[item].at[head], swap_out_refs[item].at[head], side_sems.at[2]
                    )
                )
            )

    swapped = []
    lag = 2
    for step in range(pieces + lag):
        if step < pieces:
            spread(step)
        if not step:
            move()
        if 0 < step <= pieces:
            pass_on(step - 1)
        if step >= lag:
            finish(step - lag)
    middle = hidden_ref[...] + valid_ref[...] * middle_ref[...]
    inverse = lax.rsqrt(jnp.mean(middle * middle, axis=1, keepdims=True) + epsilon)
    scaled = middle * inverse
    middle_ref[...] = middle
    scaled_ref[...] = scaled
    inverse_ref[...] = jnp.broadcast_to(inverse, inverse_ref.shape)
    own_ref[...] = (scaled * gain_ref[...]).astype(own_ref.dtype)
    stages = dispatch_stages(
        heads,
        blocks,
        False,
        (
            own_ref,
            place_ref,
            None,
            None,
            shared_weight_ref,
            plane_ref,
            queue_ref,
            shared_ref,
            out_ref,
            shared_out_ref,
            send_ref,
            held_ref,
            shared_held_ref,
            head_send,
            head_recv,
            blk_send,
            blk_recv,
            local_sems,
        ),
    )
    stages[0]()
    for copy in moved:
        if hasattr(copy, "wait_recv") and copy is not moved[-1]:
            copy.wait_recv()
        else:
            copy.wait()
    saved = pltpu.make_async_copy(held_ref, matrix_ref, side_sems.at[1])
    saved.start()
    for stage in stages[1:]:
        stage()
    saved.wait()
    for copy in moved[:-1]:
        copy.wait_send()
    for copy in swapped:
        copy.wait()
    for piece, copies in enumerate(sent):
        for number, copy in enumerate(copies):
            if number != 1:
                distant = far(head_peers[number])
                pl.when(jnp.logical_not(distant))(copy.wait_send)
                pl.when(distant)(through_copy(piece, head_peers[number]).wait_send)
            else:
                copy.wait_send()


def enter(attended, out_weight, hidden, valid, gain, places, moved, layer, shared_weight, swaps):
    heads, blocks = lax.axis_size("head"), lax.axis_size("blk")
    count, width = hidden.shape
    matrix = jax.ShapeDtypeStruct((blocks * moved.shape[2], moved.shape[3]), moved.dtype)
    rows = jax.ShapeDtypeStruct((count, width), jnp.bfloat16)
    _, _, outs, _, scratch = dispatch_plan(rows, places, None, (matrix, shared_weight), False)
    vmem = pl.BlockSpec(memory_space=pltpu.VMEM)
    anywhere = pl.BlockSpec(memory_space=pl.ANY)
    pieces = COMBINE_PIECES
    return pl.pallas_call(
        functools.partial(enter_kernel, heads, blocks, layer, len(swaps)),
        out_shape=[
            jax.ShapeDtypeStruct((count, width), jnp.float32),
            jax.ShapeDtypeStruct((count, width), jnp.float32),
            jax.ShapeDtypeStruct((count, 128), jnp.float32),
            *outs,
            matrix,
            *(jax.ShapeDtypeStruct(array.shape, array.dtype) for array in swaps),
        ],
        in_specs=[vmem] * 6 + [anywhere] * (2 + len(swaps)),
        out_specs=[vmem] * (3 + len(outs)) + [anywhere] * (1 + len(swaps)),
        scratch_shapes=[
            pltpu.VMEM((count, width), jnp.bfloat16),
            pltpu.VMEM((heads, count, width), jnp.bfloat16),
            pltpu.VMEM((heads, count, width), jnp.bfloat16),
            pltpu.VMEM((count, width), jnp.bfloat16),
            pltpu.SemaphoreType.DMA((pieces * heads,)),
            pltpu.SemaphoreType.DMA((pieces * heads,)),
            pltpu.SemaphoreType.DMA((blocks,)),
            pltpu.SemaphoreType.DMA((blocks,)),
            pltpu.SemaphoreType.DMA((max(1, len(swaps)) * heads,)),
            pltpu.SemaphoreType.DMA((max(1, len(swaps)) * heads,)),
            pltpu.SemaphoreType.DMA((3,)),
            *scratch,
        ],
        compiler_params=pltpu.CompilerParams(
            collective_id=kernel_number("enter", layer, len(swaps)),
            has_side_effects=True,
            vmem_limit_bytes=60 * 1024 * 1024,
        ),
        cost_estimate=pl.CostEstimate(flops=0, bytes_accessed=270 << 20, transcendentals=0),
        name="enter",
    )(attended, out_weight, hidden, valid, gain, places, moved, shared_weight, *swaps)


def turn_heads(values, cosine, sine):
    lane = lax.broadcasted_iota(jnp.int32, values.shape, 1) % HEAD_SIZE
    half = HEAD_SIZE // 2
    width = values.shape[1]
    swapped = jnp.where(
        lane < half, pltpu.roll(values, width - half, 1), pltpu.roll(values, half, 1)
    )
    return values * cosine + swapped * sine


def project_kernel(
    heads,
    blocks,
    pieces,
    layer,
    greeted,
    own_ref,
    weight_ref,
    cosine_ref,
    sine_ref,
    moved_ref,
    plane_ref,
    query_ref,
    pair_ref,
    moved_out_ref,
    head_send,
    head_recv,
    pair_send,
    pair_recv,
    moved_send,
    moved_recv,
    local_sem,
):
    head, blk, head_peers, blk_peers = plane_peers(heads, blocks)
    chips = blocks // 2
    chip, core = blk // 2, lax.rem(blk, 2)
    sibling = (head, chip * 2 + 1 - core)
    rows, width = own_ref.shape
    count = rows // pieces
    slots, _, _, resident, pair_columns = pair_ref.shape
    query_columns = query_ref.shape[2]
    inner = jnp.logical_and(head > 0, head < heads - 1)
    if not greeted:
        greet(head_peers + blk_peers)

    def far(peer):
        return jnp.abs(peer[0] - head) == heads - 1

    def place(piece):
        return piece * count // resident, pl.ds(piece * count % resident, count)

    head_copies = []
    relayed = []
    for piece in range(pieces):
        part = pl.ds(piece * count, count)
        copies = []
        for number, peer in enumerate(head_peers):
            copy = remote(
                own_ref.at[part],
                plane_ref.at[head, part],
                (head_send, head_recv),
                piece * heads + number,
                peer,
            )
            copies.append(copy)
            if number != 1:
                pl.when(jnp.logical_not(far(peer)))(copy.start)
            else:
                copy.start()
        head_copies.append(copies)
    moved = []
    if layer is not None:
        moved = [
            started(
                remote(
                    moved_ref.at[layer, peer[1]],
                    moved_out_ref.at[blk],
                    (moved_send, moved_recv),
                    number,
                    peer,
                )
            )
            for number, peer in enumerate(blk_peers)
        ]
        local = pltpu.make_async_copy(moved_ref.at[layer, blk], moved_out_ref.at[blk], local_sem)
        local.start()
    plane_ref[head] = own_ref[...]

    def pass_on(piece):
        head_copies[piece][1].wait_recv()
        part = pl.ds(piece * count, count)
        rows_there = plane_ref.at[lax.rem(head + 2, heads), part]
        copy = remote(
            rows_there,
            rows_there,
            (head_send, head_recv),
            piece * heads + heads - 1,
            ((head - 1) * (heads - 1), blk),
            piece * heads + jnp.where(head == 1, 0, heads - 2),
        )
        relayed.append(copy)
        pl.when(inner)(copy.start)

    pair_copies = []
    forwards = []

    def forward(piece):
        slot, part = place(piece)
        for step in range(1, chips):
            pair_copies[piece][step - 1].wait_recv()
            origin = lax.rem(chip + chips - step, chips) * 2 + core
            there = pair_ref.at[slot, :, origin, part]
            forwards.append(
                started(
                    remote(
                        there,
                        there,
                        (pair_send, pair_recv),
                        piece * blocks + chips - 1 + step,
                        sibling,
                    )
                )
            )

    tile = 2 * HEAD_SIZE
    for piece in range(pieces):
        for later in range(piece + 1 if piece else 0, min(piece + 2, pieces)):
            pass_on(later)
        for number in range(heads - 1):
            if number != 1:
                head_copies[piece][number].wait_recv()
        part = pl.ds(piece * count, count)
        slot, inside = place(piece)
        projected = jnp.dot(
            plane_ref[:, part, :].reshape(heads * count, width),
            weight_ref[:, : query_columns + pair_columns],
            preferred_element_type=jnp.float32,
        )
        cosine = cosine_ref[:, part, :].reshape(heads * count, tile)
        sine = sine_ref[:, part, :].reshape(heads * count, tile)
        turned = jnp.concatenate(
            [
                turn_heads(projected[:, start : start + tile], cosine, sine)
                for start in range(0, query_columns, tile)
            ],
            axis=1,
        ).astype(query_ref.dtype)
        is_key = lax.broadcasted_iota(jnp.int32, cosine.shape, 1) < HEAD_SIZE
        key_cosine = jnp.where(is_key, cosine, 1.0)
        key_sine = jnp.where(is_key, sine, 0.0)
        pairs = jnp.concatenate(
            [
                turn_heads(projected[:, start : start + tile], key_cosine, key_sine)
                for start in range(query_columns, query_columns + pair_columns, tile)
            ],
            axis=1,
        ).astype(pair_ref.dtype)
        for there in range(heads):
            taken = slice(there * count, (there + 1) * count)
            query_ref[slot, pl.ds(there * resident + piece * count % resident, count), :] = turned[
                taken
            ]
            pair_ref[slot, there, blk, inside, :] = pairs[taken]
        mine = pair_ref.at[slot, :, blk, inside]
        targets = [
            (head, lax.rem(chip + step, chips) * 2 + core) for step in range(1, chips)
        ] + [sibling]
        pair_copies.append(
            [
                started(
                    remote(mine, mine, (pair_send, pair_recv), piece * blocks + number, peer)
                )
                for number, peer in enumerate(targets)
            ]
        )
        if piece:
            forward(piece - 1)
    forward(pieces - 1)
    for copies in pair_copies:
        for copy in copies[:-1]:
            copy.wait_send()
        copies[-1].wait()
    for copy in forwards:
        copy.wait()
    for copies in head_copies:
        for number, copy in enumerate(copies):
            if number != 1:
                pl.when(jnp.logical_not(far(head_peers[number])))(copy.wait_send)
            else:
                copy.wait_send()
    for copy in relayed:
        pl.when(inner)(copy.wait_send)
    for copy in moved:
        copy.wait()
    if moved:
        local.wait()


PROJECT_PIECES = 4


def project_plan(count, width, moved, layer, query_columns, pair_columns, resident):
    heads, blocks = lax.axis_size("head"), lax.axis_size("blk")
    pieces = PROJECT_PIECES
    slots = count // resident
    moves = [] if layer is None else [moved]
    vmem = pl.BlockSpec(memory_space=pltpu.VMEM)
    anywhere = pl.BlockSpec(memory_space=pl.ANY)
    return (
        [
            jax.ShapeDtypeStruct((heads, count, width), jnp.bfloat16),
            jax.ShapeDtypeStruct(
                (slots, heads * resident, query_columns), jnp.bfloat16
            ),
            jax.ShapeDtypeStruct((slots, heads, blocks, resident, pair_columns), jnp.bfloat16),
            *(jax.ShapeDtypeStruct((blocks,) + array.shape[2:], array.dtype) for array in moves),
        ],
        [vmem] * 3 + [anywhere] * len(moves),
        [
            pltpu.SemaphoreType.DMA((pieces * heads,)),
            pltpu.SemaphoreType.DMA((pieces * heads,)),
            pltpu.SemaphoreType.DMA((pieces * blocks,)),
            pltpu.SemaphoreType.DMA((pieces * blocks,)),
            pltpu.SemaphoreType.DMA((blocks,)),
            pltpu.SemaphoreType.DMA((blocks,)),
            pltpu.SemaphoreType.DMA,
        ],
    )


def project(rows, weight, cosine, sine, moved, layer, query_columns, pair_columns, resident):
    heads, blocks = lax.axis_size("head"), lax.axis_size("blk")
    outs, out_specs, scratch = project_plan(
        *rows.shape, moved, layer, query_columns, pair_columns, resident
    )
    moves = [] if layer is None else [moved]
    vmem = pl.BlockSpec(memory_space=pltpu.VMEM)
    anywhere = pl.BlockSpec(memory_space=pl.ANY)
    return pl.pallas_call(
        functools.partial(project_kernel, heads, blocks, PROJECT_PIECES, layer, False),
        out_shape=outs,
        in_specs=[vmem] * 4 + [anywhere] * len(moves),
        out_specs=out_specs,
        scratch_shapes=scratch,
        compiler_params=pltpu.CompilerParams(
            collective_id=kernel_number("project", layer),
            has_side_effects=True,
            vmem_limit_bytes=56 * 1024 * 1024,
        ),
        cost_estimate=pl.CostEstimate(flops=0, bytes_accessed=130 << 20, transcendentals=0),
        name="project",
    )(rows, weight, cosine, sine, *moves)


def cross(plan, middle, valid, gain, weight, cosine, sine, moved, layer, *sizes):
    heads, blocks = lax.axis_size("head"), lax.axis_size("blk")
    key, maker, arrays, specs, outs, out_specs, scratch, scaled_rows = plan
    count, width = middle.shape
    more_outs, more_specs, more_scratch = project_plan(
        count, width, moved, layer, *sizes
    )
    inputs, results, temps = len(arrays), len(outs), len(scratch)
    vmem = pl.BlockSpec(memory_space=pltpu.VMEM)
    anywhere = pl.BlockSpec(memory_space=pl.ANY)
    norm_outs = [
        jax.ShapeDtypeStruct((count, width), jnp.float32),
        jax.ShapeDtypeStruct((count, width), jnp.float32),
        jax.ShapeDtypeStruct((count, 128), jnp.float32),
    ]

    def kernel(*refs):
        _, _, head_peers, blk_peers = plane_peers(heads, blocks)
        greet(head_peers + blk_peers)
        given, refs = list(refs[:inputs]), refs[inputs:]
        middle_ref, valid_ref, gain_ref, weight_ref, cosine_ref, sine_ref, *refs = refs
        moved_ref, *refs = refs
        given += refs[:results]
        sum_ref, refs = refs[0], refs[results:]
        hidden_ref, scaled_ref, inverse_ref, *refs = refs
        made, refs = refs[: len(more_outs)], refs[len(more_outs) :]
        given += refs[:temps]
        own_ref, *rest = refs[temps:]
        if not scaled_rows:
            given.insert(3, None)
        for stage in maker(given):
            stage()
        hidden = middle_ref[...] + valid_ref[...] * sum_ref[...]
        inverse = lax.rsqrt(jnp.mean(hidden * hidden, axis=1, keepdims=True) + epsilon)
        scaled = hidden * inverse
        hidden_ref[...] = hidden
        scaled_ref[...] = scaled
        inverse_ref[...] = jnp.broadcast_to(inverse, inverse_ref.shape)
        own_ref[...] = (scaled * gain_ref[...]).astype(own_ref.dtype)
        project_kernel(
            heads,
            blocks,
            PROJECT_PIECES,
            layer,
            True,
            own_ref,
            weight_ref,
            cosine_ref,
            sine_ref,
            moved_ref,
            *made,
            *rest,
        )

    values = pl.pallas_call(
        kernel,
        out_shape=[*outs, *norm_outs, *more_outs],
        in_specs=[*specs, *([vmem] * 6), anywhere],
        out_specs=[*out_specs, *([vmem] * 3), *more_specs],
        scratch_shapes=[*scratch, pltpu.VMEM((count, width), jnp.bfloat16), *more_scratch],
        compiler_params=pltpu.CompilerParams(
            collective_id=kernel_number("cross", key, layer),
            has_side_effects=True,
            vmem_limit_bytes=60 * 1024 * 1024,
        ),
        cost_estimate=pl.CostEstimate(flops=0, bytes_accessed=290 << 20, transcendentals=0),
        name="cross",
    )(*arrays, middle, valid, gain, weight, cosine, sine, moved)
    return values[:results], values[results : results + 3], values[results + 3 :]


def unproject_kernel(
    heads,
    blocks,
    pieces,
    items,
    grad_query_ref,
    grad_pair_ref,
    weight_ref,
    cosine_ref,
    sine_ref,
    *refs,
):
    moved_refs = refs[:items]
    grad_ref, out_ref = refs[items : items + 2]
    moved_out_refs = refs[items + 2 : 2 * items + 2]
    (
        near_ref,
        sum_ref,
        far_ref,
        product_ref,
        part_ref,
        landed_ref,
        relay_ref,
        near_send,
        near_recv,
        chip_send,
        chip_recv,
        head_send,
        head_recv,
        moved_send,
        moved_recv,
        local_sems,
    ) = refs[2 * items + 2 :]
    head, blk, head_peers, blk_peers = plane_peers(heads, blocks)
    chips = blocks // 2
    chip, core = blk // 2, lax.rem(blk, 2)
    sibling = (head, chip * 2 + 1 - core)
    rows, width = out_ref.shape
    count = rows // pieces
    resident, pair_columns = grad_pair_ref.shape[4:]
    query_columns = grad_query_ref.shape[2]
    inner = jnp.logical_and(head > 0, head < heads - 1)
    chip_peers = [(head, lax.rem(chip + step, chips) * 2 + core) for step in range(1, chips)]
    greet(head_peers + blk_peers)

    def far(peer):
        return jnp.abs(peer[0] - head) == heads - 1

    def peer_origin(peer):
        return lax.rem(2 * head + heads - peer[0], heads)

    def place(piece):
        return piece * count // resident, pl.ds(piece * count % resident, count)

    near_copies = []
    for piece in range(pieces):
        slot, inside = place(piece)
        near_copies.append(
            started(
                remote(
                    grad_pair_ref.at[slot, :, :, 1 - core, inside],
                    near_ref.at[piece],
                    (near_send, near_recv),
                    piece,
                    sibling,
                )
            )
        )
    chip_copies = []
    head_copies = []
    moved = []

    def add_cores(piece):
        slot, inside = place(piece)
        near_copies[piece].wait_recv()
        sum_ref[piece] = (
            grad_pair_ref[slot, :, :, core, inside, :].astype(jnp.float32)
            + near_ref[piece].astype(jnp.float32)
        ).astype(sum_ref.dtype)
        chip_copies.append(
            [
                started(
                    remote(
                        sum_ref.at[piece, :, peer[1] // 2],
                        far_ref.at[piece, chip],
                        (chip_send, chip_recv),
                        piece * chips + number,
                        peer,
                    )
                )
                for number, peer in enumerate(chip_peers)
            ]
        )

    def through_copy(piece, peer):
        part = pl.ds(piece * count, count)
        return remote(
            part_ref.at[peer[0], part],
            relay_ref.at[part],
            (head_send, head_recv),
            piece * heads + heads - 1,
            (jnp.where(head == 0, 1, heads - 2), blk),
        )

    tile = 2 * HEAD_SIZE

    def multiply(piece):
        slot, inside = place(piece)
        part = pl.ds(piece * count, count)
        for copy in chip_copies[piece]:
            copy.wait_recv()
        pairs = sum_ref[piece, :, chip].astype(jnp.float32)
        for peer in chip_peers:
            pairs = pairs + far_ref[piece, peer[1] // 2].astype(jnp.float32)
        pairs = pairs.reshape(heads * count, pair_columns)
        pairs = pairs.astype(jnp.bfloat16).astype(jnp.float32)
        queries = jnp.concatenate(
            [
                grad_query_ref[
                    slot, pl.ds(there * resident + piece * count % resident, count), :
                ]
                for there in range(heads)
            ],
            axis=0,
        ).astype(jnp.float32)
        cosine = cosine_ref[:, part, :].reshape(heads * count, tile)
        sine = -sine_ref[:, part, :].reshape(heads * count, tile)
        is_key = lax.broadcasted_iota(jnp.int32, cosine.shape, 1) < HEAD_SIZE
        key_cosine = jnp.where(is_key, cosine, 1.0)
        key_sine = jnp.where(is_key, sine, 0.0)
        turned = jnp.concatenate(
            [
                turn_heads(queries[:, start : start + tile], cosine, sine)
                for start in range(0, query_columns, tile)
            ]
            + [
                turn_heads(pairs[:, start : start + tile], key_cosine, key_sine)
                for start in range(0, pair_columns, tile)
            ],
            axis=1,
        ).astype(grad_ref.dtype)
        grad_ref[:, part, :] = turned.reshape(heads, count, query_columns + pair_columns)
        weight = weight_ref[:, : query_columns + pair_columns]
        product_ref[...] = dot_last(turned, weight).reshape(heads, count, width)
        sent = []
        for number, peer in enumerate(head_peers):
            part_ref[peer[0], part, :] = product_ref[peer[0]].astype(part_ref.dtype)
            copy = remote(
                part_ref.at[peer[0], part],
                landed_ref.at[head, part],
                (head_send, head_recv),
                piece * heads + number,
                peer,
            )
            sent.append(copy)
            if number == 1:
                pl.when(jnp.logical_not(inner))(copy.start)
            else:
                distant = far(peer)
                pl.when(jnp.logical_not(distant))(copy.start)
                pl.when(distant)(through_copy(piece, peer).start)
        head_copies.append(sent)
        out_ref[part, :] = product_ref[head]

    def pass_on(piece):
        part = pl.ds(piece * count, count)
        target = lax.rem(head + 2, heads)

        @pl.when(inner)
        def _():
            through_copy(piece, (target, blk)).wait_recv()
            part_ref[target, part, :] = (
                part_ref[target, part, :].astype(jnp.float32)
                + relay_ref[part, :].astype(jnp.float32)
            ).astype(part_ref.dtype)
            head_copies[piece][1].start()

    def finish(piece):
        part = pl.ds(piece * count, count)
        for number, peer in enumerate(head_peers):
            copy = head_copies[piece][number]

            def add(copy=copy, peer=peer):
                copy.wait_recv()
                out_ref[part, :] += landed_ref[peer_origin(peer), part, :].astype(jnp.float32)

            if number != 1:
                pl.when(jnp.logical_not(far((peer_origin(peer), blk))))(add)
            else:
                add()

    for step in range(pieces + 3):
        if step < pieces:
            add_cores(step)
        if step == pieces - 1:
            for item in range(items):
                source, target = moved_refs[item], moved_out_refs[item]
                moved += [
                    started(
                        remote(
                            source.at[peer[1]],
                            target.at[blk],
                            (moved_send, moved_recv),
                            item * blocks + number,
                            peer,
                        )
                    )
                    for number, peer in enumerate(blk_peers)
                ]
                local = pltpu.make_async_copy(
                    source.at[blk], target.at[blk], local_sems.at[item]
                )
                moved.append(started(local))
        if 0 < step <= pieces:
            multiply(step - 1)
        if 1 < step <= pieces + 1:
            pass_on(step - 2)
        if step > 2:
            finish(step - 3)
    for copy in near_copies:
        copy.wait_send()
    for copies in chip_copies:
        for copy in copies:
            copy.wait_send()
    for piece, copies in enumerate(head_copies):
        for number, copy in enumerate(copies):
            if number != 1:
                distant = far(head_peers[number])
                pl.when(jnp.logical_not(distant))(copy.wait_send)
                pl.when(distant)(through_copy(piece, head_peers[number]).wait_send)
            else:
                copy.wait_send()
    for copy in moved:
        copy.wait()


UNPROJECT_PIECES = 4


def unproject_plan(grad_queries, grad_pairs, weight, moved):
    heads, blocks = lax.axis_size("head"), lax.axis_size("blk")
    chips = blocks // 2
    pieces = UNPROJECT_PIECES
    slots, _, _, _, resident, pair_columns = grad_pairs.shape
    rows = slots * resident
    count = rows // pieces
    width = weight.shape[0]
    items = len(moved)
    vmem = pl.BlockSpec(memory_space=pltpu.VMEM)
    anywhere = pl.BlockSpec(memory_space=pl.ANY)
    return (
        [
            jax.ShapeDtypeStruct(
                (heads, rows, grad_queries.shape[2] + pair_columns), jnp.bfloat16
            ),
            jax.ShapeDtypeStruct((rows, width), jnp.float32),
            *(jax.ShapeDtypeStruct(array.shape, array.dtype) for array in moved),
        ],
        [vmem] * 2 + [anywhere] * items,
        [
            pltpu.VMEM((pieces, heads, chips, count, pair_columns), jnp.bfloat16),
            pltpu.VMEM((pieces, heads, chips, count, pair_columns), jnp.bfloat16),
            pltpu.VMEM((pieces, chips, heads, count, pair_columns), jnp.bfloat16),
            pltpu.VMEM((heads, count, width), jnp.float32),
            pltpu.VMEM((heads, rows, width), jnp.bfloat16),
            pltpu.VMEM((heads, rows, width), jnp.bfloat16),
            pltpu.VMEM((rows, width), jnp.bfloat16),
            pltpu.SemaphoreType.DMA((pieces,)),
            pltpu.SemaphoreType.DMA((pieces,)),
            pltpu.SemaphoreType.DMA((pieces * chips,)),
            pltpu.SemaphoreType.DMA((pieces * chips,)),
            pltpu.SemaphoreType.DMA((pieces * heads,)),
            pltpu.SemaphoreType.DMA((pieces * heads,)),
            pltpu.SemaphoreType.DMA((items * blocks,)),
            pltpu.SemaphoreType.DMA((items * blocks,)),
            pltpu.SemaphoreType.DMA((items,)),
        ],
    )


def unproject(grad_queries, grad_pairs, weight, cosine, sine, moved, after, onward=None):
    heads, blocks = lax.axis_size("head"), lax.axis_size("blk")
    outs, out_specs, scratch = unproject_plan(grad_queries, grad_pairs, weight, moved)
    results, temps = len(outs), len(scratch)
    items = len(moved)
    vmem = pl.BlockSpec(memory_space=pltpu.VMEM)
    anywhere = pl.BlockSpec(memory_space=pl.ANY)
    norm_arrays, arrays, specs, more_outs, more_specs, more_scratch = [], [], [], [], [], []
    if onward is not None:
        *norm_arrays, (places, scale, matrices) = onward
        rows, width = norm_arrays[0].shape
        arrays, specs, more_outs, more_specs, more_scratch = dispatch_plan(
            jax.ShapeDtypeStruct((rows, width), jnp.bfloat16), places, scale, matrices, True
        )
        arrays, specs = arrays[1:], specs[1:]
        more_outs = [
            jax.ShapeDtypeStruct((rows, width), jnp.float32),
            jax.ShapeDtypeStruct((1, width), jnp.float32),
            *more_outs,
        ]
        more_specs = [vmem, vmem, *more_specs]
        more_scratch = [pltpu.VMEM((rows, width), jnp.bfloat16), *more_scratch]

    def kernel(*refs):
        given, refs = refs[: 5 + items], refs[5 + items + len(after) :]
        norm_refs, refs = refs[: len(norm_arrays)], refs[len(norm_arrays) :]
        dispatch_refs, refs = list(refs[: len(arrays)]), refs[len(arrays) :]
        made, refs = refs[:results], refs[results:]
        more, refs = refs[: len(more_outs)], refs[len(more_outs) :]
        unproject_kernel(heads, blocks, UNPROJECT_PIECES, items, *given, *made, *refs[:temps])
        if onward is None:
            return
        refs = refs[temps:]
        other_ref, valid_ref, gain_ref, scaled_ref, inverse_ref = norm_refs
        hidden_ref, grad_gain_ref, *more = more
        own_ref, *rest = refs
        grad = made[1][...]
        scaled = scaled_ref[...]
        grad_gain_ref[...] = jnp.sum(grad * scaled, axis=0, keepdims=True)
        grad = grad * gain_ref[...]
        grad = inverse_ref[:, :1] * (
            grad - scaled * jnp.mean(grad * scaled, axis=1, keepdims=True)
        )
        hidden = other_ref[...] + grad
        hidden_ref[...] = hidden
        own_ref[...] = (valid_ref[...] * hidden).astype(own_ref.dtype)
        for stage in dispatch_stages(
            heads, blocks, True, (own_ref, *dispatch_refs, *more, *rest)
        ):
            stage()

    values = pl.pallas_call(
        kernel,
        out_shape=[*outs, *more_outs],
        in_specs=[vmem] * 5
        + [anywhere] * (items + len(after))
        + [vmem] * len(norm_arrays)
        + specs,
        out_specs=[*out_specs, *more_specs],
        scratch_shapes=[*scratch, *more_scratch],
        compiler_params=pltpu.CompilerParams(
            collective_id=kernel_number(
                "unproject", onward is None, *(array.shape for array in (*moved, *after))
            ),
            has_side_effects=True,
            vmem_limit_bytes=60 * 1024 * 1024,
        ),
        cost_estimate=pl.CostEstimate(
            flops=0, bytes_accessed=(150 if onward is None else 320) << 20, transcendentals=0
        ),
        name="unproject",
    )(grad_queries, grad_pairs, weight, cosine, sine, *moved, *after, *norm_arrays, *arrays)
    return values[:results], values[results:]


def combine_stages(heads, blocks, by_columns, backward, refs):
    units_ref, shared_units_ref, place_ref, scale_ref, weight_ref, shared_weight_ref, *refs = refs
    if backward:
        gate_up_ref, grad_units_ref = units_ref, refs[0]
        sources, refs = refs[1:6], refs[6:]
    out_ref, returned_ref, *refs = refs
    if backward:
        grad_in_ref, grad_down_ref, gates_ref, *refs = refs
        units_ref, dots_ref, gate_part_ref, *held = refs[-10:]
        queue_ref, inner_ref, made_grad_ref, plane_ref, came_ref, late_sems, _ = held
        refs = refs[:-10]
    (
        made_ref,
        part_ref,
        landed_ref,
        relay_ref,
        held_ref,
        shared_held_ref,
        head_send,
        head_recv,
        blk_send,
        blk_recv,
        local_sems,
    ) = refs
    pieces = COMBINE_PIECES
    head, blk, head_peers, blk_peers = plane_peers(heads, blocks)
    rows, width = out_ref.shape
    slot = returned_ref.shape[1]
    shared = shared_units_ref.shape[0]
    step_width = width // pieces
    relay = heads == 4
    inner = jnp.logical_and(head > 0, head < heads - 1)
    loads = [
        pltpu.make_async_copy(weight_ref, held_ref, local_sems.at[0]),
        pltpu.make_async_copy(shared_weight_ref, shared_held_ref, local_sems.at[1]),
    ]
    gate_copies = []
    head_copies = []
    blk_copies = []
    late = []
    if backward:
        late = [
            pltpu.make_async_copy(source, target, late_sems.at[number])
            for number, (source, target) in enumerate(
                zip(sources, (queue_ref, inner_ref, made_grad_ref, plane_ref, came_ref))
            )
        ]

    def begin():
        for load in loads + late:
            load.start()
        if backward:
            half = grad_units_ref.shape[1]

            def turn(block, carry):
                rows_here = pl.ds(pl.multiple_of(block * slot, 16), slot)
                gate = gate_up_ref[rows_here, pl.ds(0, half)]
                up = gate_up_ref[rows_here, pl.ds(half, half)]
                grad = grad_units_ref[rows_here, :]
                share = 1.0 / (1.0 + jnp.exp(-gate))
                units_ref[rows_here, pl.ds(0, half)] = (
                    grad * up * share * (1.0 + gate * (1.0 - share))
                ).astype(units_ref.dtype)
                units_ref[rows_here, pl.ds(half, half)] = (grad * gate * share).astype(
                    units_ref.dtype
                )
                return carry

            lax.fori_loop(0, blocks, turn, 0)
        for load in loads:
            load.wait()

    def fill(number):
        if number == 1:
            for load in late:
                load.wait()
        piece = number - 1
        columns = pl.ds(piece * step_width, step_width)
        if 0 <= piece < pieces:
            grad_in_ref[columns, :] = dot_first(queue_ref[:, columns], units_ref[...]).astype(
                grad_in_ref.dtype
            )
            dots = dot_last(plane_ref[:, columns], came_ref[:, columns])
            if piece:
                dots = dots + dots_ref[...]
            dots_ref[...] = dots
        tile = 128
        if 0 <= piece < inner_ref.shape[1] // tile:
            lanes = pl.ds(piece * tile, tile)
            grad_down_ref[lanes, :] = dot_first(inner_ref[:, lanes], made_grad_ref[...]).astype(
                grad_down_ref.dtype
            )
        if piece == pieces:
            count = dots_ref.shape[1]
            shape = (gate_part_ref.shape[0], count)
            spread = jnp.where(
                lax.broadcasted_iota(jnp.int32, shape, 1) // slot
                == lax.broadcasted_iota(jnp.int32, shape, 0),
                1.0,
                0.0,
            ).astype(jnp.bfloat16)
            dots = dots_ref[...].astype(jnp.bfloat16) * place_ref[...]
            gate_part_ref[...] = dot_last(spread, dots)
            gates_ref[head] = gate_part_ref[...]
            gate_copies.extend(
                started(
                    remote(
                        gate_part_ref,
                        gates_ref.at[head],
                        (head_send, head_recv),
                        pieces * heads + index,
                        peer,
                    )
                )
                for index, peer in enumerate(head_peers)
            )

    def produce(piece):
        columns = pl.ds(piece * step_width, step_width)

        def make(block, carry):
            start = pl.multiple_of(block * slot, 16)
            made_ref[block, :, columns] = meet(
                units_ref[pl.ds(start, slot), :],
                weight_part(held_ref, columns, not by_columns),
                by_columns,
            ).astype(made_ref.dtype)
            return carry

        lax.fori_loop(0, blocks, make, 0)
        blk_copies.append(
            [
                started(
                    remote(
                        made_ref.at[peer[1], :, columns],
                        returned_ref.at[blk, :, columns],
                        (blk_send, blk_recv),
                        piece * (blocks - 1) + number,
                        peer,
                    )
                )
                for number, peer in enumerate(blk_peers)
            ]
        )
        returned_ref[blk, :, columns] = made_ref[blk, :, columns]
        for expert in range(shared):
            returned_ref[blocks + expert, :, columns] = meet(
                shared_units_ref[expert],
                weight_part(shared_held_ref.at[expert], columns, not by_columns),
                by_columns,
            ).astype(returned_ref.dtype)

    def far(peer):
        return jnp.abs(peer[0] - head) == heads - 1

    def peer_origin(peer):
        return lax.rem(2 * head + heads - peer[0], heads)

    def through_copy(piece, peer):
        columns = pl.ds(piece * step_width, step_width)
        return remote(
            part_ref.at[peer[0], :, columns],
            relay_ref.at[:, columns],
            (head_send, head_recv),
            piece * heads + heads - 1,
            (jnp.where(head == 0, 1, heads - 2), blk),
        )

    def gather(piece):
        columns = pl.ds(piece * step_width, step_width)
        for copy in blk_copies[piece]:
            copy.wait_recv()
        returned = returned_ref[:, :, columns].reshape((blocks + shared) * slot, step_width)
        if scale_ref is not None:
            returned = (returned.astype(jnp.float32) * scale_ref[...]).astype(returned_ref.dtype)

        def part(owner):
            start = pl.multiple_of(owner * rows, 16)
            return jnp.dot(
                place_ref[pl.ds(start, rows), :], returned, preferred_element_type=jnp.float32
            )

        sent = []
        for number, peer in enumerate(head_peers):
            part_ref[peer[0], :, columns] = part(peer[0]).astype(part_ref.dtype)
            copy = remote(
                part_ref.at[peer[0], :, columns],
                landed_ref.at[head, :, columns],
                (head_send, head_recv),
                piece * heads + number,
                peer,
            )
            sent.append(copy)
            if not relay:
                copy.start()
            elif number == 1:
                pl.when(jnp.logical_not(inner))(copy.start)
            else:
                distant = far(peer)
                pl.when(jnp.logical_not(distant))(copy.start)
                pl.when(distant)(through_copy(piece, peer).start)
        head_copies.append(sent)
        out_ref[:, columns] = part(head)

    def pass_on(piece):
        columns = pl.ds(piece * step_width, step_width)
        target = lax.rem(head + 2, heads)

        @pl.when(inner)
        def _():
            through_copy(piece, (target, blk)).wait_recv()
            part_ref[target, :, columns] = (
                part_ref[target, :, columns].astype(jnp.float32)
                + relay_ref[:, columns].astype(jnp.float32)
            ).astype(part_ref.dtype)
            head_copies[piece][1].start()

    def finish(piece):
        columns = pl.ds(piece * step_width, step_width)
        for number, peer in enumerate(head_peers):
            copy = head_copies[piece][number]

            def add(copy=copy, peer=peer):
                copy.wait_recv()
                out_ref[:, columns] += landed_ref[peer_origin(peer), :, columns].astype(
                    jnp.float32
                )

            if relay and number != 1:
                pl.when(jnp.logical_not(far((peer_origin(peer), blk))))(add)
            else:
                add()

    lag = 3 if relay else 2

    def step(number):
        if number < pieces:
            produce(number)
        if backward:
            fill(number)
        if 0 < number <= pieces:
            gather(number - 1)
        if relay and 1 < number <= pieces + 1:
            pass_on(number - 2)
        if number >= lag:
            finish(number - lag)

    def end():
        for piece, copies in enumerate(head_copies):
            for number, copy in enumerate(copies):
                if relay and number != 1:
                    distant = far(head_peers[number])
                    pl.when(jnp.logical_not(distant))(copy.wait_send)
                    pl.when(distant)(through_copy(piece, head_peers[number]).wait_send)
                else:
                    copy.wait_send()
        for copy in gate_copies:
            copy.wait()
        for copies in blk_copies:
            for copy in copies:
                copy.wait_send()

    steps = [functools.partial(step, number) for number in range(pieces + lag)]
    return [begin, *steps, end]


def combine_call(units, shared_units, places, scale, weights, by_columns, backward=None):
    heads, blocks = lax.axis_size("head"), lax.axis_size("blk")
    (own_weight, shared_weight) = weights
    shared, slot = shared_units.shape[:2]
    count = places.shape[0] // heads
    width = own_weight.shape[0 if by_columns else 1]
    pieces = COMBINE_PIECES
    vmem = pl.BlockSpec(memory_space=pltpu.VMEM)
    anywhere = pl.BlockSpec(memory_space=pl.ANY)
    scales = [] if scale is None else [scale]
    outs = [
        jax.ShapeDtypeStruct((count, width), jnp.float32),
        jax.ShapeDtypeStruct((blocks + shared, slot, width), jnp.bfloat16),
    ]
    scratch = [
        pltpu.VMEM((blocks, slot, width), jnp.bfloat16),
        pltpu.VMEM((heads, count, width), jnp.bfloat16),
        pltpu.VMEM((heads, count, width), jnp.bfloat16),
        pltpu.VMEM((count, width), jnp.bfloat16),
        pltpu.VMEM(own_weight.shape, jnp.bfloat16),
        pltpu.VMEM(shared_weight.shape, jnp.bfloat16),
        pltpu.SemaphoreType.DMA(((pieces + 1) * heads,)),
        pltpu.SemaphoreType.DMA(((pieces + 1) * heads,)),
        pltpu.SemaphoreType.DMA((pieces * (blocks - 1),)),
        pltpu.SemaphoreType.DMA((pieces * (blocks - 1),)),
        pltpu.SemaphoreType.DMA((2,)),
    ]
    arrays = [units, shared_units, places, *scales, own_weight, shared_weight]
    specs = [vmem] * (3 + len(scales)) + [anywhere] * 2
    if backward is not None:
        grad_units, *late = backward
        arrays += [grad_units, *late]
        specs += [vmem] + [anywhere] * len(late)
        inner = late[1].shape[1]
        gate_rows = -(-(blocks + shared) // 8) * 8
        outs += [
            jax.ShapeDtypeStruct((width, units.shape[1]), jnp.bfloat16),
            jax.ShapeDtypeStruct((inner, width), jnp.bfloat16),
            jax.ShapeDtypeStruct((heads, gate_rows, places.shape[0]), jnp.float32),
        ]
        scratch += [
            pltpu.VMEM(units.shape, jnp.bfloat16),
            pltpu.VMEM(places.shape, jnp.float32),
            pltpu.VMEM((gate_rows, places.shape[0]), jnp.float32),
            *(pltpu.VMEM(array.shape, array.dtype) for array in late),
            pltpu.SemaphoreType.DMA((len(late),)),
            pltpu.SemaphoreType.DMA,
        ]
    return (
        ("combine", by_columns, scale is not None, backward is not None),
        functools.partial(combine_stages, heads, blocks, by_columns, backward is not None),
        arrays,
        specs,
        outs,
        [vmem] * len(outs),
        scratch,
        scale is not None,
    )


def depart(plan, other, valid, gain, scaled, inverse, gates, router, after):
    heads, blocks = lax.axis_size("head"), lax.axis_size("blk")
    key, maker, arrays, specs, outs, out_specs, scratch, _ = plan
    count, width = other.shape
    matrix = outs[2]
    matrix_rows = matrix.shape[0] // blocks
    inputs, results, temps = len(arrays), len(outs), len(scratch)
    vmem = pl.BlockSpec(memory_space=pltpu.VMEM)
    anywhere = pl.BlockSpec(memory_space=pl.ANY)
    more_outs = [
        jax.ShapeDtypeStruct((count, width), jnp.float32),
        jax.ShapeDtypeStruct((1, width), jnp.float32),
        jax.ShapeDtypeStruct((heads, count, width), jnp.bfloat16),
        jax.ShapeDtypeStruct((blocks, matrix_rows, matrix.shape[1]), matrix.dtype),
    ]

    def kernel(*refs):
        head, blk, head_peers, blk_peers = plane_peers(heads, blocks)
        greet(head_peers + blk_peers)
        given, refs = list(refs[:inputs]), refs[inputs:]
        other_ref, valid_ref, gain_ref, scaled_ref, inverse_ref, gates_ref, *refs = refs
        router_ref, *refs = refs
        refs = refs[len(after) :]
        made, refs = refs[:results], refs[results:]
        total_ref, _, matrix_ref, _, came_gates_ref = made
        middle_ref, grad_gain_ref, plane_ref, moved_ref, *refs = refs
        temp, refs = refs[:temps], refs[temps:]
        own_ref, row_send, row_recv, moved_send, moved_recv, moved_sem = refs
        given.insert(3, None)
        moved = []
        for number, stage in enumerate(maker([*given, *made, *temp])):
            stage()
            if number == COMBINE_PIECES + 1:
                moved = [
                    started(
                        remote(
                            matrix_ref.at[
                                pl.ds(pl.multiple_of(peer[1] * matrix_rows, 16), matrix_rows)
                            ],
                            moved_ref.at[blk],
                            (moved_send, moved_recv),
                            index,
                            peer,
                        )
                    )
                    for index, peer in enumerate(blk_peers)
                ]
                place = pl.ds(pl.multiple_of(blk * matrix_rows, 16), matrix_rows)
                moved.append(
                    started(
                        pltpu.make_async_copy(matrix_ref.at[place], moved_ref.at[blk], moved_sem)
                    )
                )
        mine = pl.ds(pl.multiple_of(head * count, 128), count)
        grad_gates = came_gates_ref[:, :, mine].reshape(-1, count).T
        shares = gates_ref[...]
        grad_logits = shares * (
            grad_gates - jnp.sum(shares * grad_gates, axis=1, keepdims=True)
        )
        grad = total_ref[...] + dot_last(grad_logits.astype(jnp.bfloat16), router_ref[...])
        scaled = scaled_ref[...]
        grad_gain_ref[...] = jnp.sum(grad * scaled, axis=0, keepdims=True)
        grad = grad * gain_ref[...]
        grad = inverse_ref[:, :1] * (
            grad - scaled * jnp.mean(grad * scaled, axis=1, keepdims=True)
        )
        middle = other_ref[...] + grad
        middle_ref[...] = middle
        own = (valid_ref[...] * middle).astype(own_ref.dtype)
        own_ref[...] = own
        plane_ref[head] = own
        relayed_gather(heads, head, blk, head_peers, own_ref, plane_ref, (row_send, row_recv), 0)
        for copy in moved:
            copy.wait()

    values = pl.pallas_call(
        kernel,
        out_shape=[*outs, *more_outs],
        in_specs=[*specs, *([vmem] * 7), *([anywhere] * len(after))],
        out_specs=[*out_specs, *([vmem] * 3), anywhere],
        scratch_shapes=[
            *scratch,
            pltpu.VMEM((count, width), jnp.bfloat16),
            pltpu.SemaphoreType.DMA((RELAY_PIECES * heads,)),
            pltpu.SemaphoreType.DMA((RELAY_PIECES * heads,)),
            pltpu.SemaphoreType.DMA((blocks,)),
            pltpu.SemaphoreType.DMA((blocks,)),
            pltpu.SemaphoreType.DMA,
        ],
        compiler_params=pltpu.CompilerParams(
            collective_id=kernel_number("depart", key, *(array.shape for array in after)),
            has_side_effects=True,
            vmem_limit_bytes=60 * 1024 * 1024,
        ),
        cost_estimate=pl.CostEstimate(flops=0, bytes_accessed=330 << 20, transcendentals=0),
        name="depart",
    )(*arrays, other, valid, gain, scaled, inverse, gates, router, *after)
    return values[:results], values[results:]


def head_parts(partial):
    heads = lax.axis_size("head")
    return partial.astype(jnp.bfloat16).reshape(heads, -1, partial.shape[-1])


def head_sum(parts):
    return jnp.sum(parts.astype(jnp.float32), axis=0)


def dot_last(left, right):
    return lax.dot_general(
        left, right, (((1,), (1,)), ((), ())), preferred_element_type=jnp.float32
    )


def dot_first(left, right):
    return lax.dot_general(
        left, right, (((0,), (0,)), ((), ())), preferred_element_type=jnp.float32
    )


def head_columns(ref, rows, first, group, shift):
    pieces = []
    for member in range(group):
        start = (first + member) * HEAD_SIZE
        piece = ref[0, rows, start : start + HEAD_SIZE]
        empty = jnp.zeros_like(piece)
        pieces.append(jnp.concatenate([empty, piece] if shift else [piece, empty], axis=1))
    return jnp.concatenate(pieces, axis=0)


def unit_scores(queries, pairs, blk, resident, chunk):
    scores = dot_last(queries, pairs) * 0.125
    count, keys = scores.shape
    places = lax.broadcasted_iota(jnp.int32, (count, chunk), 1)
    own = blk * resident + lax.broadcasted_iota(jnp.int32, (count, chunk), 0) % resident
    last = jnp.where(places <= own, scores[:, keys - chunk :], negative)
    if keys > chunk:
        scores = jnp.concatenate([scores[:, : keys - chunk], last], axis=1)
    else:
        scores = last
    exponents = jnp.exp(scores - jnp.max(scores, axis=1, keepdims=True))
    return (exponents, jnp.sum(exponents, axis=1, keepdims=True))


def attend_kernel(heads, blocks, resident, group, kv_local, info_ref, query_ref, pair_ref, out_ref):
    slot_index = pl.program_id(0)
    blk = info_ref[0]
    length = info_ref[1 + slot_index]
    chunk = blocks * resident
    for head in range(heads):
        rows = pl.ds(head * resident, resident)
        live = head * chunk + blk * resident < length

        @pl.when(live)
        def _(head=head, rows=rows):
            keys = (head + 1) * chunk
            for kv_head in range(kv_local):
                lanes = pl.ds(kv_head * 2 * HEAD_SIZE, 2 * HEAD_SIZE)
                pairs = pair_ref[0, pl.ds(0, keys), lanes]
                queries = head_columns(query_ref, rows, kv_head * group, group, False)
                exponents, totals = unit_scores(queries, pairs, blk, resident, chunk)
                weighted = jnp.dot(
                    exponents.astype(jnp.bfloat16), pairs, preferred_element_type=jnp.float32
                )
                weighted = weighted / totals
                for member in range(group):
                    start = (kv_head * group + member) * HEAD_SIZE
                    out_ref[head, 0, :, start : start + HEAD_SIZE] = weighted[
                        member * resident : (member + 1) * resident, HEAD_SIZE:
                    ].astype(out_ref.dtype)

        @pl.when(jnp.logical_not(live))
        def _(head=head):
            out_ref[head, 0] = jnp.zeros(out_ref.shape[2:], out_ref.dtype)


def attend_back_kernel(
    heads,
    blocks,
    resident,
    group,
    kv_local,
    info_ref,
    query_ref,
    pair_ref,
    grad_ref,
    grad_query_ref,
    grad_pair_ref,
    total_ref,
):
    slot_index = pl.program_id(0)
    blk = info_ref[0]
    length = info_ref[1 + slot_index]
    chunk = blocks * resident
    total_ref[...] = jnp.zeros_like(total_ref)
    for head in range(heads):
        rows = pl.ds(head * resident, resident)
        live = head * chunk + blk * resident < length

        @pl.when(live)
        def _(head=head, rows=rows):
            keys = (head + 1) * chunk
            for kv_head in range(kv_local):
                lanes = pl.ds(kv_head * 2 * HEAD_SIZE, 2 * HEAD_SIZE)
                pairs = pair_ref[0, pl.ds(0, keys), lanes]
                queries = head_columns(query_ref, rows, kv_head * group, group, False)
                grads = head_columns(grad_ref, rows, kv_head * group, group, True)
                exponents, totals = unit_scores(queries, pairs, blk, resident, chunk)
                probabilities = exponents * (1.0 / totals)
                grad_probs = dot_last(grads, pairs)
                delta = jnp.sum(probabilities * grad_probs, axis=1, keepdims=True)
                grad_scores = (probabilities * (grad_probs - delta)).astype(jnp.bfloat16)
                grad_queries = 0.125 * jnp.dot(
                    grad_scores, pairs, preferred_element_type=jnp.float32
                )
                for member in range(group):
                    start = (kv_head * group + member) * HEAD_SIZE
                    grad_query_ref[0, rows, start : start + HEAD_SIZE] = grad_queries[
                        member * resident : (member + 1) * resident, :HEAD_SIZE
                    ].astype(grad_query_ref.dtype)
                total_ref[pl.ds(0, keys), lanes] += dot_first(
                    grad_scores, queries * jnp.bfloat16(0.125)
                ) + dot_first(probabilities.astype(jnp.bfloat16), grads)

        @pl.when(jnp.logical_not(live))
        def _(rows=rows):
            grad_query_ref[0, rows, :] = jnp.zeros(
                (resident, grad_query_ref.shape[2]), grad_query_ref.dtype
            )

    grad_pair_ref[0] = total_ref[...].astype(grad_pair_ref.dtype)


def plan_kernel(heads, experts_local, slot, info_ref, routes_ref, ranks_ref, chosen_ref, place_ref, turned_ref):
    routes = routes_ref[0]
    ranks = ranks_ref[0]
    tokens = routes.shape[1]
    count = place_ref.shape[2]
    first = info_ref[0] * experts_local
    lanes = 128
    room = -(-experts_local // 8) * 8
    named = []
    for lane in range(lanes):
        plane, expert = lane // room, lane % room
        if plane < heads and expert < experts_local:
            hit = jnp.where(routes == plane * experts_local + expert, 1, 0)
            named.append(jnp.max(hit, axis=0, keepdims=True))
        else:
            named.append(jnp.zeros((1, tokens), jnp.int32))
    chosen_ref[0] = jnp.concatenate(named, axis=0).astype(jnp.float32).T
    marks = [
        jnp.sum(
            jnp.where((routes == first + expert) & (ranks < CAP), ranks + 1, 0),
            axis=0,
            keepdims=True,
        )
        for expert in range(experts_local)
    ]
    marks.append(jnp.zeros((lanes - experts_local, tokens), jnp.int32))
    marks = jnp.concatenate(marks, axis=0).astype(jnp.float32)
    slot_rows = tokens // heads

    def fits(shape, row_axis, wide):
        row = lax.broadcasted_iota(jnp.int32, shape, row_axis)
        token = lax.broadcasted_iota(jnp.int32, shape, 1 - row_axis)
        inside = row % slot
        same = (inside // CAP == token // slot_rows) & (wide.astype(jnp.int32) == inside % CAP + 1)
        return jnp.where(same, 1.0, 0.0).astype(jnp.bfloat16)

    def spread(shape, row_axis):
        row = lax.broadcasted_iota(jnp.int32, shape, row_axis)
        expert = lax.broadcasted_iota(jnp.int32, shape, 1 - row_axis)
        return jnp.where(row // slot == expert, 1.0, 0.0).astype(jnp.bfloat16)

    place_ref[0] = fits(
        (tokens, count),
        1,
        jnp.dot(
            marks.T.astype(jnp.bfloat16),
            spread((lanes, count), 1),
            preferred_element_type=jnp.float32,
        ),
    )
    turned_ref[0] = fits(
        (count, tokens),
        0,
        jnp.dot(
            spread((count, lanes), 0),
            marks.astype(jnp.bfloat16),
            preferred_element_type=jnp.float32,
        ),
    )


def plans(heads, experts_local, slot, head_index, routes, ranks):
    layers, top, tokens = routes.shape
    count = experts_local * slot

    def spec(*shape):
        return pl.BlockSpec((1,) + shape, lambda layer, info: (layer, 0, 0))

    chosen, places, turned = pl.pallas_call(
        functools.partial(plan_kernel, heads, experts_local, slot),
        grid_spec=pltpu.PrefetchScalarGridSpec(
            num_scalar_prefetch=1,
            grid=(layers,),
            in_specs=[spec(top, tokens)] * 2,
            out_specs=[spec(tokens, 128), spec(tokens, count), spec(count, tokens)],
        ),
        out_shape=[
            jax.ShapeDtypeStruct((layers, tokens, 128), jnp.float32),
            jax.ShapeDtypeStruct((layers, tokens, count), jnp.bfloat16),
            jax.ShapeDtypeStruct((layers, count, tokens), jnp.bfloat16),
        ],
        compiler_params=pltpu.CompilerParams(vmem_limit_bytes=40 * 1024 * 1024),
        cost_estimate=pl.CostEstimate(flops=0, bytes_accessed=16 << 20, transcendentals=0),
        name="plans",
    )(head_index[None].astype(jnp.int32), routes, ranks)
    gate_lanes = heads * -(-experts_local // 8) * 8
    return chosen[0, :, :gate_lanes] > 0.0, places[0], turned[0]


def attention_call(kernel, info, arrays, outs, scratch, flops, name):
    def spec(array):
        shape = array.shape
        if len(shape) == 4:
            return pl.BlockSpec(
                (shape[0], 1) + shape[2:], lambda slot, info: (0, slot, 0, 0)
            )
        return pl.BlockSpec((1,) + shape[1:], lambda slot, info: (slot, 0, 0))

    return pl.pallas_call(
        kernel,
        grid_spec=pltpu.PrefetchScalarGridSpec(
            num_scalar_prefetch=1,
            grid=(SEQUENCE_SLOTS,),
            in_specs=[spec(array) for array in arrays],
            out_specs=[spec(array) for array in outs],
            scratch_shapes=scratch,
        ),
        out_shape=outs,
        compiler_params=pltpu.CompilerParams(vmem_limit_bytes=56 * 1024 * 1024),
        cost_estimate=pl.CostEstimate(
            flops=flops, bytes_accessed=8 << 20, transcendentals=flops // 256
        ),
        name=name,
    )(info, *arrays)


def shards(
    tokens,
    lengths,
    routes,
    queue_ranks,
    query_key_value_weight,
    w_out,
    router,
    norm_gains,
    w_in,
    w_down,
    cotangent,
):
    kernel_numbers.clear()
    heads_count = lax.axis_size("head")
    blocks_count = lax.axis_size("blk")
    head_index = lax.axis_index("head")
    blk_index = lax.axis_index("blk")
    resident = tokens.shape[1]
    width = tokens.shape[2]
    weight_rows = w_out.shape[1]
    rows_local = heads_count * resident
    keys_total = blocks_count * rows_local
    kv_local = KEY_VALUE_HEADS // heads_count
    group = QUERY_HEAD_COUNT // KEY_VALUE_HEADS
    query_columns = kv_local * group * HEAD_SIZE
    pair_columns = kv_local * 2 * HEAD_SIZE
    slot_rows = SEQUENCE_SLOTS * resident
    all_tokens = heads_count * slot_rows
    experts_local = EXPERTS // heads_count
    owned = experts_local // blocks_count
    owned_total = owned * blocks_count
    slot = -(-heads_count * CAP // 16) * 16
    half = HEAD_SIZE // 2

    own_places = (head_index * blocks_count + blk_index) * resident + jnp.arange(
        resident, dtype=jnp.int32
    )
    valid_column = (
        (own_places[None, :] < lengths[:, None]).astype(jnp.float32).reshape(slot_rows, 1)
    )
    plane_ids = jnp.arange(all_tokens, dtype=jnp.int32)
    plane_places = (
        (plane_ids // slot_rows * blocks_count + blk_index) * resident + plane_ids % resident
    ).astype(jnp.float32)
    frequency = jnp.exp(jnp.arange(half, dtype=jnp.float32) * (-2.0 * theta_log / HEAD_SIZE))
    angles = plane_places[:, None] * frequency[None, :]
    cosine = jnp.cos(angles)
    sine = jnp.sin(angles)
    repeats = 2 * HEAD_SIZE // half
    tile_cosine = jnp.concatenate([cosine] * repeats, axis=1).reshape(heads_count, slot_rows, -1)
    tile_sine = jnp.concatenate([-sine, sine] * (repeats // 2), axis=1)
    tile_sine = tile_sine.reshape(heads_count, slot_rows, -1)
    info = jnp.concatenate([blk_index[None].astype(jnp.int32), lengths])

    row_ids = jnp.arange(experts_local * slot, dtype=jnp.int32)
    spread = (
        row_ids[None, :] // slot == jnp.arange(experts_local, dtype=jnp.int32)[:, None]
    ).astype(jnp.bfloat16)
    def to_experts(rows):
        rows = rows.reshape(experts_local, slot, width)
        own = None
        if owned:
            own = rows[:owned_total].reshape(blocks_count, owned * slot, width)
            own = lax.all_to_all(own, "blk", 0, 0, tiled=True)
            own = own.reshape(blocks_count, owned, slot, width).transpose(1, 0, 2, 3)
            own = own.reshape(owned, blocks_count * slot, width)
        return (own, rows[owned_total:])

    def from_experts(own, shared):
        parts = [shared]
        if owned:
            own = own.reshape(owned, blocks_count, slot, width).transpose(1, 0, 2, 3)
            own = own.reshape(blocks_count, owned * slot, width)
            own = lax.all_to_all(own, "blk", 0, 0, tiled=True)
            parts = [own.reshape(owned_total, slot, width), shared]
        return jnp.concatenate(parts, axis=0).reshape(experts_local * slot, width)

    def shared_weights(layer_index, reached):
        if owned_total == experts_local:
            return []
        parts = tuple(matrix[layer_index, owned_total:] for matrix in (w_in, w_down))
        parts, _ = lax.optimization_barrier((parts, reached))
        return [tuple(lax.all_gather(part, "blk", axis=1, tiled=True) for part in parts)]

    def to_owner(matrix, layer_index):
        if not owned:
            return []
        if owned == 1:
            return [("blk_swap", matrix, layer_index)]
        pieces = matrix[layer_index, :owned_total]
        return [("blk_swap", pieces.reshape((blocks_count, owned) + pieces.shape[1:]))]

    def owned_matrix(received):
        if not owned:
            return None
        columns = received.shape[-1]
        pieces = received.reshape(blocks_count, owned, -1, columns)
        return pieces.transpose(1, 0, 2, 3).reshape(owned, -1, columns)

    def from_owner(term):
        if not owned:
            return []
        columns = term.shape[-1]
        pieces = term.reshape(owned, blocks_count, -1, columns).transpose(1, 0, 2, 3)
        return [("blk_swap", pieces)]

    def owned_rows(received):
        if not owned:
            return []
        return [received.reshape(owned_total, -1, received.shape[-1])]

    staged = owned == 1 and owned_total < experts_local

    def matrices(sets, which):
        own_weight, shared_weight = (mats[which] for mats in sets)
        return (own_weight[0], shared_weight)

    def unpack_in(results):
        plane, own, shared, own_out, shared_out = results
        return (
            plane.reshape(all_tokens, width),
            [own.reshape(1, -1, width), shared],
            [own_out[None], shared_out],
        )

    def unpack_out(results):
        total, returned, *extras = results
        return (total, returned.reshape(-1, width), *extras)

    def moe_in(rows, turned_places, scale, sets, which, after=()):
        if staged:
            plan = dispatch_call(rows, turned_places, scale, matrices(sets, which), which == 1)
            return unpack_in(staged_call([plan], "dispatch", 170, after)[0])
        (plane,) = exchange(("head_gather", rows))
        plane = plane.reshape(all_tokens, width)
        queues = mm("rt,td->rd", turned_places, plane)
        if scale is not None:
            queues = queues * scale
        queues = [part for part in to_experts(queues.astype(jnp.bfloat16)) if part is not None]
        spec = ("erd,edf->erf", "erd,efd->erf")[which]
        return (plane, queues, [mm(spec, rows, mats[which]) for rows, mats in zip(queues, sets)])

    def moe_out(units, places, scale, sets):
        if staged:
            plan = combine_call(
                units[0][0], units[1], places, scale, matrices(sets, 1), False
            )
            return unpack_out(staged_call([plan], "combine", 170)[0])
        made = [
            mm("erf,efd->erd", part, mats[1]).astype(jnp.bfloat16)
            for part, mats in zip(units, sets)
        ]
        returned = from_experts(*(made if owned else [None] + made))
        rows = (returned.astype(jnp.float32) * scale).astype(jnp.bfloat16)
        (parts,) = exchange(("head_swap", head_parts(mm("tr,rd->td", places, rows))))
        return (head_sum(parts), returned)

    def moe_back(
        places, sets, gate_up, grad_units, incoming, units, grad_rows, plane_grads, came, onward
    ):
        grad_gate_up = [
            gated_back(*parts) if number or not staged else None
            for number, parts in enumerate(zip(gate_up, grad_units))
        ]
        grad_weights = [
            (
                mm("erd,erf->edf", rows, grads).astype(jnp.bfloat16),
                mm("erf,erd->efd", inner, out_grads).astype(jnp.bfloat16),
            )
            if grads is not None
            else None
            for rows, grads, inner, out_grads in zip(incoming, grad_gate_up, units, grad_rows)
        ]
        if staged:
            plan = combine_call(
                gate_up[0][0],
                grad_gate_up[1],
                places,
                None,
                matrices(sets, 0),
                True,
                [grad_units[0][0], incoming[0][0], units[0][0], grad_rows[0][0], plane_grads, came],
            )
            further = []
            if fused:
                (total, _, grad_in, grad_down, gates), further = depart(
                    plan, *onward, grad_weights[1]
                )
            else:
                total, _, grad_in, grad_down, gates = staged_call([plan], "combine_back", 170)[0]
            grad_weights[0] = (grad_in[None], grad_down[None])
            gates = gates.reshape(gate_lanes, all_tokens)
            return (total, gates, grad_weights, further)
        pair_dots = (mm("td,rd->tr", plane_grads, came) * places).astype(jnp.bfloat16)
        made = [
            mm("erf,edf->erd", part, mats[0]).astype(jnp.bfloat16)
            for part, mats in zip(grad_gate_up, sets)
        ]
        returned = from_experts(*(made if owned else [None] + made))
        parts, gates = exchange(
            ("head_swap", head_parts(mm("tr,rd->td", places, returned))),
            ("head_gather", mm("tr,er->te", pair_dots, spread).T),
        )
        gates = by_plane(gates.reshape(EXPERTS, all_tokens), 0)
        return (head_sum(parts), gates, grad_weights, [])

    def moe_turn(units, places, turned_places, scale, grad_rows, sets):
        if not staged:
            return (
                moe_out(units, places, scale, sets),
                moe_in(grad_rows, turned_places, scale, sets, 1),
            )
        weights = matrices(sets, 1)
        out_plan = combine_call(units[0][0], units[1], places, scale, weights, False)
        in_plan = dispatch_call(grad_rows, turned_places, scale, weights, True)
        out_results, in_results = staged_call([out_plan, in_plan], "turn", 260)
        return (unpack_out(out_results), unpack_in(in_results))

    def gated(gate_up):
        return (jax.nn.silu(gate_up[..., :FF]) * gate_up[..., FF:]).astype(jnp.bfloat16)

    def gated_back(gate_up, grad_units):
        gate_part = gate_up[..., :FF]
        up_part = gate_up[..., FF:]
        sigmoid_part = jax.nn.sigmoid(gate_part)
        return jnp.concatenate(
            [
                grad_units * up_part * sigmoid_part * (1.0 + gate_part * (1.0 - sigmoid_part)),
                grad_units * gate_part * sigmoid_part,
            ],
            axis=-1,
        ).astype(jnp.bfloat16)

    def by_slot(rows):
        return (
            rows.reshape(heads_count, SEQUENCE_SLOTS, resident, -1)
            .transpose(1, 0, 2, 3)
            .reshape(SEQUENCE_SLOTS, rows_local, -1)
        )

    def by_head(rows):
        return (
            rows.reshape(SEQUENCE_SLOTS, heads_count, resident, -1)
            .transpose(1, 0, 2, 3)
            .reshape(all_tokens, -1)
        )

    small_columns = 128
    room = -(-experts_local // 8) * 8
    gate_lanes = heads_count * room

    def by_plane(values, axis):
        shape = values.shape
        values = values.reshape(shape[:axis] + (heads_count, experts_local) + shape[axis + 1 :])
        pads = [(0, 0)] * values.ndim
        pads[axis + 1] = (0, room - experts_local)
        return jnp.pad(values, pads).reshape(shape[:axis] + (gate_lanes,) + shape[axis + 1 :])

    send = []
    for layer_index in range(DECODER_LAYERS):
        weight = query_key_value_weight[layer_index]
        split = QUERY_HEAD_COUNT * HEAD_SIZE
        small = jnp.concatenate(
            [by_plane(router[layer_index], 1), norm_gains[layer_index].T], axis=1
        )
        small = jnp.pad(small, ((0, 0), (0, small_columns - small.shape[1])))
        send.append(
            jnp.concatenate(
                [
                    weight[:, :split]
                    .reshape(weight_rows, heads_count, query_columns)
                    .transpose(1, 0, 2),
                    weight[:, split:]
                    .reshape(weight_rows, heads_count, pair_columns)
                    .transpose(1, 0, 2),
                    jnp.broadcast_to(small[None], (heads_count,) + small.shape),
                ],
                axis=-1,
            )
        )
    plan = jnp.stack([routes, queue_ranks]).reshape(2 * DECODER_LAYERS, slot_rows, TOP)
    plan = plan.transpose(0, 2, 1).reshape(2 * DECODER_LAYERS * TOP, slot_rows)
    plan, first_send = exchange(("head_gather", plan), ("head_swap", send[0]))
    plan = plan.reshape(heads_count, 2, DECODER_LAYERS, TOP, slot_rows)
    plan = plan.transpose(1, 2, 3, 0, 4).reshape(2, DECODER_LAYERS, TOP, all_tokens)

    def attention_set(wide, out_full):
        wide = wide.transpose(1, 0, 2, 3).reshape(width, -1)
        small = wide[:, query_columns + pair_columns :]
        gains = small.T[gate_lanes : gate_lanes + 2].astype(jnp.float32)
        return (wide, out_full.reshape(-1, width), small[:, :gate_lanes], gains)

    wide, first_out, *next_sends = exchange(
        ("blk_pairs", first_send),
        ("blk_pairs", w_out[0]),
        *(("head_swap", array) for array in send[1:]),
    )
    attention_weights = [
        attention_set(wide, first_out),
    ]
    for layer_index, array in enumerate(next_sends, start=1):
        attention_weights.append(
            attention_set(
                lax.all_gather(array, "blk", axis=0),
                lax.all_gather(w_out[layer_index], "blk", axis=0),
            )
        )

    hidden = tokens.reshape(slot_rows, width).astype(jnp.float32)
    stored_all = []
    for layer_index in range(DECODER_LAYERS):
        qkv_full, out_full, router_full, gains = attention_weights[layer_index]
        layer = slice(layer_index, layer_index + 1)
        chosen, places, turned_places = plans(
            heads_count, experts_local, slot, head_index, plan[0, layer], plan[1, layer]
        )
        next_layer = layer_index + 1 < DECODER_LAYERS
        fused = staged and heads_count == 4
        if not fused or not layer_index:
            scaled_a, inverse_a = norm_rows(hidden)
            normed_a = (scaled_a * gains[:1]).astype(jnp.bfloat16)
        if fused and layer_index:
            plane_normed_a, queries, pairs_all, *own_down_next = crossed
            plane_normed_a = plane_normed_a.reshape(all_tokens, width)
        elif fused:
            plane_normed_a, queries, pairs_all, own_down = project(
                normed_a,
                qkv_full,
                tile_cosine,
                tile_sine,
                w_down,
                layer_index,
                query_columns,
                pair_columns,
                resident,
            )
            plane_normed_a = plane_normed_a.reshape(all_tokens, width)
            own_down_next = [own_down]
        else:
            plane_normed_a, *own_down_next = exchange(
                ("head_gather", normed_a), *to_owner(w_down, layer_index)
            )
            plane_normed_a = plane_normed_a.reshape(all_tokens, width)
            narrow = qkv_full[:, : query_columns + pair_columns]
            projected = mm("td,de->te", plane_normed_a, narrow)
            queries = by_slot(
                rotate(projected[:, :query_columns], cosine, sine).astype(jnp.bfloat16)
            )
            pairs = projected[:, query_columns:].reshape(all_tokens, kv_local, 2, HEAD_SIZE)
            keys = rotate(pairs[:, :, 0].reshape(all_tokens, -1), cosine, sine)
            pairs = jnp.stack(
                [keys.reshape(all_tokens, kv_local, HEAD_SIZE), pairs[:, :, 1]], axis=2
            )
            pairs = pairs.reshape(all_tokens, pair_columns).astype(jnp.bfloat16)
            (pairs,) = exchange(("blk_pairs", pairs))
            pairs_all = pairs.reshape(
                blocks_count, heads_count, SEQUENCE_SLOTS, resident, pair_columns
            ).transpose(2, 1, 0, 3, 4)
        pairs_all = pairs_all.reshape(SEQUENCE_SLOTS, keys_total, pair_columns)
        (attended,) = attention_call(
            functools.partial(
                attend_kernel, heads_count, blocks_count, resident, group, kv_local
            ),
            info,
            [queries, pairs_all],
            [
                jax.ShapeDtypeStruct(
                    (heads_count, SEQUENCE_SLOTS, resident, query_columns), jnp.bfloat16
                )
            ],
            [],
            4 * rows_local * keys_total * query_columns,
            "attend",
        )
        attended = attended.reshape(all_tokens, query_columns)
        weight_sets = shared_weights(layer_index, middle if layer_index else wide)
        swaps = []
        if fused and staged:
            middle, scaled_b, inverse_b, *results = enter(
                attended,
                out_full,
                hidden,
                valid_column,
                gains[1:],
                turned_places,
                w_in,
                layer_index,
                weight_sets[0][0],
                swaps,
            )
            inverse_b = inverse_b[:, :1]
            results, own_in = results[:5], results[5]
            plane_rows, incoming, gate_up = unpack_in(results)
            weight_sets = [(own_in[None], owned_matrix(own_down_next[0]))] + weight_sets
        else:
            branch, *others = exchange(
                ("head_swap", head_parts(mm("tf,fd->td", attended, out_full))),
                *to_owner(w_in, layer_index),
            )
            own_in_next = others
            if owned:
                weight_sets = [
                    (owned_matrix(own_in_next[0]), owned_matrix(own_down_next[0]))
                ] + weight_sets
            middle = hidden + valid_column * head_sum(branch)
            scaled_b, inverse_b = norm_rows(middle)
            normed_b = (scaled_b * gains[1:]).astype(jnp.bfloat16)
            plane_rows, incoming, gate_up = moe_in(normed_b, turned_places, None, weight_sets, 0)
        units = [gated(part) for part in gate_up]
        logits = mm("td,de->te", plane_rows, router_full)
        peaks = jnp.max(jnp.where(chosen, logits, negative), axis=-1, keepdims=True)
        lifted = jnp.where(chosen, jnp.exp(logits - peaks), 0.0)
        gates_all = lifted / jnp.sum(lifted, axis=-1, keepdims=True)
        plane_gates = lax.dynamic_slice_in_dim(
            gates_all, head_index * room, experts_local, 1
        )
        row_gates = mm("rt,te->re", turned_places, plane_gates.astype(jnp.bfloat16))
        row_gates = jnp.sum(row_gates * spread.T.astype(jnp.float32), axis=1, keepdims=True)
        if next_layer and fused:
            next_weights = attention_weights[layer_index + 1]
            (_, returned), norms, crossed = cross(
                combine_call(
                    units[0][0], units[1], places, row_gates, matrices(weight_sets, 1), False
                ),
                middle,
                valid_column,
                next_weights[3][:1],
                next_weights[0],
                tile_cosine,
                tile_sine,
                w_down,
                layer_index + 1,
                query_columns,
                pair_columns,
                resident,
            )
            returned = returned.reshape(-1, width)
        elif next_layer:
            mixture, returned = moe_out(units, places, row_gates, weight_sets)
        else:
            (mixture, returned), turned = moe_turn(
                units,
                places,
                turned_places,
                row_gates,
                (valid_column * cotangent.reshape(slot_rows, width)).astype(jnp.bfloat16),
                weight_sets,
            )
        stored_all.append(
            (
                weight_sets,
                places,
                scaled_a,
                inverse_a,
                plane_normed_a,
                queries,
                pairs_all,
                attended,
                scaled_b,
                inverse_b,
                plane_rows,
                gates_all,
                turned_places,
                row_gates,
                incoming,
                gate_up,
                units,
                returned,
            )
        )
        if next_layer and fused:
            hidden, scaled_a, inverse_a = norms
            inverse_a = inverse_a[:, :1]
        else:
            hidden = middle + valid_column * mixture
    result = (valid_column * hidden).astype(jnp.bfloat16).reshape(tokens.shape)
    grad_hidden = valid_column * cotangent.reshape(slot_rows, width).astype(jnp.float32)
    qkv_list = [None] * DECODER_LAYERS
    out_list = [None] * DECODER_LAYERS
    router_list = [None] * DECODER_LAYERS
    gains_list = [None] * DECODER_LAYERS
    expert_list = [None] * DECODER_LAYERS
    pending = []
    waiting = []
    for layer_index in reversed(range(DECODER_LAYERS)):
        qkv_full, out_full, router_full, gains = attention_weights[layer_index]
        (
            weight_sets,
            places,
            scaled_a,
            inverse_a,
            plane_normed_a,
            queries,
            pairs_all,
            attended,
            scaled_b,
            inverse_b,
            plane_rows,
            gates_all,
            turned_places,
            row_gates,
            incoming,
            gate_up,
            units,
            returned,
        ) = stored_all[layer_index]
        if layer_index + 1 < DECODER_LAYERS and not fused:
            turned = moe_in(
                (valid_column * grad_hidden).astype(jnp.bfloat16),
                turned_places,
                row_gates,
                weight_sets,
                1,
                waiting,
            )
        plane_grads, grad_produced, grad_units = turned
        onward = (
            grad_hidden,
            valid_column,
            gains[1:],
            scaled_b,
            jnp.broadcast_to(inverse_b, (slot_rows, 128)),
            lax.dynamic_slice_in_dim(gates_all, head_index * slot_rows, slot_rows, 0),
            router_full,
        )
        grad_normed_b, grad_gates, grad_weight_sets, departed = moe_back(
            places,
            weight_sets,
            gate_up,
            grad_units,
            incoming,
            units,
            grad_produced,
            plane_grads,
            returned,
            onward,
        )
        grad_gates = grad_gates.T
        grad_logits = gates_all * (
            grad_gates - jnp.sum(gates_all * grad_gates, axis=-1, keepdims=True)
        )
        plane_width = width // heads_count
        grad_router = mm(
            "td,te->de",
            lax.dynamic_slice_in_dim(plane_rows, head_index * plane_width, plane_width, 1),
            grad_logits.astype(jnp.bfloat16),
        )
        if fused:
            grad_middle, grad_gain_b, plane_branch, *own_grad_in = departed
            grad_gain_b = grad_gain_b[0]
            reached_terms = pending
        else:
            own_logits = lax.dynamic_slice_in_dim(
                grad_logits, head_index * slot_rows, slot_rows, 0
            )
            grad_normed_b = grad_normed_b + mm(
                "te,de->td", own_logits.astype(jnp.bfloat16), router_full
            )
            grad_norm_b, grad_gain_b = norm_back(grad_normed_b, scaled_b, inverse_b, gains[1:])
            grad_middle = grad_hidden + grad_norm_b
            plane_branch, *own_grad_in = exchange(
                ("head_gather", (valid_column * grad_middle).astype(jnp.bfloat16)),
                *(from_owner(grad_weight_sets[0][0]) if owned else []),
                after=pending,
            )
            reached_terms = []
        plane_branch = plane_branch.reshape(all_tokens, width)
        pending = []
        shared_terms = []
        if owned_total < experts_local:
            shared_terms = [
                lax.psum_scatter(term, "blk", scatter_dimension=1, tiled=True)
                for term in grad_weight_sets[-1]
            ]
        plane_branch = plane_branch.reshape(all_tokens, width)
        grad_out_w = mm("tf,td->fd", attended, plane_branch)
        grad_attended = by_slot(mm("td,fd->tf", plane_branch, out_full).astype(jnp.bfloat16))
        grad_queries, grad_pairs = attention_call(
            functools.partial(
                attend_back_kernel, heads_count, blocks_count, resident, group, kv_local
            ),
            info,
            [queries, pairs_all, grad_attended],
            [
                jax.ShapeDtypeStruct(queries.shape, jnp.bfloat16),
                jax.ShapeDtypeStruct(pairs_all.shape, jnp.bfloat16),
            ],
            [pltpu.VMEM((keys_total, pair_columns), jnp.float32)],
            10 * rows_local * keys_total * query_columns,
            "attend_back",
        )
        grad_out_w = jnp.concatenate(
            [grad_out_w, jnp.pad(grad_router, ((0, 0), (0, small_columns - gate_lanes)))], axis=1
        ).astype(jnp.bfloat16)
        alone = fused and layer_index > 0
        if alone:
            grad_out_w = lax.psum_scatter(grad_out_w, "blk", scatter_dimension=0, tiled=True)
            pending.append(grad_out_w)
            swapped = []
        else:
            swapped = [("blk_swap", grad_out_w.reshape(blocks_count, weight_rows, -1))]
        if owned:
            swapped += from_owner(grad_weight_sets[0][1])
        if fused:
            onward = None
            if layer_index:
                before = stored_all[layer_index - 1]
                onward = (
                    grad_middle,
                    valid_column,
                    gains[:1],
                    scaled_a,
                    jnp.broadcast_to(inverse_a, (slot_rows, 128)),
                    (before[STORED_TURNED], before[STORED_GATES], matrices(before[0], 1)),
                )
            (grad_projected, grad_normed_a, *others), further = unproject(
                grad_queries,
                grad_pairs.reshape(
                    SEQUENCE_SLOTS, heads_count, blocks_count // 2, 2, resident, pair_columns
                ),
                qkv_full,
                tile_cosine,
                tile_sine,
                [array for _, array in swapped],
                [*reached_terms, *(shared_terms if layer_index else [])],
                onward,
            )
            waiting = [] if layer_index else shared_terms
            grad_projected = grad_projected.reshape(all_tokens, -1)
            if not alone:
                grad_out_w, *others = others
            own_grad_down = others
        else:
            grad_pairs = (
                grad_pairs.reshape(
                    SEQUENCE_SLOTS, heads_count, blocks_count, resident, pair_columns
                )
                .transpose(2, 1, 0, 3, 4)
                .reshape(blocks_count, all_tokens, pair_columns)
            )
            (grad_pairs,) = exchange(("blk_swap", grad_pairs))
            grad_pairs = jnp.sum(grad_pairs.astype(jnp.float32), axis=0)
            grad_pairs = grad_pairs.astype(jnp.bfloat16).astype(jnp.float32)
            grad_pairs = grad_pairs.reshape(all_tokens, kv_local, 2, HEAD_SIZE)
            grad_keys = rotate(grad_pairs[:, :, 0].reshape(all_tokens, -1), cosine, -sine)
            grad_projected = jnp.concatenate(
                [
                    rotate(by_head(grad_queries).astype(jnp.float32), cosine, -sine),
                    jnp.stack(
                        [grad_keys.reshape(all_tokens, kv_local, HEAD_SIZE), grad_pairs[:, :, 1]],
                        axis=2,
                    ).reshape(all_tokens, pair_columns),
                ],
                axis=-1,
            ).astype(jnp.bfloat16)
            grad_normed_a, grad_out_w, *own_grad_down = exchange(
                (
                    "head_swap",
                    head_parts(
                        mm(
                            "te,de->td",
                            grad_projected,
                            qkv_full[:, : query_columns + pair_columns],
                        )
                    ),
                ),
                *swapped,
                after=shared_terms,
            )
            grad_normed_a = head_sum(grad_normed_a)
        grad_out_w = grad_out_w.astype(jnp.float32)
        if not alone:
            grad_out_w = jnp.sum(grad_out_w, axis=0)
        if fused and layer_index:
            grad_hidden, grad_gain_a, *further = further
            grad_gain_a = grad_gain_a[0]
            turned = unpack_in(further)
        else:
            grad_norm_a, grad_gain_a = norm_back(grad_normed_a, scaled_a, inverse_a, gains[:1])
            grad_hidden = grad_middle + grad_norm_a
        grad_qkv = (
            mm("td,te->de", plane_normed_a, grad_projected)
            .astype(jnp.bfloat16)
            .reshape(heads_count, blocks_count, weight_rows, -1)
            .transpose(1, 0, 2, 3)
        )
        if layer_index:
            grad_qkv = lax.psum_scatter(
                grad_qkv.reshape(width, -1), "blk", scatter_dimension=0, tiled=True
            )
            pending.append(grad_qkv)
            qkv_list[layer_index] = grad_qkv
            gains_list[layer_index] = jnp.stack([grad_gain_a, grad_gain_b])
        else:
            gains_list[0] = jnp.stack([grad_gain_a, grad_gain_b])
            grad_gains = (
                jnp.stack(gains_list)
                .reshape(2 * DECODER_LAYERS, heads_count, blocks_count, weight_rows)
                .transpose(1, 2, 0, 3)
                .reshape(heads_count, -1)
            )
            grad_qkv, grad_gains, *qkv_done = exchange(
                ("blk_swap", grad_qkv),
                ("head_swap", grad_gains[:, None]),
                *(
                    ("head_swap", term.reshape(heads_count, weight_rows, -1))
                    for term in qkv_list[1:]
                ),
                after=waiting,
            )
            grad_qkv = jnp.sum(grad_qkv.astype(jnp.float32), axis=0).astype(jnp.bfloat16)
            grad_gains = jnp.sum(grad_gains, axis=0).reshape(blocks_count, 1, -1)
            grad_qkv, grad_gains = exchange(
                ("head_swap", grad_qkv.reshape(heads_count, weight_rows, -1)),
                ("blk_swap", grad_gains),
            )
            qkv_list = [grad_qkv, *qkv_done]
            qkv_list = [
                jnp.concatenate(
                    [
                        term[..., :query_columns].transpose(1, 0, 2).reshape(weight_rows, -1),
                        term[..., query_columns:].transpose(1, 0, 2).reshape(weight_rows, -1),
                    ],
                    axis=1,
                ).astype(jnp.float32)
                for term in qkv_list
            ]
            grad_gains = jnp.sum(grad_gains, axis=0).reshape(DECODER_LAYERS, 2, weight_rows)

        out_list[layer_index] = grad_out_w[:, :width]
        router_list[layer_index] = (
            grad_out_w[:, width : width + gate_lanes]
            .reshape(weight_rows, heads_count, room)[:, :, :experts_local]
            .reshape(weight_rows, EXPERTS)
        )
        terms = []
        for number, received in enumerate((own_grad_in, own_grad_down)):
            parts = owned_rows(received[0]) if owned else []
            if owned_total < experts_local:
                parts.append(shared_terms[number])
            terms.append(jnp.concatenate(parts, axis=0).astype(jnp.float32))
        expert_list[layer_index] = tuple(terms)
    return (
        result,
        grad_hidden.reshape(tokens.shape),
        jnp.stack(qkv_list),
        jnp.stack(out_list),
        jnp.stack(router_list),
        grad_gains[:, 0],
        grad_gains[:, 1],
        jnp.stack([terms[0] for terms in expert_list]),
        jnp.stack([terms[1] for terms in expert_list]),
    )


def solution(mesh):
    in_specs = (
        P(None, ("head", "blk"), None),
        P(),
        P(None, None, ("head", "blk"), None),
        P(None, None, ("head", "blk"), None),
        P(None, ("head", "blk"), None),
        P(None, ("head", "blk"), None),
        P(None, ("head", "blk"), None),
        P(None, None, ("head", "blk")),
        P(None, "head", "blk", None),
        P(None, "head", "blk", None),
        P(None, ("head", "blk"), None),
    )
    out_specs = (
        P(None, ("head", "blk"), None),
        P(None, ("head", "blk"), None),
        P(None, ("head", "blk"), None),
        P(None, ("head", "blk"), None),
        P(None, ("head", "blk"), None),
        P(None, ("head", "blk")),
        P(None, ("head", "blk")),
        P(None, "head", "blk", None),
        P(None, "head", "blk", None),
    )
    return jax.shard_map(shards, mesh=mesh, in_specs=in_specs, out_specs=out_specs, check_vma=False)
```

```python
import functools

import jax
import jax.numpy as jnp
from jax import lax
from jax.experimental import pallas as pl
from jax.experimental.pallas import tpu as pltpu
from jax.sharding import PartitionSpec as P

MODEL_WIDTH = 1536
QUERY_HEAD_COUNT = 24
KEY_VALUE_HEADS = 8
HEAD_SIZE = 64
FF = 512
EXPERTS = 40
TOP = 8
DECODER_LAYERS = 2
SEQUENCE_SLOTS = 2
CAP = 26


epsilon = 1e-06
negative = -1e30
theta_log = 9.210340371976184


MESH = pl.DeviceIdType.MESH


def mm(spec, left, right):
    return jnp.einsum(spec, left, right, preferred_element_type=jnp.float32)


def rotate(values, cosine, sine):
    rows = values.shape[0]
    half = HEAD_SIZE // 2
    heads = values.reshape(rows, -1, HEAD_SIZE)
    first_half = heads[..., :half]
    second_half = heads[..., half:]
    cosine = cosine[:, None, :]
    sine = sine[:, None, :]
    return jnp.concatenate(
        [first_half * cosine - second_half * sine, second_half * cosine + first_half * sine],
        axis=-1,
    ).reshape(values.shape)


def norm_rows(hidden):
    inverse = lax.rsqrt(jnp.mean(hidden * hidden, axis=-1, keepdims=True) + epsilon)
    return (hidden * inverse, inverse)


def norm_back(grad_normed, scaled, inverse, gain_row):
    grad_gain = jnp.sum(grad_normed * scaled, axis=0)
    grad_scaled = grad_normed * gain_row
    grad_hidden = inverse * (
        grad_scaled - scaled * jnp.mean(grad_scaled * scaled, axis=-1, keepdims=True)
    )
    return (grad_hidden, grad_gain)


RELAY_PIECES = 4


def relayed_gather(heads, head, blk, head_peers, source, target, sems, first):
    count = source.shape[0] // RELAY_PIECES
    inner = jnp.logical_and(head > 0, head < heads - 1)
    rounds = []
    for piece in range(RELAY_PIECES):
        part = pl.ds(piece * count, count)
        index = first + piece * heads
        copies = []
        for number, peer in enumerate(head_peers):
            copy = remote(source.at[part], target.at[head, part], sems, index + number, peer)
            near = jnp.abs(peer[0] - head) < heads - 1
            copies.append((copy, near))
            pl.when(near)(copy.start)
        rounds.append(copies)
    passed = []
    for piece, copies in enumerate(rounds):
        copies[1][0].wait_recv()
        there = target.at[lax.rem(head + 2, heads), pl.ds(piece * count, count)]
        index = first + piece * heads
        copy = remote(
            there,
            there,
            sems,
            index + heads - 1,
            ((head - 1) * (heads - 1), blk),
            index + jnp.where(head == 1, 0, heads - 2),
        )
        pl.when(inner)(copy.start)
        passed.append(copy)
    for copies, copy in zip(rounds, passed):
        copies[0][0].wait_recv()
        copies[2][0].wait_recv()
        for sent, near in copies:
            pl.when(near)(sent.wait_send)
        pl.when(inner)(copy.wait_send)


def exchange_kernel(heads, blocks, items, waited, *refs):
    count = len(items)
    sources = refs[:count]
    targets = refs[count + waited : 2 * count + waited]
    send_sems, recv_sems, local_sems = refs[2 * count + waited :]
    head = lax.axis_index("head")
    blk = lax.axis_index("blk")
    chips = blocks // 2
    chip, core = blk // 2, lax.rem(blk, 2)
    sibling = chip * 2 + 1 - core
    kinds = {kind for kind, _ in items}
    head_peers = [(lax.rem(head + step, heads), blk) for step in range(1, heads)]
    blk_peers = [(head, lax.rem(blk + step, blocks)) for step in range(1, blocks)]
    pair_peers = [
        (head, lax.rem(chip + step, chips) * 2 + core) for step in range(1, chips)
    ] + [(head, sibling)]
    greeted = []
    if kinds & {"head_gather", "head_swap"}:
        greeted += head_peers
    if "blk_swap" in kinds:
        greeted += blk_peers
    elif "blk_pairs" in kinds:
        greeted += pair_peers
    barrier = pltpu.get_barrier_semaphore()
    for peer in greeted:
        pl.semaphore_signal(barrier, inc=1, device_id=peer, device_id_type=MESH)
    pl.semaphore_wait(barrier, len(greeted))
    used = 0
    copies = []
    forwards = []

    def send(source, target, peer):
        nonlocal used
        copy = pltpu.make_async_remote_copy(
            src_ref=source,
            dst_ref=target,
            send_sem=send_sems.at[used],
            recv_sem=recv_sems.at[used],
            device_id=peer,
            device_id_type=MESH,
        )
        copy.start()
        used += 1
        return copy

    locals_started = []
    gathers = []
    for number, (kind, layer) in enumerate(items):
        source, target = sources[number], targets[number]

        def piece(index, source=source, layer=layer):
            return source.at[index] if layer is None else source.at[layer, index]

        if kind == "head_gather" and heads == 4 and source.shape[0] % 64 == 0:
            mine, place = source, head
            gathers.append((source, target))
        elif kind == "head_gather":
            mine, place = source, head
            copies += [send(source, target.at[head], peer) for peer in head_peers]
        elif kind == "head_swap":
            mine, place = piece(head), head
            copies += [send(piece(peer[0]), target.at[head], peer) for peer in head_peers]
        elif kind == "blk_swap":
            mine, place = piece(blk), blk
            copies += [send(piece(peer[1]), target.at[blk], peer) for peer in blk_peers]
        else:
            mine, place = source, blk
            sent = [send(source, target.at[blk], peer) for peer in pair_peers]
            copies += sent[-1:]
            forwards.append((sent[:-1], target))
        local = pltpu.make_async_copy(mine, target.at[place], local_sems.at[number])
        local.start()
        locals_started.append(local)
    for source, target in gathers:
        relayed_gather(heads, head, blk, head_peers, source, target, (send_sems, recv_sems), used)
        used += RELAY_PIECES * heads
    for sent, target in forwards:
        for step, copy in enumerate(sent, start=1):
            copy.wait_recv()
            origin = lax.rem(chip + chips - step, chips) * 2 + core
            copies.append(send(target.at[origin], target.at[origin], (head, sibling)))
    for sent, _ in forwards:
        for copy in sent:
            copy.wait_send()
    for local in locals_started:
        local.wait()
    for copy in copies:
        copy.wait()


kernel_numbers = {}


def kernel_number(*key):
    return kernel_numbers.setdefault(key, 1 + len(kernel_numbers))


def exchange(*items, after=()):
    heads, blocks = lax.axis_size("head"), lax.axis_size("blk")
    arrays = [item[1] for item in items]
    plan = [(item[0], item[2] if len(item) > 2 else None) for item in items]
    outs = []
    total = 0
    for (kind, layer), array in zip(plan, arrays):
        group = heads if kind.startswith("head") else blocks
        tail = array.shape
        if kind.endswith("swap"):
            tail = tail[1:] if layer is None else tail[2:]
        outs.append(jax.ShapeDtypeStruct((group,) + tail, array.dtype))
        total += RELAY_PIECES * group
    collective_id = kernel_number(
        "exchange", tuple(plan), *((array.shape, str(array.dtype)) for array in (*arrays, *after))
    )
    results = pl.pallas_call(
        functools.partial(exchange_kernel, heads, blocks, plan, len(after)),
        out_shape=outs,
        in_specs=[pl.BlockSpec(memory_space=pl.ANY)] * (len(arrays) + len(after)),
        out_specs=[pl.BlockSpec(memory_space=pl.ANY)] * len(arrays),
        scratch_shapes=[
            pltpu.SemaphoreType.DMA((total,)),
            pltpu.SemaphoreType.DMA((total,)),
            pltpu.SemaphoreType.DMA((len(arrays),)),
        ],
        compiler_params=pltpu.CompilerParams(collective_id=collective_id, has_side_effects=True),
        cost_estimate=pl.CostEstimate(flops=0, bytes_accessed=110 << 20, transcendentals=0),
        name="exchange",
    )(*arrays, *after)
    return results


def greet(peers):
    barrier = pltpu.get_barrier_semaphore()
    for peer in peers:
        pl.semaphore_signal(barrier, inc=1, device_id=peer, device_id_type=MESH)
    pl.semaphore_wait(barrier, len(peers))


def plane_peers(heads, blocks):
    head = lax.axis_index("head")
    blk = lax.axis_index("blk")
    head_peers = [(lax.rem(head + step, heads), blk) for step in range(1, heads)]
    blk_peers = [(head, lax.rem(blk + step, blocks)) for step in range(1, blocks)]
    return head, blk, head_peers, blk_peers


def remote(source, target, sems, index, peer, landing=None):
    return pltpu.make_async_remote_copy(
        src_ref=source,
        dst_ref=target,
        send_sem=sems[0].at[index],
        recv_sem=sems[1].at[index if landing is None else landing],
        device_id=peer,
        device_id_type=MESH,
    )


def started(copy):
    copy.start()
    return copy


def weight_part(ref, columns, by_columns):
    return ref[:, columns] if by_columns else ref[columns, :]


def meet(left, part, by_columns):
    return (
        dot_last(left, part)
        if by_columns
        else jnp.dot(left, part, preferred_element_type=jnp.float32)
    )


STORED_TURNED, STORED_GATES = 12, 13
DISPATCH_PIECES, DISPATCH_WINDOW, DISPATCH_LAG = 6, 3, 2
COMBINE_PIECES = 4


def dispatch_stages(heads, blocks, by_columns, refs):
    (
        own_ref,
        place_ref,
        scale_ref,
        weight_ref,
        shared_weight_ref,
        plane_ref,
        queue_ref,
        shared_ref,
        out_ref,
        shared_out_ref,
        send_ref,
        held_ref,
        shared_held_ref,
        head_send,
        head_recv,
        blk_send,
        blk_recv,
        local_sems,
    ) = refs
    pieces, window, lag = DISPATCH_PIECES, DISPATCH_WINDOW, DISPATCH_LAG
    head, blk, head_peers, blk_peers = plane_peers(heads, blocks)
    rows, width = own_ref.shape
    slot = queue_ref.shape[1]
    shared = shared_ref.shape[0]
    step_width = width // pieces
    outputs = out_ref.shape[1]
    tile = 256
    relay = heads == 4
    inner = jnp.logical_and(head > 0, head < heads - 1)
    loads = [pltpu.make_async_copy(shared_weight_ref, shared_held_ref, local_sems.at[1])]
    if weight_ref is not None:
        loads.append(pltpu.make_async_copy(weight_ref, held_ref, local_sems.at[0]))
    head_copies = []
    blk_copies = []
    relayed = []

    def far(peer):
        return jnp.abs(peer[0] - head) == heads - 1

    def spread(piece):
        columns = pl.ds(piece * step_width, step_width)
        copies = []
        for number, peer in enumerate(head_peers):
            copy = remote(
                own_ref.at[:, columns],
                plane_ref.at[head, :, columns],
                (head_send, head_recv),
                piece * heads + number,
                peer,
            )
            copies.append(copy)
            if relay and number != 1:
                pl.when(jnp.logical_not(far(peer)))(copy.start)
            else:
                copy.start()
        head_copies.append(copies)

    def pass_on(piece):
        columns = pl.ds(piece * step_width, step_width)
        origin = lax.rem(head + 2, heads)
        rows_there = plane_ref.at[origin, :, columns]
        copy = remote(
            rows_there,
            rows_there,
            (head_send, head_recv),
            piece * heads + heads - 1,
            ((head - 1) * (heads - 1), blk),
            piece * heads + jnp.where(head == 1, 0, heads - 2),
        )
        relayed.append(copy)
        pl.when(inner)(copy.start)

    def scaled(values, start):
        if scale_ref is not None:
            values = values * scale_ref[pl.ds(start, slot), :]
        return values.astype(queue_ref.dtype)

    def begin():
        for load in loads:
            load.start()
        for piece in range(min(window, pieces)):
            spread(piece)
        plane_ref[head] = own_ref[...]

    def consume(piece):
        columns = pl.ds(piece * step_width, step_width)
        for copy in blk_copies[piece]:
            copy.wait_recv()
        queue = queue_ref[:, :, columns].reshape(blocks * slot, step_width)

        def one_tile(index, carry):
            lanes = pl.ds(pl.multiple_of(index * tile, tile), tile)
            if by_columns:
                product = dot_last(queue, held_ref[lanes, columns])
            else:
                product = jnp.dot(
                    queue, held_ref[columns, lanes], preferred_element_type=jnp.float32
                )
            if piece:
                product = product + out_ref[:, lanes]
            out_ref[:, lanes] = product
            return carry

        lax.fori_loop(0, outputs // tile, one_tile, 0)

    def take(piece):
        columns = pl.ds(piece * step_width, step_width)
        if relay:
            for later in range(piece + 1 if piece else 0, min(piece + 2, pieces)):
                head_copies[later][1].wait_recv()
                pass_on(later)
        for number, copy in enumerate(head_copies[piece]):
            if not relay or number != 1:
                copy.wait_recv()
        if piece + window < pieces:
            spread(piece + window)
        plane = plane_ref[:, :, columns].reshape(heads * rows, step_width)

        def fill(expert, carry):
            start = pl.multiple_of(expert * slot, 16)
            taken = jnp.dot(
                place_ref[pl.ds(start, slot), :], plane, preferred_element_type=jnp.float32
            )
            send_ref[expert, :, columns] = scaled(taken, start)
            return carry

        lax.fori_loop(0, blocks, fill, 0)
        blk_copies.append(
            [
                started(
                    remote(
                        send_ref.at[peer[1], :, columns],
                        queue_ref.at[blk, :, columns],
                        (blk_send, blk_recv),
                        piece * (blocks - 1) + number,
                        peer,
                    )
                )
                for number, peer in enumerate(blk_peers)
            ]
        )
        queue_ref[blk, :, columns] = send_ref[blk, :, columns]
        if not piece:
            for load in loads:
                load.wait()
        for expert in range(shared):
            start = (blocks + expert) * slot
            taken = jnp.dot(
                place_ref[pl.ds(start, slot), :], plane, preferred_element_type=jnp.float32
            )
            taken = scaled(taken, start)
            shared_ref[expert, :, columns] = taken
            product = meet(
                taken, weight_part(shared_held_ref.at[expert], columns, by_columns), by_columns
            )
            if piece:
                product = product + shared_out_ref[expert]
            shared_out_ref[expert] = product

    def step(number):
        if number < pieces:
            take(number)
        if number >= lag:
            consume(number - lag)

    def end():
        for copies in head_copies:
            for number, copy in enumerate(copies):
                if relay and number != 1:
                    pl.when(jnp.logical_not(far(head_peers[number])))(copy.wait_send)
                else:
                    copy.wait_send()
        for copy in relayed:
            pl.when(inner)(copy.wait_send)
        for copies in blk_copies:
            for copy in copies:
                copy.wait_send()

    steps = [functools.partial(step, number) for number in range(pieces + lag)]
    return [begin, *steps, end]


def dispatch_plan(rows, places, scale, weights, by_columns):
    heads, blocks = lax.axis_size("head"), lax.axis_size("blk")
    count, width = rows.shape
    (own_weight, shared_weight) = weights
    shared = shared_weight.shape[0]
    slot = places.shape[0] // (blocks + shared)
    outputs = own_weight.shape[0 if by_columns else 1]
    pieces = DISPATCH_PIECES
    vmem = pl.BlockSpec(memory_space=pltpu.VMEM)
    anywhere = pl.BlockSpec(memory_space=pl.ANY)
    scales = [] if scale is None else [scale]
    return (
        [rows, places, *scales, own_weight, shared_weight],
        [vmem, vmem, *([vmem] * len(scales)), anywhere, anywhere],
        [
            jax.ShapeDtypeStruct((heads, count, width), jnp.bfloat16),
            jax.ShapeDtypeStruct((blocks, slot, width), jnp.bfloat16),
            jax.ShapeDtypeStruct((shared, slot, width), jnp.bfloat16),
            jax.ShapeDtypeStruct((blocks * slot, outputs), jnp.float32),
            jax.ShapeDtypeStruct((shared, slot, outputs), jnp.float32),
        ],
        [vmem] * 5,
        [
            pltpu.VMEM((blocks, slot, width), jnp.bfloat16),
            pltpu.VMEM(own_weight.shape, jnp.bfloat16),
            pltpu.VMEM(shared_weight.shape, jnp.bfloat16),
            pltpu.SemaphoreType.DMA((pieces * heads,)),
            pltpu.SemaphoreType.DMA((pieces * heads,)),
            pltpu.SemaphoreType.DMA((pieces * (blocks - 1),)),
            pltpu.SemaphoreType.DMA((pieces * (blocks - 1),)),
            pltpu.SemaphoreType.DMA((2,)),
        ],
    )


def staged_call(plans, name, millions, after=()):
    heads, blocks = lax.axis_size("head"), lax.axis_size("blk")
    inputs = [len(plan[2]) for plan in plans]
    outputs = [len(plan[4]) for plan in plans]
    scratches = [len(plan[6]) for plan in plans]

    def kernel(*refs):
        _, _, head_peers, blk_peers = plane_peers(heads, blocks)
        greet(head_peers + blk_peers)
        lists = []
        refs = refs[: sum(inputs)] + refs[sum(inputs) + len(after) :]
        for number, plan in enumerate(plans):
            first = sum(inputs[:number])
            given = list(refs[first : first + inputs[number]])
            if not plan[7]:
                given.insert(2 if plan[0][0] == "dispatch" else 3, None)
            first = sum(inputs) + sum(outputs[:number])
            given += refs[first : first + outputs[number]]
            first = sum(inputs) + sum(outputs) + sum(scratches[:number])
            given += refs[first : first + scratches[number]]
            lists.append(plan[1](given))
        for index in range(max(len(stages) for stages in lists)):
            for stages in lists:
                if index < len(stages):
                    stages[index]()

    arrays = [array for plan in plans for array in plan[2]]
    results = pl.pallas_call(
        kernel,
        out_shape=[out for plan in plans for out in plan[4]],
        in_specs=[spec for plan in plans for spec in plan[3]]
        + [pl.BlockSpec(memory_space=pl.ANY)] * len(after),
        out_specs=[spec for plan in plans for spec in plan[5]],
        scratch_shapes=[scratch for plan in plans for scratch in plan[6]],
        compiler_params=pltpu.CompilerParams(
            collective_id=kernel_number(
                *(plan[0] for plan in plans), *(array.shape for array in after)
            ),
            has_side_effects=True,
            vmem_limit_bytes=60 * 1024 * 1024,
        ),
        cost_estimate=pl.CostEstimate(
            flops=0, bytes_accessed=millions << 20, transcendentals=0
        ),
        name=name,
    )(*arrays, *after)
    return [
        results[sum(outputs[:number]) : sum(outputs[: number + 1])] for number in range(len(plans))
    ]


def dispatch_call(rows, places, scale, weights, by_columns):
    heads, blocks = lax.axis_size("head"), lax.axis_size("blk")
    return (
        ("dispatch", by_columns, scale is not None),
        functools.partial(dispatch_stages, heads, blocks, by_columns),
        *dispatch_plan(rows, places, scale, weights, by_columns),
        scale is not None,
    )


def enter_kernel(heads, blocks, layer, swaps, *refs):
    attended_ref, out_weight_ref, hidden_ref, valid_ref, gain_ref, place_ref, *refs = refs
    moved_ref, shared_weight_ref, *refs = refs
    swap_refs, refs = refs[:swaps], refs[swaps:]
    middle_ref, scaled_ref, inverse_ref, plane_ref, queue_ref, shared_ref, *refs = refs
    out_ref, shared_out_ref, matrix_ref, *refs = refs
    swap_out_refs, refs = refs[:swaps], refs[swaps:]
    own_ref, part_ref, landed_ref, relay_ref, sum_send, sum_recv, *refs = refs
    moved_send, moved_recv, swap_send, swap_recv, side_sems, *refs = refs
    send_ref, held_ref, shared_held_ref, head_send, head_recv, blk_send, blk_recv, local_sems = refs
    head, blk, head_peers, blk_peers = plane_peers(heads, blocks)
    rows, width = middle_ref.shape
    pieces = COMBINE_PIECES
    step_width = width // pieces
    matrix_rows = moved_ref.shape[2]
    inner = jnp.logical_and(head > 0, head < heads - 1)
    greet(head_peers + blk_peers)

    def far(peer):
        return jnp.abs(peer[0] - head) == heads - 1

    def peer_origin(peer):
        return lax.rem(2 * head + heads - peer[0], heads)

    sent = []

    def through_copy(piece, peer):
        columns = pl.ds(piece * step_width, step_width)
        return remote(
            part_ref.at[peer[0], :, columns],
            relay_ref.at[:, columns],
            (sum_send, sum_recv),
            piece * heads + heads - 1,
            (jnp.where(head == 0, 1, heads - 2), blk),
        )

    def spread(piece):
        columns = pl.ds(piece * step_width, step_width)
        weight = out_weight_ref[:, columns]

        def part(owner):
            start = pl.multiple_of(owner * rows, 16)
            return jnp.dot(
                attended_ref[pl.ds(start, rows), :], weight, preferred_element_type=jnp.float32
            )

        copies = []
        for number, peer in enumerate(head_peers):
            part_ref[peer[0], :, columns] = part(peer[0]).astype(part_ref.dtype)
            copy = remote(
                part_ref.at[peer[0], :, columns],
                landed_ref.at[head, :, columns],
                (sum_send, sum_recv),
                piece * heads + number,
                peer,
            )
            copies.append(copy)
            if number == 1:
                pl.when(jnp.logical_not(inner))(copy.start)
            else:
                distant = far(peer)
                pl.when(jnp.logical_not(distant))(copy.start)
                pl.when(distant)(through_copy(piece, peer).start)
        sent.append(copies)
        middle_ref[:, columns] = part(head)

    def pass_on(piece):
        columns = pl.ds(piece * step_width, step_width)
        target = lax.rem(head + 2, heads)

        @pl.when(inner)
        def _():
            through_copy(piece, (target, blk)).wait_recv()
            part_ref[target, :, columns] = (
                part_ref[target, :, columns].astype(jnp.float32)
                + relay_ref[:, columns].astype(jnp.float32)
            ).astype(part_ref.dtype)
            sent[piece][1].start()

    def finish(piece):
        columns = pl.ds(piece * step_width, step_width)
        for number, peer in enumerate(head_peers):
            copy = sent[piece][number]

            def add(copy=copy, peer=peer):
                copy.wait_recv()
                middle_ref[:, columns] += landed_ref[peer_origin(peer), :, columns].astype(
                    jnp.float32
                )

            if number != 1:
                pl.when(jnp.logical_not(far((peer_origin(peer), blk))))(add)
            else:
                add()

    moved = []

    def move():
        for number, peer in enumerate(blk_peers):
            place = pl.ds(pl.multiple_of(blk * matrix_rows, 16), matrix_rows)
            moved.append(
                started(
                    remote(
                        moved_ref.at[layer, peer[1]],
                        held_ref.at[place],
                        (moved_send, moved_recv),
                        number,
                        peer,
                    )
                )
            )
        place = pl.ds(pl.multiple_of(blk * matrix_rows, 16), matrix_rows)
        moved.append(
            started(
                pltpu.make_async_copy(
                    moved_ref.at[layer, blk], held_ref.at[place], side_sems.at[0]
                )
            )
        )
        for item in range(swaps):
            for number, peer in enumerate(head_peers):
                swapped.append(
                    started(
                        remote(
                            swap_refs[item].at[peer[0]],
                            swap_out_refs[item].at[head],
                            (swap_send, swap_recv),
                            item * heads + number,
                            peer,
                        )
                    )
                )
            swapped.append(
                started(
                    pltpu.make_async_copy(
                        swap_refs[item].at[head], swap_out_refs[item].at[head], side_sems.at[2]
                    )
                )
            )

    swapped = []
    lag = 2
    for step in range(pieces + lag):
        if step < pieces:
            spread(step)
        if not step:
            move()
        if 0 < step <= pieces:
            pass_on(step - 1)
        if step >= lag:
            finish(step - lag)
    middle = hidden_ref[...] + valid_ref[...] * middle_ref[...]
    inverse = lax.rsqrt(jnp.mean(middle * middle, axis=1, keepdims=True) + epsilon)
    scaled = middle * inverse
    middle_ref[...] = middle
    scaled_ref[...] = scaled
    inverse_ref[...] = jnp.broadcast_to(inverse, inverse_ref.shape)
    own_ref[...] = (scaled * gain_ref[...]).astype(own_ref.dtype)
    stages = dispatch_stages(
        heads,
        blocks,
        False,
        (
            own_ref,
            place_ref,
            None,
            None,
            shared_weight_ref,
            plane_ref,
            queue_ref,
            shared_ref,
            out_ref,
            shared_out_ref,
            send_ref,
            held_ref,
            shared_held_ref,
            head_send,
            head_recv,
            blk_send,
            blk_recv,
            local_sems,
        ),
    )
    stages[0]()
    for copy in moved:
        if hasattr(copy, "wait_recv") and copy is not moved[-1]:
            copy.wait_recv()
        else:
            copy.wait()
    saved = pltpu.make_async_copy(held_ref, matrix_ref, side_sems.at[1])
    saved.start()
    for stage in stages[1:]:
        stage()
    saved.wait()
    for copy in moved[:-1]:
        copy.wait_send()
    for copy in swapped:
        copy.wait()
    for piece, copies in enumerate(sent):
        for number, copy in enumerate(copies):
            if number != 1:
                distant = far(head_peers[number])
                pl.when(jnp.logical_not(distant))(copy.wait_send)
                pl.when(distant)(through_copy(piece, head_peers[number]).wait_send)
            else:
                copy.wait_send()


def enter(attended, out_weight, hidden, valid, gain, places, moved, layer, shared_weight, swaps):
    heads, blocks = lax.axis_size("head"), lax.axis_size("blk")
    count, width = hidden.shape
    matrix = jax.ShapeDtypeStruct((blocks * moved.shape[2], moved.shape[3]), moved.dtype)
    rows = jax.ShapeDtypeStruct((count, width), jnp.bfloat16)
    _, _, outs, _, scratch = dispatch_plan(rows, places, None, (matrix, shared_weight), False)
    vmem = pl.BlockSpec(memory_space=pltpu.VMEM)
    anywhere = pl.BlockSpec(memory_space=pl.ANY)
    pieces = COMBINE_PIECES
    return pl.pallas_call(
        functools.partial(enter_kernel, heads, blocks, layer, len(swaps)),
        out_shape=[
            jax.ShapeDtypeStruct((count, width), jnp.float32),
            jax.ShapeDtypeStruct((count, width), jnp.float32),
            jax.ShapeDtypeStruct((count, 128), jnp.float32),
            *outs,
            matrix,
            *(jax.ShapeDtypeStruct(array.shape, array.dtype) for array in swaps),
        ],
        in_specs=[vmem] * 6 + [anywhere] * (2 + len(swaps)),
        out_specs=[vmem] * (3 + len(outs)) + [anywhere] * (1 + len(swaps)),
        scratch_shapes=[
            pltpu.VMEM((count, width), jnp.bfloat16),
            pltpu.VMEM((heads, count, width), jnp.bfloat16),
            pltpu.VMEM((heads, count, width), jnp.bfloat16),
            pltpu.VMEM((count, width), jnp.bfloat16),
            pltpu.SemaphoreType.DMA((pieces * heads,)),
            pltpu.SemaphoreType.DMA((pieces * heads,)),
            pltpu.SemaphoreType.DMA((blocks,)),
            pltpu.SemaphoreType.DMA((blocks,)),
            pltpu.SemaphoreType.DMA((max(1, len(swaps)) * heads,)),
            pltpu.SemaphoreType.DMA((max(1, len(swaps)) * heads,)),
            pltpu.SemaphoreType.DMA((3,)),
            *scratch,
        ],
        compiler_params=pltpu.CompilerParams(
            collective_id=kernel_number("enter", layer, len(swaps)),
            has_side_effects=True,
            vmem_limit_bytes=60 * 1024 * 1024,
        ),
        cost_estimate=pl.CostEstimate(flops=0, bytes_accessed=270 << 20, transcendentals=0),
        name="enter",
    )(attended, out_weight, hidden, valid, gain, places, moved, shared_weight, *swaps)


def turn_heads(values, cosine, sine):
    lane = lax.broadcasted_iota(jnp.int32, values.shape, 1) % HEAD_SIZE
    half = HEAD_SIZE // 2
    width = values.shape[1]
    swapped = jnp.where(
        lane < half, pltpu.roll(values, width - half, 1), pltpu.roll(values, half, 1)
    )
    return values * cosine + swapped * sine


def project_kernel(
    heads,
    blocks,
    pieces,
    layer,
    greeted,
    own_ref,
    weight_ref,
    cosine_ref,
    sine_ref,
    moved_ref,
    plane_ref,
    query_ref,
    pair_ref,
    moved_out_ref,
    head_send,
    head_recv,
    pair_send,
    pair_recv,
    moved_send,
    moved_recv,
    local_sem,
):
    head, blk, head_peers, blk_peers = plane_peers(heads, blocks)
    chips = blocks // 2
    chip, core = blk // 2, lax.rem(blk, 2)
    sibling = (head, chip * 2 + 1 - core)
    rows, width = own_ref.shape
    count = rows // pieces
    slots, _, _, resident, pair_columns = pair_ref.shape
    query_columns = query_ref.shape[2]
    inner = jnp.logical_and(head > 0, head < heads - 1)
    if not greeted:
        greet(head_peers + blk_peers)

    def far(peer):
        return jnp.abs(peer[0] - head) == heads - 1

    def place(piece):
        return piece * count // resident, pl.ds(piece * count % resident, count)

    head_copies = []
    relayed = []
    for piece in range(pieces):
        part = pl.ds(piece * count, count)
        copies = []
        for number, peer in enumerate(head_peers):
            copy = remote(
                own_ref.at[part],
                plane_ref.at[head, part],
                (head_send, head_recv),
                piece * heads + number,
                peer,
            )
            copies.append(copy)
            if number != 1:
                pl.when(jnp.logical_not(far(peer)))(copy.start)
            else:
                copy.start()
        head_copies.append(copies)
    moved = []
    if layer is not None:
        moved = [
            started(
                remote(
                    moved_ref.at[layer, peer[1]],
                    moved_out_ref.at[blk],
                    (moved_send, moved_recv),
                    number,
                    peer,
                )
            )
            for number, peer in enumerate(blk_peers)
        ]
        local = pltpu.make_async_copy(moved_ref.at[layer, blk], moved_out_ref.at[blk], local_sem)
        local.start()
    plane_ref[head] = own_ref[...]

    def pass_on(piece):
        head_copies[piece][1].wait_recv()
        part = pl.ds(piece * count, count)
        rows_there = plane_ref.at[lax.rem(head + 2, heads), part]
        copy = remote(
            rows_there,
            rows_there,
            (head_send, head_recv),
            piece * heads + heads - 1,
            ((head - 1) * (heads - 1), blk),
            piece * heads + jnp.where(head == 1, 0, heads - 2),
        )
        relayed.append(copy)
        pl.when(inner)(copy.start)

    pair_copies = []
    forwards = []

    def forward(piece):
        slot, part = place(piece)
        for step in range(1, chips):
            pair_copies[piece][step - 1].wait_recv()
            origin = lax.rem(chip + chips - step, chips) * 2 + core
            there = pair_ref.at[slot, :, origin, part]
            forwards.append(
                started(
                    remote(
                        there,
                        there,
                        (pair_send, pair_recv),
                        piece * blocks + chips - 1 + step,
                        sibling,
                    )
                )
            )

    tile = 2 * HEAD_SIZE
    for piece in range(pieces):
        for later in range(piece + 1 if piece else 0, min(piece + 2, pieces)):
            pass_on(later)
        for number in range(heads - 1):
            if number != 1:
                head_copies[piece][number].wait_recv()
        part = pl.ds(piece * count, count)
        slot, inside = place(piece)
        projected = jnp.dot(
            plane_ref[:, part, :].reshape(heads * count, width),
            weight_ref[:, : query_columns + pair_columns],
            preferred_element_type=jnp.float32,
        )
        cosine = cosine_ref[:, part, :].reshape(heads * count, tile)
        sine = sine_ref[:, part, :].reshape(heads * count, tile)
        turned = jnp.concatenate(
            [
                turn_heads(projected[:, start : start + tile], cosine, sine)
                for start in range(0, query_columns, tile)
            ],
            axis=1,
        ).astype(query_ref.dtype)
        is_key = lax.broadcasted_iota(jnp.int32, cosine.shape, 1) < HEAD_SIZE
        key_cosine = jnp.where(is_key, cosine, 1.0)
        key_sine = jnp.where(is_key, sine, 0.0)
        pairs = jnp.concatenate(
            [
                turn_heads(projected[:, start : start + tile], key_cosine, key_sine)
                for start in range(query_columns, query_columns + pair_columns, tile)
            ],
            axis=1,
        ).astype(pair_ref.dtype)
        for there in range(heads):
            taken = slice(there * count, (there + 1) * count)
            query_ref[slot, pl.ds(there * resident + piece * count % resident, count), :] = turned[
                taken
            ]
            pair_ref[slot, there, blk, inside, :] = pairs[taken]
        mine = pair_ref.at[slot, :, blk, inside]
        targets = [
            (head, lax.rem(chip + step, chips) * 2 + core) for step in range(1, chips)
        ] + [sibling]
        pair_copies.append(
            [
                started(
                    remote(mine, mine, (pair_send, pair_recv), piece * blocks + number, peer)
                )
                for number, peer in enumerate(targets)
            ]
        )
        if piece:
            forward(piece - 1)
    forward(pieces - 1)
    for copies in pair_copies:
        for copy in copies[:-1]:
            copy.wait_send()
        copies[-1].wait()
    for copy in forwards:
        copy.wait()
    for copies in head_copies:
        for number, copy in enumerate(copies):
            if number != 1:
                pl.when(jnp.logical_not(far(head_peers[number])))(copy.wait_send)
            else:
                copy.wait_send()
    for copy in relayed:
        pl.when(inner)(copy.wait_send)
    for copy in moved:
        copy.wait()
    if moved:
        local.wait()


PROJECT_PIECES = 4


def project_plan(count, width, moved, layer, query_columns, pair_columns, resident):
    heads, blocks = lax.axis_size("head"), lax.axis_size("blk")
    pieces = PROJECT_PIECES
    slots = count // resident
    moves = [] if layer is None else [moved]
    vmem = pl.BlockSpec(memory_space=pltpu.VMEM)
    anywhere = pl.BlockSpec(memory_space=pl.ANY)
    return (
        [
            jax.ShapeDtypeStruct((heads, count, width), jnp.bfloat16),
            jax.ShapeDtypeStruct(
                (slots, heads * resident, query_columns), jnp.bfloat16
            ),
            jax.ShapeDtypeStruct((slots, heads, blocks, resident, pair_columns), jnp.bfloat16),
            *(jax.ShapeDtypeStruct((blocks,) + array.shape[2:], array.dtype) for array in moves),
        ],
        [vmem] * 3 + [anywhere] * len(moves),
        [
            pltpu.SemaphoreType.DMA((pieces * heads,)),
            pltpu.SemaphoreType.DMA((pieces * heads,)),
            pltpu.SemaphoreType.DMA((pieces * blocks,)),
            pltpu.SemaphoreType.DMA((pieces * blocks,)),
            pltpu.SemaphoreType.DMA((blocks,)),
            pltpu.SemaphoreType.DMA((blocks,)),
            pltpu.SemaphoreType.DMA,
        ],
    )


def project(rows, weight, cosine, sine, moved, layer, query_columns, pair_columns, resident):
    heads, blocks = lax.axis_size("head"), lax.axis_size("blk")
    outs, out_specs, scratch = project_plan(
        *rows.shape, moved, layer, query_columns, pair_columns, resident
    )
    moves = [] if layer is None else [moved]
    vmem = pl.BlockSpec(memory_space=pltpu.VMEM)
    anywhere = pl.BlockSpec(memory_space=pl.ANY)
    return pl.pallas_call(
        functools.partial(project_kernel, heads, blocks, PROJECT_PIECES, layer, False),
        out_shape=outs,
        in_specs=[vmem] * 4 + [anywhere] * len(moves),
        out_specs=out_specs,
        scratch_shapes=scratch,
        compiler_params=pltpu.CompilerParams(
            collective_id=kernel_number("project", layer),
            has_side_effects=True,
            vmem_limit_bytes=56 * 1024 * 1024,
        ),
        cost_estimate=pl.CostEstimate(flops=0, bytes_accessed=130 << 20, transcendentals=0),
        name="project",
    )(rows, weight, cosine, sine, *moves)


def cross(plan, middle, valid, gain, weight, cosine, sine, moved, layer, *sizes):
    heads, blocks = lax.axis_size("head"), lax.axis_size("blk")
    key, maker, arrays, specs, outs, out_specs, scratch, scaled_rows = plan
    count, width = middle.shape
    more_outs, more_specs, more_scratch = project_plan(
        count, width, moved, layer, *sizes
    )
    inputs, results, temps = len(arrays), len(outs), len(scratch)
    vmem = pl.BlockSpec(memory_space=pltpu.VMEM)
    anywhere = pl.BlockSpec(memory_space=pl.ANY)
    norm_outs = [
        jax.ShapeDtypeStruct((count, width), jnp.float32),
        jax.ShapeDtypeStruct((count, width), jnp.float32),
        jax.ShapeDtypeStruct((count, 128), jnp.float32),
    ]

    def kernel(*refs):
        _, _, head_peers, blk_peers = plane_peers(heads, blocks)
        greet(head_peers + blk_peers)
        given, refs = list(refs[:inputs]), refs[inputs:]
        middle_ref, valid_ref, gain_ref, weight_ref, cosine_ref, sine_ref, *refs = refs
        moved_ref, *refs = refs
        given += refs[:results]
        sum_ref, refs = refs[0], refs[results:]
        hidden_ref, scaled_ref, inverse_ref, *refs = refs
        made, refs = refs[: len(more_outs)], refs[len(more_outs) :]
        given += refs[:temps]
        own_ref, *rest = refs[temps:]
        if not scaled_rows:
            given.insert(3, None)
        for stage in maker(given):
            stage()
        hidden = middle_ref[...] + valid_ref[...] * sum_ref[...]
        inverse = lax.rsqrt(jnp.mean(hidden * hidden, axis=1, keepdims=True) + epsilon)
        scaled = hidden * inverse
        hidden_ref[...] = hidden
        scaled_ref[...] = scaled
        inverse_ref[...] = jnp.broadcast_to(inverse, inverse_ref.shape)
        own_ref[...] = (scaled * gain_ref[...]).astype(own_ref.dtype)
        project_kernel(
            heads,
            blocks,
            PROJECT_PIECES,
            layer,
            True,
            own_ref,
            weight_ref,
            cosine_ref,
            sine_ref,
            moved_ref,
            *made,
            *rest,
        )

    values = pl.pallas_call(
        kernel,
        out_shape=[*outs, *norm_outs, *more_outs],
        in_specs=[*specs, *([vmem] * 6), anywhere],
        out_specs=[*out_specs, *([vmem] * 3), *more_specs],
        scratch_shapes=[*scratch, pltpu.VMEM((count, width), jnp.bfloat16), *more_scratch],
        compiler_params=pltpu.CompilerParams(
            collective_id=kernel_number("cross", key, layer),
            has_side_effects=True,
            vmem_limit_bytes=60 * 1024 * 1024,
        ),
        cost_estimate=pl.CostEstimate(flops=0, bytes_accessed=290 << 20, transcendentals=0),
        name="cross",
    )(*arrays, middle, valid, gain, weight, cosine, sine, moved)
    return values[:results], values[results : results + 3], values[results + 3 :]


def unproject_kernel(
    heads,
    blocks,
    pieces,
    items,
    grad_query_ref,
    grad_pair_ref,
    weight_ref,
    cosine_ref,
    sine_ref,
    *refs,
):
    moved_refs = refs[:items]
    grad_ref, out_ref = refs[items : items + 2]
    moved_out_refs = refs[items + 2 : 2 * items + 2]
    (
        near_ref,
        sum_ref,
        far_ref,
        product_ref,
        part_ref,
        landed_ref,
        relay_ref,
        near_send,
        near_recv,
        chip_send,
        chip_recv,
        head_send,
        head_recv,
        moved_send,
        moved_recv,
        local_sems,
    ) = refs[2 * items + 2 :]
    head, blk, head_peers, blk_peers = plane_peers(heads, blocks)
    chips = blocks // 2
    chip, core = blk // 2, lax.rem(blk, 2)
    sibling = (head, chip * 2 + 1 - core)
    rows, width = out_ref.shape
    count = rows // pieces
    resident, pair_columns = grad_pair_ref.shape[4:]
    query_columns = grad_query_ref.shape[2]
    inner = jnp.logical_and(head > 0, head < heads - 1)
    chip_peers = [(head, lax.rem(chip + step, chips) * 2 + core) for step in range(1, chips)]
    greet(head_peers + blk_peers)

    def far(peer):
        return jnp.abs(peer[0] - head) == heads - 1

    def peer_origin(peer):
        return lax.rem(2 * head + heads - peer[0], heads)

    def place(piece):
        return piece * count // resident, pl.ds(piece * count % resident, count)

    near_copies = []
    for piece in range(pieces):
        slot, inside = place(piece)
        near_copies.append(
            started(
                remote(
                    grad_pair_ref.at[slot, :, :, 1 - core, inside],
                    near_ref.at[piece],
                    (near_send, near_recv),
                    piece,
                    sibling,
                )
            )
        )
    chip_copies = []
    head_copies = []
    moved = []

    def add_cores(piece):
        slot, inside = place(piece)
        near_copies[piece].wait_recv()
        sum_ref[piece] = (
            grad_pair_ref[slot, :, :, core, inside, :].astype(jnp.float32)
            + near_ref[piece].astype(jnp.float32)
        ).astype(sum_ref.dtype)
        chip_copies.append(
            [
                started(
                    remote(
                        sum_ref.at[piece, :, peer[1] // 2],
                        far_ref.at[piece, chip],
                        (chip_send, chip_recv),
                        piece * chips + number,
                        peer,
                    )
                )
                for number, peer in enumerate(chip_peers)
            ]
        )

    def through_copy(piece, peer):
        part = pl.ds(piece * count, count)
        return remote(
            part_ref.at[peer[0], part],
            relay_ref.at[part],
            (head_send, head_recv),
            piece * heads + heads - 1,
            (jnp.where(head == 0, 1, heads - 2), blk),
        )

    tile = 2 * HEAD_SIZE

    def multiply(piece):
        slot, inside = place(piece)
        part = pl.ds(piece * count, count)
        for copy in chip_copies[piece]:
            copy.wait_recv()
        pairs = sum_ref[piece, :, chip].astype(jnp.float32)
        for peer in chip_peers:
            pairs = pairs + far_ref[piece, peer[1] // 2].astype(jnp.float32)
        pairs = pairs.reshape(heads * count, pair_columns)
        pairs = pairs.astype(jnp.bfloat16).astype(jnp.float32)
        queries = jnp.concatenate(
            [
                grad_query_ref[
                    slot, pl.ds(there * resident + piece * count % resident, count), :
                ]
                for there in range(heads)
            ],
            axis=0,
        ).astype(jnp.float32)
        cosine = cosine_ref[:, part, :].reshape(heads * count, tile)
        sine = -sine_ref[:, part, :].reshape(heads * count, tile)
        is_key = lax.broadcasted_iota(jnp.int32, cosine.shape, 1) < HEAD_SIZE
        key_cosine = jnp.where(is_key, cosine, 1.0)
        key_sine = jnp.where(is_key, sine, 0.0)
        turned = jnp.concatenate(
            [
                turn_heads(queries[:, start : start + tile], cosine, sine)
                for start in range(0, query_columns, tile)
            ]
            + [
                turn_heads(pairs[:, start : start + tile], key_cosine, key_sine)
                for start in range(0, pair_columns, tile)
            ],
            axis=1,
        ).astype(grad_ref.dtype)
        grad_ref[:, part, :] = turned.reshape(heads, count, query_columns + pair_columns)
        weight = weight_ref[:, : query_columns + pair_columns]
        product_ref[...] = dot_last(turned, weight).reshape(heads, count, width)
        sent = []
        for number, peer in enumerate(head_peers):
            part_ref[peer[0], part, :] = product_ref[peer[0]].astype(part_ref.dtype)
            copy = remote(
                part_ref.at[peer[0], part],
                landed_ref.at[head, part],
                (head_send, head_recv),
                piece * heads + number,
                peer,
            )
            sent.append(copy)
            if number == 1:
                pl.when(jnp.logical_not(inner))(copy.start)
            else:
                distant = far(peer)
                pl.when(jnp.logical_not(distant))(copy.start)
                pl.when(distant)(through_copy(piece, peer).start)
        head_copies.append(sent)
        out_ref[part, :] = product_ref[head]

    def pass_on(piece):
        part = pl.ds(piece * count, count)
        target = lax.rem(head + 2, heads)

        @pl.when(inner)
        def _():
            through_copy(piece, (target, blk)).wait_recv()
            part_ref[target, part, :] = (
                part_ref[target, part, :].astype(jnp.float32)
                + relay_ref[part, :].astype(jnp.float32)
            ).astype(part_ref.dtype)
            head_copies[piece][1].start()

    def finish(piece):
        part = pl.ds(piece * count, count)
        for number, peer in enumerate(head_peers):
            copy = head_copies[piece][number]

            def add(copy=copy, peer=peer):
                copy.wait_recv()
                out_ref[part, :] += landed_ref[peer_origin(peer), part, :].astype(jnp.float32)

            if number != 1:
                pl.when(jnp.logical_not(far((peer_origin(peer), blk))))(add)
            else:
                add()

    for step in range(pieces + 3):
        if step < pieces:
            add_cores(step)
        if step == pieces - 1:
            for item in range(items):
                source, target = moved_refs[item], moved_out_refs[item]
                moved += [
                    started(
                        remote(
                            source.at[peer[1]],
                            target.at[blk],
                            (moved_send, moved_recv),
                            item * blocks + number,
                            peer,
                        )
                    )
                    for number, peer in enumerate(blk_peers)
                ]
                local = pltpu.make_async_copy(
                    source.at[blk], target.at[blk], local_sems.at[item]
                )
                moved.append(started(local))
        if 0 < step <= pieces:
            multiply(step - 1)
        if 1 < step <= pieces + 1:
            pass_on(step - 2)
        if step > 2:
            finish(step - 3)
    for copy in near_copies:
        copy.wait_send()
    for copies in chip_copies:
        for copy in copies:
            copy.wait_send()
    for piece, copies in enumerate(head_copies):
        for number, copy in enumerate(copies):
            if number != 1:
                distant = far(head_peers[number])
                pl.when(jnp.logical_not(distant))(copy.wait_send)
                pl.when(distant)(through_copy(piece, head_peers[number]).wait_send)
            else:
                copy.wait_send()
    for copy in moved:
        copy.wait()


UNPROJECT_PIECES = 4


def unproject_plan(grad_queries, grad_pairs, weight, moved):
    heads, blocks = lax.axis_size("head"), lax.axis_size("blk")
    chips = blocks // 2
    pieces = UNPROJECT_PIECES
    slots, _, _, _, resident, pair_columns = grad_pairs.shape
    rows = slots * resident
    count = rows // pieces
    width = weight.shape[0]
    items = len(moved)
    vmem = pl.BlockSpec(memory_space=pltpu.VMEM)
    anywhere = pl.BlockSpec(memory_space=pl.ANY)
    return (
        [
            jax.ShapeDtypeStruct(
                (heads, rows, grad_queries.shape[2] + pair_columns), jnp.bfloat16
            ),
            jax.ShapeDtypeStruct((rows, width), jnp.float32),
            *(jax.ShapeDtypeStruct(array.shape, array.dtype) for array in moved),
        ],
        [vmem] * 2 + [anywhere] * items,
        [
            pltpu.VMEM((pieces, heads, chips, count, pair_columns), jnp.bfloat16),
            pltpu.VMEM((pieces, heads, chips, count, pair_columns), jnp.bfloat16),
            pltpu.VMEM((pieces, chips, heads, count, pair_columns), jnp.bfloat16),
            pltpu.VMEM((heads, count, width), jnp.float32),
            pltpu.VMEM((heads, rows, width), jnp.bfloat16),
            pltpu.VMEM((heads, rows, width), jnp.bfloat16),
            pltpu.VMEM((rows, width), jnp.bfloat16),
            pltpu.SemaphoreType.DMA((pieces,)),
            pltpu.SemaphoreType.DMA((pieces,)),
            pltpu.SemaphoreType.DMA((pieces * chips,)),
            pltpu.SemaphoreType.DMA((pieces * chips,)),
            pltpu.SemaphoreType.DMA((pieces * heads,)),
            pltpu.SemaphoreType.DMA((pieces * heads,)),
            pltpu.SemaphoreType.DMA((items * blocks,)),
            pltpu.SemaphoreType.DMA((items * blocks,)),
            pltpu.SemaphoreType.DMA((items,)),
        ],
    )


def unproject(grad_queries, grad_pairs, weight, cosine, sine, moved, after, onward=None):
    heads, blocks = lax.axis_size("head"), lax.axis_size("blk")
    outs, out_specs, scratch = unproject_plan(grad_queries, grad_pairs, weight, moved)
    results, temps = len(outs), len(scratch)
    items = len(moved)
    vmem = pl.BlockSpec(memory_space=pltpu.VMEM)
    anywhere = pl.BlockSpec(memory_space=pl.ANY)
    norm_arrays, arrays, specs, more_outs, more_specs, more_scratch = [], [], [], [], [], []
    if onward is not None:
        *norm_arrays, (places, scale, matrices) = onward
        rows, width = norm_arrays[0].shape
        arrays, specs, more_outs, more_specs, more_scratch = dispatch_plan(
            jax.ShapeDtypeStruct((rows, width), jnp.bfloat16), places, scale, matrices, True
        )
        arrays, specs = arrays[1:], specs[1:]
        more_outs = [
            jax.ShapeDtypeStruct((rows, width), jnp.float32),
            jax.ShapeDtypeStruct((1, width), jnp.float32),
            *more_outs,
        ]
        more_specs = [vmem, vmem, *more_specs]
        more_scratch = [pltpu.VMEM((rows, width), jnp.bfloat16), *more_scratch]

    def kernel(*refs):
        given, refs = refs[: 5 + items], refs[5 + items + len(after) :]
        norm_refs, refs = refs[: len(norm_arrays)], refs[len(norm_arrays) :]
        dispatch_refs, refs = list(refs[: len(arrays)]), refs[len(arrays) :]
        made, refs = refs[:results], refs[results:]
        more, refs = refs[: len(more_outs)], refs[len(more_outs) :]
        unproject_kernel(heads, blocks, UNPROJECT_PIECES, items, *given, *made, *refs[:temps])
        if onward is None:
            return
        refs = refs[temps:]
        other_ref, valid_ref, gain_ref, scaled_ref, inverse_ref = norm_refs
        hidden_ref, grad_gain_ref, *more = more
        own_ref, *rest = refs
        grad = made[1][...]
        scaled = scaled_ref[...]
        grad_gain_ref[...] = jnp.sum(grad * scaled, axis=0, keepdims=True)
        grad = grad * gain_ref[...]
        grad = inverse_ref[:, :1] * (
            grad - scaled * jnp.mean(grad * scaled, axis=1, keepdims=True)
        )
        hidden = other_ref[...] + grad
        hidden_ref[...] = hidden
        own_ref[...] = (valid_ref[...] * hidden).astype(own_ref.dtype)
        for stage in dispatch_stages(
            heads, blocks, True, (own_ref, *dispatch_refs, *more, *rest)
        ):
            stage()

    values = pl.pallas_call(
        kernel,
        out_shape=[*outs, *more_outs],
        in_specs=[vmem] * 5
        + [anywhere] * (items + len(after))
        + [vmem] * len(norm_arrays)
        + specs,
        out_specs=[*out_specs, *more_specs],
        scratch_shapes=[*scratch, *more_scratch],
        compiler_params=pltpu.CompilerParams(
            collective_id=kernel_number(
                "unproject", onward is None, *(array.shape for array in (*moved, *after))
            ),
            has_side_effects=True,
            vmem_limit_bytes=60 * 1024 * 1024,
        ),
        cost_estimate=pl.CostEstimate(
            flops=0, bytes_accessed=(150 if onward is None else 320) << 20, transcendentals=0
        ),
        name="unproject",
    )(grad_queries, grad_pairs, weight, cosine, sine, *moved, *after, *norm_arrays, *arrays)
    return values[:results], values[results:]


def combine_stages(heads, blocks, by_columns, backward, refs):
    units_ref, shared_units_ref, place_ref, scale_ref, weight_ref, shared_weight_ref, *refs = refs
    if backward:
        gate_up_ref, grad_units_ref = units_ref, refs[0]
        sources, refs = refs[1:6], refs[6:]
    out_ref, returned_ref, *refs = refs
    if backward:
        grad_in_ref, grad_down_ref, gates_ref, *refs = refs
        units_ref, dots_ref, gate_part_ref, *held = refs[-10:]
        queue_ref, inner_ref, made_grad_ref, plane_ref, came_ref, late_sems, _ = held
        refs = refs[:-10]
    (
        made_ref,
        part_ref,
        landed_ref,
        relay_ref,
        held_ref,
        shared_held_ref,
        head_send,
        head_recv,
        blk_send,
        blk_recv,
        local_sems,
    ) = refs
    pieces = COMBINE_PIECES
    head, blk, head_peers, blk_peers = plane_peers(heads, blocks)
    rows, width = out_ref.shape
    slot = returned_ref.shape[1]
    shared = shared_units_ref.shape[0]
    step_width = width // pieces
    relay = heads == 4
    inner = jnp.logical_and(head > 0, head < heads - 1)
    loads = [
        pltpu.make_async_copy(weight_ref, held_ref, local_sems.at[0]),
        pltpu.make_async_copy(shared_weight_ref, shared_held_ref, local_sems.at[1]),
    ]
    gate_copies = []
    head_copies = []
    blk_copies = []
    late = []
    if backward:
        late = [
            pltpu.make_async_copy(source, target, late_sems.at[number])
            for number, (source, target) in enumerate(
                zip(sources, (queue_ref, inner_ref, made_grad_ref, plane_ref, came_ref))
            )
        ]

    def begin():
        for load in loads + late:
            load.start()
        if backward:
            half = grad_units_ref.shape[1]

            def turn(block, carry):
                rows_here = pl.ds(pl.multiple_of(block * slot, 16), slot)
                gate = gate_up_ref[rows_here, pl.ds(0, half)]
                up = gate_up_ref[rows_here, pl.ds(half, half)]
                grad = grad_units_ref[rows_here, :]
                share = 1.0 / (1.0 + jnp.exp(-gate))
                units_ref[rows_here, pl.ds(0, half)] = (
                    grad * up * share * (1.0 + gate * (1.0 - share))
                ).astype(units_ref.dtype)
                units_ref[rows_here, pl.ds(half, half)] = (grad * gate * share).astype(
                    units_ref.dtype
                )
                return carry

            lax.fori_loop(0, blocks, turn, 0)
        for load in loads:
            load.wait()

    def fill(number):
        if number == 1:
            for load in late:
                load.wait()
        piece = number - 1
        columns = pl.ds(piece * step_width, step_width)
        if 0 <= piece < pieces:
            grad_in_ref[columns, :] = dot_first(queue_ref[:, columns], units_ref[...]).astype(
                grad_in_ref.dtype
            )
            dots = dot_last(plane_ref[:, columns], came_ref[:, columns])
            if piece:
                dots = dots + dots_ref[...]
            dots_ref[...] = dots
        tile = 128
        if 0 <= piece < inner_ref.shape[1] // tile:
            lanes = pl.ds(piece * tile, tile)
            grad_down_ref[lanes, :] = dot_first(inner_ref[:, lanes], made_grad_ref[...]).astype(
                grad_down_ref.dtype
            )
        if piece == pieces:
            count = dots_ref.shape[1]
            shape = (gate_part_ref.shape[0], count)
            spread = jnp.where(
                lax.broadcasted_iota(jnp.int32, shape, 1) // slot
                == lax.broadcasted_iota(jnp.int32, shape, 0),
                1.0,
                0.0,
            ).astype(jnp.bfloat16)
            dots = dots_ref[...].astype(jnp.bfloat16) * place_ref[...]
            gate_part_ref[...] = dot_last(spread, dots)
            gates_ref[head] = gate_part_ref[...]
            gate_copies.extend(
                started(
                    remote(
                        gate_part_ref,
                        gates_ref.at[head],
                        (head_send, head_recv),
                        pieces * heads + index,
                        peer,
                    )
                )
                for index, peer in enumerate(head_peers)
            )

    def produce(piece):
        columns = pl.ds(piece * step_width, step_width)

        def make(block, carry):
            start = pl.multiple_of(block * slot, 16)
            made_ref[block, :, columns] = meet(
                units_ref[pl.ds(start, slot), :],
                weight_part(held_ref, columns, not by_columns),
                by_columns,
            ).astype(made_ref.dtype)
            return carry

        lax.fori_loop(0, blocks, make, 0)
        blk_copies.append(
            [
                started(
                    remote(
                        made_ref.at[peer[1], :, columns],
                        returned_ref.at[blk, :, columns],
                        (blk_send, blk_recv),
                        piece * (blocks - 1) + number,
                        peer,
                    )
                )
                for number, peer in enumerate(blk_peers)
            ]
        )
        returned_ref[blk, :, columns] = made_ref[blk, :, columns]
        for expert in range(shared):
            returned_ref[blocks + expert, :, columns] = meet(
                shared_units_ref[expert],
                weight_part(shared_held_ref.at[expert], columns, not by_columns),
                by_columns,
            ).astype(returned_ref.dtype)

    def far(peer):
        return jnp.abs(peer[0] - head) == heads - 1

    def peer_origin(peer):
        return lax.rem(2 * head + heads - peer[0], heads)

    def through_copy(piece, peer):
        columns = pl.ds(piece * step_width, step_width)
        return remote(
            part_ref.at[peer[0], :, columns],
            relay_ref.at[:, columns],
            (head_send, head_recv),
            piece * heads + heads - 1,
            (jnp.where(head == 0, 1, heads - 2), blk),
        )

    def gather(piece):
        columns = pl.ds(piece * step_width, step_width)
        for copy in blk_copies[piece]:
            copy.wait_recv()
        returned = returned_ref[:, :, columns].reshape((blocks + shared) * slot, step_width)
        if scale_ref is not None:
            returned = (returned.astype(jnp.float32) * scale_ref[...]).astype(returned_ref.dtype)

        def part(owner):
            start = pl.multiple_of(owner * rows, 16)
            return jnp.dot(
                place_ref[pl.ds(start, rows), :], returned, preferred_element_type=jnp.float32
            )

        sent = []
        for number, peer in enumerate(head_peers):
            part_ref[peer[0], :, columns] = part(peer[0]).astype(part_ref.dtype)
            copy = remote(
                part_ref.at[peer[0], :, columns],
                landed_ref.at[head, :, columns],
                (head_send, head_recv),
                piece * heads + number,
                peer,
            )
            sent.append(copy)
            if not relay:
                copy.start()
            elif number == 1:
                pl.when(jnp.logical_not(inner))(copy.start)
            else:
                distant = far(peer)
                pl.when(jnp.logical_not(distant))(copy.start)
                pl.when(distant)(through_copy(piece, peer).start)
        head_copies.append(sent)
        out_ref[:, columns] = part(head)

    def pass_on(piece):
        columns = pl.ds(piece * step_width, step_width)
        target = lax.rem(head + 2, heads)

        @pl.when(inner)
        def _():
            through_copy(piece, (target, blk)).wait_recv()
            part_ref[target, :, columns] = (
                part_ref[target, :, columns].astype(jnp.float32)
                + relay_ref[:, columns].astype(jnp.float32)
            ).astype(part_ref.dtype)
            head_copies[piece][1].start()

    def finish(piece):
        columns = pl.ds(piece * step_width, step_width)
        for number, peer in enumerate(head_peers):
            copy = head_copies[piece][number]

            def add(copy=copy, peer=peer):
                copy.wait_recv()
                out_ref[:, columns] += landed_ref[peer_origin(peer), :, columns].astype(
                    jnp.float32
                )

            if relay and number != 1:
                pl.when(jnp.logical_not(far((peer_origin(peer), blk))))(add)
            else:
                add()

    lag = 3 if relay else 2

    def step(number):
        if number < pieces:
            produce(number)
        if backward:
            fill(number)
        if 0 < number <= pieces:
            gather(number - 1)
        if relay and 1 < number <= pieces + 1:
            pass_on(number - 2)
        if number >= lag:
            finish(number - lag)

    def end():
        for piece, copies in enumerate(head_copies):
            for number, copy in enumerate(copies):
                if relay and number != 1:
                    distant = far(head_peers[number])
                    pl.when(jnp.logical_not(distant))(copy.wait_send)
                    pl.when(distant)(through_copy(piece, head_peers[number]).wait_send)
                else:
                    copy.wait_send()
        for copy in gate_copies:
            copy.wait()
        for copies in blk_copies:
            for copy in copies:
                copy.wait_send()

    steps = [functools.partial(step, number) for number in range(pieces + lag)]
    return [begin, *steps, end]


def combine_call(units, shared_units, places, scale, weights, by_columns, backward=None):
    heads, blocks = lax.axis_size("head"), lax.axis_size("blk")
    (own_weight, shared_weight) = weights
    shared, slot = shared_units.shape[:2]
    count = places.shape[0] // heads
    width = own_weight.shape[0 if by_columns else 1]
    pieces = COMBINE_PIECES
    vmem = pl.BlockSpec(memory_space=pltpu.VMEM)
    anywhere = pl.BlockSpec(memory_space=pl.ANY)
    scales = [] if scale is None else [scale]
    outs = [
        jax.ShapeDtypeStruct((count, width), jnp.float32),
        jax.ShapeDtypeStruct((blocks + shared, slot, width), jnp.bfloat16),
    ]
    scratch = [
        pltpu.VMEM((blocks, slot, width), jnp.bfloat16),
        pltpu.VMEM((heads, count, width), jnp.bfloat16),
        pltpu.VMEM((heads, count, width), jnp.bfloat16),
        pltpu.VMEM((count, width), jnp.bfloat16),
        pltpu.VMEM(own_weight.shape, jnp.bfloat16),
        pltpu.VMEM(shared_weight.shape, jnp.bfloat16),
        pltpu.SemaphoreType.DMA(((pieces + 1) * heads,)),
        pltpu.SemaphoreType.DMA(((pieces + 1) * heads,)),
        pltpu.SemaphoreType.DMA((pieces * (blocks - 1),)),
        pltpu.SemaphoreType.DMA((pieces * (blocks - 1),)),
        pltpu.SemaphoreType.DMA((2,)),
    ]
    arrays = [units, shared_units, places, *scales, own_weight, shared_weight]
    specs = [vmem] * (3 + len(scales)) + [anywhere] * 2
    if backward is not None:
        grad_units, *late = backward
        arrays += [grad_units, *late]
        specs += [vmem] + [anywhere] * len(late)
        inner = late[1].shape[1]
        gate_rows = -(-(blocks + shared) // 8) * 8
        outs += [
            jax.ShapeDtypeStruct((width, units.shape[1]), jnp.bfloat16),
            jax.ShapeDtypeStruct((inner, width), jnp.bfloat16),
            jax.ShapeDtypeStruct((heads, gate_rows, places.shape[0]), jnp.float32),
        ]
        scratch += [
            pltpu.VMEM(units.shape, jnp.bfloat16),
            pltpu.VMEM(places.shape, jnp.float32),
            pltpu.VMEM((gate_rows, places.shape[0]), jnp.float32),
            *(pltpu.VMEM(array.shape, array.dtype) for array in late),
            pltpu.SemaphoreType.DMA((len(late),)),
            pltpu.SemaphoreType.DMA,
        ]
    return (
        ("combine", by_columns, scale is not None, backward is not None),
        functools.partial(combine_stages, heads, blocks, by_columns, backward is not None),
        arrays,
        specs,
        outs,
        [vmem] * len(outs),
        scratch,
        scale is not None,
    )


def depart(plan, other, valid, gain, scaled, inverse, gates, router, after):
    heads, blocks = lax.axis_size("head"), lax.axis_size("blk")
    key, maker, arrays, specs, outs, out_specs, scratch, _ = plan
    count, width = other.shape
    matrix = outs[2]
    matrix_rows = matrix.shape[0] // blocks
    inputs, results, temps = len(arrays), len(outs), len(scratch)
    vmem = pl.BlockSpec(memory_space=pltpu.VMEM)
    anywhere = pl.BlockSpec(memory_space=pl.ANY)
    more_outs = [
        jax.ShapeDtypeStruct((count, width), jnp.float32),
        jax.ShapeDtypeStruct((1, width), jnp.float32),
        jax.ShapeDtypeStruct((heads, count, width), jnp.bfloat16),
        jax.ShapeDtypeStruct((blocks, matrix_rows, matrix.shape[1]), matrix.dtype),
    ]

    def kernel(*refs):
        head, blk, head_peers, blk_peers = plane_peers(heads, blocks)
        greet(head_peers + blk_peers)
        given, refs = list(refs[:inputs]), refs[inputs:]
        other_ref, valid_ref, gain_ref, scaled_ref, inverse_ref, gates_ref, *refs = refs
        router_ref, *refs = refs
        refs = refs[len(after) :]
        made, refs = refs[:results], refs[results:]
        total_ref, _, matrix_ref, _, came_gates_ref = made
        middle_ref, grad_gain_ref, plane_ref, moved_ref, *refs = refs
        temp, refs = refs[:temps], refs[temps:]
        own_ref, row_send, row_recv, moved_send, moved_recv, moved_sem = refs
        given.insert(3, None)
        moved = []
        for number, stage in enumerate(maker([*given, *made, *temp])):
            stage()
            if number == COMBINE_PIECES + 1:
                moved = [
                    started(
                        remote(
                            matrix_ref.at[
                                pl.ds(pl.multiple_of(peer[1] * matrix_rows, 16), matrix_rows)
                            ],
                            moved_ref.at[blk],
                            (moved_send, moved_recv),
                            index,
                            peer,
                        )
                    )
                    for index, peer in enumerate(blk_peers)
                ]
                place = pl.ds(pl.multiple_of(blk * matrix_rows, 16), matrix_rows)
                moved.append(
                    started(
                        pltpu.make_async_copy(matrix_ref.at[place], moved_ref.at[blk], moved_sem)
                    )
                )
        mine = pl.ds(pl.multiple_of(head * count, 128), count)
        grad_gates = came_gates_ref[:, :, mine].reshape(-1, count).T
        shares = gates_ref[...]
        grad_logits = shares * (
            grad_gates - jnp.sum(shares * grad_gates, axis=1, keepdims=True)
        )
        grad = total_ref[...] + jnp.dot(
            grad_logits.astype(jnp.bfloat16), router_ref[...], preferred_element_type=jnp.float32
        )
        scaled = scaled_ref[...]
        grad_gain_ref[...] = jnp.sum(grad * scaled, axis=0, keepdims=True)
        grad = grad * gain_ref[...]
        grad = inverse_ref[:, :1] * (
            grad - scaled * jnp.mean(grad * scaled, axis=1, keepdims=True)
        )
        middle = other_ref[...] + grad
        middle_ref[...] = middle
        own = (valid_ref[...] * middle).astype(own_ref.dtype)
        own_ref[...] = own
        plane_ref[head] = own
        relayed_gather(heads, head, blk, head_peers, own_ref, plane_ref, (row_send, row_recv), 0)
        for copy in moved:
            copy.wait()

    values = pl.pallas_call(
        kernel,
        out_shape=[*outs, *more_outs],
        in_specs=[*specs, *([vmem] * 7), *([anywhere] * len(after))],
        out_specs=[*out_specs, *([vmem] * 3), anywhere],
        scratch_shapes=[
            *scratch,
            pltpu.VMEM((count, width), jnp.bfloat16),
            pltpu.SemaphoreType.DMA((RELAY_PIECES * heads,)),
            pltpu.SemaphoreType.DMA((RELAY_PIECES * heads,)),
            pltpu.SemaphoreType.DMA((blocks,)),
            pltpu.SemaphoreType.DMA((blocks,)),
            pltpu.SemaphoreType.DMA,
        ],
        compiler_params=pltpu.CompilerParams(
            collective_id=kernel_number("depart", key, *(array.shape for array in after)),
            has_side_effects=True,
            vmem_limit_bytes=60 * 1024 * 1024,
        ),
        cost_estimate=pl.CostEstimate(flops=0, bytes_accessed=330 << 20, transcendentals=0),
        name="depart",
    )(*arrays, other, valid, gain, scaled, inverse, gates, router, *after)
    return values[:results], values[results:]


def settle(summed, swapped, gains, after):
    heads, blocks = lax.axis_size("head"), lax.axis_size("blk")
    chips = blocks // 2
    arrays = [array.reshape((chips, 2) + array.shape[1:]) for array in summed]
    halves = [(chips,) + array.shape[2:] for array in arrays]
    count = len(arrays)
    vmem = pl.BlockSpec(memory_space=pltpu.VMEM)
    anywhere = pl.BlockSpec(memory_space=pl.ANY)
    outs = [
        jax.ShapeDtypeStruct(halves[0][1:], jnp.bfloat16),
        *(jax.ShapeDtypeStruct(half[1:], jnp.float32) for half in halves[1:]),
        *(jax.ShapeDtypeStruct(array.shape, array.dtype) for array in swapped),
        jax.ShapeDtypeStruct(gains.shape[1:], jnp.float32),
    ]
    out_specs = [vmem] * count + [anywhere] * len(swapped) + [vmem]

    def kernel(*refs):
        head, blk, head_peers, blk_peers = plane_peers(heads, blocks)
        chip, core = blk // 2, lax.rem(blk, 2)
        sibling = (head, chip * 2 + 1 - core)
        chip_peers = [(head, lax.rem(chip + step, chips) * 2 + core) for step in range(1, chips)]
        greet(head_peers + blk_peers)
        sources, refs = refs[:count], refs[count:]
        swap_refs, refs = refs[: len(swapped)], refs[len(swapped) :]
        gains_ref, refs = refs[0], refs[1 + len(after) :]
        made, refs = refs[:count], refs[count:]
        swap_outs, refs = refs[: len(swapped)], refs[len(swapped) :]
        gains_out, refs = refs[0], refs[1:]
        near, refs = refs[:count], refs[count:]
        sums, refs = refs[:count], refs[count:]
        far, refs = refs[:count], refs[count:]
        total_ref, gains_near, gains_sum, *sems = refs
        near_sems, chip_sems, head_sems, gain_sems, row_sems = zip(sems[0:5], sems[5:10])
        local_sems = sems[10]
        near_copies = [
            started(
                remote(
                    sources[item].at[:, 1 - core], near[item], near_sems, item, sibling
                )
            )
            for item in range(count)
        ]
        gain_copies = [
            started(
                remote(
                    gains_ref.at[peer[0]], gains_near.at[head], gain_sems, number, peer
                )
            )
            for number, peer in enumerate(head_peers)
        ]
        others = []
        for item in range(len(swapped)):
            others += [
                started(
                    remote(
                        swap_refs[item].at[peer[0]],
                        swap_outs[item].at[head],
                        head_sems,
                        (item + 1) * heads + number,
                        peer,
                    )
                )
                for number, peer in enumerate(head_peers)
            ]
            others.append(
                started(
                    pltpu.make_async_copy(
                        swap_refs[item].at[head], swap_outs[item].at[head], local_sems.at[item]
                    )
                )
            )
        chip_copies = []
        for item in range(count):
            near_copies[item].wait_recv()
            sums[item][...] = (
                sources[item][:, core].astype(jnp.float32) + near[item][...].astype(jnp.float32)
            ).astype(jnp.bfloat16)
            chip_copies.append(
                [
                    started(
                        remote(
                            sums[item].at[peer[1] // 2],
                            far[item].at[chip],
                            chip_sems,
                            item * chips + number,
                            peer,
                        )
                    )
                    for number, peer in enumerate(chip_peers)
                ]
            )
        total = gains_ref[head]
        for number, peer in enumerate(head_peers):
            gain_copies[number].wait_recv()
            total = total + gains_near[lax.rem(2 * head + heads - peer[0], heads)]
        gains_sum[...] = total
        row_copies = [
            started(
                remote(gains_sum.at[peer[1]], gains_out.at[blk], row_sems, number, peer)
            )
            for number, peer in enumerate(blk_peers)
        ]
        gains_out[blk] = gains_sum[blk]
        head_copies = []
        for item in range(count):
            for copy in chip_copies[item]:
                copy.wait_recv()
            total = sums[item][chip].astype(jnp.float32)
            for peer in chip_peers:
                total = total + far[item][peer[1] // 2].astype(jnp.float32)
            if item:
                made[item][...] = total
                continue
            total_ref[...] = total.astype(total_ref.dtype)
            head_copies = [
                started(
                    remote(
                        total_ref.at[peer[0]], made[0].at[head], head_sems, number, peer
                    )
                )
                for number, peer in enumerate(head_peers)
            ]
            made[0][head] = total_ref[head]
        for copy in head_copies + others + row_copies:
            copy.wait()
        for copy in near_copies + gain_copies:
            copy.wait_send()
        for copies in chip_copies:
            for copy in copies:
                copy.wait_send()

    sems = [
        pltpu.SemaphoreType.DMA((count,)),
        pltpu.SemaphoreType.DMA((count * chips,)),
        pltpu.SemaphoreType.DMA(((1 + len(swapped)) * heads,)),
        pltpu.SemaphoreType.DMA((heads,)),
        pltpu.SemaphoreType.DMA((blocks,)),
    ]
    results = pl.pallas_call(
        kernel,
        out_shape=outs,
        in_specs=[vmem] * count + [anywhere] * len(swapped) + [vmem] + [anywhere] * len(after),
        out_specs=out_specs,
        scratch_shapes=[
            *(pltpu.VMEM(half, jnp.bfloat16) for half in halves),
            *(pltpu.VMEM(half, jnp.bfloat16) for half in halves),
            *(pltpu.VMEM(half, jnp.bfloat16) for half in halves),
            pltpu.VMEM(halves[0][1:], jnp.bfloat16),
            pltpu.VMEM(gains.shape, jnp.float32),
            pltpu.VMEM(gains.shape[1:], jnp.float32),
            *sems,
            *sems,
            pltpu.SemaphoreType.DMA((max(1, len(swapped)),)),
        ],
        compiler_params=pltpu.CompilerParams(
            collective_id=kernel_number("settle"),
            has_side_effects=True,
            vmem_limit_bytes=56 * 1024 * 1024,
        ),
        cost_estimate=pl.CostEstimate(flops=0, bytes_accessed=100 << 20, transcendentals=0),
        name="settle",
    )(*arrays, *swapped, gains, *after)
    return results[:count], results[count:-1], results[-1]


def head_parts(partial):
    heads = lax.axis_size("head")
    return partial.astype(jnp.bfloat16).reshape(heads, -1, partial.shape[-1])


def head_sum(parts):
    return jnp.sum(parts.astype(jnp.float32), axis=0)


def dot_last(left, right):
    return lax.dot_general(
        left, right, (((1,), (1,)), ((), ())), preferred_element_type=jnp.float32
    )


def dot_first(left, right):
    return lax.dot_general(
        left, right, (((0,), (0,)), ((), ())), preferred_element_type=jnp.float32
    )


def head_columns(ref, rows, first, group, shift):
    pieces = []
    for member in range(group):
        start = (first + member) * HEAD_SIZE
        piece = ref[0, rows, start : start + HEAD_SIZE]
        empty = jnp.zeros_like(piece)
        pieces.append(jnp.concatenate([empty, piece] if shift else [piece, empty], axis=1))
    return jnp.concatenate(pieces, axis=0)


def unit_scores(queries, pairs, blk, resident, chunk):
    scores = dot_last(queries, pairs) * 0.125
    count, keys = scores.shape
    places = lax.broadcasted_iota(jnp.int32, (count, chunk), 1)
    own = blk * resident + lax.broadcasted_iota(jnp.int32, (count, chunk), 0) % resident
    last = jnp.where(places <= own, scores[:, keys - chunk :], negative)
    if keys > chunk:
        scores = jnp.concatenate([scores[:, : keys - chunk], last], axis=1)
    else:
        scores = last
    exponents = jnp.exp(scores - jnp.max(scores, axis=1, keepdims=True))
    return (exponents, jnp.sum(exponents, axis=1, keepdims=True))


def attend_kernel(heads, blocks, resident, group, kv_local, info_ref, query_ref, pair_ref, out_ref):
    slot_index = pl.program_id(0)
    blk = info_ref[0]
    length = info_ref[1 + slot_index]
    chunk = blocks * resident
    for head in range(heads):
        rows = pl.ds(head * resident, resident)
        live = head * chunk + blk * resident < length

        @pl.when(live)
        def _(head=head, rows=rows):
            keys = (head + 1) * chunk
            for kv_head in range(kv_local):
                lanes = pl.ds(kv_head * 2 * HEAD_SIZE, 2 * HEAD_SIZE)
                pairs = pair_ref[0, pl.ds(0, keys), lanes]
                queries = head_columns(query_ref, rows, kv_head * group, group, False)
                exponents, totals = unit_scores(queries, pairs, blk, resident, chunk)
                weighted = jnp.dot(
                    exponents.astype(jnp.bfloat16), pairs, preferred_element_type=jnp.float32
                )
                weighted = weighted / totals
                for member in range(group):
                    start = (kv_head * group + member) * HEAD_SIZE
                    out_ref[head, 0, :, start : start + HEAD_SIZE] = weighted[
                        member * resident : (member + 1) * resident, HEAD_SIZE:
                    ].astype(out_ref.dtype)

        @pl.when(jnp.logical_not(live))
        def _(head=head):
            out_ref[head, 0] = jnp.zeros(out_ref.shape[2:], out_ref.dtype)


def attend_back_kernel(
    heads,
    blocks,
    resident,
    group,
    kv_local,
    info_ref,
    query_ref,
    pair_ref,
    grad_ref,
    grad_query_ref,
    grad_pair_ref,
    total_ref,
):
    slot_index = pl.program_id(0)
    blk = info_ref[0]
    length = info_ref[1 + slot_index]
    chunk = blocks * resident
    total_ref[...] = jnp.zeros_like(total_ref)
    for head in range(heads):
        rows = pl.ds(head * resident, resident)
        live = head * chunk + blk * resident < length

        @pl.when(live)
        def _(head=head, rows=rows):
            keys = (head + 1) * chunk
            for kv_head in range(kv_local):
                lanes = pl.ds(kv_head * 2 * HEAD_SIZE, 2 * HEAD_SIZE)
                pairs = pair_ref[0, pl.ds(0, keys), lanes]
                queries = head_columns(query_ref, rows, kv_head * group, group, False)
                grads = head_columns(grad_ref, rows, kv_head * group, group, True)
                exponents, totals = unit_scores(queries, pairs, blk, resident, chunk)
                probabilities = exponents * (1.0 / totals)
                grad_probs = dot_last(grads, pairs)
                delta = jnp.sum(probabilities * grad_probs, axis=1, keepdims=True)
                grad_scores = (probabilities * (grad_probs - delta)).astype(jnp.bfloat16)
                grad_queries = 0.125 * jnp.dot(
                    grad_scores, pairs, preferred_element_type=jnp.float32
                )
                for member in range(group):
                    start = (kv_head * group + member) * HEAD_SIZE
                    grad_query_ref[0, rows, start : start + HEAD_SIZE] = grad_queries[
                        member * resident : (member + 1) * resident, :HEAD_SIZE
                    ].astype(grad_query_ref.dtype)
                total_ref[pl.ds(0, keys), lanes] += dot_first(
                    grad_scores, queries * jnp.bfloat16(0.125)
                ) + dot_first(probabilities.astype(jnp.bfloat16), grads)

        @pl.when(jnp.logical_not(live))
        def _(rows=rows):
            grad_query_ref[0, rows, :] = jnp.zeros(
                (resident, grad_query_ref.shape[2]), grad_query_ref.dtype
            )

    grad_pair_ref[0] = total_ref[...].astype(grad_pair_ref.dtype)


def plan_kernel(heads, experts_local, slot, info_ref, routes_ref, ranks_ref, chosen_ref, place_ref, turned_ref):
    routes = routes_ref[0]
    ranks = ranks_ref[0]
    tokens = routes.shape[1]
    count = place_ref.shape[2]
    first = info_ref[0] * experts_local
    lanes = 128
    room = -(-experts_local // 8) * 8
    named = []
    for lane in range(lanes):
        plane, expert = lane // room, lane % room
        if plane < heads and expert < experts_local:
            hit = jnp.where(routes == plane * experts_local + expert, 1, 0)
            named.append(jnp.max(hit, axis=0, keepdims=True))
        else:
            named.append(jnp.zeros((1, tokens), jnp.int32))
    chosen_ref[0] = jnp.concatenate(named, axis=0).astype(jnp.float32).T
    marks = [
        jnp.sum(
            jnp.where((routes == first + expert) & (ranks < CAP), ranks + 1, 0),
            axis=0,
            keepdims=True,
        )
        for expert in range(experts_local)
    ]
    marks.append(jnp.zeros((lanes - experts_local, tokens), jnp.int32))
    marks = jnp.concatenate(marks, axis=0).astype(jnp.float32)
    slot_rows = tokens // heads

    def fits(shape, row_axis, wide):
        row = lax.broadcasted_iota(jnp.int32, shape, row_axis)
        token = lax.broadcasted_iota(jnp.int32, shape, 1 - row_axis)
        inside = row % slot
        same = (inside // CAP == token // slot_rows) & (wide.astype(jnp.int32) == inside % CAP + 1)
        return jnp.where(same, 1.0, 0.0).astype(jnp.bfloat16)

    def spread(shape, row_axis):
        row = lax.broadcasted_iota(jnp.int32, shape, row_axis)
        expert = lax.broadcasted_iota(jnp.int32, shape, 1 - row_axis)
        return jnp.where(row // slot == expert, 1.0, 0.0).astype(jnp.bfloat16)

    place_ref[0] = fits(
        (tokens, count),
        1,
        jnp.dot(
            marks.T.astype(jnp.bfloat16),
            spread((lanes, count), 1),
            preferred_element_type=jnp.float32,
        ),
    )
    turned_ref[0] = fits(
        (count, tokens),
        0,
        jnp.dot(
            spread((count, lanes), 0),
            marks.astype(jnp.bfloat16),
            preferred_element_type=jnp.float32,
        ),
    )


def plans(heads, experts_local, slot, head_index, routes, ranks):
    layers, top, tokens = routes.shape
    count = experts_local * slot

    def spec(*shape):
        return pl.BlockSpec((1,) + shape, lambda layer, info: (layer, 0, 0))

    chosen, places, turned = pl.pallas_call(
        functools.partial(plan_kernel, heads, experts_local, slot),
        grid_spec=pltpu.PrefetchScalarGridSpec(
            num_scalar_prefetch=1,
            grid=(layers,),
            in_specs=[spec(top, tokens)] * 2,
            out_specs=[spec(tokens, 128), spec(tokens, count), spec(count, tokens)],
        ),
        out_shape=[
            jax.ShapeDtypeStruct((layers, tokens, 128), jnp.float32),
            jax.ShapeDtypeStruct((layers, tokens, count), jnp.bfloat16),
            jax.ShapeDtypeStruct((layers, count, tokens), jnp.bfloat16),
        ],
        compiler_params=pltpu.CompilerParams(vmem_limit_bytes=40 * 1024 * 1024),
        cost_estimate=pl.CostEstimate(flops=0, bytes_accessed=16 << 20, transcendentals=0),
        name="plans",
    )(head_index[None].astype(jnp.int32), routes, ranks)
    gate_lanes = heads * -(-experts_local // 8) * 8
    return chosen[0, :, :gate_lanes] > 0.0, places[0], turned[0]


def attention_call(kernel, info, arrays, outs, scratch, flops, name):
    def spec(array):
        shape = array.shape
        if len(shape) == 4:
            return pl.BlockSpec(
                (shape[0], 1) + shape[2:], lambda slot, info: (0, slot, 0, 0)
            )
        return pl.BlockSpec((1,) + shape[1:], lambda slot, info: (slot, 0, 0))

    return pl.pallas_call(
        kernel,
        grid_spec=pltpu.PrefetchScalarGridSpec(
            num_scalar_prefetch=1,
            grid=(SEQUENCE_SLOTS,),
            in_specs=[spec(array) for array in arrays],
            out_specs=[spec(array) for array in outs],
            scratch_shapes=scratch,
        ),
        out_shape=outs,
        compiler_params=pltpu.CompilerParams(vmem_limit_bytes=56 * 1024 * 1024),
        cost_estimate=pl.CostEstimate(
            flops=flops, bytes_accessed=8 << 20, transcendentals=flops // 256
        ),
        name=name,
    )(info, *arrays)


def shards(
    tokens,
    lengths,
    routes,
    queue_ranks,
    query_key_value_weight,
    w_out,
    router,
    norm_gains,
    w_in,
    w_down,
    cotangent,
):
    kernel_numbers.clear()
    heads_count = lax.axis_size("head")
    blocks_count = lax.axis_size("blk")
    head_index = lax.axis_index("head")
    blk_index = lax.axis_index("blk")
    resident = tokens.shape[1]
    width = tokens.shape[2]
    weight_rows = w_out.shape[1]
    rows_local = heads_count * resident
    keys_total = blocks_count * rows_local
    kv_local = KEY_VALUE_HEADS // heads_count
    group = QUERY_HEAD_COUNT // KEY_VALUE_HEADS
    query_columns = kv_local * group * HEAD_SIZE
    pair_columns = kv_local * 2 * HEAD_SIZE
    slot_rows = SEQUENCE_SLOTS * resident
    all_tokens = heads_count * slot_rows
    experts_local = EXPERTS // heads_count
    owned = experts_local // blocks_count
    owned_total = owned * blocks_count
    slot = -(-heads_count * CAP // 16) * 16
    half = HEAD_SIZE // 2

    own_places = (head_index * blocks_count + blk_index) * resident + jnp.arange(
        resident, dtype=jnp.int32
    )
    valid_column = (
        (own_places[None, :] < lengths[:, None]).astype(jnp.float32).reshape(slot_rows, 1)
    )
    plane_ids = jnp.arange(all_tokens, dtype=jnp.int32)
    plane_places = (
        (plane_ids // slot_rows * blocks_count + blk_index) * resident + plane_ids % resident
    ).astype(jnp.float32)
    frequency = jnp.exp(jnp.arange(half, dtype=jnp.float32) * (-2.0 * theta_log / HEAD_SIZE))
    angles = plane_places[:, None] * frequency[None, :]
    cosine = jnp.cos(angles)
    sine = jnp.sin(angles)
    repeats = 2 * HEAD_SIZE // half
    tile_cosine = jnp.concatenate([cosine] * repeats, axis=1).reshape(heads_count, slot_rows, -1)
    tile_sine = jnp.concatenate([-sine, sine] * (repeats // 2), axis=1)
    tile_sine = tile_sine.reshape(heads_count, slot_rows, -1)
    info = jnp.concatenate([blk_index[None].astype(jnp.int32), lengths])

    row_ids = jnp.arange(experts_local * slot, dtype=jnp.int32)
    spread = (
        row_ids[None, :] // slot == jnp.arange(experts_local, dtype=jnp.int32)[:, None]
    ).astype(jnp.bfloat16)
    def to_experts(rows):
        rows = rows.reshape(experts_local, slot, width)
        own = None
        if owned:
            own = rows[:owned_total].reshape(blocks_count, owned * slot, width)
            own = lax.all_to_all(own, "blk", 0, 0, tiled=True)
            own = own.reshape(blocks_count, owned, slot, width).transpose(1, 0, 2, 3)
            own = own.reshape(owned, blocks_count * slot, width)
        return (own, rows[owned_total:])

    def from_experts(own, shared):
        parts = [shared]
        if owned:
            own = own.reshape(owned, blocks_count, slot, width).transpose(1, 0, 2, 3)
            own = own.reshape(blocks_count, owned * slot, width)
            own = lax.all_to_all(own, "blk", 0, 0, tiled=True)
            parts = [own.reshape(owned_total, slot, width), shared]
        return jnp.concatenate(parts, axis=0).reshape(experts_local * slot, width)

    def shared_weights(layer_index, reached):
        if owned_total == experts_local:
            return []
        parts = tuple(matrix[layer_index, owned_total:] for matrix in (w_in, w_down))
        parts, _ = lax.optimization_barrier((parts, reached))
        return [tuple(lax.all_gather(part, "blk", axis=1, tiled=True) for part in parts)]

    def to_owner(matrix, layer_index):
        if not owned:
            return []
        if owned == 1:
            return [("blk_swap", matrix, layer_index)]
        pieces = matrix[layer_index, :owned_total]
        return [("blk_swap", pieces.reshape((blocks_count, owned) + pieces.shape[1:]))]

    def owned_matrix(received):
        if not owned:
            return None
        columns = received.shape[-1]
        pieces = received.reshape(blocks_count, owned, -1, columns)
        return pieces.transpose(1, 0, 2, 3).reshape(owned, -1, columns)

    def from_owner(term):
        if not owned:
            return []
        columns = term.shape[-1]
        pieces = term.reshape(owned, blocks_count, -1, columns).transpose(1, 0, 2, 3)
        return [("blk_swap", pieces)]

    def owned_rows(received):
        if not owned:
            return []
        return [received.reshape(owned_total, -1, received.shape[-1])]

    staged = owned == 1 and owned_total < experts_local

    def matrices(sets, which):
        own_weight, shared_weight = (mats[which] for mats in sets)
        return (own_weight[0], shared_weight)

    def unpack_in(results):
        plane, own, shared, own_out, shared_out = results
        return (
            plane.reshape(all_tokens, width),
            [own.reshape(1, -1, width), shared],
            [own_out[None], shared_out],
        )

    def unpack_out(results):
        total, returned, *extras = results
        return (total, returned.reshape(-1, width), *extras)

    def moe_in(rows, turned_places, scale, sets, which, after=()):
        if staged:
            plan = dispatch_call(rows, turned_places, scale, matrices(sets, which), which == 1)
            return unpack_in(staged_call([plan], "dispatch", 170, after)[0])
        (plane,) = exchange(("head_gather", rows))
        plane = plane.reshape(all_tokens, width)
        queues = mm("rt,td->rd", turned_places, plane)
        if scale is not None:
            queues = queues * scale
        queues = [part for part in to_experts(queues.astype(jnp.bfloat16)) if part is not None]
        spec = ("erd,edf->erf", "erd,efd->erf")[which]
        return (plane, queues, [mm(spec, rows, mats[which]) for rows, mats in zip(queues, sets)])

    def moe_out(units, places, scale, sets):
        if staged:
            plan = combine_call(
                units[0][0], units[1], places, scale, matrices(sets, 1), False
            )
            return unpack_out(staged_call([plan], "combine", 170)[0])
        made = [
            mm("erf,efd->erd", part, mats[1]).astype(jnp.bfloat16)
            for part, mats in zip(units, sets)
        ]
        returned = from_experts(*(made if owned else [None] + made))
        rows = (returned.astype(jnp.float32) * scale).astype(jnp.bfloat16)
        (parts,) = exchange(("head_swap", head_parts(mm("tr,rd->td", places, rows))))
        return (head_sum(parts), returned)

    def moe_back(
        places, sets, gate_up, grad_units, incoming, units, grad_rows, plane_grads, came, onward
    ):
        grad_gate_up = [
            gated_back(*parts) if number or not staged else None
            for number, parts in enumerate(zip(gate_up, grad_units))
        ]
        grad_weights = [
            (
                mm("erd,erf->edf", rows, grads).astype(jnp.bfloat16),
                mm("erf,erd->efd", inner, out_grads).astype(jnp.bfloat16),
            )
            if grads is not None
            else None
            for rows, grads, inner, out_grads in zip(incoming, grad_gate_up, units, grad_rows)
        ]
        if staged:
            plan = combine_call(
                gate_up[0][0],
                grad_gate_up[1],
                places,
                None,
                matrices(sets, 0),
                True,
                [grad_units[0][0], incoming[0][0], units[0][0], grad_rows[0][0], plane_grads, came],
            )
            further = []
            if fused:
                (total, _, grad_in, grad_down, gates), further = depart(
                    plan, *onward, grad_weights[1]
                )
            else:
                total, _, grad_in, grad_down, gates = staged_call([plan], "combine_back", 170)[0]
            grad_weights[0] = (grad_in[None], grad_down[None])
            gates = gates.reshape(gate_lanes, all_tokens)
            return (total, gates, grad_weights, further)
        pair_dots = (mm("td,rd->tr", plane_grads, came) * places).astype(jnp.bfloat16)
        made = [
            mm("erf,edf->erd", part, mats[0]).astype(jnp.bfloat16)
            for part, mats in zip(grad_gate_up, sets)
        ]
        returned = from_experts(*(made if owned else [None] + made))
        parts, gates = exchange(
            ("head_swap", head_parts(mm("tr,rd->td", places, returned))),
            ("head_gather", mm("tr,er->te", pair_dots, spread).T),
        )
        gates = by_plane(gates.reshape(EXPERTS, all_tokens), 0)
        return (head_sum(parts), gates, grad_weights, [])

    def moe_turn(units, places, turned_places, scale, grad_rows, sets):
        if not staged:
            return (
                moe_out(units, places, scale, sets),
                moe_in(grad_rows, turned_places, scale, sets, 1),
            )
        weights = matrices(sets, 1)
        out_plan = combine_call(units[0][0], units[1], places, scale, weights, False)
        in_plan = dispatch_call(grad_rows, turned_places, scale, weights, True)
        out_results, in_results = staged_call([out_plan, in_plan], "turn", 260)
        return (unpack_out(out_results), unpack_in(in_results))

    def gated(gate_up):
        return (jax.nn.silu(gate_up[..., :FF]) * gate_up[..., FF:]).astype(jnp.bfloat16)

    def gated_back(gate_up, grad_units):
        gate_part = gate_up[..., :FF]
        up_part = gate_up[..., FF:]
        sigmoid_part = jax.nn.sigmoid(gate_part)
        return jnp.concatenate(
            [
                grad_units * up_part * sigmoid_part * (1.0 + gate_part * (1.0 - sigmoid_part)),
                grad_units * gate_part * sigmoid_part,
            ],
            axis=-1,
        ).astype(jnp.bfloat16)

    def by_slot(rows):
        return (
            rows.reshape(heads_count, SEQUENCE_SLOTS, resident, -1)
            .transpose(1, 0, 2, 3)
            .reshape(SEQUENCE_SLOTS, rows_local, -1)
        )

    def by_head(rows):
        return (
            rows.reshape(SEQUENCE_SLOTS, heads_count, resident, -1)
            .transpose(1, 0, 2, 3)
            .reshape(all_tokens, -1)
        )

    small_columns = 128
    room = -(-experts_local // 8) * 8
    gate_lanes = heads_count * room

    def by_plane(values, axis):
        shape = values.shape
        values = values.reshape(shape[:axis] + (heads_count, experts_local) + shape[axis + 1 :])
        pads = [(0, 0)] * values.ndim
        pads[axis + 1] = (0, room - experts_local)
        return jnp.pad(values, pads).reshape(shape[:axis] + (gate_lanes,) + shape[axis + 1 :])

    send = []
    for layer_index in range(DECODER_LAYERS):
        weight = query_key_value_weight[layer_index]
        split = QUERY_HEAD_COUNT * HEAD_SIZE
        small = jnp.concatenate(
            [by_plane(router[layer_index], 1), norm_gains[layer_index].T], axis=1
        )
        small = jnp.pad(small, ((0, 0), (0, small_columns - small.shape[1])))
        send.append(
            jnp.concatenate(
                [
                    weight[:, :split]
                    .reshape(weight_rows, heads_count, query_columns)
                    .transpose(1, 0, 2),
                    weight[:, split:]
                    .reshape(weight_rows, heads_count, pair_columns)
                    .transpose(1, 0, 2),
                    jnp.broadcast_to(small[None], (heads_count,) + small.shape),
                ],
                axis=-1,
            )
        )
    plan = jnp.stack([routes, queue_ranks]).reshape(2 * DECODER_LAYERS, slot_rows, TOP)
    plan = plan.transpose(0, 2, 1).reshape(2 * DECODER_LAYERS * TOP, slot_rows)
    plan, first_send = exchange(("head_gather", plan), ("head_swap", send[0]))
    plan = plan.reshape(heads_count, 2, DECODER_LAYERS, TOP, slot_rows)
    plan = plan.transpose(1, 2, 3, 0, 4).reshape(2, DECODER_LAYERS, TOP, all_tokens)

    def attention_set(wide, out_full):
        wide = wide.transpose(1, 0, 2, 3).reshape(width, -1)
        small = wide[:, query_columns + pair_columns :]
        small = small.T
        gains = small[gate_lanes : gate_lanes + 2].astype(jnp.float32)
        return (wide, out_full.reshape(-1, width), small[:gate_lanes], gains)

    wide, first_out, *next_sends = exchange(
        ("blk_pairs", first_send),
        ("blk_pairs", w_out[0]),
        *(("head_swap", array) for array in send[1:]),
    )
    attention_weights = [
        attention_set(wide, first_out),
    ]
    for layer_index, array in enumerate(next_sends, start=1):
        attention_weights.append(
            attention_set(
                lax.all_gather(array, "blk", axis=0),
                lax.all_gather(w_out[layer_index], "blk", axis=0),
            )
        )

    hidden = tokens.reshape(slot_rows, width).astype(jnp.float32)
    stored_all = []
    for layer_index in range(DECODER_LAYERS):
        qkv_full, out_full, router_full, gains = attention_weights[layer_index]
        layer = slice(layer_index, layer_index + 1)
        chosen, places, turned_places = plans(
            heads_count, experts_local, slot, head_index, plan[0, layer], plan[1, layer]
        )
        next_layer = layer_index + 1 < DECODER_LAYERS
        fused = staged and heads_count == 4
        if not fused or not layer_index:
            scaled_a, inverse_a = norm_rows(hidden)
            normed_a = (scaled_a * gains[:1]).astype(jnp.bfloat16)
        if fused and layer_index:
            plane_normed_a, queries, pairs_all, *own_down_next = crossed
            plane_normed_a = plane_normed_a.reshape(all_tokens, width)
        elif fused:
            plane_normed_a, queries, pairs_all, own_down = project(
                normed_a,
                qkv_full,
                tile_cosine,
                tile_sine,
                w_down,
                layer_index,
                query_columns,
                pair_columns,
                resident,
            )
            plane_normed_a = plane_normed_a.reshape(all_tokens, width)
            own_down_next = [own_down]
        else:
            plane_normed_a, *own_down_next = exchange(
                ("head_gather", normed_a), *to_owner(w_down, layer_index)
            )
            plane_normed_a = plane_normed_a.reshape(all_tokens, width)
            narrow = qkv_full[:, : query_columns + pair_columns]
            projected = mm("td,de->te", plane_normed_a, narrow)
            queries = by_slot(
                rotate(projected[:, :query_columns], cosine, sine).astype(jnp.bfloat16)
            )
            pairs = projected[:, query_columns:].reshape(all_tokens, kv_local, 2, HEAD_SIZE)
            keys = rotate(pairs[:, :, 0].reshape(all_tokens, -1), cosine, sine)
            pairs = jnp.stack(
                [keys.reshape(all_tokens, kv_local, HEAD_SIZE), pairs[:, :, 1]], axis=2
            )
            pairs = pairs.reshape(all_tokens, pair_columns).astype(jnp.bfloat16)
            (pairs,) = exchange(("blk_pairs", pairs))
            pairs_all = pairs.reshape(
                blocks_count, heads_count, SEQUENCE_SLOTS, resident, pair_columns
            ).transpose(2, 1, 0, 3, 4)
        pairs_all = pairs_all.reshape(SEQUENCE_SLOTS, keys_total, pair_columns)
        (attended,) = attention_call(
            functools.partial(
                attend_kernel, heads_count, blocks_count, resident, group, kv_local
            ),
            info,
            [queries, pairs_all],
            [
                jax.ShapeDtypeStruct(
                    (heads_count, SEQUENCE_SLOTS, resident, query_columns), jnp.bfloat16
                )
            ],
            [],
            4 * rows_local * keys_total * query_columns,
            "attend",
        )
        attended = attended.reshape(all_tokens, query_columns)
        weight_sets = shared_weights(layer_index, middle if layer_index else wide)
        swaps = []
        if fused and staged:
            middle, scaled_b, inverse_b, *results = enter(
                attended,
                out_full,
                hidden,
                valid_column,
                gains[1:],
                turned_places,
                w_in,
                layer_index,
                weight_sets[0][0],
                swaps,
            )
            inverse_b = inverse_b[:, :1]
            results, own_in = results[:5], results[5]
            plane_rows, incoming, gate_up = unpack_in(results)
            weight_sets = [(own_in[None], owned_matrix(own_down_next[0]))] + weight_sets
        else:
            branch, *others = exchange(
                ("head_swap", head_parts(mm("tf,fd->td", attended, out_full))),
                *to_owner(w_in, layer_index),
            )
            own_in_next = others
            if owned:
                weight_sets = [
                    (owned_matrix(own_in_next[0]), owned_matrix(own_down_next[0]))
                ] + weight_sets
            middle = hidden + valid_column * head_sum(branch)
            scaled_b, inverse_b = norm_rows(middle)
            normed_b = (scaled_b * gains[1:]).astype(jnp.bfloat16)
            plane_rows, incoming, gate_up = moe_in(normed_b, turned_places, None, weight_sets, 0)
        units = [gated(part) for part in gate_up]
        logits = mm("td,ed->te", plane_rows, router_full)
        peaks = jnp.max(jnp.where(chosen, logits, negative), axis=-1, keepdims=True)
        lifted = jnp.where(chosen, jnp.exp(logits - peaks), 0.0)
        gates_all = lifted / jnp.sum(lifted, axis=-1, keepdims=True)
        plane_gates = lax.dynamic_slice_in_dim(
            gates_all, head_index * room, experts_local, 1
        )
        row_gates = mm("rt,te->re", turned_places, plane_gates.astype(jnp.bfloat16))
        row_gates = jnp.sum(row_gates * spread.T.astype(jnp.float32), axis=1, keepdims=True)
        if next_layer and fused:
            next_weights = attention_weights[layer_index + 1]
            (_, returned), norms, crossed = cross(
                combine_call(
                    units[0][0], units[1], places, row_gates, matrices(weight_sets, 1), False
                ),
                middle,
                valid_column,
                next_weights[3][:1],
                next_weights[0],
                tile_cosine,
                tile_sine,
                w_down,
                layer_index + 1,
                query_columns,
                pair_columns,
                resident,
            )
            returned = returned.reshape(-1, width)
        elif next_layer:
            mixture, returned = moe_out(units, places, row_gates, weight_sets)
        else:
            (mixture, returned), turned = moe_turn(
                units,
                places,
                turned_places,
                row_gates,
                (valid_column * cotangent.reshape(slot_rows, width)).astype(jnp.bfloat16),
                weight_sets,
            )
        stored_all.append(
            (
                weight_sets,
                places,
                scaled_a,
                inverse_a,
                plane_normed_a,
                queries,
                pairs_all,
                attended,
                scaled_b,
                inverse_b,
                plane_rows,
                gates_all,
                turned_places,
                row_gates,
                incoming,
                gate_up,
                units,
                returned,
            )
        )
        if next_layer and fused:
            hidden, scaled_a, inverse_a = norms
            inverse_a = inverse_a[:, :1]
        else:
            hidden = middle + valid_column * mixture
    result = (valid_column * hidden).astype(jnp.bfloat16).reshape(tokens.shape)
    grad_hidden = valid_column * cotangent.reshape(slot_rows, width).astype(jnp.float32)
    qkv_list = [None] * DECODER_LAYERS
    out_list = [None] * DECODER_LAYERS
    router_list = [None] * DECODER_LAYERS
    gains_list = [None] * DECODER_LAYERS
    expert_list = [None] * DECODER_LAYERS
    pending = []
    waiting = []
    for layer_index in reversed(range(DECODER_LAYERS)):
        qkv_full, out_full, router_full, gains = attention_weights[layer_index]
        (
            weight_sets,
            places,
            scaled_a,
            inverse_a,
            plane_normed_a,
            queries,
            pairs_all,
            attended,
            scaled_b,
            inverse_b,
            plane_rows,
            gates_all,
            turned_places,
            row_gates,
            incoming,
            gate_up,
            units,
            returned,
        ) = stored_all[layer_index]
        if layer_index + 1 < DECODER_LAYERS and not fused:
            turned = moe_in(
                (valid_column * grad_hidden).astype(jnp.bfloat16),
                turned_places,
                row_gates,
                weight_sets,
                1,
                waiting,
            )
        plane_grads, grad_produced, grad_units = turned
        onward = (
            grad_hidden,
            valid_column,
            gains[1:],
            scaled_b,
            jnp.broadcast_to(inverse_b, (slot_rows, 128)),
            lax.dynamic_slice_in_dim(gates_all, head_index * slot_rows, slot_rows, 0),
            router_full,
        )
        grad_normed_b, grad_gates, grad_weight_sets, departed = moe_back(
            places,
            weight_sets,
            gate_up,
            grad_units,
            incoming,
            units,
            grad_produced,
            plane_grads,
            returned,
            onward,
        )
        grad_gates = grad_gates.T
        grad_logits = gates_all * (
            grad_gates - jnp.sum(gates_all * grad_gates, axis=-1, keepdims=True)
        )
        plane_width = width // heads_count
        grad_router = mm(
            "td,te->de",
            lax.dynamic_slice_in_dim(plane_rows, head_index * plane_width, plane_width, 1),
            grad_logits.astype(jnp.bfloat16),
        )
        if fused:
            grad_middle, grad_gain_b, plane_branch, *own_grad_in = departed
            grad_gain_b = grad_gain_b[0]
            reached_terms = pending
        else:
            own_logits = lax.dynamic_slice_in_dim(
                grad_logits, head_index * slot_rows, slot_rows, 0
            )
            grad_normed_b = grad_normed_b + mm(
                "te,ed->td", own_logits.astype(jnp.bfloat16), router_full
            )
            grad_norm_b, grad_gain_b = norm_back(grad_normed_b, scaled_b, inverse_b, gains[1:])
            grad_middle = grad_hidden + grad_norm_b
            plane_branch, *own_grad_in = exchange(
                ("head_gather", (valid_column * grad_middle).astype(jnp.bfloat16)),
                *(from_owner(grad_weight_sets[0][0]) if owned else []),
                after=pending,
            )
            reached_terms = []
        plane_branch = plane_branch.reshape(all_tokens, width)
        pending = []
        shared_terms = []
        if owned_total < experts_local:
            shared_terms = [
                lax.psum_scatter(term, "blk", scatter_dimension=1, tiled=True)
                for term in grad_weight_sets[-1]
            ]
        plane_branch = plane_branch.reshape(all_tokens, width)
        grad_out_w = mm("tf,td->fd", attended, plane_branch)
        grad_attended = by_slot(mm("td,fd->tf", plane_branch, out_full).astype(jnp.bfloat16))
        grad_queries, grad_pairs = attention_call(
            functools.partial(
                attend_back_kernel, heads_count, blocks_count, resident, group, kv_local
            ),
            info,
            [queries, pairs_all, grad_attended],
            [
                jax.ShapeDtypeStruct(queries.shape, jnp.bfloat16),
                jax.ShapeDtypeStruct(pairs_all.shape, jnp.bfloat16),
            ],
            [pltpu.VMEM((keys_total, pair_columns), jnp.float32)],
            10 * rows_local * keys_total * query_columns,
            "attend_back",
        )
        grad_out_w = jnp.concatenate(
            [grad_out_w, jnp.pad(grad_router, ((0, 0), (0, small_columns - gate_lanes)))], axis=1
        ).astype(jnp.bfloat16)
        alone = fused and layer_index > 0
        last = fused and not layer_index
        if last:
            swapped = []
        elif alone:
            grad_out_w = lax.psum_scatter(grad_out_w, "blk", scatter_dimension=0, tiled=True)
            pending.append(grad_out_w)
            swapped = []
        else:
            swapped = [("blk_swap", grad_out_w.reshape(blocks_count, weight_rows, -1))]
        if owned:
            swapped += from_owner(grad_weight_sets[0][1])
        if fused:
            onward = None
            if layer_index:
                before = stored_all[layer_index - 1]
                onward = (
                    grad_middle,
                    valid_column,
                    gains[:1],
                    scaled_a,
                    jnp.broadcast_to(inverse_a, (slot_rows, 128)),
                    (before[STORED_TURNED], before[STORED_GATES], matrices(before[0], 1)),
                )
            (grad_projected, grad_normed_a, *others), further = unproject(
                grad_queries,
                grad_pairs.reshape(
                    SEQUENCE_SLOTS, heads_count, blocks_count // 2, 2, resident, pair_columns
                ),
                qkv_full,
                tile_cosine,
                tile_sine,
                [array for _, array in swapped],
                [*reached_terms, *(shared_terms if layer_index else [])],
                onward,
            )
            waiting = [] if layer_index else shared_terms
            grad_projected = grad_projected.reshape(all_tokens, -1)
            own_grad_down = others
        else:
            grad_pairs = (
                grad_pairs.reshape(
                    SEQUENCE_SLOTS, heads_count, blocks_count, resident, pair_columns
                )
                .transpose(2, 1, 0, 3, 4)
                .reshape(blocks_count, all_tokens, pair_columns)
            )
            (grad_pairs,) = exchange(("blk_swap", grad_pairs))
            grad_pairs = jnp.sum(grad_pairs.astype(jnp.float32), axis=0)
            grad_pairs = grad_pairs.astype(jnp.bfloat16).astype(jnp.float32)
            grad_pairs = grad_pairs.reshape(all_tokens, kv_local, 2, HEAD_SIZE)
            grad_keys = rotate(grad_pairs[:, :, 0].reshape(all_tokens, -1), cosine, -sine)
            grad_projected = jnp.concatenate(
                [
                    rotate(by_head(grad_queries).astype(jnp.float32), cosine, -sine),
                    jnp.stack(
                        [grad_keys.reshape(all_tokens, kv_local, HEAD_SIZE), grad_pairs[:, :, 1]],
                        axis=2,
                    ).reshape(all_tokens, pair_columns),
                ],
                axis=-1,
            ).astype(jnp.bfloat16)
            grad_normed_a, grad_out_w, *own_grad_down = exchange(
                (
                    "head_swap",
                    head_parts(
                        mm(
                            "te,de->td",
                            grad_projected,
                            qkv_full[:, : query_columns + pair_columns],
                        )
                    ),
                ),
                *swapped,
                after=shared_terms,
            )
            grad_normed_a = head_sum(grad_normed_a)
        if not last:
            grad_out_w = grad_out_w.astype(jnp.float32)
        if not alone and not last:
            grad_out_w = jnp.sum(grad_out_w, axis=0)
        if fused and layer_index:
            grad_hidden, grad_gain_a, *further = further
            grad_gain_a = grad_gain_a[0]
            turned = unpack_in(further)
        else:
            grad_norm_a, grad_gain_a = norm_back(grad_normed_a, scaled_a, inverse_a, gains[:1])
            grad_hidden = grad_middle + grad_norm_a
        grad_qkv = (
            mm("td,te->de", plane_normed_a, grad_projected)
            .astype(jnp.bfloat16)
            .reshape(heads_count, blocks_count, weight_rows, -1)
            .transpose(1, 0, 2, 3)
        )
        if layer_index:
            grad_qkv = lax.psum_scatter(
                grad_qkv.reshape(width, -1), "blk", scatter_dimension=0, tiled=True
            )
            pending.append(grad_qkv)
            qkv_list[layer_index] = grad_qkv
            gains_list[layer_index] = jnp.stack([grad_gain_a, grad_gain_b])
        else:
            gains_list[0] = jnp.stack([grad_gain_a, grad_gain_b])
            lanes = 2 * DECODER_LAYERS * weight_rows // 8
            grad_gains = (
                jnp.stack(gains_list)
                .reshape(2 * DECODER_LAYERS, heads_count, blocks_count, weight_rows)
                .transpose(1, 2, 0, 3)
                .reshape(heads_count, blocks_count, 8, lanes)
            )
            if last:
                (grad_qkv, grad_out_w), qkv_done, grad_gains = settle(
                    [grad_qkv, grad_out_w.reshape(blocks_count, weight_rows, -1)],
                    [term.reshape(heads_count, weight_rows, -1) for term in qkv_list[1:]],
                    jnp.pad(grad_gains, ((0, 0), (0, 0), (0, 0), (0, 128 - lanes))),
                    waiting,
                )
                grad_gains = grad_gains[..., :lanes]
            else:
                grad_gains = grad_gains.reshape(heads_count, 1, -1)
                grad_qkv, grad_gains, *qkv_done = exchange(
                    ("blk_swap", grad_qkv),
                    ("head_swap", grad_gains),
                    *(
                        ("head_swap", term.reshape(heads_count, weight_rows, -1))
                        for term in qkv_list[1:]
                    ),
                    after=waiting,
                )
                grad_qkv = jnp.sum(grad_qkv.astype(jnp.float32), axis=0).astype(jnp.bfloat16)
                grad_gains = jnp.sum(grad_gains, axis=0).reshape(blocks_count, 1, -1)
                grad_qkv, grad_gains = exchange(
                    ("head_swap", grad_qkv.reshape(heads_count, weight_rows, -1)),
                    ("blk_swap", grad_gains),
                )
            qkv_list = [grad_qkv, *qkv_done]
            qkv_list = [
                jnp.concatenate(
                    [
                        term[..., :query_columns].transpose(1, 0, 2).reshape(weight_rows, -1),
                        term[..., query_columns:].transpose(1, 0, 2).reshape(weight_rows, -1),
                    ],
                    axis=1,
                ).astype(jnp.float32)
                for term in qkv_list
            ]
            grad_gains = jnp.sum(grad_gains, axis=0).reshape(DECODER_LAYERS, 2, weight_rows)

        out_list[layer_index] = grad_out_w[:, :width]
        router_list[layer_index] = (
            grad_out_w[:, width : width + gate_lanes]
            .reshape(weight_rows, heads_count, room)[:, :, :experts_local]
            .reshape(weight_rows, EXPERTS)
        )
        terms = []
        for number, received in enumerate((own_grad_in, own_grad_down)):
            parts = owned_rows(received[0]) if owned else []
            if owned_total < experts_local:
                parts.append(shared_terms[number])
            terms.append(jnp.concatenate(parts, axis=0).astype(jnp.float32))
        expert_list[layer_index] = tuple(terms)
    return (
        result,
        grad_hidden.reshape(tokens.shape),
        jnp.stack(qkv_list),
        jnp.stack(out_list),
        jnp.stack(router_list),
        grad_gains[:, 0],
        grad_gains[:, 1],
        jnp.stack([terms[0] for terms in expert_list]),
        jnp.stack([terms[1] for terms in expert_list]),
    )


def solution(mesh):
    in_specs = (
        P(None, ("head", "blk"), None),
        P(),
        P(None, None, ("head", "blk"), None),
        P(None, None, ("head", "blk"), None),
        P(None, ("head", "blk"), None),
        P(None, ("head", "blk"), None),
        P(None, ("head", "blk"), None),
        P(None, None, ("head", "blk")),
        P(None, "head", "blk", None),
        P(None, "head", "blk", None),
        P(None, ("head", "blk"), None),
    )
    out_specs = (
        P(None, ("head", "blk"), None),
        P(None, ("head", "blk"), None),
        P(None, ("head", "blk"), None),
        P(None, ("head", "blk"), None),
        P(None, ("head", "blk"), None),
        P(None, ("head", "blk")),
        P(None, ("head", "blk")),
        P(None, "head", "blk", None),
        P(None, "head", "blk", None),
    )
    return jax.shard_map(shards, mesh=mesh, in_specs=in_specs, out_specs=out_specs, check_vma=False)
```
